32 devices in a mesh: head: 2 (over x), blk: 16 (over z, y, core).
Axes of the slice: x: 2, y: 2, z: 4, core: 2. Of those that a mesh axis runs over, the one named last changes fastest.
Arguments:
- states: bfloat16 [16, 2, 128, 1536], P('blk', 'head'), may hold values from -6 to 6
- teacher: bfloat16 [16, 2, 128, 1536], P('blk', 'head'), may hold values from -6 to 6
- valid: int32 [16, 2, 128], P('blk', 'head'), may hold values from 0 to 1
- routes: int32 [16, 2, 128, 4], P('blk', 'head'), may hold values from 0 to 7, all different within a row; in each aligned block of 128 rows (0 to 127, 128 to 255, ..., all dimensions but the last counted through in order) at most 96 rows name the same one
- gates: float32 [16, 2, 128, 4], P('blk', 'head'), may hold values from 0.1 to 0.4
- doc_starts: int32 [3], replicated, may hold values from 0 to 4095, as said below
- norm_one: bfloat16 [1536], P(('head', 'blk')), may hold values from 0.5 to 1.5
- w_query: bfloat16 [1536, 1536], P(('head', 'blk')), may hold values from -0.15625 to 0.15625
- key_weight: bfloat16 [1536, 256], P(('head', 'blk')), may hold values from -0.15625 to 0.15625
- value_weight: bfloat16 [1536, 256], P(('head', 'blk')), may hold values from -0.15625 to 0.15625
- w_output: bfloat16 [1536, 1536], P(('head', 'blk')), may hold values from -1.25 to 1.25
- norm_two: bfloat16 [1536], P(('head', 'blk')), may hold values from 0.5 to 1.5
- expert_in: bfloat16 [8, 1536, 1536], P(None, ('head', 'blk')), may hold values from -0.15625 to 0.15625
- expert_out: bfloat16 [8, 768, 1536], P(None, ('head', 'blk')), may hold values from -0.625 to 0.625
Outputs:
- final_states: bfloat16 [16, 2, 128, 1536], P('blk', 'head')
- loss: float32 [], replicated
- grad_states: float32 [16, 2, 128, 1536], P('blk', 'head')
- grad_norm_one: float32 [1536], P(('head', 'blk'))
- grad_query: float32 [1536, 1536], P(('head', 'blk'))
- grad_key: float32 [1536, 256], P(('head', 'blk'))
- grad_value: float32 [1536, 256], P(('head', 'blk'))
- grad_output: float32 [1536, 1536], P(('head', 'blk'))
- grad_norm_two: float32 [1536], P(('head', 'blk'))
- grad_expert_in: float32 [8, 1536, 1536], P(None, ('head', 'blk'))
- grad_expert_out: float32 [8, 768, 1536], P(None, ('head', 'blk'))
The draws below stay inside these ranges and needn't reach their ends.
Inputs may be any that keep to these rules, and one draw needn't show every extreme that they name: `routes`: at most 96 of one device's rows name one expert, and some expert reaches 96. `doc_starts`: strictly rising, the first is 0.
All inputs are finite; a program needn't handle non-finite values.
Results may differ from the reference program's by a relative error of at most 0.019.
Values may be sent and summed in bfloat16 or wider, within the bound.
A program may use at most 448 MiB of HBM per device.

```python
import math
import jax
import jax.numpy as jnp
import numpy as np
from jax import lax

MODEL_WIDTH = 1536
F = 768
QUERY_HEADS = 12
KEY_VALUE_HEADS = 2
HEAD_SIZE = 128
TOP = 4
E = 8
TOK_DEV = 128
CAP = 96
BLOCKS = 16
PAIRS = 2
TOKENS = 4096


def draw_valid(key, part):
    key = jax.random.fold_in(key, 11)
    token_count = BLOCKS * PAIRS * TOK_DEV
    where = jnp.arange(token_count, dtype=jnp.int32)
    level = 250 + 550 * where // token_count
    roll = jax.random.randint(key, (token_count,), 0, 1000)
    return (roll < level).astype(jnp.int32).reshape(BLOCKS, PAIRS, TOK_DEV)


def draw_doc_starts(key, part):
    key = jax.random.fold_in(key, 13)
    first_key, second_key = jax.random.split(key)
    total = BLOCKS * PAIRS * TOK_DEV
    first = jax.random.randint(first_key, (), 1, TOK_DEV)
    second = jax.random.randint(second_key, (), total - TOK_DEV + 1, total)
    return jnp.stack([jnp.zeros((), jnp.int32), first.astype(jnp.int32), second.astype(jnp.int32)]).astype(jnp.int32)


def level_of(stream_key, extent, cuts, least, high):
    loudness = 1.0
    for position, blocks in cuts:
        heights = jax.random.uniform(jax.random.fold_in(jax.random.fold_in(stream_key, 6), position), (blocks,), jnp.float32, least / len(cuts), high / len(cuts))
        loudness = loudness * jnp.repeat(jnp.exp(heights), extent[position] // blocks).reshape((-1,) + (1,) * (len(extent) - 1 - position))
    return loudness


def assign_block(key, own, number, rows, number_of, top, reach, skew):
    sequence = jax.random.permutation(key, number_of)
    packed, usual = load_shares(number_of, rows * top, reach, skew, True), load_shares(number_of, rows * top, reach, skew, False)
    places = jnp.arange(number_of)

    def named(tallies, offset_by):
        used = int((tallies > 0).sum())
        fixed = max(1, used // 4)
        shifted = fixed + (places - fixed + offset_by * (used - fixed)) % max(1, number_of - fixed)
        return jnp.zeros((number_of,), jnp.int32).at[sequence[jnp.where(places < fixed, places, shifted)]].set(jnp.asarray(tallies, jnp.int32))

    tallies = jnp.where(number % 4 == 0, named(packed, number // 4), named(usual, number - number // 4 - 1))
    mixed = jax.random.permutation(jax.random.fold_in(own, 3), number_of)
    giver, sink = mixed[0:number_of // 2 * 2:2], mixed[1:number_of // 2 * 2:2]
    slack = jnp.minimum(tallies[giver] - 1, reach - tallies[sink]) // 2
    slack = jnp.where((giver == sequence[0]) | (sink == sequence[0]) | (tallies[sink] == 0), 0, jnp.maximum(slack, 0))
    shifted = jax.random.randint(jax.random.fold_in(own, 4), (number_of // 2,), 0, 1 << 20) % (slack + 1)
    tallies = tallies.at[giver].add(-shifted).at[sink].add(shifted)
    members = jnp.searchsorted(jnp.cumsum(tallies), jnp.arange(rows * top), side="right").astype(jnp.int32)
    grid = members.reshape(top, rows).T
    grid = grid[jax.random.permutation(jax.random.fold_in(own, 1), rows)]
    offset_by = jax.random.randint(jax.random.fold_in(own, 2), (rows, 1), 0, top)
    return jnp.take_along_axis(grid, (jnp.arange(top)[None, :] + offset_by) % top, axis=1)


def load_shares(amount, total, bound, lean, full):
    portions = [(1 << 20) // math.isqrt(standing ** lean) + 1 for standing in range(1, amount + 1)]
    largest = bound if full else min(bound, max(-(-total // amount), total * portions[0] // sum(portions)))
    least = 1 if total - largest >= amount - 1 else 0
    counts, surplus = [largest] + [least] * (amount - 1), total - largest - least * (amount - 1)
    while surplus > 0:
        free = [i for i in range(1, amount) if counts[i] < largest] or [i for i in range(1, amount) if counts[i] < bound]
        whole, budget = sum([portions[i] for i in free]), surplus
        for i in free:
            extra = min(bound - counts[i], max(1, budget * portions[i] // whole), surplus)
            counts[i] = counts[i] + extra
            surplus = surplus - extra
    return np.array(counts)


def scatter_about(rng, dims, spread, reach, cuts=(), held_as=jnp.bfloat16):
    drawn = spread * jax.random.normal(rng, dims, jnp.float32)
    if cuts:
        drawn = drawn * level_of(rng, dims, cuts, -0.22, 0.18)
    return jnp.clip(drawn, -reach, reach).astype(held_as)


def setup_inputs(seed: int = 0) -> dict:
    seeds = jax.random.split(jax.random.key(seed), 15)
    states = scatter_about(seeds[0], (BLOCKS, PAIRS, TOK_DEV, MODEL_WIDTH), 1.0, 6.0, ((0, 16), (1, 2)))
    teacher = scatter_about(seeds[1], (BLOCKS, PAIRS, TOK_DEV, MODEL_WIDTH), 1.0, 6.0, ((0, 16), (1, 2)))
    valid = draw_valid(jax.random.fold_in(seeds[14], 71), 0)
    routes_keys = jax.random.split(jax.random.fold_in(seeds[3], 1), BLOCKS * PAIRS * TOK_DEV // TOK_DEV)
    routes_turns = jax.random.permutation(jax.random.fold_in(seeds[3], 3), BLOCKS * PAIRS * TOK_DEV // TOK_DEV)
    routes = jax.vmap(lambda own, number: assign_block(jax.random.fold_in(seeds[3], 2), own, number, TOK_DEV, E, TOP, CAP, 1))(routes_keys, routes_turns).reshape((BLOCKS, PAIRS, TOK_DEV, TOP))
    gates = jnp.clip(0.1 + 0.3 * jax.random.uniform(seeds[4], (BLOCKS, PAIRS, TOK_DEV, TOP), jnp.float32) ** level_of(seeds[4], (BLOCKS, PAIRS, TOK_DEV, TOP), ((0, 16), (1, 2)), -0.2, 0.2), 0.1, 0.4)
    doc_starts = draw_doc_starts(jax.random.fold_in(seeds[14], 71), 0)
    norm_one = jnp.clip(1.0 + 0.1 * jax.random.normal(seeds[6], (MODEL_WIDTH,), jnp.float32), 0.5, 1.5).astype(jnp.bfloat16)
    w_query = scatter_about(seeds[7], (MODEL_WIDTH, QUERY_HEADS * HEAD_SIZE), MODEL_WIDTH ** -0.5, 0.15625, ((0, 32),))
    key_weight = scatter_about(seeds[8], (MODEL_WIDTH, KEY_VALUE_HEADS * HEAD_SIZE), MODEL_WIDTH ** -0.5, 0.15625, ((0, 32),))
    value_weight = scatter_about(seeds[9], (MODEL_WIDTH, KEY_VALUE_HEADS * HEAD_SIZE), MODEL_WIDTH ** -0.5, 0.15625, ((0, 32),))
    w_output = scatter_about(seeds[10], (QUERY_HEADS * HEAD_SIZE, MODEL_WIDTH), (QUERY_HEADS * HEAD_SIZE // 64) ** -0.5, 1.25, ((0, 32),))
    norm_two = jnp.clip(1.0 + 0.1 * jax.random.normal(seeds[11], (MODEL_WIDTH,), jnp.float32), 0.5, 1.5).astype(jnp.bfloat16)
    expert_in = scatter_about(seeds[12], (E, MODEL_WIDTH, 2 * F), MODEL_WIDTH ** -0.5, 0.15625, ((1, 32),))
    expert_out = scatter_about(seeds[13], (E, F, MODEL_WIDTH), (F // 8) ** -0.5, 0.625, ((1, 32),))
    return {"states": states, "teacher": teacher, "valid": valid, "routes": routes, "gates": gates, "doc_starts": doc_starts, "norm_one": norm_one, "w_query": w_query, "key_weight": key_weight, "value_weight": value_weight, "w_output": w_output, "norm_two": norm_two, "expert_in": expert_in, "expert_out": expert_out}


ROTARY_BASE = 10000.0
FLOOR_SCORE = -1e+30

@jax.custom_vjp
def reduced_precision(v):
    return lax.optimization_barrier(v.astype(jnp.bfloat16)).astype(jnp.float32)

@jax.custom_vjp
def low_back(v):
    return v

def low_keep(v):
    return (reduced_precision(v), None)

def low_pass(kept, grad):
    return (grad,)

def back_keep(v):
    return (v, None)

def back_low(kept, grad):
    return (reduced_precision(grad),)
reduced_precision.defvjp(low_keep, low_pass)
low_back.defvjp(back_keep, back_low)

def multiply(left, right):
    return jnp.dot(left, right, precision=lax.Precision.HIGHEST, preferred_element_type=jnp.float32)

def rms_norm(values, gain):
    scale = lax.rsqrt(lax.optimization_barrier(jnp.mean(values * values, axis=-1, keepdims=True)) + 1e-06)
    return values * scale * gain

def rotary_apply(values, where, sign):
    half = values.shape[-1] // 2
    freq = ROTARY_BASE ** (-jnp.arange(half).astype(jnp.float32) / half)
    angle = where.astype(jnp.float32)[:, None] * freq[None, :]
    cosine = jnp.cos(angle)[:, None, :]
    sine = jnp.sin(angle)[:, None, :] * sign
    first = values[..., :half]
    second = values[..., half:]
    return jnp.concatenate([first * cosine - second * sine, second * cosine + first * sine], axis=-1)

def doc_layout(position_index, doc_starts):
    inside = (position_index[:, None] >= doc_starts[None, :]).astype(jnp.int32)
    document_segment = lax.optimization_barrier(jnp.sum(inside, axis=-1)) - 1
    begin = lax.optimization_barrier(jnp.max(jnp.where(inside > 0, doc_starts[None, :], 0), axis=-1))
    return (document_segment, position_index - begin)

def gated(pair):
    half = pair.shape[-1] // 2
    return jax.nn.gelu(pair[..., :half], approximate=True) * pair[..., half:]

def attention_layer(query_rotated, key_rotated, value_reduced, document_segment, position_index):
    token_count = query_rotated.shape[0]
    block_size = min(512, token_count)
    head_group = QUERY_HEADS // KEY_VALUE_HEADS
    query_block_list = query_rotated.reshape(token_count // block_size, block_size, KEY_VALUE_HEADS, head_group, HEAD_SIZE)
    index_blocks = position_index.reshape(token_count // block_size, block_size)
    segment_blocks = document_segment.reshape(token_count // block_size, block_size)

    def one_block(item):
        queries, rows_index, rows_segment = item
        raw = jnp.einsum('qgjd,kgd->gjqk', queries, key_rotated, precision=lax.Precision.HIGHEST) * HEAD_SIZE ** (-0.5)
        raw = low_back(raw)
        allowed = (position_index[None, :] <= rows_index[:, None]) & (document_segment[None, :] == rows_segment[:, None])
        masked = jnp.where(allowed[None, None], raw, FLOOR_SCORE)
        top = lax.optimization_barrier(jnp.max(masked, axis=-1, keepdims=True))
        expo = jnp.exp(masked - top)
        probs = reduced_precision(expo / lax.optimization_barrier(jnp.sum(expo, axis=-1, keepdims=True)))
        return jnp.einsum('gjqk,kgd->qgjd', probs, value_reduced, precision=lax.Precision.HIGHEST)
    mixed_output = lax.map(jax.checkpoint(one_block), (query_block_list, index_blocks, segment_blocks))
    return mixed_output.reshape(token_count, QUERY_HEADS * HEAD_SIZE)

def forward(inputs, weights, token_position, document_segment, position_index, dense_gates):
    gain_one, query_w, key_w, value_w, out_w, gain_two, up_w, down_w = weights
    token_count = inputs.shape[0]
    normed = reduced_precision(rms_norm(inputs, gain_one))
    query_lin = low_back(multiply(normed, query_w))
    key_linear = low_back(multiply(normed, key_w))
    value_reduced = low_back(reduced_precision(multiply(normed, value_w)))
    query_rotated = reduced_precision(rotary_apply(query_lin.reshape(token_count, QUERY_HEADS, HEAD_SIZE), token_position, 1.0))
    key_rotated = reduced_precision(rotary_apply(key_linear.reshape(token_count, KEY_VALUE_HEADS, HEAD_SIZE), token_position, 1.0))
    mixed_output = attention_layer(query_rotated, key_rotated, value_reduced.reshape(token_count, KEY_VALUE_HEADS, HEAD_SIZE), document_segment, position_index)
    mixed_output = low_back(reduced_precision(mixed_output))
    residual = inputs + low_back(multiply(mixed_output, out_w))
    normed_two = reduced_precision(rms_norm(residual, gain_two))
    total = residual
    for expert in range(E):
        pair = low_back(multiply(normed_two, up_w[expert]))
        hidden = reduced_precision(gated(pair))
        result = low_back(multiply(hidden, down_w[expert]))
        total = total + dense_gates[:, expert:expert + 1] * result
    return total

def reference(states, teacher, valid, routes, gates, doc_starts, norm_one, w_query, key_weight, value_weight, w_output, norm_two, expert_in, expert_out):
    inputs = states.reshape(-1, MODEL_WIDTH).astype(jnp.float32)
    target = teacher.reshape(-1, MODEL_WIDTH).astype(jnp.float32)
    keep_mask = valid.reshape(-1).astype(jnp.float32)
    route_rows = routes.reshape(-1, TOP)
    gate_rows = gates.reshape(-1, TOP).astype(jnp.float32)
    position_index = jnp.arange(inputs.shape[0]).astype(jnp.int32)
    document_segment, token_position = doc_layout(position_index, doc_starts.astype(jnp.int32))
    experts_range = jnp.arange(E).astype(jnp.int32)
    dense_gates = lax.optimization_barrier(jnp.sum(gate_rows[:, :, None] * (route_rows[:, :, None] == experts_range[None, None, :]).astype(jnp.float32), axis=1))
    weights = tuple((item.astype(jnp.float32) for item in (norm_one, w_query, key_weight, value_weight, w_output, norm_two, expert_in, expert_out)))

    def run(inputs_in, *weights_in):
        return forward(inputs_in, weights_in, token_position, document_segment, position_index, dense_gates)
    final, pull = jax.vjp(run, inputs, *weights)
    token_count = jnp.sum(keep_mask)
    diff = final - target
    loss = jnp.sum(keep_mask * lax.optimization_barrier(jnp.sum(diff * diff, axis=-1))) / (MODEL_WIDTH * token_count)
    grad_final = keep_mask[:, None] * diff * (TOKENS / token_count)
    grads = pull(grad_final)
    shape = states.shape
    return (final.astype(jnp.bfloat16).reshape(shape), loss, grads[0].reshape(shape), grads[1], grads[2], grads[3], grads[4], grads[5], grads[6], grads[7], grads[8])
```

```python
import functools

import jax
import jax.numpy as jnp
from jax import lax
from jax.experimental import pallas as pl
from jax.experimental.pallas import tpu as pltpu
from jax.sharding import PartitionSpec as P

QUERY_HEADS = 12
KEY_VALUE_HEADS = 2
HEAD_SIZE = 128
TOP = 4
E = 8
CAP = 96

ROTARY_BASE = 10000.0
FLOOR_SCORE = -1e30

MESH = pl.DeviceIdType.MESH
NZ = 4
BF = jnp.bfloat16
F32 = jnp.float32

def product(left, right):
    return jnp.dot(left, right, preferred_element_type=jnp.float32)


def rms_norm(values, gain):
    scale = lax.rsqrt(jnp.mean(values * values, axis=-1, keepdims=True) + 1e-06)
    return values * scale * gain


def rotary_apply(values, where, sign):
    half = values.shape[-1] // 2
    freq = ROTARY_BASE ** (-jnp.arange(half).astype(jnp.float32) / half)
    angle = where.astype(jnp.float32)[:, None] * freq[None, :]
    cosine = jnp.cos(angle)[:, None, :]
    sine = jnp.sin(angle)[:, None, :] * sign
    first = values[..., :half]
    second = values[..., half:]
    return jnp.concatenate(
        [first * cosine - second * sine, second * cosine + first * sine], axis=-1
    )


def doc_layout(position_index, doc_starts):
    inside = (position_index[:, None] >= doc_starts[None, :]).astype(jnp.int32)
    document_segment = jnp.sum(inside, axis=-1) - 1
    begin = jnp.max(jnp.where(inside > 0, doc_starts[None, :], 0), axis=-1)
    return (document_segment, position_index - begin)


def gated(pair):
    half = pair.shape[-1] // 2
    return jax.nn.gelu(pair[..., :half], approximate=True) * pair[..., half:]


def in_blocks(step_fn, carry, piece, rows):
    count_blocks = piece[0].shape[0] // rows

    def turn(number, state):
        part = tuple((lax.dynamic_slice_in_dim(item, number * rows, rows, 0) for item in piece))
        return step_fn(state, part, number * rows)

    return lax.fori_loop(0, count_blocks, turn, carry)


def per_device_plain(
    states,
    teacher,
    valid,
    routes,
    gates,
    doc_starts,
    norm_one,
    w_query,
    key_weight,
    value_weight,
    w_output,
    norm_two,
    expert_in,
    expert_out,
):
    count_per_token = states.shape[2]
    width = states.shape[3]
    pairs = lax.axis_size("head")
    blocks = lax.axis_size("blk")
    rows = count_per_token * pairs
    span = rows * blocks
    head_group = QUERY_HEADS // KEY_VALUE_HEADS
    scale = HEAD_SIZE ** (-0.5)
    highest = lax.Precision.HIGHEST
    block_index = lax.axis_index("blk")
    pair_index = lax.axis_index("head")
    token_index = (block_index * pairs + pair_index) * count_per_token + jnp.arange(
        count_per_token, dtype=jnp.int32
    )
    unused_segment, token_position = doc_layout(token_index, doc_starts)
    query_index = block_index * rows + jnp.arange(rows, dtype=jnp.int32)
    query_segment, query_where = doc_layout(query_index, doc_starts)
    last_query = block_index * rows + rows - 1
    inputs = states.reshape(count_per_token, width).astype(jnp.float32)
    target = teacher.reshape(count_per_token, width).astype(jnp.float32)
    keep_mask = valid.reshape(count_per_token).astype(jnp.float32)
    route_rows = routes.reshape(count_per_token, TOP)
    gate_rows = gates.reshape(count_per_token, TOP)
    query_w, key_w, value_w, out_w, gain_low_one, gain_low_two = (
        lax.all_gather(w_query, ("head", "blk"), axis=0, tiled=True),
        lax.all_gather(key_weight, ("head", "blk"), axis=0, tiled=True),
        lax.all_gather(value_weight, ("head", "blk"), axis=0, tiled=True),
        lax.all_gather(w_output, ("head", "blk"), axis=0, tiled=True),
        lax.all_gather(norm_one, ("head", "blk"), axis=0, tiled=True),
        lax.all_gather(norm_two, ("head", "blk"), axis=0, tiled=True),
    )
    gain_one = gain_low_one.astype(jnp.float32)
    gain_two = gain_low_two.astype(jnp.float32)
    normed_one = rms_norm(inputs, gain_one)
    normed_low = normed_one.astype(jnp.bfloat16)
    query_lin = product(normed_low, query_w)
    key_linear = product(normed_low, key_w)
    value_linear = product(normed_low, value_w)
    query_rotated = rotary_apply(
        query_lin.reshape(count_per_token, QUERY_HEADS, HEAD_SIZE), token_position, 1.0
    )
    key_rotated = rotary_apply(
        key_linear.reshape(count_per_token, KEY_VALUE_HEADS, HEAD_SIZE), token_position, 1.0
    )
    query_outgoing = query_rotated.astype(jnp.bfloat16).reshape(
        count_per_token, KEY_VALUE_HEADS, head_group * HEAD_SIZE
    )
    key_send = key_rotated.astype(jnp.bfloat16)
    value_outgoing = value_linear.astype(jnp.bfloat16).reshape(
        count_per_token, KEY_VALUE_HEADS, HEAD_SIZE
    )
    query_grp, key_grp, value_grp = (
        lax.all_to_all(query_outgoing, "head", split_axis=1, concat_axis=0, tiled=True),
        lax.all_to_all(key_send, "head", split_axis=1, concat_axis=0, tiled=True),
        lax.all_to_all(value_outgoing, "head", split_axis=1, concat_axis=0, tiled=True),
    )
    query_heads = query_grp.reshape(rows, head_group, HEAD_SIZE)
    key_rows = key_grp.reshape(rows, HEAD_SIZE)
    value_rows = value_grp.reshape(rows, HEAD_SIZE)

    def scores_for(keys, start):
        block_size = keys.shape[0]
        key_index = start + jnp.arange(block_size, dtype=jnp.int32)
        key_segment, unused_where = doc_layout(key_index, doc_starts)
        allowed = (key_index[None, :] <= query_index[:, None]) & (
            key_segment[None, :] == query_segment[:, None]
        )
        raw = (
            jnp.einsum("qhd,kd->hqk", query_heads, keys, preferred_element_type=jnp.float32) * scale
        )
        return (raw, allowed[None])

    def attend(carry, piece, start):
        keys, values = piece

        def work(state):
            running, total, accum = state
            raw, allowed = scores_for(keys, start)
            masked = jnp.where(allowed, raw, FLOOR_SCORE)
            newest = jnp.maximum(running, jnp.max(masked, axis=-1))
            factor = jnp.exp(running - newest)
            weights = jnp.where(allowed, jnp.exp(masked - newest[..., None]), 0.0)
            total = total * factor + jnp.sum(weights, axis=-1)
            update = jnp.einsum(
                "hqk,kd->qhd",
                weights.astype(jnp.bfloat16),
                values,
                preferred_element_type=jnp.float32,
            )
            accum = accum * factor.T[:, :, None] + update
            return (newest, total, accum)

        return lax.cond(start <= last_query, work, lambda state: state, carry)

    start_state = (
        jnp.full((head_group, rows), FLOOR_SCORE, jnp.float32),
        jnp.zeros((head_group, rows), jnp.float32),
        jnp.zeros((rows, head_group, HEAD_SIZE), jnp.float32),
    )
    running, total, accum = in_blocks(
        attend,
        start_state,
        (
            lax.all_gather(key_rows, "blk", axis=0, tiled=True),
            lax.all_gather(value_rows, "blk", axis=0, tiled=True),
        ),
        rows,
    )
    attn_full = accum / total.T[:, :, None]
    log_total = running + jnp.log(total)
    out_send = attn_full.astype(jnp.bfloat16).reshape(rows, 1, head_group * HEAD_SIZE)
    out_tok = lax.all_to_all(out_send, "head", split_axis=0, concat_axis=1, tiled=True).reshape(
        count_per_token, QUERY_HEADS * HEAD_SIZE
    )
    residual = inputs + product(out_tok, out_w)
    normed_two = rms_norm(residual, gain_two)
    normed_two_low = normed_two.astype(jnp.bfloat16)
    up_w, down_w = (
        lax.all_gather(expert_in, ("head", "blk"), axis=1, tiled=True),
        lax.all_gather(expert_out, ("head", "blk"), axis=1, tiled=True),
    )
    route_hot = (route_rows[:, :, None] == jnp.arange(E, dtype=jnp.int32)[None, None, :]).astype(
        jnp.int32
    )
    flat_hot = route_hot.reshape(count_per_token * TOP, E)
    before = jnp.cumsum(flat_hot, axis=0) - flat_hot
    slot = jnp.sum(before * flat_hot, axis=-1).reshape(count_per_token, TOP)
    slot_hot = (slot[:, :, None] == jnp.arange(CAP, dtype=jnp.int32)[None, None, :]).astype(
        jnp.float32
    )
    route_float = route_hot.astype(jnp.float32)
    dispatch = jnp.einsum("tje,tjc->ect", route_float, slot_hot, precision=highest)
    combine = jnp.einsum("tje,tjc,tj->ect", route_float, slot_hot, gate_rows, precision=highest)
    expert_rows = jnp.einsum(
        "ect,td->ecd",
        dispatch.astype(jnp.bfloat16),
        normed_two_low,
        preferred_element_type=jnp.float32,
    ).astype(jnp.bfloat16)
    pair = jnp.einsum("ecd,edf->ecf", expert_rows, up_w, preferred_element_type=jnp.float32)
    hidden_low = gated(pair).astype(jnp.bfloat16)
    expert_result = jnp.einsum(
        "ecf,efd->ecd", hidden_low, down_w, preferred_element_type=jnp.float32
    )
    mixture = jnp.einsum("ect,ecd->td", combine, expert_result, precision=highest)
    final = residual + mixture
    diff = final - target
    local_count = jnp.sum(keep_mask)
    local_error = jnp.sum(keep_mask * jnp.sum(diff * diff, axis=-1))
    count_all, error_all = lax.psum((local_count, local_error), ("head", "blk"))
    loss = error_all / (width * count_all)
    grad_final = keep_mask[:, None] * diff * (span * 1.0 / count_all)
    up_back, down_back = (
        lax.all_gather(expert_in, ("head", "blk"), axis=1, tiled=True),
        lax.all_gather(expert_out, ("head", "blk"), axis=1, tiled=True),
    )
    grad_result = jnp.einsum("ect,td->ecd", combine, grad_final, precision=highest).astype(
        jnp.bfloat16
    )
    grad_down = jnp.einsum(
        "ecf,ecd->efd", hidden_low, grad_result, preferred_element_type=jnp.float32
    )
    grad_hidden = jnp.einsum(
        "ecd,efd->ecf", grad_result, down_back, preferred_element_type=jnp.float32
    )
    unused_value, pull_gate = jax.vjp(gated, pair)
    grad_pair = pull_gate(grad_hidden)[0].astype(jnp.bfloat16)
    grad_up = jnp.einsum("ecd,ecf->edf", expert_rows, grad_pair, preferred_element_type=jnp.float32)
    grad_rows = jnp.einsum("ecf,edf->ecd", grad_pair, up_back, preferred_element_type=jnp.float32)
    grad_normed_two = jnp.einsum("ect,ecd->td", dispatch, grad_rows, precision=highest)
    unused_value, pull_two = jax.vjp(rms_norm, residual, gain_two)
    grad_res_norm, grad_gain_two = pull_two(grad_normed_two)
    grad_residual = grad_final + grad_res_norm
    grad_attn_low = grad_residual.astype(jnp.bfloat16)
    grad_out_w = jnp.einsum("tk,td->kd", out_tok, grad_attn_low, preferred_element_type=jnp.float32)
    output_gradient_token = jnp.einsum(
        "td,kd->tk", grad_attn_low, out_w, preferred_element_type=jnp.float32
    ).astype(jnp.bfloat16)
    grad_out_grp = lax.all_to_all(
        output_gradient_token.reshape(count_per_token, KEY_VALUE_HEADS, head_group * HEAD_SIZE),
        "head",
        split_axis=1,
        concat_axis=0,
        tiled=True,
    ).reshape(rows, head_group, HEAD_SIZE)
    delta = jnp.einsum(
        "qhd,qhd->hq", grad_out_grp.astype(jnp.float32), attn_full, precision=highest
    )

    def attend_back(carry, piece, start):
        keys, values = piece

        def work(state):
            grad_query, grad_keys, grad_values = state
            raw, allowed = scores_for(keys, start)
            weights = jnp.where(allowed, jnp.exp(raw - log_total[..., None]), 0.0)
            grad_weights = jnp.einsum(
                "qhd,kd->hqk", grad_out_grp, values, preferred_element_type=jnp.float32
            )
            grad_raw = (weights * (grad_weights - delta[..., None])).astype(jnp.bfloat16)
            grad_query = (
                grad_query
                + jnp.einsum("hqk,kd->qhd", grad_raw, keys, preferred_element_type=jnp.float32)
                * scale
            )
            key_part = (
                jnp.einsum("hqk,qhd->kd", grad_raw, query_heads, preferred_element_type=jnp.float32)
                * scale
            )
            value_part = jnp.einsum(
                "hqk,qhd->kd",
                weights.astype(jnp.bfloat16),
                grad_out_grp,
                preferred_element_type=jnp.float32,
            )
            block_size = keys.shape[0]
            grad_keys = lax.dynamic_update_slice_in_dim(
                grad_keys,
                lax.dynamic_slice_in_dim(grad_keys, start, block_size, 0) + key_part,
                start,
                0,
            )
            grad_values = lax.dynamic_update_slice_in_dim(
                grad_values,
                lax.dynamic_slice_in_dim(grad_values, start, block_size, 0) + value_part,
                start,
                0,
            )
            return (grad_query, grad_keys, grad_values)

        return lax.cond(start <= last_query, work, lambda state: state, carry)

    back_state = (
        jnp.zeros((rows, head_group, HEAD_SIZE), jnp.float32),
        jnp.zeros((span, HEAD_SIZE), jnp.float32),
        jnp.zeros((span, HEAD_SIZE), jnp.float32),
    )
    grad_query, grad_keys_full, grad_values_full = in_blocks(
        attend_back,
        back_state,
        (
            lax.all_gather(key_rows, "blk", axis=0, tiled=True),
            lax.all_gather(value_rows, "blk", axis=0, tiled=True),
        ),
        rows,
    )
    grad_keys, grad_values = (
        lax.psum_scatter(grad_keys_full, "blk", scatter_dimension=0, tiled=True),
        lax.psum_scatter(grad_values_full, "blk", scatter_dimension=0, tiled=True),
    )
    grad_query_lin = (
        rotary_apply(grad_query, query_where, -1.0)
        .astype(jnp.bfloat16)
        .reshape(rows, 1, head_group * HEAD_SIZE)
    )
    grad_key_lin = rotary_apply(grad_keys.reshape(rows, 1, HEAD_SIZE), query_where, -1.0).astype(
        jnp.bfloat16
    )
    grad_value_lin = grad_values.astype(jnp.bfloat16).reshape(rows, 1, HEAD_SIZE)
    back_query, key_backward, value_backward = (
        lax.all_to_all(grad_query_lin, "head", split_axis=0, concat_axis=1, tiled=True),
        lax.all_to_all(grad_key_lin, "head", split_axis=0, concat_axis=1, tiled=True),
        lax.all_to_all(grad_value_lin, "head", split_axis=0, concat_axis=1, tiled=True),
    )
    back_query = back_query.reshape(count_per_token, QUERY_HEADS * HEAD_SIZE)
    key_backward = key_backward.reshape(count_per_token, KEY_VALUE_HEADS * HEAD_SIZE)
    value_backward = value_backward.reshape(count_per_token, KEY_VALUE_HEADS * HEAD_SIZE)
    grad_query_w = jnp.einsum(
        "td,tk->dk", normed_low, back_query, preferred_element_type=jnp.float32
    )
    grad_key_w = jnp.einsum(
        "td,tk->dk", normed_low, key_backward, preferred_element_type=jnp.float32
    )
    grad_value_w = jnp.einsum(
        "td,tk->dk", normed_low, value_backward, preferred_element_type=jnp.float32
    )
    grad_normed_one = jnp.einsum(
        "tk,dk->td", back_query, query_w, preferred_element_type=jnp.float32
    )
    grad_normed_one = grad_normed_one + jnp.einsum(
        "tk,dk->td", key_backward, key_w, preferred_element_type=jnp.float32
    )
    grad_normed_one = grad_normed_one + jnp.einsum(
        "tk,dk->td", value_backward, value_w, preferred_element_type=jnp.float32
    )
    unused_value, pull_one = jax.vjp(rms_norm, inputs, gain_one)
    grad_in_norm, grad_gain_one = pull_one(grad_normed_one)
    grad_inputs = grad_residual + grad_in_norm
    sums = (
        lax.psum_scatter(grad_query_w, ("head", "blk"), scatter_dimension=0, tiled=True),
        lax.psum_scatter(grad_key_w, ("head", "blk"), scatter_dimension=0, tiled=True),
        lax.psum_scatter(grad_value_w, ("head", "blk"), scatter_dimension=0, tiled=True),
        lax.psum_scatter(grad_out_w, ("head", "blk"), scatter_dimension=0, tiled=True),
        lax.psum_scatter(grad_gain_one, ("head", "blk"), scatter_dimension=0, tiled=True),
        lax.psum_scatter(grad_gain_two, ("head", "blk"), scatter_dimension=0, tiled=True),
        lax.psum_scatter(grad_up, ("head", "blk"), scatter_dimension=1, tiled=True),
        lax.psum_scatter(grad_down, ("head", "blk"), scatter_dimension=1, tiled=True),
    )
    shape = states.shape
    return (
        final.astype(jnp.bfloat16).reshape(shape),
        loss,
        grad_inputs.reshape(shape),
        sums[4],
        sums[0],
        sums[1],
        sums[2],
        sums[3],
        sums[5],
        sums[6],
        sums[7],
    )


class Place:
    def __init__(self):
        self.x = lax.axis_index("head")
        self.b = lax.axis_index("blk")
        self.c = self.b % 2
        self.y = (self.b // 2) % 2
        self.z = self.b // 4

    def near(self, kind):
        x, y, z, c = self.x, self.y, self.z, self.c
        if kind == "up":
            z = jnp.minimum(z + 1, NZ - 1)
        elif kind == "down":
            z = jnp.maximum(z - 1, 0)
        elif kind == "y":
            y = 1 - y
        elif kind == "x":
            x = 1 - x
        elif kind == "c":
            c = 1 - c
        return (x, z * 4 + y * 2 + c)

    def blk(self, z, y, c):
        return z * 4 + y * 2 + c

    def outward(self, j):
        inner = jnp.where(j < 2, 1 - j, j)
        order = jnp.where((self.z == 0) | (self.z == NZ - 1), j, inner)
        return jnp.where(self.z < 2, order, NZ - 1 - order)

    def inward(self, j):
        inner = jnp.where(j == 0, 3, jnp.where(j == 1, 0, jnp.where(j == 2, 2, 1)))
        order = jnp.where((self.z == 0) | (self.z == NZ - 1), NZ - 1 - j, inner)
        return jnp.where(self.z < 2, order, NZ - 1 - order)


def greet_all(me):
    barrier = pltpu.get_barrier_semaphore()

    def one(k, carry):
        pl.semaphore_signal(
            barrier, inc=1, device_id=((me.x + k // 16) % 2, (me.b + k) % 16), device_id_type=MESH
        )
        return carry

    lax.fori_loop(1, 32, one, 0)
    pl.semaphore_wait(barrier, 31)


def remote(src, dst, send, recv, to):
    return pltpu.make_async_remote_copy(
        src_ref=src, dst_ref=dst, send_sem=send, recv_sem=recv, device_id=to, device_id_type=MESH
    )


def arrived(ref, sem, me):
    remote(ref, ref, sem, sem, me.near("c")).wait_recv()


def left(ref, sem, me):
    remote(ref, ref, sem, sem, me.near("c")).wait_send()


def gather_all(me, g, index, send, recv, between=None):
    x, y, c = me.x, me.y, me.c
    half = g.shape[2] // 2
    first, second = pl.ds(0, half), pl.ds(half, half)

    def put(j, kind, n, s, cols=None, slot=0):
        ref = g.at[s] if cols is None else g.at[s, :, cols]
        remote(ref, ref, send.at[j, n], recv.at[s, slot], me.near(kind)).start()

    def turn(j, carry):
        zz = me.outward(j)
        own = index(x, zz, y, c)

        @pl.when((j > 0) & (j < 4))
        def _():
            arrived(g.at[own], recv.at[own, 0], me)

        @pl.when(j < 4)
        def _():
            pl.when((zz <= me.z) & (me.z < NZ - 1))(lambda: put(j, "up", 0, own))
            pl.when((zz >= me.z) & (me.z > 0))(lambda: put(j, "down", 1, own))
            put(j, "y", 2, own)
            put(j, "x", 3, own)
            put(j, "c", 6, own)

        @pl.when((j > 0) & (j < 5))
        def _():
            i = j - 1
            zp = me.outward(i)
            s = index(x, zp, 1 - y, c)
            arrived(g.at[s], recv.at[s, 0], me)
            put(i, "x", 4, s, first, 0)
            put(i, "c", 7, s)
            t = index(1 - x, zp, y, c)
            arrived(g.at[t], recv.at[t, 0], me)
            put(i, "y", 5, t, second, 1)
            put(i, "c", 8, t)

        @pl.when(j > 1)
        def _():
            i = j - 2
            s = index(1 - x, me.outward(i), 1 - y, c)
            arrived(g.at[s, :, first], recv.at[s, 0], me)
            arrived(g.at[s, :, second], recv.at[s, 1], me)
            put(i, "c", 9, s)

        if between is not None:
            between(j)
        return carry

    lax.fori_loop(0, 6, turn, 0)

    def close(j, carry):
        zz = me.outward(j)
        own = index(x, zz, y, c)
        whole, part = g.at[own], g.at[own, :, first]
        pl.when((zz <= me.z) & (me.z < NZ - 1))(lambda: left(whole, send.at[j, 0], me))
        pl.when((zz >= me.z) & (me.z > 0))(lambda: left(whole, send.at[j, 1], me))
        for n in (2, 3, 6, 7, 8, 9):
            left(whole, send.at[j, n], me)
        for n in (4, 5):
            left(part, send.at[j, n], me)
        for xx in (x, 1 - x):
            for yy in (y, 1 - y):
                s = index(xx, zz, yy, 1 - c)
                arrived(g.at[s], recv.at[s, 0], me)
        return carry

    lax.fori_loop(0, 4, close, 0)


def sum_all(me, part, index, out, rc, rd, rn, rz, acc, sc, ss, vc, vn, vz, between=None):
    x, y, z, c = me.x, me.y, me.z, me.c
    half = part.shape[2] // 2
    first, second = pl.ds(0, half), pl.ds(half, half)

    def slot(xx, zz, yy):
        return zz * 4 + xx * 2 + yy

    def lead(j, carry):
        zz = me.inward(j)
        for xx in (1 - x, x):
            for yy in (1 - y, y):
                k = slot(xx, zz, yy)
                remote(part.at[index(xx, zz, yy, 1 - c)], rc.at[k], sc.at[k], vc.at[k], me.near("c")).start()
        return carry

    lax.fori_loop(0, 4, lead, 0)

    def with_core(xx, zz, yy):
        k = slot(xx, zz, yy)
        arrived(rc.at[k], vc.at[k], me)
        return k, part[index(xx, zz, yy, c)].astype(F32) + rc[k].astype(F32)

    def turn(j, carry):
        @pl.when(j < 4)
        def _():
            zz = me.inward(j)
            k, total = with_core(1 - x, zz, 1 - y)
            rc[k] = total.astype(BF)
            remote(rc.at[k, :, first], rd.at[0, zz], ss.at[j, 0], vn.at[zz, 0], me.near("x")).start()
            remote(rc.at[k, :, second], rd.at[1, zz], ss.at[j, 1], vn.at[zz, 1], me.near("y")).start()

        @pl.when((j > 0) & (j < 5))
        def _():
            i = j - 1
            zz = me.inward(i)
            k, total = with_core(x, zz, 1 - y)
            arrived(rd.at[0, zz], vn.at[zz, 0], me)
            rc[k, :, second] = total[:, half:].astype(BF)
            rc[k, :, first] = (total[:, :half] + rd[0, zz].astype(F32)).astype(BF)
            remote(rc.at[k], rn.at[0, zz], ss.at[i, 2], vn.at[zz, 2], me.near("y")).start()
            k, total = with_core(1 - x, zz, y)
            arrived(rd.at[1, zz], vn.at[zz, 1], me)
            rc[k, :, first] = total[:, :half].astype(BF)
            rc[k, :, second] = (total[:, half:] + rd[1, zz].astype(F32)).astype(BF)
            remote(rc.at[k], rn.at[1, zz], ss.at[i, 3], vn.at[zz, 3], me.near("x")).start()

        @pl.when(j > 1)
        def _():
            i = j - 2
            zz = me.inward(i)
            k, total = with_core(x, zz, y)
            arrived(rn.at[0, zz], vn.at[zz, 2], me)
            arrived(rn.at[1, zz], vn.at[zz, 3], me)
            acc[...] = total + rn[0, zz].astype(F32) + rn[1, zz].astype(F32)
            along_z(me, i, zz, acc, rc.at[k], rz, ss, 4, vz)

        if between is not None:
            between(j)
        return carry

    lax.fori_loop(0, 6, turn, 0)
    out[...] = acc[...]

    def close(j, carry):
        zz = me.inward(j)
        whole, piece = rc.at[0], rc.at[0, :, first]
        for xx in (1 - x, x):
            for yy in (1 - y, y):
                left(whole, sc.at[slot(xx, zz, yy)], me)
        for n in (0, 1):
            left(piece, ss.at[j, n], me)
        for n in (2, 3):
            left(whole, ss.at[j, n], me)
        pl.when(zz > z)(lambda: left(whole, ss.at[j, 4], me))
        pl.when(zz < z)(lambda: left(whole, ss.at[j, 5], me))
        return carry

    lax.fori_loop(0, 4, close, 0)


def along_z(me, i, zz, acc, room, rz, ss, n, vz):
    z = me.z

    def add(slot):
        arrived(rz.at[slot], vz.at[slot], me)
        acc[...] += rz[slot].astype(F32)

    pl.when((zz >= z) & (z > 0))(lambda: add(zz))
    pl.when((zz < z) & (z < NZ - 1))(lambda: add(zz))
    pl.when((zz == z) & (z < NZ - 1))(lambda: add(4))

    @pl.when(zz > z)
    def _():
        room[...] = acc[...].astype(BF)
        remote(room, rz.at[zz], ss.at[i, n], vz.at[zz], me.near("up")).start()

    @pl.when(zz < z)
    def _():
        room[...] = acc[...].astype(BF)
        there = jnp.where(zz == z - 1, 4, zz)
        remote(room, rz.at[there], ss.at[i, n + 1], vz.at[there], me.near("down")).start()


def by_weight(x, z, y, c):
    return x * 16 + z * 4 + y * 2 + c


def by_token(x, z, y, c):
    return (z * 4 + y * 2 + c) * 2 + x


ANY = pl.BlockSpec(memory_space=pl.ANY)
VMEM = pl.BlockSpec(memory_space=pltpu.VMEM)
DMA = pltpu.SemaphoreType.DMA


def params(number, mib):
    return pltpu.CompilerParams(
        collective_id=number, has_side_effects=True, vmem_limit_bytes=mib << 20
    )


def weights_kernel(
    dense, up, down, g, win, wout, own_sem, send, recv, asend, arecv, xsend, xrecv, osend, orecv
):
    me = Place()
    x, b, c = me.x, me.b, me.c
    here = by_weight(x, me.z, me.y, c)
    mine = pltpu.make_async_copy(dense, g.at[here], own_sem.at[0])
    mine.start()
    pieces = []
    for k in range(2):
        col = pl.multiple_of(k * 768 + c * 384, 128)
        pieces.append(
            pltpu.make_async_copy(
                up.at[b // 2, :, pl.ds(col, 384)],
                win.at[x, b, :, pl.ds(k * 384, 384)],
                own_sem.at[1 + k],
            )
        )
    for piece in pieces:
        piece.start()
    held = pltpu.make_async_copy(down.at[b // 2], wout.at[b], own_sem.at[3])
    pl.when(c == x)(held.start)
    greet_all(me)
    mine.wait()

    def deal(k, carry):
        t = (b + k) % 16
        for h in range(2):
            col = pl.multiple_of(h * 768 + (t % 2) * 384, 128)
            remote(
                up.at[t // 2, :, pl.ds(col, 384)],
                win.at[x, b, :, pl.ds(h * 384, 384)],
                asend.at[k, h],
                arecv.at[b, h],
                (x, t),
            ).start()
        pl.when(t % 2 == x)(
            lambda: remote(down.at[t // 2], wout.at[b], osend.at[k], orecv.at[b], (x, t)).start()
        )
        return carry

    def pass_on(k, carry):
        f = (b + 16 - k) % 16

        @pl.when(k > 0)
        def _():
            for h in range(2):
                arrived(win.at[x, f, :, pl.ds(h * 384, 384)], arecv.at[f, h], me)

        remote(win.at[x, f], win.at[x, f], xsend.at[k], xrecv.at[f], me.near("x")).start()

        @pl.when(c == x)
        def _():
            pl.when(k > 0)(lambda: arrived(wout.at[f], orecv.at[f], me))
            remote(wout.at[f], wout.at[f], osend.at[16 + k], orecv.at[f], me.near("x")).start()

        return carry

    def between(j):
        @pl.when(j == 0)
        def _():
            lax.fori_loop(1, 16, deal, 0)
            for piece in pieces:
                piece.wait()
            pl.when(c == x)(held.wait)

        @pl.when(j >= 2)
        def _():
            lax.fori_loop((j - 2) * 4, (j - 2) * 4 + 4, pass_on, 0)

    gather_all(me, g, by_weight, send, recv, between)

    def close(k, carry):
        slab, piece = win.at[x, b], win.at[x, b, :, pl.ds(0, 384)]

        @pl.when(k > 0)
        def _():
            for h in range(2):
                left(piece, asend.at[k, h], me)
            pl.when((b + k) % 2 == x)(lambda: left(wout.at[b], osend.at[k], me))

        left(slab, xsend.at[k], me)
        pl.when(c == x)(lambda: left(wout.at[b], osend.at[16 + k], me))
        arrived(win.at[1 - x, k], xrecv.at[k], me)
        pl.when(c != x)(lambda: arrived(wout.at[k], orecv.at[k], me))
        return carry

    lax.fori_loop(0, 16, close, 0)


def bring_weights(dense, up, down):
    columns = dense.shape[1]
    return pl.pallas_call(
        weights_kernel,
        out_shape=(
            jax.ShapeDtypeStruct((32, 48, columns), BF),
            jax.ShapeDtypeStruct((2, 16, 48, 768), BF),
            jax.ShapeDtypeStruct((16, 48, 768), BF),
        ),
        in_specs=[ANY] * 3,
        out_specs=(ANY,) * 3,
        scratch_shapes=[
            DMA((4,)),
            DMA((4, 10)),
            DMA((32, 2)),
            DMA((16, 2)),
            DMA((16, 2)),
            DMA((16,)),
            DMA((16,)),
            DMA((32,)),
            DMA((16,)),
        ],
        compiler_params=params(1, 8),
        name="bring_weights",
    )(dense, up, down)


NT = (((1,), (1,)), ((), ()))
TN = (((0,), (0,)), ((), ()))
GELU_A = 0.7978845608028654
GELU_B = 0.044715


def experts_kernel(
    n2, h, teacher, weight, gate, win, wout,
    final, err, dn2, dy_out, dwin, dwout,
    nall, dyall, pairs, zg, dpairs, part, rc, ry, rz, acc, errs,
    gsend, grecv, csend, crecv, ysend, yrecv, zsend, zrecv, esend, erecv,
):
    me = Place()
    x, y, z, b, c = me.x, me.y, me.z, me.b, me.c
    greet_all(me)

    def gather(buf, way, chunk):
        def put(j, kind, n, s):
            remote(buf.at[s], buf.at[s], gsend.at[way, j, n], grecv.at[way, s], me.near(kind)).start()

        def turn(j, carry):
            zz = me.outward(j)
            own = me.blk(zz, y, c)

            @pl.when((j > 0) & (j < 4))
            def _():
                arrived(buf.at[own], grecv.at[way, own], me)

            @pl.when(j < 4)
            def _():
                pl.when((zz <= z) & (z < NZ - 1))(lambda: put(j, "up", 0, own))
                pl.when((zz >= z) & (z > 0))(lambda: put(j, "down", 1, own))
                put(j, "y", 2, own)
                put(j, "c", 3, own)

            @pl.when(j > 0)
            def _():
                i = j - 1
                zp = me.outward(i)
                s = me.blk(zp, 1 - y, c)
                arrived(buf.at[s], grecv.at[way, s], me)
                put(i, "c", 4, s)

                def both(n, carry):
                    yy = (y + n) % 2
                    s = me.blk(zp, yy, 1 - c)
                    arrived(buf.at[s], grecv.at[way, s], me)
                    chunk(zp * 2 + yy)
                    return carry

                lax.fori_loop(0, 2, both, 0)

            return carry

        lax.fori_loop(0, 5, turn, 0)

        def close(j, carry):
            zz = me.outward(j)
            whole = buf.at[b]
            pl.when((zz <= z) & (z < NZ - 1))(lambda: left(whole, gsend.at[way, j, 0], me))
            pl.when((zz >= z) & (z > 0))(lambda: left(whole, gsend.at[way, j, 1], me))
            for n in (2, 3, 4):
                left(whole, gsend.at[way, j, n], me)
            return carry

        lax.fori_loop(0, 4, close, 0)

    def to_other_core(way, q):
        remote(part.at[q * 2 + 1 - c], rc.at[way, q], csend.at[way, q], crecv.at[way, q], me.near("c")).start()

    def reduce(way, between):
        def lead(j, carry):
            zz = me.inward(j)
            q = zz * 2 + 1 - y
            s = q * 2 + c
            arrived(rc.at[way, q], crecv.at[way, q], me)
            part[s] = (part[s].astype(F32) + rc[way, q].astype(F32)).astype(BF)
            remote(part.at[s], ry.at[way, zz], ysend.at[way, j], yrecv.at[way, zz], me.near("y")).start()
            return carry

        lax.fori_loop(0, 4, lead, 0)

        def turn(j, carry):
            between(j)
            zz = me.inward(j)
            q = zz * 2 + y
            s = q * 2 + c
            arrived(rc.at[way, q], crecv.at[way, q], me)
            arrived(ry.at[way, zz], yrecv.at[way, zz], me)
            acc[...] = part[s].astype(F32) + rc[way, q].astype(F32) + ry[way, zz].astype(F32)
            along_z(me, j, zz, acc, part.at[s], rz.at[way], zsend.at[way], 0, zrecv.at[way])
            return carry

        lax.fori_loop(0, 4, turn, 0)

        def close(j, carry):
            zz = me.inward(j)
            whole = part.at[b]
            left(whole, ysend.at[way, j], me)
            left(whole, csend.at[way, j], me)
            left(whole, csend.at[way, j + 4], me)
            pl.when(zz > z)(lambda: left(whole, zsend.at[way, j, 0], me))
            pl.when(zz < z)(lambda: left(whole, zsend.at[way, j, 1], me))
            return carry

        lax.fori_loop(0, 4, close, 0)

    def gelu_parts(g):
        t = jnp.tanh(GELU_A * (g + GELU_B * g * g * g))
        return t, 0.5 * g * (1.0 + t)

    def forward(q):
        rows = nall[pl.ds(q * 2, 2)].reshape(256, 1536)
        pair = jnp.dot(rows, win[...], preferred_element_type=F32)
        pairs[q] = pair
        unused, a = gelu_parts(pair[:, :384])
        zq = (a * pair[:, 384:] * gate[q]).astype(BF)
        zg[q] = zq
        out = jnp.dot(zq, wout[...], preferred_element_type=F32)
        part[pl.ds(q * 2, 2)] = out.astype(BF).reshape(2, 128, 1536)
        to_other_core(0, q)

    def backward(q):
        rows = dyall[pl.ds(q * 2, 2)].reshape(256, 1536)
        dz = lax.dot_general(rows, wout[...], NT, preferred_element_type=F32) * gate[q]
        g, u = pairs[q, :, :384], pairs[q, :, 384:]
        t, a = gelu_parts(g)
        slope = 0.5 * (1.0 + t) + 0.5 * g * (1.0 - t * t) * (GELU_A * (1.0 + 3.0 * GELU_B * g * g))
        dpairs[q, :, :384] = (dz * u * slope).astype(BF)
        dpairs[q, :, 384:] = (dz * a).astype(BF)
        out = lax.dot_general(dpairs[q], win[...], NT, preferred_element_type=F32)
        part[pl.ds(q * 2, 2)] = out.astype(BF).reshape(2, 128, 1536)
        to_other_core(1, q)

    nall[b] = n2[...]
    gather(nall, 0, forward)
    reduce(0, lambda j: None)

    done = h[...] + acc[...]
    final[...] = done.astype(BF)
    diff = done - teacher[...].astype(F32)
    scaled = weight[:, 0:1] * diff
    dy_out[...] = scaled
    dyall[b] = scaled.astype(BF)
    kept = jnp.sum(weight[:, 1:2] * diff * diff)
    me_index = x * 16 + b
    errs[me_index] = jnp.zeros((8, 128), F32) + kept

    def tell(k, carry):
        to = ((x + k // 16) % 2, (b + k) % 16)
        remote(errs.at[me_index], errs.at[me_index], esend.at[k], erecv.at[me_index], to).start()
        return carry

    lax.fori_loop(1, 32, tell, 0)
    gather(dyall, 1, backward)

    def weight_part(j):
        for i in range(2):

            @pl.when(j * 2 + i < 6)
            def _():
                col = pl.ds(pl.multiple_of((j * 2 + i) * 256, 256), 256)
                rows = nall[:, :, col].reshape(2048, 256)
                both = dpairs[...].reshape(2048, 768)
                dwin[col, :] = lax.dot_general(rows, both, TN, preferred_element_type=F32).astype(BF)
                right = dyall[:, :, col].reshape(2048, 256)
                zall = zg[...].reshape(2048, 384)
                dwout[:, col] = lax.dot_general(zall, right, TN, preferred_element_type=F32).astype(BF)

    reduce(1, weight_part)
    dn2[...] = acc[...]

    def hear(k, carry):
        left(errs.at[0], esend.at[k], me)
        s = ((x + k // 16) % 2) * 16 + (b + k) % 16
        arrived(errs.at[s], erecv.at[s], me)
        return carry

    lax.fori_loop(1, 32, hear, 0)
    total = errs[0]
    for s in range(1, 32):
        total = total + errs[s]
    err[...] = total


def run_experts(n2, h, teacher, weight, gate, win, wout):
    wide = (128, 1536)
    shard = (16,) + wide
    return pl.pallas_call(
        experts_kernel,
        out_shape=(
            jax.ShapeDtypeStruct(wide, BF),
            jax.ShapeDtypeStruct((8, 128), F32),
            jax.ShapeDtypeStruct(wide, F32),
            jax.ShapeDtypeStruct(wide, F32),
            jax.ShapeDtypeStruct((1536, 768), BF),
            jax.ShapeDtypeStruct((384, 1536), BF),
        ),
        in_specs=[VMEM] * 7,
        out_specs=(VMEM,) * 6,
        scratch_shapes=[
            pltpu.VMEM(shard, BF),
            pltpu.VMEM(shard, BF),
            pltpu.VMEM((8, 256, 768), F32),
            pltpu.VMEM((8, 256, 384), BF),
            pltpu.VMEM((8, 256, 768), BF),
            pltpu.VMEM(shard, BF),
            pltpu.VMEM((2, 8) + wide, BF),
            pltpu.VMEM((2, 4) + wide, BF),
            pltpu.VMEM((2, 5) + wide, BF),
            pltpu.VMEM(wide, F32),
            pltpu.VMEM((32, 8, 128), F32),
            DMA((2, 4, 5)),
            DMA((2, 16)),
            DMA((2, 8)),
            DMA((2, 8)),
            DMA((2, 4)),
            DMA((2, 4)),
            DMA((2, 4, 2)),
            DMA((2, 5)),
            DMA((32,)),
            DMA((32,)),
        ],
        compiler_params=params(2, 61),
        name="experts",
    )(n2, h, teacher, weight, gate, win, wout)


def grads_kernel(
    dense, dwin, dwout, g, gup, gdown,
    rc, rd, rn, rz, acc, xin, xout,
    sc, ss, vc, vn, vz, xsend, xrecv, asend, arecv, osend, orecv, own_sem,
):
    me = Place()
    x, b, c = me.x, me.b, me.c
    greet_all(me)

    def over(k, carry):
        t = (b + k) % 16
        remote(dwin.at[1 - x, t], xin.at[t], xsend.at[k], xrecv.at[t], me.near("x")).start()
        pl.when(c != x)(
            lambda: remote(dwout.at[t], xout.at[t], osend.at[k], orecv.at[t], me.near("x")).start()
        )
        return carry

    lax.fori_loop(0, 16, over, 0)

    def deal(k, carry):
        t = (b + k) % 16
        arrived(xin.at[t], xrecv.at[t], me)
        xin[t] = (xin[t].astype(F32) + dwin[x, t].astype(F32)).astype(BF)

        @pl.when(k > 0)
        def _():
            for h in range(2):
                col = pl.multiple_of(h * 768 + c * 384, 128)
                remote(
                    xin.at[t, :, pl.ds(h * 384, 384)],
                    gup.at[b // 2, :, pl.ds(col, 384)],
                    asend.at[k, h],
                    arecv.at[b, h],
                    (x, t),
                ).start()

        @pl.when(k == 0)
        def _():
            for h in range(2):
                col = pl.multiple_of(h * 768 + c * 384, 128)
                pltpu.make_async_copy(
                    xin.at[t, :, pl.ds(h * 384, 384)],
                    gup.at[b // 2, :, pl.ds(col, 384)],
                    own_sem.at[h],
                ).start()

        @pl.when(c == x)
        def _():
            arrived(xout.at[t], orecv.at[t], me)
            xout[t] = (xout[t].astype(F32) + dwout[t].astype(F32)).astype(BF)
            pl.when(k > 0)(
                lambda: remote(
                    xout.at[t], gdown.at[b // 2], osend.at[16 + k], orecv.at[16 + b // 2], (x, t)
                ).start()
            )
            pl.when(k == 0)(
                pltpu.make_async_copy(xout.at[t], gdown.at[b // 2], own_sem.at[2]).start
            )

        return carry

    def between(j):
        @pl.when(j >= 2)
        def _():
            lax.fori_loop((j - 2) * 4, (j - 2) * 4 + 4, deal, 0)

    sum_all(me, dense, by_weight, g, rc, rd, rn, rz, acc, sc, ss, vc, vn, vz, between)

    def close(k, carry):
        left(xin.at[0], xsend.at[k], me)
        pl.when(c != x)(lambda: left(xout.at[0], osend.at[k], me))

        @pl.when(k > 0)
        def _():
            f = (b + 16 - k) % 16
            for h in range(2):
                left(xin.at[0, :, pl.ds(0, 384)], asend.at[k, h], me)
                col = pl.multiple_of(h * 768 + (f % 2) * 384, 128)
                arrived(gup.at[f // 2, :, pl.ds(col, 384)], arecv.at[f, h], me)
            pl.when(c == x)(lambda: left(xout.at[0], osend.at[16 + k], me))
            pl.when(f % 2 == x)(lambda: arrived(gdown.at[f // 2], orecv.at[16 + f // 2], me))

        @pl.when(k == 0)
        def _():
            for h in range(2):
                col = pl.multiple_of(h * 768 + c * 384, 128)
                pltpu.make_async_copy(
                    xin.at[b, :, pl.ds(h * 384, 384)],
                    gup.at[b // 2, :, pl.ds(col, 384)],
                    own_sem.at[h],
                ).wait()
            pl.when(c == x)(
                pltpu.make_async_copy(xout.at[b], gdown.at[b // 2], own_sem.at[2]).wait
            )

        return carry

    lax.fori_loop(0, 16, close, 0)


def return_grads(dense, dwin, dwout):
    rows, columns = dense.shape[1:]
    shard = (rows, columns)
    return pl.pallas_call(
        grads_kernel,
        out_shape=(
            jax.ShapeDtypeStruct(shard, F32),
            jax.ShapeDtypeStruct((8, 48, 1536), BF),
            jax.ShapeDtypeStruct((8, 48, 768), BF),
        ),
        in_specs=[VMEM] * 3,
        out_specs=(VMEM,) * 3,
        scratch_shapes=[
            pltpu.VMEM((16,) + shard, BF),
            pltpu.VMEM((2, 4, rows, columns // 2), BF),
            pltpu.VMEM((2, 4) + shard, BF),
            pltpu.VMEM((5,) + shard, BF),
            pltpu.VMEM(shard, F32),
            pltpu.VMEM((16, 48, 768), BF),
            pltpu.VMEM((16, 48, 768), BF),
            DMA((16,)),
            DMA((4, 6)),
            DMA((16,)),
            DMA((4, 4)),
            DMA((5,)),
            DMA((16,)),
            DMA((16,)),
            DMA((16, 2)),
            DMA((16, 2)),
            DMA((32,)),
            DMA((32,)),
            DMA((3,)),
        ],
        compiler_params=params(3, 56),
        name="return_grads",
    )(dense, dwin, dwout)


def per_device(
    states, teacher, valid, routes, gates, doc_starts, norm_one,
    w_query, key_weight, value_weight, w_output, norm_two, expert_in, expert_out,
):
    count_per_token = states.shape[2]
    width = states.shape[3]
    pairs = lax.axis_size("head")
    blocks = lax.axis_size("blk")
    rows = count_per_token * pairs
    span = rows * blocks
    head_group = QUERY_HEADS // KEY_VALUE_HEADS
    scale = HEAD_SIZE ** (-0.5)
    highest = lax.Precision.HIGHEST
    block_index = lax.axis_index("blk")
    pair_index = lax.axis_index("head")
    token_index = (block_index * pairs + pair_index) * count_per_token + jnp.arange(
        count_per_token, dtype=jnp.int32
    )
    unused_segment, token_position = doc_layout(token_index, doc_starts)
    query_index = block_index * rows + jnp.arange(rows, dtype=jnp.int32)
    query_segment, query_where = doc_layout(query_index, doc_starts)
    last_query = block_index * rows + rows - 1
    inputs = states.reshape(count_per_token, width).astype(jnp.float32)
    keep_mask = valid.reshape(count_per_token).astype(jnp.float32)
    route_rows = routes.reshape(count_per_token, TOP)
    gate_rows = gates.reshape(count_per_token, TOP)

    table = jnp.sum(
        jnp.where(route_rows[None] == jnp.arange(E, dtype=jnp.int32)[:, None, None], gate_rows[None], 0.0), axis=-1
    )
    high = lax.reduce_precision(table, 8, 7)
    column = jnp.arange(128)[None, :]
    gains = jnp.where(
        column == 0,
        norm_one[:, None].astype(F32),
        jnp.where(column == 1, norm_two[:, None].astype(F32), jnp.sum(keep_mask)),
    ).astype(BF)
    routed = jnp.concatenate([high, table - high, jnp.zeros((32, 128), F32)], axis=0).astype(BF)
    dense = jnp.concatenate([w_query, key_weight, value_weight, w_output, gains, routed], axis=1)
    gathered, win, wout = bring_weights(dense, expert_in, expert_out.reshape(E, 48, 768))
    flat = gathered.reshape(1536, 3840)
    query_w, key_w, value_w, out_w = flat[:, :1536], flat[:, 1536:1792], flat[:, 1792:2048], flat[:, 2048:3584]
    gain_one = flat[:, 3584].astype(F32)
    gain_two = flat[:, 3585].astype(F32)
    count_all = jnp.sum(gathered[:, 0, 3586].astype(F32))
    tables = lax.dynamic_slice_in_dim(gathered[:, :16, 3712:], pair_index * 16, 16, 0).astype(F32)
    mine = lax.dynamic_slice_in_dim(tables, block_index // 2, 1, 1) + lax.dynamic_slice_in_dim(
        tables, 8 + block_index // 2, 1, 1
    )
    gate_plane = mine.reshape(8, 256, 1)

    normed_one = rms_norm(inputs, gain_one)
    normed_low = normed_one.astype(jnp.bfloat16)
    query_lin = product(normed_low, query_w)
    key_linear = product(normed_low, key_w)
    value_linear = product(normed_low, value_w)
    query_rotated = rotary_apply(
        query_lin.reshape(count_per_token, QUERY_HEADS, HEAD_SIZE), token_position, 1.0
    )
    key_rotated = rotary_apply(
        key_linear.reshape(count_per_token, KEY_VALUE_HEADS, HEAD_SIZE), token_position, 1.0
    )
    query_outgoing = query_rotated.astype(jnp.bfloat16).reshape(
        count_per_token, KEY_VALUE_HEADS, head_group * HEAD_SIZE
    )
    key_send = key_rotated.astype(jnp.bfloat16)
    value_outgoing = value_linear.astype(jnp.bfloat16).reshape(
        count_per_token, KEY_VALUE_HEADS, HEAD_SIZE
    )
    query_grp, key_grp, value_grp = (
        lax.all_to_all(query_outgoing, "head", split_axis=1, concat_axis=0, tiled=True),
        lax.all_to_all(key_send, "head", split_axis=1, concat_axis=0, tiled=True),
        lax.all_to_all(value_outgoing, "head", split_axis=1, concat_axis=0, tiled=True),
    )
    query_heads = query_grp.reshape(rows, head_group, HEAD_SIZE)
    key_rows = key_grp.reshape(rows, HEAD_SIZE)
    value_rows = value_grp.reshape(rows, HEAD_SIZE)

    def scores_for(keys, start):
        block_size = keys.shape[0]
        key_index = start + jnp.arange(block_size, dtype=jnp.int32)
        key_segment, unused_where = doc_layout(key_index, doc_starts)
        allowed = (key_index[None, :] <= query_index[:, None]) & (
            key_segment[None, :] == query_segment[:, None]
        )
        raw = (
            jnp.einsum("qhd,kd->hqk", query_heads, keys, preferred_element_type=jnp.float32) * scale
        )
        return (raw, allowed[None])

    def attend(carry, piece, start):
        keys, values = piece

        def work(state):
            running, total, accum = state
            raw, allowed = scores_for(keys, start)
            masked = jnp.where(allowed, raw, FLOOR_SCORE)
            newest = jnp.maximum(running, jnp.max(masked, axis=-1))
            factor = jnp.exp(running - newest)
            weights = jnp.where(allowed, jnp.exp(masked - newest[..., None]), 0.0)
            total = total * factor + jnp.sum(weights, axis=-1)
            update = jnp.einsum(
                "hqk,kd->qhd",
                weights.astype(jnp.bfloat16),
                values,
                preferred_element_type=jnp.float32,
            )
            accum = accum * factor.T[:, :, None] + update
            return (newest, total, accum)

        return lax.cond(start <= last_query, work, lambda state: state, carry)

    start_state = (
        jnp.full((head_group, rows), FLOOR_SCORE, jnp.float32),
        jnp.zeros((head_group, rows), jnp.float32),
        jnp.zeros((rows, head_group, HEAD_SIZE), jnp.float32),
    )
    running, total, accum = in_blocks(
        attend,
        start_state,
        (
            lax.all_gather(key_rows, "blk", axis=0, tiled=True),
            lax.all_gather(value_rows, "blk", axis=0, tiled=True),
        ),
        rows,
    )
    attn_full = accum / total.T[:, :, None]
    log_total = running + jnp.log(total)
    out_send = attn_full.astype(jnp.bfloat16).reshape(rows, 1, head_group * HEAD_SIZE)
    out_tok = lax.all_to_all(out_send, "head", split_axis=0, concat_axis=1, tiled=True).reshape(
        count_per_token, QUERY_HEADS * HEAD_SIZE
    )
    residual = inputs + product(out_tok, out_w)
    normed_two_low = rms_norm(residual, gain_two).astype(jnp.bfloat16)
    weight = jnp.stack([keep_mask * (span * 1.0 / count_all), keep_mask], axis=1)
    final, error, grad_normed_two, grad_final, dwin, dwout = run_experts(
        normed_two_low,
        residual,
        teacher.reshape(count_per_token, width),
        weight,
        gate_plane,
        win.reshape(1536, 768),
        wout.reshape(384, 1536),
    )
    loss = error[0, 0] / (width * count_all)
    unused_value, pull_two = jax.vjp(rms_norm, residual, gain_two)
    grad_res_norm, grad_gain_two = pull_two(grad_normed_two)
    grad_residual = grad_final + grad_res_norm
    grad_attn_low = grad_residual.astype(jnp.bfloat16)
    grad_out_w = jnp.einsum("tk,td->kd", out_tok, grad_attn_low, preferred_element_type=jnp.float32)
    output_gradient_token = jnp.einsum(
        "td,kd->tk", grad_attn_low, out_w, preferred_element_type=jnp.float32
    ).astype(jnp.bfloat16)
    grad_out_grp = lax.all_to_all(
        output_gradient_token.reshape(count_per_token, KEY_VALUE_HEADS, head_group * HEAD_SIZE),
        "head",
        split_axis=1,
        concat_axis=0,
        tiled=True,
    ).reshape(rows, head_group, HEAD_SIZE)
    delta = jnp.einsum(
        "qhd,qhd->hq", grad_out_grp.astype(jnp.float32), attn_full, precision=highest
    )

    def attend_back(carry, piece, start):
        keys, values = piece

        def work(state):
            grad_query, grad_keys, grad_values = state
            raw, allowed = scores_for(keys, start)
            weights = jnp.where(allowed, jnp.exp(raw - log_total[..., None]), 0.0)
            grad_weights = jnp.einsum(
                "qhd,kd->hqk", grad_out_grp, values, preferred_element_type=jnp.float32
            )
            grad_raw = (weights * (grad_weights - delta[..., None])).astype(jnp.bfloat16)
            grad_query = (
                grad_query
                + jnp.einsum("hqk,kd->qhd", grad_raw, keys, preferred_element_type=jnp.float32)
                * scale
            )
            key_part = (
                jnp.einsum("hqk,qhd->kd", grad_raw, query_heads, preferred_element_type=jnp.float32)
                * scale
            )
            value_part = jnp.einsum(
                "hqk,qhd->kd",
                weights.astype(jnp.bfloat16),
                grad_out_grp,
                preferred_element_type=jnp.float32,
            )
            block_size = keys.shape[0]
            grad_keys = lax.dynamic_update_slice_in_dim(
                grad_keys,
                lax.dynamic_slice_in_dim(grad_keys, start, block_size, 0) + key_part,
                start,
                0,
            )
            grad_values = lax.dynamic_update_slice_in_dim(
                grad_values,
                lax.dynamic_slice_in_dim(grad_values, start, block_size, 0) + value_part,
                start,
                0,
            )
            return (grad_query, grad_keys, grad_values)

        return lax.cond(start <= last_query, work, lambda state: state, carry)

    back_state = (
        jnp.zeros((rows, head_group, HEAD_SIZE), jnp.float32),
        jnp.zeros((span, HEAD_SIZE), jnp.float32),
        jnp.zeros((span, HEAD_SIZE), jnp.float32),
    )
    grad_query, grad_keys_full, grad_values_full = in_blocks(
        attend_back,
        back_state,
        (
            lax.all_gather(key_rows, "blk", axis=0, tiled=True),
            lax.all_gather(value_rows, "blk", axis=0, tiled=True),
        ),
        rows,
    )
    grad_keys, grad_values = (
        lax.psum_scatter(grad_keys_full, "blk", scatter_dimension=0, tiled=True),
        lax.psum_scatter(grad_values_full, "blk", scatter_dimension=0, tiled=True),
    )
    grad_query_lin = (
        rotary_apply(grad_query, query_where, -1.0)
        .astype(jnp.bfloat16)
        .reshape(rows, 1, head_group * HEAD_SIZE)
    )
    grad_key_lin = rotary_apply(grad_keys.reshape(rows, 1, HEAD_SIZE), query_where, -1.0).astype(
        jnp.bfloat16
    )
    grad_value_lin = grad_values.astype(jnp.bfloat16).reshape(rows, 1, HEAD_SIZE)
    back_query, key_backward, value_backward = (
        lax.all_to_all(grad_query_lin, "head", split_axis=0, concat_axis=1, tiled=True),
        lax.all_to_all(grad_key_lin, "head", split_axis=0, concat_axis=1, tiled=True),
        lax.all_to_all(grad_value_lin, "head", split_axis=0, concat_axis=1, tiled=True),
    )
    back_query = back_query.reshape(count_per_token, QUERY_HEADS * HEAD_SIZE)
    key_backward = key_backward.reshape(count_per_token, KEY_VALUE_HEADS * HEAD_SIZE)
    value_backward = value_backward.reshape(count_per_token, KEY_VALUE_HEADS * HEAD_SIZE)
    back = jnp.concatenate([back_query, key_backward, value_backward], axis=1)
    grad_qkv = jnp.einsum("td,tk->dk", normed_low, back, preferred_element_type=jnp.float32)
    grad_normed_one = jnp.einsum(
        "tk,dk->td", back, flat[:, :2048], preferred_element_type=jnp.float32
    )
    unused_value, pull_one = jax.vjp(rms_norm, inputs, gain_one)
    grad_in_norm, grad_gain_one = pull_one(grad_normed_one)
    grad_inputs = grad_residual + grad_in_norm
    tail = jnp.where(
        column == 0, grad_gain_one[:, None], jnp.where(column == 1, grad_gain_two[:, None], 0.0)
    )
    packed = jnp.concatenate([grad_qkv, grad_out_w, tail], axis=1).astype(BF).reshape(32, 48, 3712)
    packed = jnp.pad(packed, ((0, 0), (0, 0), (0, 128)))
    sums, gup, gdown = return_grads(packed, dwin.reshape(2, 16, 48, 768), dwout.reshape(16, 48, 768))
    shape = states.shape
    return (
        final.reshape(shape),
        loss,
        grad_inputs.reshape(shape),
        sums[:, 3584],
        sums[:, :1536],
        sums[:, 1536:1792],
        sums[:, 1792:2048],
        sums[:, 2048:3584],
        sums[:, 3585],
        gup.astype(F32),
        gdown.astype(F32).reshape(E, 24, 1536),
    )


def solution(mesh):
    in_specs = (
        P("blk", "head", None, None),
        P("blk", "head", None, None),
        P("blk", "head", None),
        P("blk", "head", None, None),
        P("blk", "head", None, None),
        P(),
        P(("head", "blk")),
        P(("head", "blk"), None),
        P(("head", "blk"), None),
        P(("head", "blk"), None),
        P(("head", "blk"), None),
        P(("head", "blk")),
        P(None, ("head", "blk"), None),
        P(None, ("head", "blk"), None),
    )
    out_specs = (
        P("blk", "head", None, None),
        P(),
        P("blk", "head", None, None),
        P(("head", "blk")),
        P(("head", "blk"), None),
        P(("head", "blk"), None),
        P(("head", "blk"), None),
        P(("head", "blk"), None),
        P(("head", "blk")),
        P(None, ("head", "blk"), None),
        P(None, ("head", "blk"), None),
    )
    sizes = dict(mesh.shape)
    plan = per_device if sizes == {"head": 2, "blk": 4 * NZ} else per_device_plain
    return jax.shard_map(
        plan, mesh=mesh, in_specs=in_specs, out_specs=out_specs, check_vma=False
    )
```

```python
import functools

import jax
import jax.numpy as jnp
from jax import lax
from jax.experimental import pallas as pl
from jax.experimental.pallas import tpu as pltpu
from jax.sharding import PartitionSpec as P

QUERY_HEADS = 12
KEY_VALUE_HEADS = 2
HEAD_SIZE = 128
TOP = 4
E = 8
CAP = 96

ROTARY_BASE = 10000.0
FLOOR_SCORE = -1e30

MESH = pl.DeviceIdType.MESH
NZ = 4
BF = jnp.bfloat16
F32 = jnp.float32

def product(left, right):
    return jnp.dot(left, right, preferred_element_type=jnp.float32)


def rms_norm(values, gain):
    scale = lax.rsqrt(jnp.mean(values * values, axis=-1, keepdims=True) + 1e-06)
    return values * scale * gain


def rotary_apply(values, where, sign):
    half = values.shape[-1] // 2
    freq = ROTARY_BASE ** (-jnp.arange(half).astype(jnp.float32) / half)
    angle = where.astype(jnp.float32)[:, None] * freq[None, :]
    cosine = jnp.cos(angle)[:, None, :]
    sine = jnp.sin(angle)[:, None, :] * sign
    first = values[..., :half]
    second = values[..., half:]
    return jnp.concatenate(
        [first * cosine - second * sine, second * cosine + first * sine], axis=-1
    )


def doc_layout(position_index, doc_starts):
    inside = (position_index[:, None] >= doc_starts[None, :]).astype(jnp.int32)
    document_segment = jnp.sum(inside, axis=-1) - 1
    begin = jnp.max(jnp.where(inside > 0, doc_starts[None, :], 0), axis=-1)
    return (document_segment, position_index - begin)


def gated(pair):
    half = pair.shape[-1] // 2
    return jax.nn.gelu(pair[..., :half], approximate=True) * pair[..., half:]


def in_blocks(step_fn, carry, piece, rows):
    count_blocks = piece[0].shape[0] // rows

    def turn(number, state):
        part = tuple((lax.dynamic_slice_in_dim(item, number * rows, rows, 0) for item in piece))
        return step_fn(state, part, number * rows)

    return lax.fori_loop(0, count_blocks, turn, carry)


def per_device_plain(
    states,
    teacher,
    valid,
    routes,
    gates,
    doc_starts,
    norm_one,
    w_query,
    key_weight,
    value_weight,
    w_output,
    norm_two,
    expert_in,
    expert_out,
):
    count_per_token = states.shape[2]
    width = states.shape[3]
    pairs = lax.axis_size("head")
    blocks = lax.axis_size("blk")
    rows = count_per_token * pairs
    span = rows * blocks
    head_group = QUERY_HEADS // KEY_VALUE_HEADS
    scale = HEAD_SIZE ** (-0.5)
    highest = lax.Precision.HIGHEST
    block_index = lax.axis_index("blk")
    pair_index = lax.axis_index("head")
    token_index = (block_index * pairs + pair_index) * count_per_token + jnp.arange(
        count_per_token, dtype=jnp.int32
    )
    unused_segment, token_position = doc_layout(token_index, doc_starts)
    query_index = block_index * rows + jnp.arange(rows, dtype=jnp.int32)
    query_segment, query_where = doc_layout(query_index, doc_starts)
    last_query = block_index * rows + rows - 1
    inputs = states.reshape(count_per_token, width).astype(jnp.float32)
    target = teacher.reshape(count_per_token, width).astype(jnp.float32)
    keep_mask = valid.reshape(count_per_token).astype(jnp.float32)
    route_rows = routes.reshape(count_per_token, TOP)
    gate_rows = gates.reshape(count_per_token, TOP)
    query_w, key_w, value_w, out_w, gain_low_one, gain_low_two = (
        lax.all_gather(w_query, ("head", "blk"), axis=0, tiled=True),
        lax.all_gather(key_weight, ("head", "blk"), axis=0, tiled=True),
        lax.all_gather(value_weight, ("head", "blk"), axis=0, tiled=True),
        lax.all_gather(w_output, ("head", "blk"), axis=0, tiled=True),
        lax.all_gather(norm_one, ("head", "blk"), axis=0, tiled=True),
        lax.all_gather(norm_two, ("head", "blk"), axis=0, tiled=True),
    )
    gain_one = gain_low_one.astype(jnp.float32)
    gain_two = gain_low_two.astype(jnp.float32)
    normed_one = rms_norm(inputs, gain_one)
    normed_low = normed_one.astype(jnp.bfloat16)
    query_lin = product(normed_low, query_w)
    key_linear = product(normed_low, key_w)
    value_linear = product(normed_low, value_w)
    query_rotated = rotary_apply(
        query_lin.reshape(count_per_token, QUERY_HEADS, HEAD_SIZE), token_position, 1.0
    )
    key_rotated = rotary_apply(
        key_linear.reshape(count_per_token, KEY_VALUE_HEADS, HEAD_SIZE), token_position, 1.0
    )
    query_outgoing = query_rotated.astype(jnp.bfloat16).reshape(
        count_per_token, KEY_VALUE_HEADS, head_group * HEAD_SIZE
    )
    key_send = key_rotated.astype(jnp.bfloat16)
    value_outgoing = value_linear.astype(jnp.bfloat16).reshape(
        count_per_token, KEY_VALUE_HEADS, HEAD_SIZE
    )
    query_grp, key_grp, value_grp = (
        lax.all_to_all(query_outgoing, "head", split_axis=1, concat_axis=0, tiled=True),
        lax.all_to_all(key_send, "head", split_axis=1, concat_axis=0, tiled=True),
        lax.all_to_all(value_outgoing, "head", split_axis=1, concat_axis=0, tiled=True),
    )
    query_heads = query_grp.reshape(rows, head_group, HEAD_SIZE)
    key_rows = key_grp.reshape(rows, HEAD_SIZE)
    value_rows = value_grp.reshape(rows, HEAD_SIZE)

    def scores_for(keys, start):
        block_size = keys.shape[0]
        key_index = start + jnp.arange(block_size, dtype=jnp.int32)
        key_segment, unused_where = doc_layout(key_index, doc_starts)
        allowed = (key_index[None, :] <= query_index[:, None]) & (
            key_segment[None, :] == query_segment[:, None]
        )
        raw = (
            jnp.einsum("qhd,kd->hqk", query_heads, keys, preferred_element_type=jnp.float32) * scale
        )
        return (raw, allowed[None])

    def attend(carry, piece, start):
        keys, values = piece

        def work(state):
            running, total, accum = state
            raw, allowed = scores_for(keys, start)
            masked = jnp.where(allowed, raw, FLOOR_SCORE)
            newest = jnp.maximum(running, jnp.max(masked, axis=-1))
            factor = jnp.exp(running - newest)
            weights = jnp.where(allowed, jnp.exp(masked - newest[..., None]), 0.0)
            total = total * factor + jnp.sum(weights, axis=-1)
            update = jnp.einsum(
                "hqk,kd->qhd",
                weights.astype(jnp.bfloat16),
                values,
                preferred_element_type=jnp.float32,
            )
            accum = accum * factor.T[:, :, None] + update
            return (newest, total, accum)

        return lax.cond(start <= last_query, work, lambda state: state, carry)

    start_state = (
        jnp.full((head_group, rows), FLOOR_SCORE, jnp.float32),
        jnp.zeros((head_group, rows), jnp.float32),
        jnp.zeros((rows, head_group, HEAD_SIZE), jnp.float32),
    )
    running, total, accum = in_blocks(
        attend,
        start_state,
        (
            lax.all_gather(key_rows, "blk", axis=0, tiled=True),
            lax.all_gather(value_rows, "blk", axis=0, tiled=True),
        ),
        rows,
    )
    attn_full = accum / total.T[:, :, None]
    log_total = running + jnp.log(total)
    out_send = attn_full.astype(jnp.bfloat16).reshape(rows, 1, head_group * HEAD_SIZE)
    out_tok = lax.all_to_all(out_send, "head", split_axis=0, concat_axis=1, tiled=True).reshape(
        count_per_token, QUERY_HEADS * HEAD_SIZE
    )
    residual = inputs + product(out_tok, out_w)
    normed_two = rms_norm(residual, gain_two)
    normed_two_low = normed_two.astype(jnp.bfloat16)
    up_w, down_w = (
        lax.all_gather(expert_in, ("head", "blk"), axis=1, tiled=True),
        lax.all_gather(expert_out, ("head", "blk"), axis=1, tiled=True),
    )
    route_hot = (route_rows[:, :, None] == jnp.arange(E, dtype=jnp.int32)[None, None, :]).astype(
        jnp.int32
    )
    flat_hot = route_hot.reshape(count_per_token * TOP, E)
    before = jnp.cumsum(flat_hot, axis=0) - flat_hot
    slot = jnp.sum(before * flat_hot, axis=-1).reshape(count_per_token, TOP)
    slot_hot = (slot[:, :, None] == jnp.arange(CAP, dtype=jnp.int32)[None, None, :]).astype(
        jnp.float32
    )
    route_float = route_hot.astype(jnp.float32)
    dispatch = jnp.einsum("tje,tjc->ect", route_float, slot_hot, precision=highest)
    combine = jnp.einsum("tje,tjc,tj->ect", route_float, slot_hot, gate_rows, precision=highest)
    expert_rows = jnp.einsum(
        "ect,td->ecd",
        dispatch.astype(jnp.bfloat16),
        normed_two_low,
        preferred_element_type=jnp.float32,
    ).astype(jnp.bfloat16)
    pair = jnp.einsum("ecd,edf->ecf", expert_rows, up_w, preferred_element_type=jnp.float32)
    hidden_low = gated(pair).astype(jnp.bfloat16)
    expert_result = jnp.einsum(
        "ecf,efd->ecd", hidden_low, down_w, preferred_element_type=jnp.float32
    )
    mixture = jnp.einsum("ect,ecd->td", combine, expert_result, precision=highest)
    final = residual + mixture
    diff = final - target
    local_count = jnp.sum(keep_mask)
    local_error = jnp.sum(keep_mask * jnp.sum(diff * diff, axis=-1))
    count_all, error_all = lax.psum((local_count, local_error), ("head", "blk"))
    loss = error_all / (width * count_all)
    grad_final = keep_mask[:, None] * diff * (span * 1.0 / count_all)
    up_back, down_back = (
        lax.all_gather(expert_in, ("head", "blk"), axis=1, tiled=True),
        lax.all_gather(expert_out, ("head", "blk"), axis=1, tiled=True),
    )
    grad_result = jnp.einsum("ect,td->ecd", combine, grad_final, precision=highest).astype(
        jnp.bfloat16
    )
    grad_down = jnp.einsum(
        "ecf,ecd->efd", hidden_low, grad_result, preferred_element_type=jnp.float32
    )
    grad_hidden = jnp.einsum(
        "ecd,efd->ecf", grad_result, down_back, preferred_element_type=jnp.float32
    )
    unused_value, pull_gate = jax.vjp(gated, pair)
    grad_pair = pull_gate(grad_hidden)[0].astype(jnp.bfloat16)
    grad_up = jnp.einsum("ecd,ecf->edf", expert_rows, grad_pair, preferred_element_type=jnp.float32)
    grad_rows = jnp.einsum("ecf,edf->ecd", grad_pair, up_back, preferred_element_type=jnp.float32)
    grad_normed_two = jnp.einsum("ect,ecd->td", dispatch, grad_rows, precision=highest)
    unused_value, pull_two = jax.vjp(rms_norm, residual, gain_two)
    grad_res_norm, grad_gain_two = pull_two(grad_normed_two)
    grad_residual = grad_final + grad_res_norm
    grad_attn_low = grad_residual.astype(jnp.bfloat16)
    grad_out_w = jnp.einsum("tk,td->kd", out_tok, grad_attn_low, preferred_element_type=jnp.float32)
    output_gradient_token = jnp.einsum(
        "td,kd->tk", grad_attn_low, out_w, preferred_element_type=jnp.float32
    ).astype(jnp.bfloat16)
    grad_out_grp = lax.all_to_all(
        output_gradient_token.reshape(count_per_token, KEY_VALUE_HEADS, head_group * HEAD_SIZE),
        "head",
        split_axis=1,
        concat_axis=0,
        tiled=True,
    ).reshape(rows, head_group, HEAD_SIZE)
    delta = jnp.einsum(
        "qhd,qhd->hq", grad_out_grp.astype(jnp.float32), attn_full, precision=highest
    )

    def attend_back(carry, piece, start):
        keys, values = piece

        def work(state):
            grad_query, grad_keys, grad_values = state
            raw, allowed = scores_for(keys, start)
            weights = jnp.where(allowed, jnp.exp(raw - log_total[..., None]), 0.0)
            grad_weights = jnp.einsum(
                "qhd,kd->hqk", grad_out_grp, values, preferred_element_type=jnp.float32
            )
            grad_raw = (weights * (grad_weights - delta[..., None])).astype(jnp.bfloat16)
            grad_query = (
                grad_query
                + jnp.einsum("hqk,kd->qhd", grad_raw, keys, preferred_element_type=jnp.float32)
                * scale
            )
            key_part = (
                jnp.einsum("hqk,qhd->kd", grad_raw, query_heads, preferred_element_type=jnp.float32)
                * scale
            )
            value_part = jnp.einsum(
                "hqk,qhd->kd",
                weights.astype(jnp.bfloat16),
                grad_out_grp,
                preferred_element_type=jnp.float32,
            )
            block_size = keys.shape[0]
            grad_keys = lax.dynamic_update_slice_in_dim(
                grad_keys,
                lax.dynamic_slice_in_dim(grad_keys, start, block_size, 0) + key_part,
                start,
                0,
            )
            grad_values = lax.dynamic_update_slice_in_dim(
                grad_values,
                lax.dynamic_slice_in_dim(grad_values, start, block_size, 0) + value_part,
                start,
                0,
            )
            return (grad_query, grad_keys, grad_values)

        return lax.cond(start <= last_query, work, lambda state: state, carry)

    back_state = (
        jnp.zeros((rows, head_group, HEAD_SIZE), jnp.float32),
        jnp.zeros((span, HEAD_SIZE), jnp.float32),
        jnp.zeros((span, HEAD_SIZE), jnp.float32),
    )
    grad_query, grad_keys_full, grad_values_full = in_blocks(
        attend_back,
        back_state,
        (
            lax.all_gather(key_rows, "blk", axis=0, tiled=True),
            lax.all_gather(value_rows, "blk", axis=0, tiled=True),
        ),
        rows,
    )
    grad_keys, grad_values = (
        lax.psum_scatter(grad_keys_full, "blk", scatter_dimension=0, tiled=True),
        lax.psum_scatter(grad_values_full, "blk", scatter_dimension=0, tiled=True),
    )
    grad_query_lin = (
        rotary_apply(grad_query, query_where, -1.0)
        .astype(jnp.bfloat16)
        .reshape(rows, 1, head_group * HEAD_SIZE)
    )
    grad_key_lin = rotary_apply(grad_keys.reshape(rows, 1, HEAD_SIZE), query_where, -1.0).astype(
        jnp.bfloat16
    )
    grad_value_lin = grad_values.astype(jnp.bfloat16).reshape(rows, 1, HEAD_SIZE)
    back_query, key_backward, value_backward = (
        lax.all_to_all(grad_query_lin, "head", split_axis=0, concat_axis=1, tiled=True),
        lax.all_to_all(grad_key_lin, "head", split_axis=0, concat_axis=1, tiled=True),
        lax.all_to_all(grad_value_lin, "head", split_axis=0, concat_axis=1, tiled=True),
    )
    back_query = back_query.reshape(count_per_token, QUERY_HEADS * HEAD_SIZE)
    key_backward = key_backward.reshape(count_per_token, KEY_VALUE_HEADS * HEAD_SIZE)
    value_backward = value_backward.reshape(count_per_token, KEY_VALUE_HEADS * HEAD_SIZE)
    grad_query_w = jnp.einsum(
        "td,tk->dk", normed_low, back_query, preferred_element_type=jnp.float32
    )
    grad_key_w = jnp.einsum(
        "td,tk->dk", normed_low, key_backward, preferred_element_type=jnp.float32
    )
    grad_value_w = jnp.einsum(
        "td,tk->dk", normed_low, value_backward, preferred_element_type=jnp.float32
    )
    grad_normed_one = jnp.einsum(
        "tk,dk->td", back_query, query_w, preferred_element_type=jnp.float32
    )
    grad_normed_one = grad_normed_one + jnp.einsum(
        "tk,dk->td", key_backward, key_w, preferred_element_type=jnp.float32
    )
    grad_normed_one = grad_normed_one + jnp.einsum(
        "tk,dk->td", value_backward, value_w, preferred_element_type=jnp.float32
    )
    unused_value, pull_one = jax.vjp(rms_norm, inputs, gain_one)
    grad_in_norm, grad_gain_one = pull_one(grad_normed_one)
    grad_inputs = grad_residual + grad_in_norm
    sums = (
        lax.psum_scatter(grad_query_w, ("head", "blk"), scatter_dimension=0, tiled=True),
        lax.psum_scatter(grad_key_w, ("head", "blk"), scatter_dimension=0, tiled=True),
        lax.psum_scatter(grad_value_w, ("head", "blk"), scatter_dimension=0, tiled=True),
        lax.psum_scatter(grad_out_w, ("head", "blk"), scatter_dimension=0, tiled=True),
        lax.psum_scatter(grad_gain_one, ("head", "blk"), scatter_dimension=0, tiled=True),
        lax.psum_scatter(grad_gain_two, ("head", "blk"), scatter_dimension=0, tiled=True),
        lax.psum_scatter(grad_up, ("head", "blk"), scatter_dimension=1, tiled=True),
        lax.psum_scatter(grad_down, ("head", "blk"), scatter_dimension=1, tiled=True),
    )
    shape = states.shape
    return (
        final.astype(jnp.bfloat16).reshape(shape),
        loss,
        grad_inputs.reshape(shape),
        sums[4],
        sums[0],
        sums[1],
        sums[2],
        sums[3],
        sums[5],
        sums[6],
        sums[7],
    )


class Place:
    def __init__(self):
        self.x = lax.axis_index("head")
        self.b = lax.axis_index("blk")
        self.c = self.b % 2
        self.y = (self.b // 2) % 2
        self.z = self.b // 4

    def near(self, kind):
        x, y, z, c = self.x, self.y, self.z, self.c
        if kind == "up":
            z = jnp.minimum(z + 1, NZ - 1)
        elif kind == "down":
            z = jnp.maximum(z - 1, 0)
        elif kind == "y":
            y = 1 - y
        elif kind == "x":
            x = 1 - x
        elif kind == "c":
            c = 1 - c
        return (x, z * 4 + y * 2 + c)

    def blk(self, z, y, c):
        return z * 4 + y * 2 + c

    def outward(self, j):
        inner = jnp.where(j < 2, 1 - j, j)
        order = jnp.where((self.z == 0) | (self.z == NZ - 1), j, inner)
        return jnp.where(self.z < 2, order, NZ - 1 - order)

    def inward(self, j):
        inner = jnp.where(j == 0, 3, jnp.where(j == 1, 0, jnp.where(j == 2, 2, 1)))
        order = jnp.where((self.z == 0) | (self.z == NZ - 1), NZ - 1 - j, inner)
        return jnp.where(self.z < 2, order, NZ - 1 - order)


def greet_all(me):
    barrier = pltpu.get_barrier_semaphore()

    def one(k, carry):
        pl.semaphore_signal(
            barrier, inc=1, device_id=((me.x + k // 16) % 2, (me.b + k) % 16), device_id_type=MESH
        )
        return carry

    lax.fori_loop(1, 32, one, 0)
    pl.semaphore_wait(barrier, 31)


def remote(src, dst, send, recv, to):
    return pltpu.make_async_remote_copy(
        src_ref=src, dst_ref=dst, send_sem=send, recv_sem=recv, device_id=to, device_id_type=MESH
    )


def arrived(ref, sem, me):
    remote(ref, ref, sem, sem, me.near("c")).wait_recv()


def left(ref, sem, me):
    remote(ref, ref, sem, sem, me.near("c")).wait_send()


class Gather:
    def __init__(self, me, g, index, send, recv, causal=False):
        self.me, self.g, self.index, self.send, self.recv, self.causal = me, g, index, send, recv, causal
        half = g.shape[2] // 2
        self.first, self.second = pl.ds(0, half), pl.ds(half, half)

    def place(self, j):
        return self.me.z - j if self.causal else self.me.outward(j)

    def valid(self, j):
        return (j >= 0) & (j <= (self.me.z if self.causal else NZ - 1))

    def ups(self, zz):
        if self.causal:
            return self.me.z < NZ - 1
        return (zz <= self.me.z) & (self.me.z < NZ - 1)

    def downs(self, zz):
        return (zz >= self.me.z) & (self.me.z > 0)

    def put(self, j, kind, n, s, cols=None, slot=0):
        ref = self.g.at[s] if cols is None else self.g.at[s, :, cols]
        remote(ref, ref, self.send.at[j, n], self.recv.at[s, slot], self.me.near(kind)).start()

    def wait(self, s):
        arrived(self.g.at[s], self.recv.at[s, 0], self.me)

    def turn(self, j):
        me, index = self.me, self.index
        x, y, c = me.x, me.y, me.c

        @pl.when(self.valid(j) & (j > 0))
        def _():
            self.wait(index(x, self.place(j), y, c))

        @pl.when(self.valid(j))
        def _():
            zz = self.place(j)
            own = index(x, zz, y, c)
            pl.when(self.ups(zz))(lambda: self.put(j, "up", 0, own))
            if not self.causal:
                pl.when(self.downs(zz))(lambda: self.put(j, "down", 1, own))
            self.put(j, "y", 2, own)
            self.put(j, "x", 3, own)
            self.put(j, "c", 6, own)

        @pl.when(self.valid(j - 1))
        def _():
            i = j - 1
            zp = self.place(i)
            s = index(x, zp, 1 - y, c)
            self.wait(s)
            self.put(i, "x", 4, s, self.first, 0)
            self.put(i, "c", 7, s)
            t = index(1 - x, zp, y, c)
            self.wait(t)
            self.put(i, "y", 5, t, self.second, 1)
            self.put(i, "c", 8, t)

        @pl.when(self.valid(j - 2))
        def _():
            i = j - 2
            s = index(1 - x, self.place(i), 1 - y, c)
            arrived(self.g.at[s, :, self.first], self.recv.at[s, 0], me)
            arrived(self.g.at[s, :, self.second], self.recv.at[s, 1], me)
            self.put(i, "c", 9, s)

    def from_core(self, j):
        me = self.me
        for xx in (me.x, 1 - me.x):
            for yy in (me.y, 1 - me.y):
                self.wait(self.index(xx, self.place(j), yy, 1 - me.c))

    def close(self, cores=True):
        me = self.me

        def one(j, carry):
            @pl.when(self.valid(j))
            def _():
                zz = self.place(j)
                own = self.index(me.x, zz, me.y, me.c)
                whole, part = self.g.at[own], self.g.at[own, :, self.first]
                pl.when(self.ups(zz))(lambda: left(whole, self.send.at[j, 0], me))
                if not self.causal:
                    pl.when(self.downs(zz))(lambda: left(whole, self.send.at[j, 1], me))
                for n in (2, 3, 6, 7, 8, 9):
                    left(whole, self.send.at[j, n], me)
                for n in (4, 5):
                    left(part, self.send.at[j, n], me)
                if cores:
                    self.from_core(j)

            return carry

        lax.fori_loop(0, 4, one, 0)

    def run(self, between=None):
        def one(j, carry):
            self.turn(j)
            if between is not None:
                between(j)
            return carry

        lax.fori_loop(0, 6, one, 0)
        self.close()


class Sum:
    def __init__(self, me, part, index, out, room, sems, causal=False):
        self.me, self.part, self.index, self.out, self.causal = me, part, index, out, causal
        self.rc, self.rd, self.rn, self.rz, self.acc = room
        self.sc, self.ss, self.vc, self.vn, self.vz = sems
        self.half = part.shape[2] // 2
        self.first, self.second = pl.ds(0, self.half), pl.ds(self.half, self.half)

    @staticmethod
    def room(rows, columns):
        return [
            pltpu.VMEM((16, rows, columns), BF),
            pltpu.VMEM((2, 4, rows, columns // 2), BF),
            pltpu.VMEM((2, 4, rows, columns), BF),
            pltpu.VMEM((5, rows, columns), BF),
            pltpu.VMEM((rows, columns), F32),
            DMA((16,)),
            DMA((4, 6)),
            DMA((16,)),
            DMA((4, 4)),
            DMA((5,)),
        ]

    def place(self, j):
        return j if self.causal else self.me.inward(j)

    def valid(self, j):
        return (j >= 0) & (j <= (self.me.z if self.causal else NZ - 1))

    def slot(self, xx, zz, yy):
        return zz * 4 + xx * 2 + yy

    def lead(self, j):
        me = self.me
        zz = self.place(j)
        for xx in (1 - me.x, me.x):
            for yy in (1 - me.y, me.y):
                k = self.slot(xx, zz, yy)
                src = self.part.at[self.index(xx, zz, yy, 1 - me.c)]
                remote(src, self.rc.at[k], self.sc.at[k], self.vc.at[k], me.near("c")).start()

    def with_core(self, xx, zz, yy):
        k = self.slot(xx, zz, yy)
        arrived(self.rc.at[k], self.vc.at[k], self.me)
        return k, self.part[self.index(xx, zz, yy, self.me.c)].astype(F32) + self.rc[k].astype(F32)

    def turn(self, j):
        me, half, first, second = self.me, self.half, self.first, self.second
        rc, rd, rn, ss, vn = self.rc, self.rd, self.rn, self.ss, self.vn
        x, y = me.x, me.y

        @pl.when(self.valid(j))
        def _():
            zz = self.place(j)
            k, total = self.with_core(1 - x, zz, 1 - y)
            rc[k] = total.astype(BF)
            remote(rc.at[k, :, first], rd.at[0, zz], ss.at[j, 0], vn.at[zz, 0], me.near("x")).start()
            remote(rc.at[k, :, second], rd.at[1, zz], ss.at[j, 1], vn.at[zz, 1], me.near("y")).start()

        @pl.when(self.valid(j - 1))
        def _():
            i = j - 1
            zz = self.place(i)
            k, total = self.with_core(x, zz, 1 - y)
            arrived(rd.at[0, zz], vn.at[zz, 0], me)
            rc[k, :, second] = total[:, half:].astype(BF)
            rc[k, :, first] = (total[:, :half] + rd[0, zz].astype(F32)).astype(BF)
            remote(rc.at[k], rn.at[0, zz], ss.at[i, 2], vn.at[zz, 2], me.near("y")).start()
            k, total = self.with_core(1 - x, zz, y)
            arrived(rd.at[1, zz], vn.at[zz, 1], me)
            rc[k, :, first] = total[:, :half].astype(BF)
            rc[k, :, second] = (total[:, half:] + rd[1, zz].astype(F32)).astype(BF)
            remote(rc.at[k], rn.at[1, zz], ss.at[i, 3], vn.at[zz, 3], me.near("x")).start()

        @pl.when(self.valid(j - 2))
        def _():
            i = j - 2
            zz = self.place(i)
            k, total = self.with_core(x, zz, y)
            arrived(rn.at[0, zz], vn.at[zz, 2], me)
            arrived(rn.at[1, zz], vn.at[zz, 3], me)
            self.acc[...] = total + rn[0, zz].astype(F32) + rn[1, zz].astype(F32)
            along_z(me, i, zz, self.acc, rc.at[k], self.rz, ss, 4, self.vz, self.causal)

            @pl.when(zz == me.z)
            def _():
                self.out[...] = self.acc[...]

    def close(self):
        me = self.me
        whole, piece = self.rc.at[0], self.rc.at[0, :, self.first]

        def one(j, carry):
            @pl.when(self.valid(j))
            def _():
                zz = self.place(j)
                for xx in (1 - me.x, me.x):
                    for yy in (1 - me.y, me.y):
                        left(whole, self.sc.at[self.slot(xx, zz, yy)], me)
                for n in (0, 1):
                    left(piece, self.ss.at[j, n], me)
                for n in (2, 3):
                    left(whole, self.ss.at[j, n], me)
                if not self.causal:
                    pl.when(zz > me.z)(lambda: left(whole, self.ss.at[j, 4], me))
                pl.when(zz < me.z)(lambda: left(whole, self.ss.at[j, 5], me))

            return carry

        lax.fori_loop(0, 4, one, 0)

    def run(self, between=None):
        def one(j, carry):
            self.lead(j)
            return carry

        lax.fori_loop(0, 4, one, 0)

        def two(j, carry):
            self.turn(j)
            if between is not None:
                between(j)
            return carry

        lax.fori_loop(0, 6, two, 0)
        self.close()


def along_z(me, i, zz, acc, room, rz, ss, n, vz, causal=False):
    z = me.z

    def add(slot):
        arrived(rz.at[slot], vz.at[slot], me)
        acc[...] += rz[slot].astype(F32)

    if not causal:
        pl.when((zz >= z) & (z > 0))(lambda: add(zz))
    pl.when((zz < z) & (z < NZ - 1))(lambda: add(zz))
    pl.when((zz == z) & (z < NZ - 1))(lambda: add(4))

    if not causal:

        @pl.when(zz > z)
        def _():
            room[...] = acc[...].astype(BF)
            remote(room, rz.at[zz], ss.at[i, n], vz.at[zz], me.near("up")).start()

    @pl.when(zz < z)
    def _():
        room[...] = acc[...].astype(BF)
        there = jnp.where(zz == z - 1, 4, zz)
        remote(room, rz.at[there], ss.at[i, n + 1], vz.at[there], me.near("down")).start()


def by_weight(x, z, y, c):
    return x * 16 + z * 4 + y * 2 + c


def by_token(x, z, y, c):
    return (z * 4 + y * 2 + c) * 2 + x


ANY = pl.BlockSpec(memory_space=pl.ANY)
VMEM = pl.BlockSpec(memory_space=pltpu.VMEM)
DMA = pltpu.SemaphoreType.DMA


def params(number, mib):
    return pltpu.CompilerParams(
        collective_id=number, has_side_effects=True, vmem_limit_bytes=mib << 20
    )


NT = (((1,), (1,)), ((), ()))
TN = (((0,), (0,)), ((), ()))
GROUP = QUERY_HEADS // KEY_VALUE_HEADS
LANES = GROUP * 128
SCALE = HEAD_SIZE ** (-0.5)
POWER = SCALE * 1.4426950408889634


def turned(u, cosine, sine):
    return u * cosine + pltpu.roll(u, 64, 1) * sine


def allowed_keys(start, bounds):
    key = start + lax.broadcasted_iota(jnp.int32, (256, LANES), 0)
    return (key >= bounds[0:1, :]) & (key <= bounds[1:2, :])


def front_kernel(
    states, wq, wk, wv, wo, extra, up, down, cosine, sine, bounds,
    gq_out, go_out, kv_out, win, wout, h, n2, n1, qs, o_out, lse,
    gq, go, kv, top, total, acc,
    own_sem, qsend, qrecv, gsend, grecv, ksend, krecv, asend, arecv, xsend, xrecv, osend, orecv,
):
    me = Place()
    x, y, z, b, c = me.x, me.y, me.z, me.b, me.c
    here = by_weight(x, z, y, c)
    mine = [
        pltpu.make_async_copy(wq, gq.at[here, :, pl.ds(0, 1536)], own_sem.at[0]),
        pltpu.make_async_copy(wk, gq.at[here, :, pl.ds(1536, 256)], own_sem.at[1]),
        pltpu.make_async_copy(wv, gq.at[here, :, pl.ds(1792, 256)], own_sem.at[2]),
        pltpu.make_async_copy(extra, gq.at[here, :, pl.ds(2048, 256)], own_sem.at[3]),
        pltpu.make_async_copy(wo, go.at[here], own_sem.at[4]),
    ]
    for k in range(2):
        col = pl.multiple_of(k * 768 + c * 384, 128)
        mine.append(
            pltpu.make_async_copy(
                up.at[b // 2, :, pl.ds(col, 384)], win.at[x, b, :, pl.ds(k * 384, 384)], own_sem.at[5 + k]
            )
        )
    held = pltpu.make_async_copy(down.at[b // 2], wout.at[b], own_sem.at[7])
    for copy in mine:
        copy.start()
    pl.when(c == x)(held.start)
    greet_all(me)
    for copy in mine:
        copy.wait()
    pl.when(c == x)(held.wait)

    def deal(k, carry):
        t = (b + k) % 16
        for n in range(2):
            col = pl.multiple_of(n * 768 + (t % 2) * 384, 128)
            remote(
                up.at[t // 2, :, pl.ds(col, 384)],
                win.at[x, b, :, pl.ds(n * 384, 384)],
                asend.at[k, n],
                arecv.at[b, n],
                (x, t),
            ).start()
        pl.when(t % 2 == x)(
            lambda: remote(down.at[t // 2], wout.at[b], osend.at[k], orecv.at[b], (x, t)).start()
        )
        return carry

    def pass_on(k, carry):
        f = (b + 16 - k) % 16

        @pl.when(k > 0)
        def _():
            for n in range(2):
                arrived(win.at[x, f, :, pl.ds(n * 384, 384)], arecv.at[f, n], me)

        remote(win.at[x, f], win.at[x, f], xsend.at[k], xrecv.at[f], me.near("x")).start()

        @pl.when(c == x)
        def _():
            pl.when(k > 0)(lambda: arrived(wout.at[f], orecv.at[f], me))
            remote(wout.at[f], wout.at[f], osend.at[16 + k], orecv.at[f], me.near("x")).start()

        return carry

    Gather(me, gq, by_weight, qsend, qrecv).run()
    lax.fori_loop(1, 16, deal, 0)
    keep = pltpu.make_async_copy(gq, gq_out, own_sem.at[0])
    keep.start()

    rows = states[...].astype(F32)
    gains = gq[:, :, pl.ds(2048, 128)].reshape(1536, 128).astype(F32).T
    n1[...] = (
        rows * lax.rsqrt(jnp.mean(rows * rows, axis=-1, keepdims=True) + 1e-06) * gains[0:1]
    ).astype(BF)
    qkv = jnp.dot(n1[...], gq[:, :, pl.ds(0, 2048)].reshape(1536, 2048), preferred_element_type=F32)
    cos, sin = cosine[...], sine[...]
    at = by_token(x, z, y, c)
    for i in range(2):
        kv[at, :, i * 128 : i * 128 + 128] = turned(qkv[:, 1536 + i * 128 : 1664 + i * 128], cos, sin).astype(BF)
        kv[at, :, 256 + i * 128 : 384 + i * 128] = qkv[:, 1792 + i * 128 : 1920 + i * 128].astype(BF)
    for i in range(QUERY_HEADS):
        r = (i % GROUP) * 128
        qs[i // GROUP, r : r + 128] = turned(qkv[:, i * 128 : i * 128 + 128], cos, sin).astype(BF)

    top[...] = jnp.full_like(top, FLOOR_SCORE)
    total[...] = jnp.zeros_like(total)
    acc[...] = jnp.zeros_like(acc)
    keys = Gather(me, kv, by_token, ksend, krecv, causal=True)
    output = Gather(me, go, by_weight, gsend, grecv)

    def block(n):
        ok = allowed_keys(n * 256, bounds)
        for i in range(2):
            k = kv[pl.ds(n * 2, 2), :, i * 128 : i * 128 + 128].reshape(256, 128)
            v = kv[pl.ds(n * 2, 2), :, 256 + i * 128 : 384 + i * 128].reshape(256, 128)
            s = lax.dot_general(k, qs[i], NT, preferred_element_type=F32)
            s = jnp.where(ok, s, FLOOR_SCORE)
            old = top[i]
            new = jnp.maximum(old, jnp.max(s, axis=0, keepdims=True))
            factor = jnp.exp2((old - new) * POWER)
            p = jnp.exp2((s - new) * POWER)
            top[i] = new
            total[i] = total[i] * factor + jnp.sum(p, axis=0, keepdims=True)
            acc[i] = acc[i] * factor + lax.dot_general(v, p.astype(BF), TN, preferred_element_type=F32)

    def turn(j, carry):
        keys.turn(j)
        output.turn(j - 2)

        @pl.when(j == 4)
        def _():
            lax.fori_loop(0, 4, pass_on, 0)

        @pl.when(j == 5)
        def _():
            lax.fori_loop(4, 8, pass_on, 0)

        @pl.when(keys.valid(j - 2))
        def _():
            i = j - 2
            keys.from_core(i)
            zz = z - i
            last = jnp.where(i == 0, y * 2 + c, 3)

            def one(n, carry):
                block(zz * 4 + last - n)
                return carry

            lax.fori_loop(0, last + 1, one, 0)

        return carry

    lax.fori_loop(0, 8, turn, 0)
    lax.fori_loop(8, 16, pass_on, 0)
    output.close()
    keep_o = pltpu.make_async_copy(go, go_out, own_sem.at[1])
    keep_o.start()
    keep_k = pltpu.make_async_copy(kv, kv_out, own_sem.at[2])
    keep_k.start()
    for i in range(2):
        lse[i] = top[i] * POWER + jnp.log2(total[i])
        done = acc[i] / total[i]
        for r in range(GROUP):
            col = (i * GROUP + r) * 128
            o_out[:, col : col + 128] = done[:, r * 128 : r * 128 + 128].T
    res = rows + jnp.dot(
        o_out[...].astype(BF), go[...].reshape(1536, 1536), preferred_element_type=F32
    )
    h[...] = res
    n2[...] = (
        res * lax.rsqrt(jnp.mean(res * res, axis=-1, keepdims=True) + 1e-06) * gains[1:2]
    ).astype(BF)

    keys.close(False)

    def close(k, carry):
        slab, piece = win.at[x, b], win.at[x, b, :, pl.ds(0, 384)]

        @pl.when(k > 0)
        def _():
            for n in range(2):
                left(piece, asend.at[k, n], me)
            pl.when((b + k) % 2 == x)(lambda: left(wout.at[b], osend.at[k], me))

        left(slab, xsend.at[k], me)
        pl.when(c == x)(lambda: left(wout.at[b], osend.at[16 + k], me))
        arrived(win.at[1 - x, k], xrecv.at[k], me)
        pl.when(c != x)(lambda: arrived(wout.at[k], orecv.at[k], me))
        return carry

    lax.fori_loop(0, 16, close, 0)
    keep.wait()
    keep_o.wait()
    keep_k.wait()


def run_front(states, wq, wk, wv, wo, extra, up, down, cosine, sine, bounds):
    shape = jax.ShapeDtypeStruct
    return pl.pallas_call(
        front_kernel,
        out_shape=(
            shape((32, 48, 2304), BF),
            shape((32, 48, 1536), BF),
            shape((32, 128, 512), BF),
            shape((2, 16, 48, 768), BF),
            shape((16, 48, 768), BF),
            shape((128, 1536), F32),
            shape((128, 1536), BF),
            shape((128, 1536), BF),
            shape((2, LANES, 128), BF),
            shape((128, 1536), F32),
            shape((2, 1, LANES), F32),
        ),
        in_specs=[VMEM] + [ANY] * 7 + [VMEM] * 3,
        out_specs=(ANY,) * 5 + (VMEM,) * 6,
        scratch_shapes=[
            pltpu.VMEM((32, 48, 2304), BF),
            pltpu.VMEM((32, 48, 1536), BF),
            pltpu.VMEM((32, 128, 512), BF),
            pltpu.VMEM((2, 1, LANES), F32),
            pltpu.VMEM((2, 1, LANES), F32),
            pltpu.VMEM((2, 128, LANES), F32),
            DMA((8,)),
            DMA((4, 10)),
            DMA((32, 2)),
            DMA((4, 10)),
            DMA((32, 2)),
            DMA((4, 10)),
            DMA((32, 2)),
            DMA((16, 2)),
            DMA((16, 2)),
            DMA((16,)),
            DMA((16,)),
            DMA((32,)),
            DMA((16,)),
        ],
        compiler_params=params(1, 48),
        name="front",
    )(states, wq, wk, wv, wo, extra, up, down, cosine, sine, bounds)


GELU_A = 0.7978845608028654
GELU_B = 0.044715


def experts_kernel(
    n2, h, teacher, weight, gate, win, wout,
    final, err, dn2, dy_out, dwin, dwout,
    nall, dyall, pairs, zg, dpairs, part, rc, ry, rz, acc, errs,
    gsend, grecv, csend, crecv, ysend, yrecv, zsend, zrecv, esend, erecv,
):
    me = Place()
    x, y, z, b, c = me.x, me.y, me.z, me.b, me.c
    greet_all(me)

    def gather(buf, way, chunk):
        def put(j, kind, n, s):
            remote(buf.at[s], buf.at[s], gsend.at[way, j, n], grecv.at[way, s], me.near(kind)).start()

        def turn(j, carry):
            zz = me.outward(j)
            own = me.blk(zz, y, c)

            @pl.when((j > 0) & (j < 4))
            def _():
                arrived(buf.at[own], grecv.at[way, own], me)

            @pl.when(j < 4)
            def _():
                pl.when((zz <= z) & (z < NZ - 1))(lambda: put(j, "up", 0, own))
                pl.when((zz >= z) & (z > 0))(lambda: put(j, "down", 1, own))
                put(j, "y", 2, own)
                put(j, "c", 3, own)

            @pl.when(j > 0)
            def _():
                i = j - 1
                zp = me.outward(i)
                s = me.blk(zp, 1 - y, c)
                arrived(buf.at[s], grecv.at[way, s], me)
                put(i, "c", 4, s)

                def both(n, carry):
                    yy = (y + n) % 2
                    s = me.blk(zp, yy, 1 - c)
                    arrived(buf.at[s], grecv.at[way, s], me)
                    chunk(zp * 2 + yy)
                    return carry

                lax.fori_loop(0, 2, both, 0)

            return carry

        lax.fori_loop(0, 5, turn, 0)

        def close(j, carry):
            zz = me.outward(j)
            whole = buf.at[b]
            pl.when((zz <= z) & (z < NZ - 1))(lambda: left(whole, gsend.at[way, j, 0], me))
            pl.when((zz >= z) & (z > 0))(lambda: left(whole, gsend.at[way, j, 1], me))
            for n in (2, 3, 4):
                left(whole, gsend.at[way, j, n], me)
            return carry

        lax.fori_loop(0, 4, close, 0)

    def to_other_core(way, q):
        remote(part.at[q * 2 + 1 - c], rc.at[way, q], csend.at[way, q], crecv.at[way, q], me.near("c")).start()

    def reduce(way, between):
        def lead(j, carry):
            zz = me.inward(j)
            q = zz * 2 + 1 - y
            s = q * 2 + c
            arrived(rc.at[way, q], crecv.at[way, q], me)
            part[s] = (part[s].astype(F32) + rc[way, q].astype(F32)).astype(BF)
            remote(part.at[s], ry.at[way, zz], ysend.at[way, j], yrecv.at[way, zz], me.near("y")).start()
            return carry

        lax.fori_loop(0, 4, lead, 0)

        def turn(j, carry):
            between(j)
            zz = me.inward(j)
            q = zz * 2 + y
            s = q * 2 + c
            arrived(rc.at[way, q], crecv.at[way, q], me)
            arrived(ry.at[way, zz], yrecv.at[way, zz], me)
            acc[...] = part[s].astype(F32) + rc[way, q].astype(F32) + ry[way, zz].astype(F32)
            along_z(me, j, zz, acc, part.at[s], rz.at[way], zsend.at[way], 0, zrecv.at[way])
            return carry

        lax.fori_loop(0, 4, turn, 0)

        def close(j, carry):
            zz = me.inward(j)
            whole = part.at[b]
            left(whole, ysend.at[way, j], me)
            left(whole, csend.at[way, j], me)
            left(whole, csend.at[way, j + 4], me)
            pl.when(zz > z)(lambda: left(whole, zsend.at[way, j, 0], me))
            pl.when(zz < z)(lambda: left(whole, zsend.at[way, j, 1], me))
            return carry

        lax.fori_loop(0, 4, close, 0)

    def gelu_parts(g):
        t = jnp.tanh(GELU_A * (g + GELU_B * g * g * g))
        return t, 0.5 * g * (1.0 + t)

    def forward(q):
        rows = nall[pl.ds(q * 2, 2)].reshape(256, 1536)
        pair = jnp.dot(rows, win[...], preferred_element_type=F32)
        pairs[q] = pair
        unused, a = gelu_parts(pair[:, :384])
        zq = (a * pair[:, 384:] * gate[q]).astype(BF)
        zg[q] = zq
        out = jnp.dot(zq, wout[...], preferred_element_type=F32)
        part[pl.ds(q * 2, 2)] = out.astype(BF).reshape(2, 128, 1536)
        to_other_core(0, q)

    def backward(q):
        rows = dyall[pl.ds(q * 2, 2)].reshape(256, 1536)
        dz = lax.dot_general(rows, wout[...], NT, preferred_element_type=F32) * gate[q]
        g, u = pairs[q, :, :384], pairs[q, :, 384:]
        t, a = gelu_parts(g)
        slope = 0.5 * (1.0 + t) + 0.5 * g * (1.0 - t * t) * (GELU_A * (1.0 + 3.0 * GELU_B * g * g))
        dpairs[q, :, :384] = (dz * u * slope).astype(BF)
        dpairs[q, :, 384:] = (dz * a).astype(BF)
        out = lax.dot_general(dpairs[q], win[...], NT, preferred_element_type=F32)
        part[pl.ds(q * 2, 2)] = out.astype(BF).reshape(2, 128, 1536)
        to_other_core(1, q)

    nall[b] = n2[...]
    gather(nall, 0, forward)
    reduce(0, lambda j: None)

    done = h[...] + acc[...]
    final[...] = done.astype(BF)
    diff = done - teacher[...].astype(F32)
    scaled = weight[:, 0:1] * diff
    dy_out[...] = scaled
    dyall[b] = scaled.astype(BF)
    kept = jnp.sum(weight[:, 1:2] * diff * diff)
    me_index = x * 16 + b
    errs[me_index] = jnp.zeros((8, 128), F32) + kept

    def tell(k, carry):
        to = ((x + k // 16) % 2, (b + k) % 16)
        remote(errs.at[me_index], errs.at[me_index], esend.at[k], erecv.at[me_index], to).start()
        return carry

    lax.fori_loop(1, 32, tell, 0)
    gather(dyall, 1, backward)

    def weight_part(j):
        for i in range(2):

            @pl.when(j * 2 + i < 6)
            def _():
                col = pl.ds(pl.multiple_of((j * 2 + i) * 256, 256), 256)
                rows = nall[:, :, col].reshape(2048, 256)
                both = dpairs[...].reshape(2048, 768)
                dwin[col, :] = lax.dot_general(rows, both, TN, preferred_element_type=F32).astype(BF)
                right = dyall[:, :, col].reshape(2048, 256)
                zall = zg[...].reshape(2048, 384)
                dwout[:, col] = lax.dot_general(zall, right, TN, preferred_element_type=F32).astype(BF)

    reduce(1, weight_part)
    dn2[...] = acc[...]

    def hear(k, carry):
        left(errs.at[0], esend.at[k], me)
        s = ((x + k // 16) % 2) * 16 + (b + k) % 16
        arrived(errs.at[s], erecv.at[s], me)
        return carry

    lax.fori_loop(1, 32, hear, 0)
    total = errs[0]
    for s in range(1, 32):
        total = total + errs[s]
    err[...] = total


def run_experts(n2, h, teacher, weight, gate, win, wout):
    wide = (128, 1536)
    shard = (16,) + wide
    return pl.pallas_call(
        experts_kernel,
        out_shape=(
            jax.ShapeDtypeStruct(wide, BF),
            jax.ShapeDtypeStruct((8, 128), F32),
            jax.ShapeDtypeStruct(wide, F32),
            jax.ShapeDtypeStruct(wide, F32),
            jax.ShapeDtypeStruct((1536, 768), BF),
            jax.ShapeDtypeStruct((384, 1536), BF),
        ),
        in_specs=[VMEM] * 7,
        out_specs=(VMEM,) * 6,
        scratch_shapes=[
            pltpu.VMEM(shard, BF),
            pltpu.VMEM(shard, BF),
            pltpu.VMEM((8, 256, 768), F32),
            pltpu.VMEM((8, 256, 384), BF),
            pltpu.VMEM((8, 256, 768), BF),
            pltpu.VMEM(shard, BF),
            pltpu.VMEM((2, 8) + wide, BF),
            pltpu.VMEM((2, 4) + wide, BF),
            pltpu.VMEM((2, 5) + wide, BF),
            pltpu.VMEM(wide, F32),
            pltpu.VMEM((32, 8, 128), F32),
            DMA((2, 4, 5)),
            DMA((2, 16)),
            DMA((2, 8)),
            DMA((2, 8)),
            DMA((2, 4)),
            DMA((2, 4)),
            DMA((2, 4, 2)),
            DMA((2, 5)),
            DMA((32,)),
            DMA((32,)),
        ],
        compiler_params=params(2, 61),
        name="experts",
    )(n2, h, teacher, weight, gate, win, wout)


def norm_back(values, gain, grad):
    scale = lax.rsqrt(jnp.mean(values * values, axis=-1, keepdims=True) + 1e-06)
    inner = grad * gain
    mean = jnp.mean(inner * values, axis=-1, keepdims=True)
    return scale * inner - values * (scale * scale * scale * mean), jnp.sum(
        grad * values * scale, axis=0, keepdims=True
    )


def back_kernel(
    states, h, n1, qs, o, lse, dn2, dy, cosine, sine, bounds, dwin, dwout, gq, go, kv_in,
    gx, gqkv, gout, gup, gdown,
    wq, wo, kv, pk, dos, delta, dh, dq, dkv, dqkv, xin, xout, *rest,
):
    sums = [(rest[i * 10 : i * 10 + 5], rest[i * 10 + 5 : i * 10 + 10]) for i in range(3)]
    own_sem, xsend, xrecv, asend, arecv, osend, orecv = rest[30:]
    me = Place()
    x, y, z, b, c = me.x, me.y, me.z, me.b, me.c
    loads = [
        pltpu.make_async_copy(go, wo, own_sem.at[0]),
        pltpu.make_async_copy(kv_in, kv, own_sem.at[1]),
        pltpu.make_async_copy(gq, wq, own_sem.at[2]),
    ]
    for load in loads:
        load.start()
    greet_all(me)

    def over(k, carry):
        t = (b + k) % 16
        remote(dwin.at[1 - x, t], xin.at[t], xsend.at[k], xrecv.at[t], me.near("x")).start()
        pl.when(c != x)(
            lambda: remote(dwout.at[t], xout.at[t], osend.at[k], orecv.at[t], me.near("x")).start()
        )
        return carry

    lax.fori_loop(0, 16, over, 0)

    def own_piece(n, t):
        col = pl.multiple_of(n * 768 + c * 384, 128)
        return (
            xin.at[t, :, pl.ds(n * 384, 384)],
            gup.at[b // 2, :, pl.ds(col, 384)],
        )

    def deal(k, carry):
        t = (b + k) % 16
        arrived(xin.at[t], xrecv.at[t], me)
        xin[t] = (xin[t].astype(F32) + dwin[x, t].astype(F32)).astype(BF)

        @pl.when(k > 0)
        def _():
            for n in range(2):
                src, dst = own_piece(n, t)
                remote(src, dst, asend.at[k, n], arecv.at[b, n], (x, t)).start()

        @pl.when(k == 0)
        def _():
            for n in range(2):
                src, dst = own_piece(n, t)
                pltpu.make_async_copy(src, dst, own_sem.at[3 + n]).start()

        @pl.when(c == x)
        def _():
            arrived(xout.at[t], orecv.at[t], me)
            xout[t] = (xout[t].astype(F32) + dwout[t].astype(F32)).astype(BF)
            pl.when(k > 0)(
                lambda: remote(
                    xout.at[t], gdown.at[b // 2], osend.at[16 + k], orecv.at[16 + b // 2], (x, t)
                ).start()
            )
            pl.when(k == 0)(
                lambda: pltpu.make_async_copy(xout.at[t], gdown.at[b // 2], own_sem.at[5]).start()
            )

        return carry

    loads[2].wait()
    gains = wq[:, :, pl.ds(2048, 128)].reshape(1536, 128).astype(F32).T
    res_grad, gain_two = norm_back(h[...], gains[1:2], dn2[...])
    dh[...] = dy[...] + res_grad
    da = dh[...].astype(BF)
    loads[0].wait()
    do = lax.dot_general(
        da, wo[...].reshape(1536, 1536), NT, preferred_element_type=F32
    ).astype(BF)
    low = o[...].astype(BF)
    for i in range(4):
        part = lax.dot_general(low[:, i * 384 : i * 384 + 384], da, TN, preferred_element_type=F32)
        wo[i * 8 : i * 8 + 8] = part.astype(BF).reshape(8, 48, 1536)
    out_sum = Sum(me, wo, by_weight, gout, *sums[0])
    key_sum = Sum(me, pk, by_token, dkv, *sums[1], causal=True)

    def lead_all(which):
        def one(j, carry):
            which.lead(j)
            return carry

        lax.fori_loop(0, 4, one, 0)

    lead_all(out_sum)
    for i in range(QUERY_HEADS):
        col, r = i * 128, (i % GROUP) * 128
        dos[i // GROUP, r : r + 128] = do[:, col : col + 128]
        prod = do[:, col : col + 128].astype(F32) * o[:, col : col + 128]
        delta[i // GROUP, :, r : r + 128] = jnp.sum(prod.T, axis=0, keepdims=True)
    dq[...] = jnp.zeros_like(dq)
    loads[1].wait()

    def block(n):
        ok = allowed_keys(n * 256, bounds)
        for i in range(2):
            k = kv[pl.ds(n * 2, 2), :, i * 128 : i * 128 + 128].reshape(256, 128)
            v = kv[pl.ds(n * 2, 2), :, 256 + i * 128 : 384 + i * 128].reshape(256, 128)
            s = lax.dot_general(k, qs[i], NT, preferred_element_type=F32)
            p = jnp.where(ok, jnp.exp2(s * POWER - lse[i]), 0.0)
            dp = lax.dot_general(v, dos[i], NT, preferred_element_type=F32)
            ds = (p * (dp - delta[i])).astype(BF)
            dv = jnp.dot(p.astype(BF), dos[i], preferred_element_type=F32)
            dk = jnp.dot(ds, qs[i], preferred_element_type=F32) * SCALE
            pk[pl.ds(n * 2, 2), :, i * 128 : i * 128 + 128] = dk.astype(BF).reshape(2, 128, 128)
            pk[pl.ds(n * 2, 2), :, 256 + i * 128 : 384 + i * 128] = dv.astype(BF).reshape(2, 128, 128)
            dq[i] += lax.dot_general(k, ds, TN, preferred_element_type=F32)

    def turn(j, carry):
        out_sum.turn(j)

        @pl.when((j >= 2) & (j < 4))
        def _():
            lax.fori_loop((j - 2) * 8, (j - 2) * 8 + 8, deal, 0)

        @pl.when(key_sum.valid(j))
        def _():
            last = jnp.where(j == z, y * 2 + c, 3)

            def one(n, carry):
                block(j * 4 + n)
                return carry

            lax.fori_loop(0, last + 1, one, 0)

            def blank(n, carry):
                pk[pl.ds((j * 4 + n) * 2, 2)] = jnp.zeros((2, 128, 512), BF)
                return carry

            lax.fori_loop(last + 1, 4, blank, 0)
            key_sum.lead(j)

        key_sum.turn(j)
        return carry

    lax.fori_loop(0, 6, turn, 0)

    cos, sin = cosine[...], -sine[...]
    for i in range(QUERY_HEADS):
        r = (i % GROUP) * 128
        head = dq[i // GROUP, :, r : r + 128].T * SCALE
        dqkv[:, i * 128 : i * 128 + 128] = turned(head, cos, sin).astype(BF)
    for i in range(2):
        dqkv[:, 1536 + i * 128 : 1664 + i * 128] = turned(dkv[:, i * 128 : i * 128 + 128], cos, sin).astype(BF)
        dqkv[:, 1792 + i * 128 : 1920 + i * 128] = dkv[:, 256 + i * 128 : 384 + i * 128].astype(BF)
    dn1 = lax.dot_general(
        dqkv[...], wq[:, :, pl.ds(0, 2048)].reshape(1536, 2048), NT, preferred_element_type=F32
    )
    in_grad, gain_one = norm_back(states[...].astype(F32), gains[0:1], dn1)
    gx[...] = dh[...] + in_grad
    rows = lax.broadcasted_iota(jnp.int32, (128, 1536), 0)
    tail = jnp.where(rows == 0, gain_one, jnp.where(rows == 1, gain_two, 0.0)).T
    wq[:, :, pl.ds(2048, 128)] = tail.astype(BF).reshape(32, 48, 128)
    for i in range(4):
        part = lax.dot_general(
            n1[:, i * 384 : i * 384 + 384], dqkv[...], TN, preferred_element_type=F32
        )
        wq[i * 8 : i * 8 + 8, :, 0:2048] = part.astype(BF).reshape(8, 48, 2048)
    proj_sum = Sum(me, wq, by_weight, gqkv, *sums[2])
    lead_all(proj_sum)

    def last_turn(j, carry):
        proj_sum.turn(j)
        return carry

    lax.fori_loop(0, 6, last_turn, 0)
    out_sum.close()
    key_sum.close()
    proj_sum.close()

    def close(k, carry):
        left(xin.at[0], xsend.at[k], me)
        pl.when(c != x)(lambda: left(xout.at[0], osend.at[k], me))

        @pl.when(k > 0)
        def _():
            f = (b + 16 - k) % 16
            for n in range(2):
                left(xin.at[0, :, pl.ds(0, 384)], asend.at[k, n], me)
                col = pl.multiple_of(n * 768 + (f % 2) * 384, 128)
                arrived(gup.at[f // 2, :, pl.ds(col, 384)], arecv.at[f, n], me)
            pl.when(c == x)(lambda: left(xout.at[0], osend.at[16 + k], me))
            pl.when(f % 2 == x)(lambda: arrived(gdown.at[f // 2], orecv.at[16 + f // 2], me))

        @pl.when(k == 0)
        def _():
            for n in range(2):
                src, dst = own_piece(n, b)
                pltpu.make_async_copy(src, dst, own_sem.at[3 + n]).wait()
            pl.when(c == x)(
                lambda: pltpu.make_async_copy(xout.at[b], gdown.at[b // 2], own_sem.at[5]).wait()
            )

        return carry

    lax.fori_loop(0, 16, close, 0)


def run_back(*operands):
    shape = jax.ShapeDtypeStruct
    return pl.pallas_call(
        back_kernel,
        out_shape=(
            shape((128, 1536), F32),
            shape((48, 2304), F32),
            shape((48, 1536), F32),
            shape((8, 48, 1536), BF),
            shape((8, 48, 768), BF),
        ),
        in_specs=[VMEM] * 13 + [ANY] * 3,
        out_specs=(VMEM,) * 3 + (ANY,) * 2,
        scratch_shapes=[
            pltpu.VMEM((32, 48, 2304), BF),
            pltpu.VMEM((32, 48, 1536), BF),
            pltpu.VMEM((32, 128, 512), BF),
            pltpu.VMEM((32, 128, 512), BF),
            pltpu.VMEM((2, LANES, 128), BF),
            pltpu.VMEM((2, 1, LANES), F32),
            pltpu.VMEM((128, 1536), F32),
            pltpu.VMEM((2, 128, LANES), F32),
            pltpu.VMEM((128, 512), F32),
            pltpu.VMEM((128, 2048), BF),
            pltpu.VMEM((16, 48, 768), BF),
            pltpu.VMEM((16, 48, 768), BF),
        ]
        + Sum.room(48, 1536)
        + Sum.room(128, 512)
        + Sum.room(48, 2304)
        + [DMA((6,)), DMA((16,)), DMA((16,)), DMA((16, 2)), DMA((16, 2)), DMA((32,)), DMA((32,))],
        compiler_params=params(3, 61),
        name="back",
    )(*operands)


def per_device(
    states, teacher, valid, routes, gates, doc_starts, norm_one,
    w_query, key_weight, value_weight, w_output, norm_two, expert_in, expert_out,
):
    tokens = states.shape[2]
    width = states.shape[3]
    b, x = lax.axis_index("blk"), lax.axis_index("head")
    span = tokens * lax.axis_size("head") * lax.axis_size("blk")
    place = (b * 2 + x) * tokens + jnp.arange(tokens, dtype=jnp.int32)
    unused_segment, position = doc_layout(place, doc_starts)
    half = HEAD_SIZE // 2
    freq = ROTARY_BASE ** (-jnp.arange(half).astype(jnp.float32) / half)
    angle = position.astype(jnp.float32)[:, None] * freq[None, :]
    cosine, sine = jnp.cos(angle), jnp.sin(angle)
    cosine = jnp.concatenate([cosine, cosine], axis=1)
    sine = jnp.concatenate([-sine, sine], axis=1)
    bounds = jnp.tile(jnp.stack([place - position, place]), (1, GROUP))
    keep_mask = valid.reshape(tokens).astype(F32)
    route_rows = routes.reshape(tokens, TOP)
    gate_rows = gates.reshape(tokens, TOP)

    table = jnp.sum(
        jnp.where(route_rows[None] == jnp.arange(E, dtype=jnp.int32)[:, None, None], gate_rows[None], 0.0), axis=-1
    )
    high = lax.reduce_precision(table, 8, 7)
    column = jnp.arange(128)[None, :]
    gains = jnp.where(
        column == 0,
        norm_one[:, None].astype(F32),
        jnp.where(column == 1, norm_two[:, None].astype(F32), jnp.sum(keep_mask)),
    )
    routed = jnp.concatenate([high, table - high, jnp.zeros((32, 128), F32)], axis=0)
    extra = jnp.concatenate([gains, routed], axis=1).astype(BF)
    rows = states.reshape(tokens, width)
    gq, go, kv, win, wout, h, n2, n1, qs, o, lse = run_front(
        rows, w_query, key_weight, value_weight, w_output, extra, expert_in,
        expert_out.reshape(E, 48, 768), cosine, sine, bounds,
    )
    count_all = jnp.sum(gq[:, 0, 2050].astype(F32))
    tables = lax.dynamic_slice_in_dim(gq[:, :16, 2176:], x * 16, 16, 0).astype(F32)
    mine = lax.dynamic_slice_in_dim(tables, b // 2, 1, 1) + lax.dynamic_slice_in_dim(tables, 8 + b // 2, 1, 1)
    weight = jnp.stack([keep_mask * (span * 1.0 / count_all), keep_mask], axis=1)
    final, error, dn2, dy, dwin, dwout = run_experts(
        n2, h, teacher.reshape(tokens, width), weight, mine.reshape(8, 256, 1),
        win.reshape(1536, 768), wout.reshape(384, 1536),
    )
    gx, gqkv, gout, gup, gdown = run_back(
        rows, h, n1, qs, o, lse, dn2, dy, cosine, sine, bounds,
        dwin.reshape(2, 16, 48, 768), dwout.reshape(16, 48, 768), gq, go, kv,
    )
    shape = states.shape
    return (
        final.reshape(shape),
        error[0, 0] / (width * count_all),
        gx.reshape(shape),
        gqkv[:, 2048],
        gqkv[:, :1536],
        gqkv[:, 1536:1792],
        gqkv[:, 1792:2048],
        gout,
        gqkv[:, 2049],
        gup.astype(F32),
        gdown.astype(F32).reshape(E, 24, 1536),
    )


def solution(mesh):
    in_specs = (
        P("blk", "head", None, None),
        P("blk", "head", None, None),
        P("blk", "head", None),
        P("blk", "head", None, None),
        P("blk", "head", None, None),
        P(),
        P(("head", "blk")),
        P(("head", "blk"), None),
        P(("head", "blk"), None),
        P(("head", "blk"), None),
        P(("head", "blk"), None),
        P(("head", "blk")),
        P(None, ("head", "blk"), None),
        P(None, ("head", "blk"), None),
    )
    out_specs = (
        P("blk", "head", None, None),
        P(),
        P("blk", "head", None, None),
        P(("head", "blk")),
        P(("head", "blk"), None),
        P(("head", "blk"), None),
        P(("head", "blk"), None),
        P(("head", "blk"), None),
        P(("head", "blk")),
        P(None, ("head", "blk"), None),
        P(None, ("head", "blk"), None),
    )
    sizes = dict(mesh.shape)
    plan = per_device if sizes == {"head": 2, "blk": 4 * NZ} else per_device_plain
    return jax.shard_map(
        plan, mesh=mesh, in_specs=in_specs, out_specs=out_specs, check_vma=False
    )
```

```python
import functools

import jax
import jax.numpy as jnp
import numpy as np
from jax import lax
from jax.experimental import pallas as pl
from jax.experimental.pallas import tpu as pltpu
from jax.sharding import PartitionSpec as P

QUERY_HEADS = 12
KEY_VALUE_HEADS = 2
HEAD_SIZE = 128
TOP = 4
E = 8
CAP = 96

ROTARY_BASE = 10000.0
FLOOR_SCORE = -1e30

MESH = pl.DeviceIdType.MESH
NZ = 4
SPAN = 32 * 128.0
BF = jnp.bfloat16
F32 = jnp.float32

def product(left, right):
    return jnp.dot(left, right, preferred_element_type=jnp.float32)


def rms_norm(values, gain):
    scale = lax.rsqrt(jnp.mean(values * values, axis=-1, keepdims=True) + 1e-06)
    return values * scale * gain


def rotary_apply(values, where, sign):
    half = values.shape[-1] // 2
    freq = ROTARY_BASE ** (-jnp.arange(half).astype(jnp.float32) / half)
    angle = where.astype(jnp.float32)[:, None] * freq[None, :]
    cosine = jnp.cos(angle)[:, None, :]
    sine = jnp.sin(angle)[:, None, :] * sign
    first = values[..., :half]
    second = values[..., half:]
    return jnp.concatenate(
        [first * cosine - second * sine, second * cosine + first * sine], axis=-1
    )


def doc_layout(position_index, doc_starts):
    inside = (position_index[:, None] >= doc_starts[None, :]).astype(jnp.int32)
    document_segment = jnp.sum(inside, axis=-1) - 1
    begin = jnp.max(jnp.where(inside > 0, doc_starts[None, :], 0), axis=-1)
    return (document_segment, position_index - begin)


def gated(pair):
    half = pair.shape[-1] // 2
    return jax.nn.gelu(pair[..., :half], approximate=True) * pair[..., half:]


def in_blocks(step_fn, carry, piece, rows):
    count_blocks = piece[0].shape[0] // rows

    def turn(number, state):
        part = tuple((lax.dynamic_slice_in_dim(item, number * rows, rows, 0) for item in piece))
        return step_fn(state, part, number * rows)

    return lax.fori_loop(0, count_blocks, turn, carry)


def per_device_plain(
    states,
    teacher,
    valid,
    routes,
    gates,
    doc_starts,
    norm_one,
    w_query,
    key_weight,
    value_weight,
    w_output,
    norm_two,
    expert_in,
    expert_out,
):
    count_per_token = states.shape[2]
    width = states.shape[3]
    pairs = lax.axis_size("head")
    blocks = lax.axis_size("blk")
    rows = count_per_token * pairs
    span = rows * blocks
    head_group = QUERY_HEADS // KEY_VALUE_HEADS
    scale = HEAD_SIZE ** (-0.5)
    highest = lax.Precision.HIGHEST
    block_index = lax.axis_index("blk")
    pair_index = lax.axis_index("head")
    token_index = (block_index * pairs + pair_index) * count_per_token + jnp.arange(
        count_per_token, dtype=jnp.int32
    )
    unused_segment, token_position = doc_layout(token_index, doc_starts)
    query_index = block_index * rows + jnp.arange(rows, dtype=jnp.int32)
    query_segment, query_where = doc_layout(query_index, doc_starts)
    last_query = block_index * rows + rows - 1
    inputs = states.reshape(count_per_token, width).astype(jnp.float32)
    target = teacher.reshape(count_per_token, width).astype(jnp.float32)
    keep_mask = valid.reshape(count_per_token).astype(jnp.float32)
    route_rows = routes.reshape(count_per_token, TOP)
    gate_rows = gates.reshape(count_per_token, TOP)
    query_w, key_w, value_w, out_w, gain_low_one, gain_low_two = (
        lax.all_gather(w_query, ("head", "blk"), axis=0, tiled=True),
        lax.all_gather(key_weight, ("head", "blk"), axis=0, tiled=True),
        lax.all_gather(value_weight, ("head", "blk"), axis=0, tiled=True),
        lax.all_gather(w_output, ("head", "blk"), axis=0, tiled=True),
        lax.all_gather(norm_one, ("head", "blk"), axis=0, tiled=True),
        lax.all_gather(norm_two, ("head", "blk"), axis=0, tiled=True),
    )
    gain_one = gain_low_one.astype(jnp.float32)
    gain_two = gain_low_two.astype(jnp.float32)
    normed_one = rms_norm(inputs, gain_one)
    normed_low = normed_one.astype(jnp.bfloat16)
    query_lin = product(normed_low, query_w)
    key_linear = product(normed_low, key_w)
    value_linear = product(normed_low, value_w)
    query_rotated = rotary_apply(
        query_lin.reshape(count_per_token, QUERY_HEADS, HEAD_SIZE), token_position, 1.0
    )
    key_rotated = rotary_apply(
        key_linear.reshape(count_per_token, KEY_VALUE_HEADS, HEAD_SIZE), token_position, 1.0
    )
    query_outgoing = query_rotated.astype(jnp.bfloat16).reshape(
        count_per_token, KEY_VALUE_HEADS, head_group * HEAD_SIZE
    )
    key_send = key_rotated.astype(jnp.bfloat16)
    value_outgoing = value_linear.astype(jnp.bfloat16).reshape(
        count_per_token, KEY_VALUE_HEADS, HEAD_SIZE
    )
    query_grp, key_grp, value_grp = (
        lax.all_to_all(query_outgoing, "head", split_axis=1, concat_axis=0, tiled=True),
        lax.all_to_all(key_send, "head", split_axis=1, concat_axis=0, tiled=True),
        lax.all_to_all(value_outgoing, "head", split_axis=1, concat_axis=0, tiled=True),
    )
    query_heads = query_grp.reshape(rows, head_group, HEAD_SIZE)
    key_rows = key_grp.reshape(rows, HEAD_SIZE)
    value_rows = value_grp.reshape(rows, HEAD_SIZE)

    def scores_for(keys, start):
        block_size = keys.shape[0]
        key_index = start + jnp.arange(block_size, dtype=jnp.int32)
        key_segment, unused_where = doc_layout(key_index, doc_starts)
        allowed = (key_index[None, :] <= query_index[:, None]) & (
            key_segment[None, :] == query_segment[:, None]
        )
        raw = (
            jnp.einsum("qhd,kd->hqk", query_heads, keys, preferred_element_type=jnp.float32) * scale
        )
        return (raw, allowed[None])

    def attend(carry, piece, start):
        keys, values = piece

        def work(state):
            running, total, accum = state
            raw, allowed = scores_for(keys, start)
            masked = jnp.where(allowed, raw, FLOOR_SCORE)
            newest = jnp.maximum(running, jnp.max(masked, axis=-1))
            factor = jnp.exp(running - newest)
            weights = jnp.where(allowed, jnp.exp(masked - newest[..., None]), 0.0)
            total = total * factor + jnp.sum(weights, axis=-1)
            update = jnp.einsum(
                "hqk,kd->qhd",
                weights.astype(jnp.bfloat16),
                values,
                preferred_element_type=jnp.float32,
            )
            accum = accum * factor.T[:, :, None] + update
            return (newest, total, accum)

        return lax.cond(start <= last_query, work, lambda state: state, carry)

    start_state = (
        jnp.full((head_group, rows), FLOOR_SCORE, jnp.float32),
        jnp.zeros((head_group, rows), jnp.float32),
        jnp.zeros((rows, head_group, HEAD_SIZE), jnp.float32),
    )
    running, total, accum = in_blocks(
        attend,
        start_state,
        (
            lax.all_gather(key_rows, "blk", axis=0, tiled=True),
            lax.all_gather(value_rows, "blk", axis=0, tiled=True),
        ),
        rows,
    )
    attn_full = accum / total.T[:, :, None]
    log_total = running + jnp.log(total)
    out_send = attn_full.astype(jnp.bfloat16).reshape(rows, 1, head_group * HEAD_SIZE)
    out_tok = lax.all_to_all(out_send, "head", split_axis=0, concat_axis=1, tiled=True).reshape(
        count_per_token, QUERY_HEADS * HEAD_SIZE
    )
    residual = inputs + product(out_tok, out_w)
    normed_two = rms_norm(residual, gain_two)
    normed_two_low = normed_two.astype(jnp.bfloat16)
    up_w, down_w = (
        lax.all_gather(expert_in, ("head", "blk"), axis=1, tiled=True),
        lax.all_gather(expert_out, ("head", "blk"), axis=1, tiled=True),
    )
    route_hot = (route_rows[:, :, None] == jnp.arange(E, dtype=jnp.int32)[None, None, :]).astype(
        jnp.int32
    )
    flat_hot = route_hot.reshape(count_per_token * TOP, E)
    before = jnp.cumsum(flat_hot, axis=0) - flat_hot
    slot = jnp.sum(before * flat_hot, axis=-1).reshape(count_per_token, TOP)
    slot_hot = (slot[:, :, None] == jnp.arange(CAP, dtype=jnp.int32)[None, None, :]).astype(
        jnp.float32
    )
    route_float = route_hot.astype(jnp.float32)
    dispatch = jnp.einsum("tje,tjc->ect", route_float, slot_hot, precision=highest)
    combine = jnp.einsum("tje,tjc,tj->ect", route_float, slot_hot, gate_rows, precision=highest)
    expert_rows = jnp.einsum(
        "ect,td->ecd",
        dispatch.astype(jnp.bfloat16),
        normed_two_low,
        preferred_element_type=jnp.float32,
    ).astype(jnp.bfloat16)
    pair = jnp.einsum("ecd,edf->ecf", expert_rows, up_w, preferred_element_type=jnp.float32)
    hidden_low = gated(pair).astype(jnp.bfloat16)
    expert_result = jnp.einsum(
        "ecf,efd->ecd", hidden_low, down_w, preferred_element_type=jnp.float32
    )
    mixture = jnp.einsum("ect,ecd->td", combine, expert_result, precision=highest)
    final = residual + mixture
    diff = final - target
    local_count = jnp.sum(keep_mask)
    local_error = jnp.sum(keep_mask * jnp.sum(diff * diff, axis=-1))
    count_all, error_all = lax.psum((local_count, local_error), ("head", "blk"))
    loss = error_all / (width * count_all)
    grad_final = keep_mask[:, None] * diff * (span * 1.0 / count_all)
    up_back, down_back = (
        lax.all_gather(expert_in, ("head", "blk"), axis=1, tiled=True),
        lax.all_gather(expert_out, ("head", "blk"), axis=1, tiled=True),
    )
    grad_result = jnp.einsum("ect,td->ecd", combine, grad_final, precision=highest).astype(
        jnp.bfloat16
    )
    grad_down = jnp.einsum(
        "ecf,ecd->efd", hidden_low, grad_result, preferred_element_type=jnp.float32
    )
    grad_hidden = jnp.einsum(
        "ecd,efd->ecf", grad_result, down_back, preferred_element_type=jnp.float32
    )
    unused_value, pull_gate = jax.vjp(gated, pair)
    grad_pair = pull_gate(grad_hidden)[0].astype(jnp.bfloat16)
    grad_up = jnp.einsum("ecd,ecf->edf", expert_rows, grad_pair, preferred_element_type=jnp.float32)
    grad_rows = jnp.einsum("ecf,edf->ecd", grad_pair, up_back, preferred_element_type=jnp.float32)
    grad_normed_two = jnp.einsum("ect,ecd->td", dispatch, grad_rows, precision=highest)
    unused_value, pull_two = jax.vjp(rms_norm, residual, gain_two)
    grad_res_norm, grad_gain_two = pull_two(grad_normed_two)
    grad_residual = grad_final + grad_res_norm
    grad_attn_low = grad_residual.astype(jnp.bfloat16)
    grad_out_w = jnp.einsum("tk,td->kd", out_tok, grad_attn_low, preferred_element_type=jnp.float32)
    output_gradient_token = jnp.einsum(
        "td,kd->tk", grad_attn_low, out_w, preferred_element_type=jnp.float32
    ).astype(jnp.bfloat16)
    grad_out_grp = lax.all_to_all(
        output_gradient_token.reshape(count_per_token, KEY_VALUE_HEADS, head_group * HEAD_SIZE),
        "head",
        split_axis=1,
        concat_axis=0,
        tiled=True,
    ).reshape(rows, head_group, HEAD_SIZE)
    delta = jnp.einsum(
        "qhd,qhd->hq", grad_out_grp.astype(jnp.float32), attn_full, precision=highest
    )

    def attend_back(carry, piece, start):
        keys, values = piece

        def work(state):
            grad_query, grad_keys, grad_values = state
            raw, allowed = scores_for(keys, start)
            weights = jnp.where(allowed, jnp.exp(raw - log_total[..., None]), 0.0)
            grad_weights = jnp.einsum(
                "qhd,kd->hqk", grad_out_grp, values, preferred_element_type=jnp.float32
            )
            grad_raw = (weights * (grad_weights - delta[..., None])).astype(jnp.bfloat16)
            grad_query = (
                grad_query
                + jnp.einsum("hqk,kd->qhd", grad_raw, keys, preferred_element_type=jnp.float32)
                * scale
            )
            key_part = (
                jnp.einsum("hqk,qhd->kd", grad_raw, query_heads, preferred_element_type=jnp.float32)
                * scale
            )
            value_part = jnp.einsum(
                "hqk,qhd->kd",
                weights.astype(jnp.bfloat16),
                grad_out_grp,
                preferred_element_type=jnp.float32,
            )
            block_size = keys.shape[0]
            grad_keys = lax.dynamic_update_slice_in_dim(
                grad_keys,
                lax.dynamic_slice_in_dim(grad_keys, start, block_size, 0) + key_part,
                start,
                0,
            )
            grad_values = lax.dynamic_update_slice_in_dim(
                grad_values,
                lax.dynamic_slice_in_dim(grad_values, start, block_size, 0) + value_part,
                start,
                0,
            )
            return (grad_query, grad_keys, grad_values)

        return lax.cond(start <= last_query, work, lambda state: state, carry)

    back_state = (
        jnp.zeros((rows, head_group, HEAD_SIZE), jnp.float32),
        jnp.zeros((span, HEAD_SIZE), jnp.float32),
        jnp.zeros((span, HEAD_SIZE), jnp.float32),
    )
    grad_query, grad_keys_full, grad_values_full = in_blocks(
        attend_back,
        back_state,
        (
            lax.all_gather(key_rows, "blk", axis=0, tiled=True),
            lax.all_gather(value_rows, "blk", axis=0, tiled=True),
        ),
        rows,
    )
    grad_keys, grad_values = (
        lax.psum_scatter(grad_keys_full, "blk", scatter_dimension=0, tiled=True),
        lax.psum_scatter(grad_values_full, "blk", scatter_dimension=0, tiled=True),
    )
    grad_query_lin = (
        rotary_apply(grad_query, query_where, -1.0)
        .astype(jnp.bfloat16)
        .reshape(rows, 1, head_group * HEAD_SIZE)
    )
    grad_key_lin = rotary_apply(grad_keys.reshape(rows, 1, HEAD_SIZE), query_where, -1.0).astype(
        jnp.bfloat16
    )
    grad_value_lin = grad_values.astype(jnp.bfloat16).reshape(rows, 1, HEAD_SIZE)
    back_query, key_backward, value_backward = (
        lax.all_to_all(grad_query_lin, "head", split_axis=0, concat_axis=1, tiled=True),
        lax.all_to_all(grad_key_lin, "head", split_axis=0, concat_axis=1, tiled=True),
        lax.all_to_all(grad_value_lin, "head", split_axis=0, concat_axis=1, tiled=True),
    )
    back_query = back_query.reshape(count_per_token, QUERY_HEADS * HEAD_SIZE)
    key_backward = key_backward.reshape(count_per_token, KEY_VALUE_HEADS * HEAD_SIZE)
    value_backward = value_backward.reshape(count_per_token, KEY_VALUE_HEADS * HEAD_SIZE)
    grad_query_w = jnp.einsum(
        "td,tk->dk", normed_low, back_query, preferred_element_type=jnp.float32
    )
    grad_key_w = jnp.einsum(
        "td,tk->dk", normed_low, key_backward, preferred_element_type=jnp.float32
    )
    grad_value_w = jnp.einsum(
        "td,tk->dk", normed_low, value_backward, preferred_element_type=jnp.float32
    )
    grad_normed_one = jnp.einsum(
        "tk,dk->td", back_query, query_w, preferred_element_type=jnp.float32
    )
    grad_normed_one = grad_normed_one + jnp.einsum(
        "tk,dk->td", key_backward, key_w, preferred_element_type=jnp.float32
    )
    grad_normed_one = grad_normed_one + jnp.einsum(
        "tk,dk->td", value_backward, value_w, preferred_element_type=jnp.float32
    )
    unused_value, pull_one = jax.vjp(rms_norm, inputs, gain_one)
    grad_in_norm, grad_gain_one = pull_one(grad_normed_one)
    grad_inputs = grad_residual + grad_in_norm
    sums = (
        lax.psum_scatter(grad_query_w, ("head", "blk"), scatter_dimension=0, tiled=True),
        lax.psum_scatter(grad_key_w, ("head", "blk"), scatter_dimension=0, tiled=True),
        lax.psum_scatter(grad_value_w, ("head", "blk"), scatter_dimension=0, tiled=True),
        lax.psum_scatter(grad_out_w, ("head", "blk"), scatter_dimension=0, tiled=True),
        lax.psum_scatter(grad_gain_one, ("head", "blk"), scatter_dimension=0, tiled=True),
        lax.psum_scatter(grad_gain_two, ("head", "blk"), scatter_dimension=0, tiled=True),
        lax.psum_scatter(grad_up, ("head", "blk"), scatter_dimension=1, tiled=True),
        lax.psum_scatter(grad_down, ("head", "blk"), scatter_dimension=1, tiled=True),
    )
    shape = states.shape
    return (
        final.astype(jnp.bfloat16).reshape(shape),
        loss,
        grad_inputs.reshape(shape),
        sums[4],
        sums[0],
        sums[1],
        sums[2],
        sums[3],
        sums[5],
        sums[6],
        sums[7],
    )


class Place:
    def __init__(self):
        self.x = lax.axis_index("head")
        self.b = lax.axis_index("blk")
        self.c = self.b % 2
        self.y = (self.b // 2) % 2
        self.z = self.b // 4

    def near(self, kind):
        x, y, z, c = self.x, self.y, self.z, self.c
        if kind == "up":
            z = jnp.minimum(z + 1, NZ - 1)
        elif kind == "down":
            z = jnp.maximum(z - 1, 0)
        elif kind == "y":
            y = 1 - y
        elif kind == "x":
            x = 1 - x
        elif kind == "c":
            c = 1 - c
        return (x, z * 4 + y * 2 + c)

    def blk(self, z, y, c):
        return z * 4 + y * 2 + c

    def outward(self, j):
        inner = jnp.where(j < 2, 1 - j, j)
        order = jnp.where((self.z == 0) | (self.z == NZ - 1), j, inner)
        return jnp.where(self.z < 2, order, NZ - 1 - order)

    def inward(self, j):
        inner = jnp.where(j == 0, 3, jnp.where(j == 1, 0, jnp.where(j == 2, 2, 1)))
        order = jnp.where((self.z == 0) | (self.z == NZ - 1), NZ - 1 - j, inner)
        return jnp.where(self.z < 2, order, NZ - 1 - order)


def greet_all(me):
    barrier = pltpu.get_barrier_semaphore()

    def one(k, carry):
        pl.semaphore_signal(
            barrier, inc=1, device_id=((me.x + k // 16) % 2, (me.b + k) % 16), device_id_type=MESH
        )
        return carry

    lax.fori_loop(1, 32, one, 0)
    pl.semaphore_wait(barrier, 31)


def remote(src, dst, send, recv, to):
    return pltpu.make_async_remote_copy(
        src_ref=src, dst_ref=dst, send_sem=send, recv_sem=recv, device_id=to, device_id_type=MESH
    )


def arrived(ref, sem, me):
    remote(ref, ref, sem, sem, me.near("c")).wait_recv()


def left(ref, sem, me):
    remote(ref, ref, sem, sem, me.near("c")).wait_send()


class Gather:
    def __init__(self, me, g, index, send, recv, cols=None, causal=False):
        self.me, self.g, self.index, self.send, self.recv, self.causal = me, g, index, send, recv, causal
        start, width = cols or (0, g.shape[2])
        cut = (width // 2 + 127) // 128 * 128
        self.cols = pl.ds(start, width)
        self.first, self.second = pl.ds(start, cut), pl.ds(start + cut, width - cut)

    def place(self, j):
        return self.me.z - j if self.causal else self.me.outward(j)

    def valid(self, j):
        return (j >= 0) & (j <= (self.me.z if self.causal else NZ - 1))

    def ups(self, zz):
        if self.causal:
            return self.me.z < NZ - 1
        return (zz <= self.me.z) & (self.me.z < NZ - 1)

    def downs(self, zz):
        return (zz >= self.me.z) & (self.me.z > 0)

    def put(self, j, kind, n, s, cols=None, slot=0):
        ref = self.g.at[s, :, self.cols if cols is None else cols]
        remote(ref, ref, self.send.at[j, n], self.recv.at[s, slot], self.me.near(kind)).start()

    def wait(self, s):
        arrived(self.g.at[s, :, self.cols], self.recv.at[s, 0], self.me)

    def turn(self, j):
        me, index = self.me, self.index
        x, y, c = me.x, me.y, me.c

        @pl.when(self.valid(j) & (j > 0))
        def _():
            self.wait(index(x, self.place(j), y, c))

        @pl.when(self.valid(j))
        def _():
            zz = self.place(j)
            own = index(x, zz, y, c)
            pl.when(self.ups(zz))(lambda: self.put(j, "up", 0, own))
            if not self.causal:
                pl.when(self.downs(zz))(lambda: self.put(j, "down", 1, own))
            self.put(j, "y", 2, own)
            self.put(j, "x", 3, own)
            self.put(j, "c", 6, own)

        @pl.when(self.valid(j - 1))
        def _():
            i = j - 1
            zp = self.place(i)
            s = index(x, zp, 1 - y, c)
            self.wait(s)
            self.put(i, "x", 4, s, self.first, 0)
            self.put(i, "c", 7, s)
            t = index(1 - x, zp, y, c)
            self.wait(t)
            self.put(i, "y", 5, t, self.second, 1)
            self.put(i, "c", 8, t)

        @pl.when(self.valid(j - 2))
        def _():
            i = j - 2
            s = index(1 - x, self.place(i), 1 - y, c)
            arrived(self.g.at[s, :, self.first], self.recv.at[s, 0], me)
            arrived(self.g.at[s, :, self.second], self.recv.at[s, 1], me)
            self.put(i, "c", 9, s)

    def from_core(self, j):
        me = self.me
        for xx in (me.x, 1 - me.x):
            for yy in (me.y, 1 - me.y):
                self.wait(self.index(xx, self.place(j), yy, 1 - me.c))

    def close(self, cores=True):
        me = self.me

        def one(j, carry):
            @pl.when(self.valid(j))
            def _():
                zz = self.place(j)
                own = self.index(me.x, zz, me.y, me.c)
                whole = self.g.at[own, :, self.cols]
                first, second = self.g.at[own, :, self.first], self.g.at[own, :, self.second]
                pl.when(self.ups(zz))(lambda: left(whole, self.send.at[j, 0], me))
                if not self.causal:
                    pl.when(self.downs(zz))(lambda: left(whole, self.send.at[j, 1], me))
                for n in (2, 3, 6, 7, 8, 9):
                    left(whole, self.send.at[j, n], me)
                left(first, self.send.at[j, 4], me)
                left(second, self.send.at[j, 5], me)
                if cores:
                    self.from_core(j)

            return carry

        lax.fori_loop(0, 4, one, 0)


class Sum:
    def __init__(self, me, part, index, out, room, sems, cols=None, causal=False):
        self.me, self.part, self.index, self.out, self.causal = me, part, index, out, causal
        start, width = cols or (0, part.shape[2])
        self.cols = pl.ds(start, width)
        self.rc, self.rx, self.ry, self.rn, self.rz, self.acc = room
        self.sc, self.ss, self.vc, self.vn, self.vz = sems
        self.half = (width // 2 + 127) // 128 * 128
        self.first, self.second = pl.ds(0, self.half), pl.ds(self.half, width - self.half)

    @staticmethod
    def room(rows, columns):
        half = (columns // 2 + 127) // 128 * 128
        return [
            pltpu.VMEM((16, rows, columns), BF),
            pltpu.VMEM((4, rows, half), BF),
            pltpu.VMEM((4, rows, columns - half), BF),
            pltpu.VMEM((2, 4, rows, columns), BF),
            pltpu.VMEM((5, rows, columns), BF),
            pltpu.VMEM((rows, columns), F32),
            DMA((16,)),
            DMA((4, 6)),
            DMA((16,)),
            DMA((4, 4)),
            DMA((5,)),
        ]

    def place(self, j):
        return j if self.causal else self.me.inward(j)

    def valid(self, j):
        return (j >= 0) & (j <= (self.me.z if self.causal else NZ - 1))

    def slot(self, xx, zz, yy):
        return zz * 4 + xx * 2 + yy

    def lead(self, j):
        me = self.me
        zz = self.place(j)
        for xx in (1 - me.x, me.x):
            for yy in (1 - me.y, me.y):
                k = self.slot(xx, zz, yy)
                src = self.part.at[self.index(xx, zz, yy, 1 - me.c), :, self.cols]
                remote(src, self.rc.at[k], self.sc.at[k], self.vc.at[k], me.near("c")).start()

    def with_core(self, xx, zz, yy):
        k = self.slot(xx, zz, yy)
        arrived(self.rc.at[k], self.vc.at[k], self.me)
        own = self.part[self.index(xx, zz, yy, self.me.c), :, self.cols]
        return k, own.astype(F32) + self.rc[k].astype(F32)

    def turn(self, j):
        me, half, first, second = self.me, self.half, self.first, self.second
        rc, rx, ry, rn, ss, vn = self.rc, self.rx, self.ry, self.rn, self.ss, self.vn
        x, y = me.x, me.y

        @pl.when(self.valid(j))
        def _():
            zz = self.place(j)
            k, total = self.with_core(1 - x, zz, 1 - y)
            rc[k] = total.astype(BF)
            remote(rc.at[k, :, first], rx.at[zz], ss.at[j, 0], vn.at[zz, 0], me.near("x")).start()
            remote(rc.at[k, :, second], ry.at[zz], ss.at[j, 1], vn.at[zz, 1], me.near("y")).start()

        @pl.when(self.valid(j - 1))
        def _():
            i = j - 1
            zz = self.place(i)
            k, total = self.with_core(x, zz, 1 - y)
            arrived(rx.at[zz], vn.at[zz, 0], me)
            rc[k, :, second] = total[:, half:].astype(BF)
            rc[k, :, first] = (total[:, :half] + rx[zz].astype(F32)).astype(BF)
            remote(rc.at[k], rn.at[0, zz], ss.at[i, 2], vn.at[zz, 2], me.near("y")).start()
            k, total = self.with_core(1 - x, zz, y)
            arrived(ry.at[zz], vn.at[zz, 1], me)
            rc[k, :, first] = total[:, :half].astype(BF)
            rc[k, :, second] = (total[:, half:] + ry[zz].astype(F32)).astype(BF)
            remote(rc.at[k], rn.at[1, zz], ss.at[i, 3], vn.at[zz, 3], me.near("x")).start()

        @pl.when(self.valid(j - 2))
        def _():
            i = j - 2
            zz = self.place(i)
            k, total = self.with_core(x, zz, y)
            arrived(rn.at[0, zz], vn.at[zz, 2], me)
            arrived(rn.at[1, zz], vn.at[zz, 3], me)
            self.acc[...] = total + rn[0, zz].astype(F32) + rn[1, zz].astype(F32)
            along_z(me, i, zz, self.acc, rc.at[k], self.rz, ss, 4, self.vz, self.causal)

            @pl.when(zz == me.z)
            def _():
                self.out[:, self.cols] = self.acc[...]

    def close(self):
        me = self.me
        whole = self.rc.at[0]
        first, second = self.rc.at[0, :, self.first], self.rc.at[0, :, self.second]

        def one(j, carry):
            @pl.when(self.valid(j))
            def _():
                zz = self.place(j)
                for xx in (1 - me.x, me.x):
                    for yy in (1 - me.y, me.y):
                        left(whole, self.sc.at[self.slot(xx, zz, yy)], me)
                left(first, self.ss.at[j, 0], me)
                left(second, self.ss.at[j, 1], me)
                for n in (2, 3):
                    left(whole, self.ss.at[j, n], me)
                if not self.causal:
                    pl.when(zz > me.z)(lambda: left(whole, self.ss.at[j, 4], me))
                pl.when(zz < me.z)(lambda: left(whole, self.ss.at[j, 5], me))

            return carry

        lax.fori_loop(0, 4, one, 0)


def along_z(me, i, zz, acc, room, rz, ss, n, vz, causal=False):
    z = me.z

    def add(slot):
        arrived(rz.at[slot], vz.at[slot], me)
        acc[...] += rz[slot].astype(F32)

    if not causal:
        pl.when((zz >= z) & (z > 0))(lambda: add(zz))
    pl.when((zz < z) & (z < NZ - 1))(lambda: add(zz))
    pl.when((zz == z) & (z < NZ - 1))(lambda: add(4))

    if not causal:

        @pl.when(zz > z)
        def _():
            room[...] = acc[...].astype(BF)
            remote(room, rz.at[zz], ss.at[i, n], vz.at[zz], me.near("up")).start()

    @pl.when(zz < z)
    def _():
        room[...] = acc[...].astype(BF)
        there = jnp.where(zz == z - 1, 4, zz)
        remote(room, rz.at[there], ss.at[i, n + 1], vz.at[there], me.near("down")).start()


def by_weight(x, z, y, c):
    return x * 16 + z * 4 + y * 2 + c


def by_token(x, z, y, c):
    return (z * 4 + y * 2 + c) * 2 + x


ANY = pl.BlockSpec(memory_space=pl.ANY)
VMEM = pl.BlockSpec(memory_space=pltpu.VMEM)
DMA = pltpu.SemaphoreType.DMA


def params(number, mib):
    return pltpu.CompilerParams(
        collective_id=number, has_side_effects=True, vmem_limit_bytes=mib << 20
    )


NT = (((1,), (1,)), ((), ()))
TN = (((0,), (0,)), ((), ()))
GROUP = QUERY_HEADS // KEY_VALUE_HEADS
LANES = GROUP * 128
SCALE = HEAD_SIZE ** (-0.5)
POWER = SCALE * 1.4426950408889634


def turned(u, cosine, sine):
    return u * cosine + pltpu.roll(u, 64, 1) * sine


def begin_of(place, doc):
    begin = jnp.zeros_like(place)
    for i in range(doc.shape[0]):
        begin = jnp.where(place >= doc[i], jnp.maximum(begin, doc[i]), begin)
    return begin


def rotary_tables(me, doc, freq):
    first = (me.b * 2 + me.x) * 128
    place = first + lax.broadcasted_iota(jnp.int32, (128, 128), 0)
    angle = (place - begin_of(place, doc)).astype(F32) * freq[...]
    sine = jnp.sin(angle)
    lane = lax.broadcasted_iota(jnp.int32, (128, 128), 1)
    return jnp.cos(angle), jnp.where(lane < 64, -sine, sine)


def query_bounds(me, doc):
    place = (me.b * 2 + me.x) * 128 + lax.broadcasted_iota(jnp.int32, (1, LANES), 1) % 128
    return begin_of(place, doc), place


def allowed_keys(start, bounds):
    key = start + lax.broadcasted_iota(jnp.int32, (256, LANES), 0)
    return (key >= bounds[0]) & (key <= bounds[1])


def eye(n):
    return lax.broadcasted_iota(jnp.int32, (n, n), 0) == lax.broadcasted_iota(jnp.int32, (n, n), 1)


def as_column(row):
    return jnp.sum(jnp.where(eye(row.shape[1]), row, 0.0), axis=1, keepdims=True)


def as_row(column):
    return jnp.sum(jnp.where(eye(column.shape[0]), column, 0.0), axis=0, keepdims=True)


QKV = 2048
WIDE = QKV + 128
PIECES = ((0, 1152), (1152, 1024))


def front_kernel(
    states, doc, freq, norm_one, norm_two, valid, down_in, wq, wk, wv, wo, up,
    gq_out, go_out, kv_out, win, wout, h, n2, n1, qs, o_out, lse, count,
    gq, go, kv, down, top, total, acc,
    own_sem, qsend, qrecv, gsend, grecv, ksend, krecv, asend, arecv, osend, orecv,
):
    me = Place()
    x, y, z, b, c = me.x, me.y, me.z, me.b, me.c
    here = by_weight(x, z, y, c)
    mine = [
        pltpu.make_async_copy(wq, gq.at[here, :, pl.ds(0, 1536)], own_sem.at[0]),
        pltpu.make_async_copy(wk, gq.at[here, :, pl.ds(1536, 256)], own_sem.at[1]),
        pltpu.make_async_copy(wv, gq.at[here, :, pl.ds(1792, 256)], own_sem.at[2]),
        pltpu.make_async_copy(wo, go.at[here], own_sem.at[3]),
    ]
    for copy in mine:
        copy.start()

    lane = lax.broadcasted_iota(jnp.int32, (48, 128), 1)
    kept = jnp.sum(valid[...].astype(F32))
    extra = jnp.where(
        lane == 0,
        as_column(norm_one[...].astype(F32)),
        jnp.where(lane == 1, as_column(norm_two[...].astype(F32)), jnp.where(lane == 2, kept, 0.0)),
    )
    gq[here, :, pl.ds(QKV, 128)] = extra.astype(BF)
    for e in range(E):
        wide = down_in[e].astype(F32)
        down[e] = jnp.concatenate([wide[:, :768], wide[:, 768:]], axis=0).astype(BF)
    greet_all(me)
    for copy in mine:
        copy.wait()

    def own_piece(n):
        col = pl.multiple_of(n * 768 + c * 384, 128)
        return pltpu.make_async_copy(
            up.at[b // 2, :, pl.ds(col, 384)], win.at[b, :, pl.ds(n * 384, 384)], own_sem.at[4 + n]
        )

    def own_down():
        return pltpu.make_async_copy(down.at[b // 2], wout.at[b], own_sem.at[6])

    def deal(k, carry):
        t = (b + k) % 16
        for n in range(2):
            col = pl.multiple_of(n * 768 + (t % 2) * 384, 128)
            remote(
                up.at[t // 2, :, pl.ds(col, 384)],
                win.at[b, :, pl.ds(n * 384, 384)],
                asend.at[k, n],
                arecv.at[b, n],
                (x, t),
            ).start()
        pl.when(t % 2 == x)(
            lambda: remote(down.at[t // 2], wout.at[b], osend.at[k], orecv.at[b], (x, t)).start()
        )
        return carry

    weights = [
        Gather(me, gq, by_weight, qsend.at[i], qrecv.at[i], PIECES[i]) for i in range(len(PIECES))
    ]

    def first_turn(j, carry):
        for piece in weights:
            piece.turn(j)
        lax.fori_loop(1 + j * 3, jnp.minimum(4 + j * 3, 16), deal, 0)
        return carry

    lax.fori_loop(0, 6, first_turn, 0)
    for n in range(2):
        own_piece(n).start()
    pl.when(c == x)(lambda: own_down().start())
    cos, sin = rotary_tables(me, doc, freq)
    bounds = query_bounds(me, doc)
    for piece in weights:
        piece.close()
    keep = pltpu.make_async_copy(gq, gq_out, own_sem.at[0])
    keep.start()

    rows = states[...].astype(F32)
    gains = gq[:, :, pl.ds(QKV, 128)].reshape(1536, 128).astype(F32).T
    count[...] = jnp.zeros((8, 128), F32) + jnp.sum(gains[2:3]) / 48.0
    n1[...] = (
        rows * lax.rsqrt(jnp.mean(rows * rows, axis=-1, keepdims=True) + 1e-06) * gains[0:1]
    ).astype(BF)
    qkv = jnp.dot(n1[...], gq[:, :, pl.ds(0, QKV)].reshape(1536, QKV), preferred_element_type=F32)
    at = by_token(x, z, y, c)
    for i in range(2):
        kv[at, :, i * 128 : i * 128 + 128] = turned(qkv[:, 1536 + i * 128 : 1664 + i * 128], cos, sin).astype(BF)
        kv[at, :, 256 + i * 128 : 384 + i * 128] = qkv[:, 1792 + i * 128 : 1920 + i * 128].astype(BF)
    for i in range(QUERY_HEADS):
        r = (i % GROUP) * 128
        qs[i // GROUP, r : r + 128] = turned(qkv[:, i * 128 : i * 128 + 128], cos, sin).astype(BF)

    top[...] = jnp.full_like(top, FLOOR_SCORE)
    total[...] = jnp.zeros_like(total)
    acc[...] = jnp.zeros_like(acc)
    keys = Gather(me, kv, by_token, ksend, krecv, causal=True)
    output = Gather(me, go, by_weight, gsend, grecv)

    def block(n):
        ok = allowed_keys(n * 256, bounds)
        for i in range(2):
            k = kv[pl.ds(n * 2, 2), :, i * 128 : i * 128 + 128].reshape(256, 128)
            v = kv[pl.ds(n * 2, 2), :, 256 + i * 128 : 384 + i * 128].reshape(256, 128)
            s = lax.dot_general(k, qs[i], NT, preferred_element_type=F32)
            s = jnp.where(ok, s, FLOOR_SCORE)
            old = top[i]
            new = jnp.maximum(old, jnp.max(s, axis=0, keepdims=True))
            factor = jnp.exp2((old - new) * POWER)
            p = jnp.exp2((s - new) * POWER)
            top[i] = new
            total[i] = total[i] * factor + jnp.sum(p, axis=0, keepdims=True)
            acc[i] = acc[i] * factor + lax.dot_general(v, p.astype(BF), TN, preferred_element_type=F32)

    def turn(j, carry):
        keys.turn(j)
        output.turn(j - 2)

        @pl.when(keys.valid(j - 2))
        def _():
            i = j - 2
            keys.from_core(i)
            zz = z - i
            last = jnp.where(i == 0, y * 2 + c, 3)

            def one(n, carry):
                block(zz * 4 + last - n)
                return carry

            lax.fori_loop(0, last + 1, one, 0)

        return carry

    lax.fori_loop(0, 8, turn, 0)
    output.close()
    keep_o = pltpu.make_async_copy(go, go_out, own_sem.at[1])
    keep_o.start()
    keep_k = pltpu.make_async_copy(kv, kv_out, own_sem.at[2])
    keep_k.start()
    for i in range(2):
        lse[i] = top[i] * POWER + jnp.log2(total[i])
        done = acc[i] / total[i]
        for r in range(GROUP):
            col = (i * GROUP + r) * 128
            o_out[:, col : col + 128] = done[:, r * 128 : r * 128 + 128].T
    res = rows + jnp.dot(
        o_out[...].astype(BF), go[...].reshape(1536, 1536), preferred_element_type=F32
    )
    h[...] = res
    n2[...] = (
        res * lax.rsqrt(jnp.mean(res * res, axis=-1, keepdims=True) + 1e-06) * gains[1:2]
    ).astype(BF)

    keys.close(False)

    def close(k, carry):
        piece = win.at[b, :, pl.ds(0, 384)]
        f = (b + 16 - k) % 16
        for n in range(2):
            left(piece, asend.at[k, n], me)
            arrived(win.at[f, :, pl.ds(n * 384, 384)], arecv.at[f, n], me)
        pl.when((b + k) % 2 == x)(lambda: left(wout.at[b], osend.at[k], me))
        pl.when(c == x)(lambda: arrived(wout.at[f], orecv.at[f], me))
        return carry

    lax.fori_loop(1, 16, close, 0)
    for n in range(2):
        own_piece(n).wait()
    pl.when(c == x)(lambda: own_down().wait())
    keep.wait()
    keep_o.wait()
    keep_k.wait()


def run_front(*operands):
    shape = jax.ShapeDtypeStruct
    smem = pl.BlockSpec(memory_space=pltpu.SMEM)
    return pl.pallas_call(
        front_kernel,
        out_shape=(
            shape((32, 48, WIDE), BF),
            shape((32, 48, 1536), BF),
            shape((32, 128, 512), BF),
            shape((16, 48, 768), BF),
            shape((16, 48, 768), BF),
            shape((128, 1536), F32),
            shape((128, 1536), BF),
            shape((128, 1536), BF),
            shape((2, LANES, 128), BF),
            shape((128, 1536), F32),
            shape((2, 1, LANES), F32),
            shape((8, 128), F32),
        ),
        in_specs=[VMEM, smem] + [VMEM] * 5 + [ANY] * 5,
        out_specs=(ANY,) * 5 + (VMEM,) * 7,
        scratch_shapes=[
            pltpu.VMEM((32, 48, WIDE), BF),
            pltpu.VMEM((32, 48, 1536), BF),
            pltpu.VMEM((32, 128, 512), BF),
            pltpu.VMEM((8, 48, 768), BF),
            pltpu.VMEM((2, 1, LANES), F32),
            pltpu.VMEM((2, 1, LANES), F32),
            pltpu.VMEM((2, 128, LANES), F32),
            DMA((7,)),
            DMA((2, 4, 10)),
            DMA((2, 32, 2)),
            DMA((4, 10)),
            DMA((32, 2)),
            DMA((4, 10)),
            DMA((32, 2)),
            DMA((16, 2)),
            DMA((16, 2)),
            DMA((16,)),
            DMA((16,)),
        ],
        compiler_params=params(1, 48),
        name="front",
    )(*operands)


GELU_A = 0.7978845608028654
GELU_B = 0.044715


CUTS = 2
CUT = 128 // CUTS


def experts_kernel(
    n2, h, teacher, routes, gates, valid, count, win, wout,
    final, err, dn2, dy_out, dwin_out, dwout_out,
    nall, dyall, pairs, zg, dpairs, part, rc, ry, rz, acc, errs, tables, gate,
    wfull, slab, wdown, dwin, dwin_in, dwout, dwout_in,
    own_sem, gsend, grecv, csend, crecv, ysend, yrecv, zsend, zrecv, esend, erecv,
    tsend, trecv, xsend, xrecv,
):
    me = Place()
    x, y, z, b, c = me.x, me.y, me.z, me.b, me.c
    half = pltpu.make_async_copy(win, wfull.at[x], own_sem.at[0])
    half.start()
    held = pltpu.make_async_copy(wout, slab, own_sem.at[1])
    pl.when(c == x)(held.start)
    lane = lax.broadcasted_iota(jnp.int32, (128, 128), 1)
    table = jnp.zeros((128, 128), F32)
    for k in range(TOP):
        table = table + jnp.where(routes[:, k : k + 1] == lane, gates[:, k : k + 1], 0.0)
    tables[b] = table.T[0:8]
    greet_all(me)

    def rows_of(p):
        return pl.ds(p * CUT, CUT)

    def over_weights(k):
        cut = pl.ds(k * 4, 4)
        return remote(win.at[cut], wfull.at[x, cut], xsend.at[k], xrecv.at[k], me.near("x"))

    def over_down():
        return remote(wout, slab, xsend.at[4], xrecv.at[4], me.near("x"))

    def gather(buf, way, between):
        def put(j, p, kind, n, s):
            ref = buf.at[s, rows_of(p)]
            remote(ref, ref, gsend.at[way, j, p, n], grecv.at[way, s, p], me.near(kind)).start()

        def turn(j, carry):
            for p in range(CUTS):
                zz = me.outward(j)
                own = me.blk(zz, y, c)

                @pl.when((j > 0) & (j < 4))
                def _():
                    arrived(buf.at[own, rows_of(p)], grecv.at[way, own, p], me)

                @pl.when(j < 4)
                def _():
                    pl.when((zz <= z) & (z < NZ - 1))(lambda: put(j, p, "up", 0, own))
                    pl.when((zz >= z) & (z > 0))(lambda: put(j, p, "down", 1, own))
                    put(j, p, "y", 2, own)
                    put(j, p, "c", 3, own)

                @pl.when((j > 0) & (j < 5))
                def _():
                    i = j - 1
                    s = me.blk(me.outward(i), 1 - y, c)
                    arrived(buf.at[s, rows_of(p)], grecv.at[way, s, p], me)
                    put(i, p, "c", 4, s)

                between(j, p)
            return carry

        lax.fori_loop(0, 6, turn, 0)

        def close(j, carry):
            zz = me.outward(j)
            whole = buf.at[b, rows_of(0)]
            for p in range(CUTS):
                pl.when((zz <= z) & (z < NZ - 1))(lambda: left(whole, gsend.at[way, j, p, 0], me))
                pl.when((zz >= z) & (z > 0))(lambda: left(whole, gsend.at[way, j, p, 1], me))
                for n in (2, 3, 4):
                    left(whole, gsend.at[way, j, p, n], me)
            return carry

        lax.fori_loop(0, 4, close, 0)

    def from_core(buf, way, zz, yy):
        s = me.blk(zz, yy, 1 - c)
        for p in range(CUTS):
            arrived(buf.at[s, rows_of(p)], grecv.at[way, s, p], me)

    def to_other_core(way, q):
        remote(part.at[q * 2 + 1 - c], rc.at[q], csend.at[way, q], crecv.at[way, q], me.near("c")).start()

    def lead(way, j):
        zz = me.inward(j)
        q = zz * 2 + 1 - y
        s = q * 2 + c
        arrived(rc.at[q], crecv.at[way, q], me)
        part[s] = (part[s].astype(F32) + rc[q].astype(F32)).astype(BF)
        for p in range(CUTS):
            remote(
                part.at[s, rows_of(p)], ry.at[zz, rows_of(p)], ysend.at[way, j, p], yrecv.at[way, zz, p], me.near("y")
            ).start()

    def follow(way, j):
        zz = me.inward(j)
        q = zz * 2 + y
        s = q * 2 + c
        arrived(rc.at[q], crecv.at[way, q], me)
        for p in range(CUTS):
            cut = rows_of(p)
            arrived(ry.at[zz, cut], yrecv.at[way, zz, p], me)
            piece = acc.at[cut]
            piece[...] = part[s, cut].astype(F32) + rc[q, cut].astype(F32) + ry[zz, cut].astype(F32)
            along_z(
                me, j, zz, piece, part.at[s, cut], rz.at[:, cut], zsend.at[way, :, p], 0, zrecv.at[way, :, p]
            )

    def close_sum(way):
        def close(j, carry):
            zz = me.inward(j)
            whole, piece = part.at[b], part.at[b, rows_of(0)]
            left(whole, csend.at[way, j], me)
            left(whole, csend.at[way, j + 4], me)
            for p in range(CUTS):
                left(piece, ysend.at[way, j, p], me)
                pl.when(zz > z)(lambda: left(piece, zsend.at[way, j, p, 0], me))
                pl.when(zz < z)(lambda: left(piece, zsend.at[way, j, p, 1], me))
            return carry

        lax.fori_loop(0, 4, close, 0)

    def gelu_parts(g):
        t = jnp.tanh(GELU_A * (g + GELU_B * g * g * g))
        return t, 0.5 * g * (1.0 + t)

    def forward(q):
        rows = nall[pl.ds(q * 2, 2)].reshape(256, 1536)
        pair = jnp.dot(rows, wfull[...].reshape(1536, 768), preferred_element_type=F32)
        pairs[q] = pair
        unused, a = gelu_parts(pair[:, :384])
        scale = gate[pl.ds(q * 2, 2)].reshape(256, 1)
        zq = (a * pair[:, 384:] * scale).astype(BF)
        zg[q] = zq
        out = jnp.dot(zq, wdown[...], preferred_element_type=F32)
        part[pl.ds(q * 2, 2)] = out.astype(BF).reshape(2, 128, 1536)
        to_other_core(0, q)

    def backward(q):
        rows = dyall[pl.ds(q * 2, 2)].reshape(256, 1536)
        scale = gate[pl.ds(q * 2, 2)].reshape(256, 1)
        dz = lax.dot_general(rows, wdown[...], NT, preferred_element_type=F32) * scale
        g, u = pairs[q, :, :384], pairs[q, :, 384:]
        t, a = gelu_parts(g)
        slope = 0.5 * (1.0 + t) + 0.5 * g * (1.0 - t * t) * (GELU_A * (1.0 + 3.0 * GELU_B * g * g))
        dpairs[q, :, :384] = (dz * u * slope).astype(BF)
        dpairs[q, :, 384:] = (dz * a).astype(BF)
        out = lax.dot_general(dpairs[q], wfull[...].reshape(1536, 768), NT, preferred_element_type=F32)
        part[pl.ds(q * 2, 2)] = out.astype(BF).reshape(2, 128, 1536)
        to_other_core(1, q)

    nall[b] = n2[...]
    held_wait = held.wait
    pl.when(c == x)(held_wait)

    def tell_gates(k, carry):
        to = (b + k) % 16
        remote(tables.at[b], tables.at[b], tsend.at[k], trecv.at[b], (x, to)).start()
        return carry

    def with_tokens(j, p):
        if p == 0:
            pl.when((j == 0) & (c == x))(lambda: over_down().start())
            for k in range(4):
                pl.when(j == k)(over_weights(k).start)
        else:

            @pl.when(j == 0)
            def _():
                lax.fori_loop(1, 16, tell_gates, 0)

    gather(nall, 0, with_tokens)

    def all_cores(buf, way):
        def one(j, carry):
            from_core(buf, way, j, y)
            from_core(buf, way, j, 1 - y)
            return carry

        lax.fori_loop(0, 4, one, 0)

    all_cores(nall, 0)
    def hear_gates(k, carry):
        left(tables.at[0], tsend.at[k], me)
        arrived(tables.at[(b + 16 - k) % 16], trecv.at[(b + 16 - k) % 16], me)
        return carry

    lax.fori_loop(1, 16, hear_gates, 0)

    def gate_of(s, carry):
        row = lax.broadcasted_iota(jnp.int32, (8, 128), 0)
        picked = jnp.sum(jnp.where(row == b // 2, tables[s], 0.0), axis=0, keepdims=True)
        gate[s] = as_column(picked)
        return carry

    lax.fori_loop(0, 16, gate_of, 0)
    half.wait()
    for k in range(4):
        arrived(wfull.at[1 - x, pl.ds(k * 4, 4)], xrecv.at[k], me)
    pl.when(c != x)(lambda: arrived(slab, xrecv.at[4], me))
    wide = slab[...].astype(F32).reshape(16, 2, 24, 768)
    wdown[:, :768] = wide[:, 0].reshape(384, 768).astype(BF)
    wdown[:, 768:] = wide[:, 1].reshape(384, 768).astype(BF)

    def outputs(j, carry):
        @pl.when(j < 4)
        def _():
            forward(me.inward(j) * 2 + 1 - y)

        pl.when(j > 0)(lambda: follow(0, j - 1))

        @pl.when(j < 4)
        def _():
            lead(0, j)
            forward(me.inward(j) * 2 + y)

        return carry

    lax.fori_loop(0, 5, outputs, 0)
    close_sum(0)

    keep = as_column(valid[...].astype(F32))
    done = h[...] + acc[...]
    final[...] = done.astype(BF)
    diff = done - teacher[...].astype(F32)
    scaled = (keep * (SPAN / count[0:1, 0:1])) * diff
    dy_out[...] = scaled
    dyall[b] = scaled.astype(BF)
    kept = jnp.sum(keep * diff * diff)
    me_index = x * 16 + b
    errs[me_index] = jnp.zeros((8, 128), F32) + kept

    def tell(k, carry):
        to = ((x + k // 16) % 2, (b + k) % 16)
        remote(errs.at[me_index], errs.at[me_index], esend.at[k], erecv.at[me_index], to).start()
        return carry

    def with_dy(j, p):
        if p == 0:

            @pl.when((j > 0) & (j < 5))
            def _():
                zz = me.outward(j - 1)
                from_core(dyall, 1, zz, y)
                backward(zz * 2 + y)

        else:

            @pl.when(j == 0)
            def _():
                lax.fori_loop(1, 32, tell, 0)

            @pl.when(j > 1)
            def _():
                zz = me.outward(j - 2)
                from_core(dyall, 1, zz, 1 - y)
                backward(zz * 2 + 1 - y)

    gather(dyall, 1, with_dy)

    def in_grad(i):
        col = pl.ds(pl.multiple_of(i * 256, 256), 256)
        rows = nall[:, :, col].reshape(2048, 256)
        dwin[col, :] = lax.dot_general(
            rows, dpairs[...].reshape(2048, 768), TN, preferred_element_type=F32
        ).astype(BF)

    def out_grad(i):
        col = pl.ds(i * 256, 256)
        right = dyall[:, :, col].reshape(2048, 256)
        value = lax.dot_general(zg[...].reshape(2048, 384), right, TN, preferred_element_type=F32)
        there = i // 3 * 24
        dwout[:, there : there + 24, (i % 3) * 256 : (i % 3) * 256 + 256] = value.reshape(16, 24, 256)

    def over_in(k):
        src = dwin.at[pl.ds(pl.multiple_of((1 - x) * 768 + k * 256, 256), 256)]
        return remote(src, dwin_in.at[pl.ds(k * 256, 256)], xsend.at[5 + k], xrecv.at[5 + k], me.near("x"))

    def over_out():
        return remote(slab, dwout_in, xsend.at[8], xrecv.at[8], me.near("x"))

    def leads(j, carry):
        lead(1, j)
        return carry

    lax.fori_loop(0, 4, leads, 0)

    def sums(j, carry):
        @pl.when(j == 0)
        def _():
            for k in range(3):
                in_grad((1 - x) * 3 + k)
                over_in(k).start()

        @pl.when(j == 1)
        def _():
            for k in range(6):
                out_grad(k)
            slab[...] = dwout[...].astype(BF)
            pl.when(c != x)(lambda: over_out().start())

        @pl.when(j == 2)
        def _():
            for k in range(3):
                in_grad(x * 3 + k)

        follow(1, j)
        return carry

    for k in range(4):
        over_weights(k).wait_send()
    pl.when(c == x)(lambda: over_down().wait_send())
    lax.fori_loop(0, 4, sums, 0)
    dn2[...] = acc[...]
    close_sum(1)

    def hear(k, carry):
        left(errs.at[0], esend.at[k], me)
        s = ((x + k // 16) % 2) * 16 + (b + k) % 16
        arrived(errs.at[s], erecv.at[s], me)
        return carry

    lax.fori_loop(1, 32, hear, 0)
    total = errs[0]
    for s in range(1, 32):
        total = total + errs[s]
    err[...] = total / (1536.0 * count[...])

    for k in range(3):
        over_in(k).wait_send()
        here = pl.ds(pl.multiple_of(x * 768 + k * 256, 256), 256)
        there = pl.ds(k * 256, 256)
        arrived(dwin_in.at[there], xrecv.at[5 + k], me)
        dwin_in[there] = (dwin_in[there].astype(F32) + dwin[here, :].astype(F32)).astype(BF)
    out = pltpu.make_async_copy(dwin_in, dwin_out, own_sem.at[0])
    out.start()

    @pl.when(c == x)
    def _():
        arrived(dwout_in, xrecv.at[8], me)
        dwout_in[...] = (dwout_in[...].astype(F32) + dwout[...]).astype(BF)
        copy = pltpu.make_async_copy(dwout_in, dwout_out, own_sem.at[1])
        copy.start()
        copy.wait()

    pl.when(c != x)(lambda: over_out().wait_send())
    out.wait()


def run_experts(*operands):
    wide = (128, 1536)
    shard = (16,) + wide
    shape = jax.ShapeDtypeStruct
    return pl.pallas_call(
        experts_kernel,
        out_shape=(
            shape(wide, BF),
            shape((8, 128), F32),
            shape(wide, F32),
            shape(wide, F32),
            shape((768, 768), BF),
            shape((16, 48, 768), BF),
        ),
        in_specs=[VMEM] * 7 + [ANY] * 2,
        out_specs=(VMEM,) * 4 + (ANY,) * 2,
        scratch_shapes=[
            pltpu.VMEM(shard, BF),
            pltpu.VMEM(shard, BF),
            pltpu.VMEM((8, 256, 768), F32),
            pltpu.VMEM((8, 256, 384), BF),
            pltpu.VMEM((8, 256, 768), BF),
            pltpu.VMEM(shard, BF),
            pltpu.VMEM((8,) + wide, BF),
            pltpu.VMEM((4,) + wide, BF),
            pltpu.VMEM((5,) + wide, BF),
            pltpu.VMEM(wide, F32),
            pltpu.VMEM((32, 8, 128), F32),
            pltpu.VMEM((16, 8, 128), F32),
            pltpu.VMEM((16, 128, 1), F32),
            pltpu.VMEM((2, 16, 48, 768), BF),
            pltpu.VMEM((16, 48, 768), BF),
            pltpu.VMEM((384, 1536), BF),
            pltpu.VMEM((1536, 768), BF),
            pltpu.VMEM((768, 768), BF),
            pltpu.VMEM((16, 48, 768), F32),
            pltpu.VMEM((16, 48, 768), BF),
            DMA((2,)),
            DMA((2, 4, CUTS, 5)),
            DMA((2, 16, CUTS)),
            DMA((2, 8)),
            DMA((2, 8)),
            DMA((2, 4, CUTS)),
            DMA((2, 4, CUTS)),
            DMA((2, 4, CUTS, 2)),
            DMA((2, 5, CUTS)),
            DMA((32,)),
            DMA((32,)),
            DMA((16,)),
            DMA((16,)),
            DMA((9,)),
            DMA((9,)),
        ],
        compiler_params=params(2, 62),
        name="experts",
    )(*operands)


def norm_back(values, gain, grad):
    scale = lax.rsqrt(jnp.mean(values * values, axis=-1, keepdims=True) + 1e-06)
    inner = grad * gain
    mean = jnp.mean(inner * values, axis=-1, keepdims=True)
    return scale * inner - values * (scale * scale * scale * mean), jnp.sum(
        grad * values * scale, axis=0, keepdims=True
    )


def back_kernel(
    states, h, n1, qs, o, lse, dn2, dy, doc, freq, dwin, dwout, gq, go, kv_in,
    gx, gqw, gkw, gvw, gnorm, gout, gup, gdown,
    wq, wo, kv, pk, dos, delta, dh, dq, dkv, dqkv, gqkv, *rest,
):
    sums = [(rest[i * 11 : i * 11 + 6], rest[i * 11 + 6 : i * 11 + 11]) for i in range(4)]
    own_sem, asend, arecv, osend, orecv = rest[44:]
    me = Place()
    x, y, z, b, c = me.x, me.y, me.z, me.b, me.c
    loads = [
        pltpu.make_async_copy(go, wo, own_sem.at[0]),
        pltpu.make_async_copy(kv_in, kv, own_sem.at[1]),
        pltpu.make_async_copy(gq, wq, own_sem.at[2]),
    ]
    for load in loads:
        load.start()
    greet_all(me)

    def own_piece(n):
        col = pl.multiple_of(n * 768 + c * 384, 128)
        return pltpu.make_async_copy(
            dwin.at[b, :, pl.ds(n * 384, 384)], gup.at[b // 2, :, pl.ds(col, 384)], own_sem.at[3 + n]
        )

    def own_down():
        return pltpu.make_async_copy(dwout.at[b], gdown.at[b // 2], own_sem.at[5])

    def deal(k, carry):
        t = (b + k) % 16
        for n in range(2):
            col = pl.multiple_of(n * 768 + c * 384, 128)
            remote(
                dwin.at[t, :, pl.ds(n * 384, 384)],
                gup.at[b // 2, :, pl.ds(col, 384)],
                asend.at[k, n],
                arecv.at[b, n],
                (x, t),
            ).start()
        pl.when(c == x)(
            lambda: remote(dwout.at[t], gdown.at[b // 2], osend.at[k], orecv.at[b // 2], (x, t)).start()
        )
        return carry

    for n in range(2):
        own_piece(n).start()
    pl.when(c == x)(lambda: own_down().start())
    loads[2].wait()
    gains = wq[:, :, pl.ds(QKV, 128)].reshape(1536, 128).astype(F32).T
    res_grad, gain_two = norm_back(h[...], gains[1:2], dn2[...])
    dh[...] = dy[...] + res_grad
    da = dh[...].astype(BF)
    loads[0].wait()
    do = lax.dot_general(
        da, wo[...].reshape(1536, 1536), NT, preferred_element_type=F32
    ).astype(BF)
    low = o[...].astype(BF)
    for i in range(4):
        part = lax.dot_general(low[:, i * 384 : i * 384 + 384], da, TN, preferred_element_type=F32)
        wo[i * 8 : i * 8 + 8] = part.astype(BF).reshape(8, 48, 1536)
    out_sum = Sum(me, wo, by_weight, gout, *sums[0])
    key_sum = Sum(me, pk, by_token, dkv, *sums[1], causal=True)

    def lead_all(which):
        def one(j, carry):
            which.lead(j)
            return carry

        lax.fori_loop(0, 4, one, 0)

    lead_all(out_sum)
    for i in range(QUERY_HEADS):
        col, r = i * 128, (i % GROUP) * 128
        dos[i // GROUP, r : r + 128] = do[:, col : col + 128]
        prod = do[:, col : col + 128].astype(F32) * o[:, col : col + 128]
        delta[i // GROUP, :, r : r + 128] = jnp.sum(prod.T, axis=0, keepdims=True)
    dq[...] = jnp.zeros_like(dq)
    bounds = query_bounds(me, doc)
    loads[1].wait()

    def block(n):
        ok = allowed_keys(n * 256, bounds)
        for i in range(2):
            k = kv[pl.ds(n * 2, 2), :, i * 128 : i * 128 + 128].reshape(256, 128)
            v = kv[pl.ds(n * 2, 2), :, 256 + i * 128 : 384 + i * 128].reshape(256, 128)
            s = lax.dot_general(k, qs[i], NT, preferred_element_type=F32)
            p = jnp.where(ok, jnp.exp2(s * POWER - lse[i]), 0.0)
            dp = lax.dot_general(v, dos[i], NT, preferred_element_type=F32)
            ds = (p * (dp - delta[i])).astype(BF)
            dv = jnp.dot(p.astype(BF), dos[i], preferred_element_type=F32)
            dk = jnp.dot(ds, qs[i], preferred_element_type=F32) * SCALE
            pk[pl.ds(n * 2, 2), :, i * 128 : i * 128 + 128] = dk.astype(BF).reshape(2, 128, 128)
            pk[pl.ds(n * 2, 2), :, 256 + i * 128 : 384 + i * 128] = dv.astype(BF).reshape(2, 128, 128)
            dq[i] += lax.dot_general(k, ds, TN, preferred_element_type=F32)

    def turn(j, carry):
        out_sum.turn(j)
        lax.fori_loop(1 + j * 3, jnp.minimum(4 + j * 3, 16), deal, 0)

        @pl.when(key_sum.valid(j))
        def _():
            last = jnp.where(j == z, y * 2 + c, 3)

            def one(n, carry):
                block(j * 4 + n)
                return carry

            lax.fori_loop(0, last + 1, one, 0)

            def blank(n, carry):
                pk[pl.ds((j * 4 + n) * 2, 2)] = jnp.zeros((2, 128, 512), BF)
                return carry

            lax.fori_loop(last + 1, 4, blank, 0)
            key_sum.lead(j)

        key_sum.turn(j)
        return carry

    lax.fori_loop(0, 6, turn, 0)

    cos, sin = rotary_tables(me, doc, freq)
    for i in range(QUERY_HEADS):
        r = (i % GROUP) * 128
        head = dq[i // GROUP, :, r : r + 128].T * SCALE
        dqkv[:, i * 128 : i * 128 + 128] = turned(head, cos, -sin).astype(BF)
    for i in range(2):
        dqkv[:, 1536 + i * 128 : 1664 + i * 128] = turned(dkv[:, i * 128 : i * 128 + 128], cos, -sin).astype(BF)
        dqkv[:, 1792 + i * 128 : 1920 + i * 128] = dkv[:, 256 + i * 128 : 384 + i * 128].astype(BF)
    dn1 = lax.dot_general(
        dqkv[...], wq[:, :, pl.ds(0, QKV)].reshape(1536, QKV), NT, preferred_element_type=F32
    )
    in_grad, gain_one = norm_back(states[...].astype(F32), gains[0:1], dn1)
    gx[...] = dh[...] + in_grad
    rows = lax.broadcasted_iota(jnp.int32, (128, 1536), 0)
    tail = jnp.where(rows == 0, gain_one, jnp.where(rows == 1, gain_two, 0.0)).T
    wq[:, :, pl.ds(QKV, 128)] = tail.astype(BF).reshape(32, 48, 128)
    for i in range(4):
        part = lax.dot_general(
            n1[:, i * 384 : i * 384 + 384], dqkv[...], TN, preferred_element_type=F32
        )
        wq[i * 8 : i * 8 + 8, :, 0:QKV] = part.astype(BF).reshape(8, 48, QKV)
    proj = [Sum(me, wq, by_weight, gqkv, *sums[2 + i], PIECES[i]) for i in range(2)]
    for piece in proj:
        lead_all(piece)

    def last_turn(j, carry):
        for piece in proj:
            piece.turn(j)
        return carry

    lax.fori_loop(0, 6, last_turn, 0)
    gqw[...] = gqkv[:, 0:1536]
    gkw[...] = gqkv[:, 1536:1792]
    gvw[...] = gqkv[:, 1792:2048]
    gnorm[0:1, :] = as_row(gqkv[:, 2048:2049])
    gnorm[1:2, :] = as_row(gqkv[:, 2049:2050])
    out_sum.close()
    key_sum.close()
    for piece in proj:
        piece.close()

    def close(k, carry):
        f = (b + 16 - k) % 16
        for n in range(2):
            left(dwin.at[0, :, pl.ds(0, 384)], asend.at[k, n], me)
            col = pl.multiple_of(n * 768 + (f % 2) * 384, 128)
            arrived(gup.at[f // 2, :, pl.ds(col, 384)], arecv.at[f, n], me)
        pl.when(c == x)(lambda: left(dwout.at[0], osend.at[k], me))
        pl.when(f % 2 == x)(lambda: arrived(gdown.at[f // 2], orecv.at[f // 2], me))
        return carry

    lax.fori_loop(1, 16, close, 0)
    for n in range(2):
        own_piece(n).wait()
    pl.when(c == x)(lambda: own_down().wait())


def run_back(*operands):
    shape = jax.ShapeDtypeStruct
    smem = pl.BlockSpec(memory_space=pltpu.SMEM)
    return pl.pallas_call(
        back_kernel,
        out_shape=(
            shape((128, 1536), F32),
            shape((48, 1536), F32),
            shape((48, 256), F32),
            shape((48, 256), F32),
            shape((2, 48), F32),
            shape((48, 1536), F32),
            shape((8, 48, 1536), BF),
            shape((8, 48, 768), BF),
        ),
        in_specs=[VMEM] * 8 + [smem, VMEM] + [ANY] * 5,
        out_specs=(VMEM,) * 6 + (ANY,) * 2,
        scratch_shapes=[
            pltpu.VMEM((32, 48, WIDE), BF),
            pltpu.VMEM((32, 48, 1536), BF),
            pltpu.VMEM((32, 128, 512), BF),
            pltpu.VMEM((32, 128, 512), BF),
            pltpu.VMEM((2, LANES, 128), BF),
            pltpu.VMEM((2, 1, LANES), F32),
            pltpu.VMEM((128, 1536), F32),
            pltpu.VMEM((2, 128, LANES), F32),
            pltpu.VMEM((128, 512), F32),
            pltpu.VMEM((128, QKV), BF),
            pltpu.VMEM((48, WIDE), F32),
        ]
        + Sum.room(48, 1536)
        + Sum.room(128, 512)
        + Sum.room(48, PIECES[0][1])
        + Sum.room(48, PIECES[1][1])
        + [DMA((6,)), DMA((16, 2)), DMA((16, 2)), DMA((16,)), DMA((8,))],
        compiler_params=params(3, 61),
        name="back",
    )(*operands)


def per_device(
    states, teacher, valid, routes, gates, doc_starts, norm_one,
    w_query, key_weight, value_weight, w_output, norm_two, expert_in, expert_out,
):
    tokens = states.shape[2]
    width = states.shape[3]
    half = HEAD_SIZE // 2
    freq = np.float32(ROTARY_BASE) ** (-np.arange(half).astype(np.float32) / np.float32(half))
    freq = jnp.asarray(np.concatenate([freq, freq])[None, :], F32)
    rows = states.reshape(tokens, width)
    kept = valid.reshape(1, tokens)
    gq, go, kv, win, wout, h, n2, n1, qs, o, lse, count = run_front(
        rows, doc_starts, freq, norm_one.reshape(1, -1), norm_two.reshape(1, -1), kept, expert_out,
        w_query, key_weight, value_weight, w_output, expert_in,
    )
    final, error, dn2, dy, dwin, dwout = run_experts(
        n2, h, teacher.reshape(tokens, width), routes.reshape(tokens, TOP), gates.reshape(tokens, TOP),
        kept, count, win, wout,
    )
    gx, gqw, gkw, gvw, gnorm, gout, gup, gdown = run_back(
        rows, h, n1, qs, o, lse, dn2, dy, doc_starts, freq, dwin.reshape(16, 48, 768), dwout, gq, go, kv
    )
    shape = states.shape
    return (
        final.reshape(shape),
        error[0, 0],
        gx.reshape(shape),
        gnorm[0],
        gqw,
        gkw,
        gvw,
        gout,
        gnorm[1],
        gup.astype(F32),
        gdown.astype(F32).reshape(E, 2, 24, 768).transpose(0, 2, 1, 3).reshape(E, 24, 1536),
    )


def solution(mesh):
    in_specs = (
        P("blk", "head", None, None),
        P("blk", "head", None, None),
        P("blk", "head", None),
        P("blk", "head", None, None),
        P("blk", "head", None, None),
        P(),
        P(("head", "blk")),
        P(("head", "blk"), None),
        P(("head", "blk"), None),
        P(("head", "blk"), None),
        P(("head", "blk"), None),
        P(("head", "blk")),
        P(None, ("head", "blk"), None),
        P(None, ("head", "blk"), None),
    )
    out_specs = (
        P("blk", "head", None, None),
        P(),
        P("blk", "head", None, None),
        P(("head", "blk")),
        P(("head", "blk"), None),
        P(("head", "blk"), None),
        P(("head", "blk"), None),
        P(("head", "blk"), None),
        P(("head", "blk")),
        P(None, ("head", "blk"), None),
        P(None, ("head", "blk"), None),
    )
    sizes = dict(mesh.shape)
    plan = per_device if sizes == {"head": 2, "blk": 4 * NZ} else per_device_plain
    return jax.shard_map(
        plan, mesh=mesh, in_specs=in_specs, out_specs=out_specs, check_vma=False
    )
```

```python
import functools

import jax
import jax.numpy as jnp
import numpy as np
from jax import lax
from jax.experimental import pallas as pl
from jax.experimental.pallas import tpu as pltpu
from jax.sharding import PartitionSpec as P

QUERY_HEADS = 12
KEY_VALUE_HEADS = 2
HEAD_SIZE = 128
TOP = 4
E = 8
CAP = 96

ROTARY_BASE = 10000.0
FLOOR_SCORE = -1e30

MESH = pl.DeviceIdType.MESH
NZ = 4
SPAN = 32 * 128.0
BF = jnp.bfloat16
F32 = jnp.float32

def product(left, right):
    return jnp.dot(left, right, preferred_element_type=jnp.float32)


def rms_norm(values, gain):
    scale = lax.rsqrt(jnp.mean(values * values, axis=-1, keepdims=True) + 1e-06)
    return values * scale * gain


def rotary_apply(values, where, sign):
    half = values.shape[-1] // 2
    freq = ROTARY_BASE ** (-jnp.arange(half).astype(jnp.float32) / half)
    angle = where.astype(jnp.float32)[:, None] * freq[None, :]
    cosine = jnp.cos(angle)[:, None, :]
    sine = jnp.sin(angle)[:, None, :] * sign
    first = values[..., :half]
    second = values[..., half:]
    return jnp.concatenate(
        [first * cosine - second * sine, second * cosine + first * sine], axis=-1
    )


def doc_layout(position_index, doc_starts):
    inside = (position_index[:, None] >= doc_starts[None, :]).astype(jnp.int32)
    document_segment = jnp.sum(inside, axis=-1) - 1
    begin = jnp.max(jnp.where(inside > 0, doc_starts[None, :], 0), axis=-1)
    return (document_segment, position_index - begin)


def gated(pair):
    half = pair.shape[-1] // 2
    return jax.nn.gelu(pair[..., :half], approximate=True) * pair[..., half:]


def in_blocks(step_fn, carry, piece, rows):
    count_blocks = piece[0].shape[0] // rows

    def turn(number, state):
        part = tuple((lax.dynamic_slice_in_dim(item, number * rows, rows, 0) for item in piece))
        return step_fn(state, part, number * rows)

    return lax.fori_loop(0, count_blocks, turn, carry)


def per_device_plain(
    states,
    teacher,
    valid,
    routes,
    gates,
    doc_starts,
    norm_one,
    w_query,
    key_weight,
    value_weight,
    w_output,
    norm_two,
    expert_in,
    expert_out,
):
    count_per_token = states.shape[2]
    width = states.shape[3]
    pairs = lax.axis_size("head")
    blocks = lax.axis_size("blk")
    rows = count_per_token * pairs
    span = rows * blocks
    head_group = QUERY_HEADS // KEY_VALUE_HEADS
    scale = HEAD_SIZE ** (-0.5)
    highest = lax.Precision.HIGHEST
    block_index = lax.axis_index("blk")
    pair_index = lax.axis_index("head")
    token_index = (block_index * pairs + pair_index) * count_per_token + jnp.arange(
        count_per_token, dtype=jnp.int32
    )
    unused_segment, token_position = doc_layout(token_index, doc_starts)
    query_index = block_index * rows + jnp.arange(rows, dtype=jnp.int32)
    query_segment, query_where = doc_layout(query_index, doc_starts)
    last_query = block_index * rows + rows - 1
    inputs = states.reshape(count_per_token, width).astype(jnp.float32)
    target = teacher.reshape(count_per_token, width).astype(jnp.float32)
    keep_mask = valid.reshape(count_per_token).astype(jnp.float32)
    route_rows = routes.reshape(count_per_token, TOP)
    gate_rows = gates.reshape(count_per_token, TOP)
    query_w, key_w, value_w, out_w, gain_low_one, gain_low_two = (
        lax.all_gather(w_query, ("head", "blk"), axis=0, tiled=True),
        lax.all_gather(key_weight, ("head", "blk"), axis=0, tiled=True),
        lax.all_gather(value_weight, ("head", "blk"), axis=0, tiled=True),
        lax.all_gather(w_output, ("head", "blk"), axis=0, tiled=True),
        lax.all_gather(norm_one, ("head", "blk"), axis=0, tiled=True),
        lax.all_gather(norm_two, ("head", "blk"), axis=0, tiled=True),
    )
    gain_one = gain_low_one.astype(jnp.float32)
    gain_two = gain_low_two.astype(jnp.float32)
    normed_one = rms_norm(inputs, gain_one)
    normed_low = normed_one.astype(jnp.bfloat16)
    query_lin = product(normed_low, query_w)
    key_linear = product(normed_low, key_w)
    value_linear = product(normed_low, value_w)
    query_rotated = rotary_apply(
        query_lin.reshape(count_per_token, QUERY_HEADS, HEAD_SIZE), token_position, 1.0
    )
    key_rotated = rotary_apply(
        key_linear.reshape(count_per_token, KEY_VALUE_HEADS, HEAD_SIZE), token_position, 1.0
    )
    query_outgoing = query_rotated.astype(jnp.bfloat16).reshape(
        count_per_token, KEY_VALUE_HEADS, head_group * HEAD_SIZE
    )
    key_send = key_rotated.astype(jnp.bfloat16)
    value_outgoing = value_linear.astype(jnp.bfloat16).reshape(
        count_per_token, KEY_VALUE_HEADS, HEAD_SIZE
    )
    query_grp, key_grp, value_grp = (
        lax.all_to_all(query_outgoing, "head", split_axis=1, concat_axis=0, tiled=True),
        lax.all_to_all(key_send, "head", split_axis=1, concat_axis=0, tiled=True),
        lax.all_to_all(value_outgoing, "head", split_axis=1, concat_axis=0, tiled=True),
    )
    query_heads = query_grp.reshape(rows, head_group, HEAD_SIZE)
    key_rows = key_grp.reshape(rows, HEAD_SIZE)
    value_rows = value_grp.reshape(rows, HEAD_SIZE)

    def scores_for(keys, start):
        block_size = keys.shape[0]
        key_index = start + jnp.arange(block_size, dtype=jnp.int32)
        key_segment, unused_where = doc_layout(key_index, doc_starts)
        allowed = (key_index[None, :] <= query_index[:, None]) & (
            key_segment[None, :] == query_segment[:, None]
        )
        raw = (
            jnp.einsum("qhd,kd->hqk", query_heads, keys, preferred_element_type=jnp.float32) * scale
        )
        return (raw, allowed[None])

    def attend(carry, piece, start):
        keys, values = piece

        def work(state):
            running, total, accum = state
            raw, allowed = scores_for(keys, start)
            masked = jnp.where(allowed, raw, FLOOR_SCORE)
            newest = jnp.maximum(running, jnp.max(masked, axis=-1))
            factor = jnp.exp(running - newest)
            weights = jnp.where(allowed, jnp.exp(masked - newest[..., None]), 0.0)
            total = total * factor + jnp.sum(weights, axis=-1)
            update = jnp.einsum(
                "hqk,kd->qhd",
                weights.astype(jnp.bfloat16),
                values,
                preferred_element_type=jnp.float32,
            )
            accum = accum * factor.T[:, :, None] + update
            return (newest, total, accum)

        return lax.cond(start <= last_query, work, lambda state: state, carry)

    start_state = (
        jnp.full((head_group, rows), FLOOR_SCORE, jnp.float32),
        jnp.zeros((head_group, rows), jnp.float32),
        jnp.zeros((rows, head_group, HEAD_SIZE), jnp.float32),
    )
    running, total, accum = in_blocks(
        attend,
        start_state,
        (
            lax.all_gather(key_rows, "blk", axis=0, tiled=True),
            lax.all_gather(value_rows, "blk", axis=0, tiled=True),
        ),
        rows,
    )
    attn_full = accum / total.T[:, :, None]
    log_total = running + jnp.log(total)
    out_send = attn_full.astype(jnp.bfloat16).reshape(rows, 1, head_group * HEAD_SIZE)
    out_tok = lax.all_to_all(out_send, "head", split_axis=0, concat_axis=1, tiled=True).reshape(
        count_per_token, QUERY_HEADS * HEAD_SIZE
    )
    residual = inputs + product(out_tok, out_w)
    normed_two = rms_norm(residual, gain_two)
    normed_two_low = normed_two.astype(jnp.bfloat16)
    up_w, down_w = (
        lax.all_gather(expert_in, ("head", "blk"), axis=1, tiled=True),
        lax.all_gather(expert_out, ("head", "blk"), axis=1, tiled=True),
    )
    route_hot = (route_rows[:, :, None] == jnp.arange(E, dtype=jnp.int32)[None, None, :]).astype(
        jnp.int32
    )
    flat_hot = route_hot.reshape(count_per_token * TOP, E)
    before = jnp.cumsum(flat_hot, axis=0) - flat_hot
    slot = jnp.sum(before * flat_hot, axis=-1).reshape(count_per_token, TOP)
    slot_hot = (slot[:, :, None] == jnp.arange(CAP, dtype=jnp.int32)[None, None, :]).astype(
        jnp.float32
    )
    route_float = route_hot.astype(jnp.float32)
    dispatch = jnp.einsum("tje,tjc->ect", route_float, slot_hot, precision=highest)
    combine = jnp.einsum("tje,tjc,tj->ect", route_float, slot_hot, gate_rows, precision=highest)
    expert_rows = jnp.einsum(
        "ect,td->ecd",
        dispatch.astype(jnp.bfloat16),
        normed_two_low,
        preferred_element_type=jnp.float32,
    ).astype(jnp.bfloat16)
    pair = jnp.einsum("ecd,edf->ecf", expert_rows, up_w, preferred_element_type=jnp.float32)
    hidden_low = gated(pair).astype(jnp.bfloat16)
    expert_result = jnp.einsum(
        "ecf,efd->ecd", hidden_low, down_w, preferred_element_type=jnp.float32
    )
    mixture = jnp.einsum("ect,ecd->td", combine, expert_result, precision=highest)
    final = residual + mixture
    diff = final - target
    local_count = jnp.sum(keep_mask)
    local_error = jnp.sum(keep_mask * jnp.sum(diff * diff, axis=-1))
    count_all, error_all = lax.psum((local_count, local_error), ("head", "blk"))
    loss = error_all / (width * count_all)
    grad_final = keep_mask[:, None] * diff * (span * 1.0 / count_all)
    up_back, down_back = (
        lax.all_gather(expert_in, ("head", "blk"), axis=1, tiled=True),
        lax.all_gather(expert_out, ("head", "blk"), axis=1, tiled=True),
    )
    grad_result = jnp.einsum("ect,td->ecd", combine, grad_final, precision=highest).astype(
        jnp.bfloat16
    )
    grad_down = jnp.einsum(
        "ecf,ecd->efd", hidden_low, grad_result, preferred_element_type=jnp.float32
    )
    grad_hidden = jnp.einsum(
        "ecd,efd->ecf", grad_result, down_back, preferred_element_type=jnp.float32
    )
    unused_value, pull_gate = jax.vjp(gated, pair)
    grad_pair = pull_gate(grad_hidden)[0].astype(jnp.bfloat16)
    grad_up = jnp.einsum("ecd,ecf->edf", expert_rows, grad_pair, preferred_element_type=jnp.float32)
    grad_rows = jnp.einsum("ecf,edf->ecd", grad_pair, up_back, preferred_element_type=jnp.float32)
    grad_normed_two = jnp.einsum("ect,ecd->td", dispatch, grad_rows, precision=highest)
    unused_value, pull_two = jax.vjp(rms_norm, residual, gain_two)
    grad_res_norm, grad_gain_two = pull_two(grad_normed_two)
    grad_residual = grad_final + grad_res_norm
    grad_attn_low = grad_residual.astype(jnp.bfloat16)
    grad_out_w = jnp.einsum("tk,td->kd", out_tok, grad_attn_low, preferred_element_type=jnp.float32)
    output_gradient_token = jnp.einsum(
        "td,kd->tk", grad_attn_low, out_w, preferred_element_type=jnp.float32
    ).astype(jnp.bfloat16)
    grad_out_grp = lax.all_to_all(
        output_gradient_token.reshape(count_per_token, KEY_VALUE_HEADS, head_group * HEAD_SIZE),
        "head",
        split_axis=1,
        concat_axis=0,
        tiled=True,
    ).reshape(rows, head_group, HEAD_SIZE)
    delta = jnp.einsum(
        "qhd,qhd->hq", grad_out_grp.astype(jnp.float32), attn_full, precision=highest
    )

    def attend_back(carry, piece, start):
        keys, values = piece

        def work(state):
            grad_query, grad_keys, grad_values = state
            raw, allowed = scores_for(keys, start)
            weights = jnp.where(allowed, jnp.exp(raw - log_total[..., None]), 0.0)
            grad_weights = jnp.einsum(
                "qhd,kd->hqk", grad_out_grp, values, preferred_element_type=jnp.float32
            )
            grad_raw = (weights * (grad_weights - delta[..., None])).astype(jnp.bfloat16)
            grad_query = (
                grad_query
                + jnp.einsum("hqk,kd->qhd", grad_raw, keys, preferred_element_type=jnp.float32)
                * scale
            )
            key_part = (
                jnp.einsum("hqk,qhd->kd", grad_raw, query_heads, preferred_element_type=jnp.float32)
                * scale
            )
            value_part = jnp.einsum(
                "hqk,qhd->kd",
                weights.astype(jnp.bfloat16),
                grad_out_grp,
                preferred_element_type=jnp.float32,
            )
            block_size = keys.shape[0]
            grad_keys = lax.dynamic_update_slice_in_dim(
                grad_keys,
                lax.dynamic_slice_in_dim(grad_keys, start, block_size, 0) + key_part,
                start,
                0,
            )
            grad_values = lax.dynamic_update_slice_in_dim(
                grad_values,
                lax.dynamic_slice_in_dim(grad_values, start, block_size, 0) + value_part,
                start,
                0,
            )
            return (grad_query, grad_keys, grad_values)

        return lax.cond(start <= last_query, work, lambda state: state, carry)

    back_state = (
        jnp.zeros((rows, head_group, HEAD_SIZE), jnp.float32),
        jnp.zeros((span, HEAD_SIZE), jnp.float32),
        jnp.zeros((span, HEAD_SIZE), jnp.float32),
    )
    grad_query, grad_keys_full, grad_values_full = in_blocks(
        attend_back,
        back_state,
        (
            lax.all_gather(key_rows, "blk", axis=0, tiled=True),
            lax.all_gather(value_rows, "blk", axis=0, tiled=True),
        ),
        rows,
    )
    grad_keys, grad_values = (
        lax.psum_scatter(grad_keys_full, "blk", scatter_dimension=0, tiled=True),
        lax.psum_scatter(grad_values_full, "blk", scatter_dimension=0, tiled=True),
    )
    grad_query_lin = (
        rotary_apply(grad_query, query_where, -1.0)
        .astype(jnp.bfloat16)
        .reshape(rows, 1, head_group * HEAD_SIZE)
    )
    grad_key_lin = rotary_apply(grad_keys.reshape(rows, 1, HEAD_SIZE), query_where, -1.0).astype(
        jnp.bfloat16
    )
    grad_value_lin = grad_values.astype(jnp.bfloat16).reshape(rows, 1, HEAD_SIZE)
    back_query, key_backward, value_backward = (
        lax.all_to_all(grad_query_lin, "head", split_axis=0, concat_axis=1, tiled=True),
        lax.all_to_all(grad_key_lin, "head", split_axis=0, concat_axis=1, tiled=True),
        lax.all_to_all(grad_value_lin, "head", split_axis=0, concat_axis=1, tiled=True),
    )
    back_query = back_query.reshape(count_per_token, QUERY_HEADS * HEAD_SIZE)
    key_backward = key_backward.reshape(count_per_token, KEY_VALUE_HEADS * HEAD_SIZE)
    value_backward = value_backward.reshape(count_per_token, KEY_VALUE_HEADS * HEAD_SIZE)
    grad_query_w = jnp.einsum(
        "td,tk->dk", normed_low, back_query, preferred_element_type=jnp.float32
    )
    grad_key_w = jnp.einsum(
        "td,tk->dk", normed_low, key_backward, preferred_element_type=jnp.float32
    )
    grad_value_w = jnp.einsum(
        "td,tk->dk", normed_low, value_backward, preferred_element_type=jnp.float32
    )
    grad_normed_one = jnp.einsum(
        "tk,dk->td", back_query, query_w, preferred_element_type=jnp.float32
    )
    grad_normed_one = grad_normed_one + jnp.einsum(
        "tk,dk->td", key_backward, key_w, preferred_element_type=jnp.float32
    )
    grad_normed_one = grad_normed_one + jnp.einsum(
        "tk,dk->td", value_backward, value_w, preferred_element_type=jnp.float32
    )
    unused_value, pull_one = jax.vjp(rms_norm, inputs, gain_one)
    grad_in_norm, grad_gain_one = pull_one(grad_normed_one)
    grad_inputs = grad_residual + grad_in_norm
    sums = (
        lax.psum_scatter(grad_query_w, ("head", "blk"), scatter_dimension=0, tiled=True),
        lax.psum_scatter(grad_key_w, ("head", "blk"), scatter_dimension=0, tiled=True),
        lax.psum_scatter(grad_value_w, ("head", "blk"), scatter_dimension=0, tiled=True),
        lax.psum_scatter(grad_out_w, ("head", "blk"), scatter_dimension=0, tiled=True),
        lax.psum_scatter(grad_gain_one, ("head", "blk"), scatter_dimension=0, tiled=True),
        lax.psum_scatter(grad_gain_two, ("head", "blk"), scatter_dimension=0, tiled=True),
        lax.psum_scatter(grad_up, ("head", "blk"), scatter_dimension=1, tiled=True),
        lax.psum_scatter(grad_down, ("head", "blk"), scatter_dimension=1, tiled=True),
    )
    shape = states.shape
    return (
        final.astype(jnp.bfloat16).reshape(shape),
        loss,
        grad_inputs.reshape(shape),
        sums[4],
        sums[0],
        sums[1],
        sums[2],
        sums[3],
        sums[5],
        sums[6],
        sums[7],
    )


class Place:
    def __init__(self):
        self.x = lax.axis_index("head")
        self.b = lax.axis_index("blk")
        self.c = self.b % 2
        self.y = (self.b // 2) % 2
        self.z = self.b // 4

    def near(self, kind):
        x, y, z, c = self.x, self.y, self.z, self.c
        if kind == "up":
            z = jnp.minimum(z + 1, NZ - 1)
        elif kind == "down":
            z = jnp.maximum(z - 1, 0)
        elif kind == "y":
            y = 1 - y
        elif kind == "x":
            x = 1 - x
        elif kind == "c":
            c = 1 - c
        return (x, z * 4 + y * 2 + c)

    def blk(self, z, y, c):
        return z * 4 + y * 2 + c

    def outward(self, j):
        inner = jnp.where(j < 2, 1 - j, j)
        order = jnp.where((self.z == 0) | (self.z == NZ - 1), j, inner)
        return jnp.where(self.z < 2, order, NZ - 1 - order)

    def inward(self, j):
        inner = jnp.where(j == 0, 3, jnp.where(j == 1, 0, jnp.where(j == 2, 2, 1)))
        order = jnp.where((self.z == 0) | (self.z == NZ - 1), NZ - 1 - j, inner)
        return jnp.where(self.z < 2, order, NZ - 1 - order)


def greet_all(me):
    barrier = pltpu.get_barrier_semaphore()

    def one(k, carry):
        pl.semaphore_signal(
            barrier, inc=1, device_id=((me.x + k // 16) % 2, (me.b + k) % 16), device_id_type=MESH
        )
        return carry

    lax.fori_loop(1, 32, one, 0)
    pl.semaphore_wait(barrier, 31)


def remote(src, dst, send, recv, to):
    return pltpu.make_async_remote_copy(
        src_ref=src, dst_ref=dst, send_sem=send, recv_sem=recv, device_id=to, device_id_type=MESH
    )


def arrived(ref, sem, me):
    remote(ref, ref, sem, sem, me.near("c")).wait_recv()


def left(ref, sem, me):
    remote(ref, ref, sem, sem, me.near("c")).wait_send()


class Gather:
    def __init__(self, me, g, index, send, recv, cols=None, causal=False):
        self.me, self.g, self.index, self.send, self.recv, self.causal = me, g, index, send, recv, causal
        start, width = cols or (0, g.shape[2])
        cut = (width // 2 + 127) // 128 * 128
        self.cols = pl.ds(start, width)
        self.first, self.second = pl.ds(start, cut), pl.ds(start + cut, width - cut)

    def place(self, j):
        return self.me.z - j if self.causal else self.me.outward(j)

    def valid(self, j):
        return (j >= 0) & (j <= (self.me.z if self.causal else NZ - 1))

    def ups(self, zz):
        if self.causal:
            return self.me.z < NZ - 1
        return (zz <= self.me.z) & (self.me.z < NZ - 1)

    def downs(self, zz):
        return (zz >= self.me.z) & (self.me.z > 0)

    def put(self, j, kind, n, s, cols=None, slot=0):
        ref = self.g.at[s, :, self.cols if cols is None else cols]
        remote(ref, ref, self.send.at[j, n], self.recv.at[s, slot], self.me.near(kind)).start()

    def wait(self, s):
        arrived(self.g.at[s, :, self.cols], self.recv.at[s, 0], self.me)

    def turn(self, j):
        me, index = self.me, self.index
        x, y, c = me.x, me.y, me.c

        @pl.when(self.valid(j) & (j > 0))
        def _():
            self.wait(index(x, self.place(j), y, c))

        @pl.when(self.valid(j))
        def _():
            zz = self.place(j)
            own = index(x, zz, y, c)
            pl.when(self.ups(zz))(lambda: self.put(j, "up", 0, own))
            if not self.causal:
                pl.when(self.downs(zz))(lambda: self.put(j, "down", 1, own))
            self.put(j, "y", 2, own)
            self.put(j, "x", 3, own)
            self.put(j, "c", 6, own)

        @pl.when(self.valid(j - 1))
        def _():
            i = j - 1
            zp = self.place(i)
            s = index(x, zp, 1 - y, c)
            self.wait(s)
            self.put(i, "x", 4, s, self.first, 0)
            self.put(i, "c", 7, s)
            t = index(1 - x, zp, y, c)
            self.wait(t)
            self.put(i, "y", 5, t, self.second, 1)
            self.put(i, "c", 8, t)

        @pl.when(self.valid(j - 2))
        def _():
            i = j - 2
            s = index(1 - x, self.place(i), 1 - y, c)
            arrived(self.g.at[s, :, self.first], self.recv.at[s, 0], me)
            arrived(self.g.at[s, :, self.second], self.recv.at[s, 1], me)
            self.put(i, "c", 9, s)

    def from_core(self, j):
        me = self.me
        for xx in (me.x, 1 - me.x):
            for yy in (me.y, 1 - me.y):
                self.wait(self.index(xx, self.place(j), yy, 1 - me.c))

    def close(self, cores=True):
        me = self.me

        def one(j, carry):
            @pl.when(self.valid(j))
            def _():
                zz = self.place(j)
                own = self.index(me.x, zz, me.y, me.c)
                whole = self.g.at[own, :, self.cols]
                first, second = self.g.at[own, :, self.first], self.g.at[own, :, self.second]
                pl.when(self.ups(zz))(lambda: left(whole, self.send.at[j, 0], me))
                if not self.causal:
                    pl.when(self.downs(zz))(lambda: left(whole, self.send.at[j, 1], me))
                for n in (2, 3, 6, 7, 8, 9):
                    left(whole, self.send.at[j, n], me)
                left(first, self.send.at[j, 4], me)
                left(second, self.send.at[j, 5], me)
                if cores:
                    self.from_core(j)

            return carry

        lax.fori_loop(0, 4, one, 0)


class Sum:
    def __init__(self, me, part, index, out, room, sems, cols=None, causal=False):
        self.me, self.part, self.index, self.out, self.causal = me, part, index, out, causal
        start, width = cols or (0, part.shape[2])
        self.cols = pl.ds(start, width)
        self.rc, self.rx, self.ry, self.rn, self.rz, self.acc = room
        self.sc, self.ss, self.vc, self.vn, self.vz = sems
        self.half = (width // 2 + 127) // 128 * 128
        self.first, self.second = pl.ds(0, self.half), pl.ds(self.half, width - self.half)

    @staticmethod
    def room(rows, columns):
        half = (columns // 2 + 127) // 128 * 128
        return [
            pltpu.VMEM((16, rows, columns), BF),
            pltpu.VMEM((4, rows, half), BF),
            pltpu.VMEM((4, rows, columns - half), BF),
            pltpu.VMEM((2, 4, rows, columns), BF),
            pltpu.VMEM((5, rows, columns), BF),
            pltpu.VMEM((rows, columns), F32),
            DMA((16,)),
            DMA((4, 6)),
            DMA((16,)),
            DMA((4, 4)),
            DMA((5,)),
        ]

    def place(self, j):
        return j if self.causal else self.me.inward(j)

    def valid(self, j):
        return (j >= 0) & (j <= (self.me.z if self.causal else NZ - 1))

    def slot(self, xx, zz, yy):
        return zz * 4 + xx * 2 + yy

    def lead(self, j):
        me = self.me
        zz = self.place(j)
        for xx in (1 - me.x, me.x):
            for yy in (1 - me.y, me.y):
                k = self.slot(xx, zz, yy)
                src = self.part.at[self.index(xx, zz, yy, 1 - me.c), :, self.cols]
                remote(src, self.rc.at[k], self.sc.at[k], self.vc.at[k], me.near("c")).start()

    def with_core(self, xx, zz, yy):
        k = self.slot(xx, zz, yy)
        arrived(self.rc.at[k], self.vc.at[k], self.me)
        own = self.part[self.index(xx, zz, yy, self.me.c), :, self.cols]
        return k, own.astype(F32) + self.rc[k].astype(F32)

    def turn(self, j):
        me, half, first, second = self.me, self.half, self.first, self.second
        rc, rx, ry, rn, ss, vn = self.rc, self.rx, self.ry, self.rn, self.ss, self.vn
        x, y = me.x, me.y

        @pl.when(self.valid(j))
        def _():
            zz = self.place(j)
            k, total = self.with_core(1 - x, zz, 1 - y)
            rc[k] = total.astype(BF)
            remote(rc.at[k, :, first], rx.at[zz], ss.at[j, 0], vn.at[zz, 0], me.near("x")).start()
            remote(rc.at[k, :, second], ry.at[zz], ss.at[j, 1], vn.at[zz, 1], me.near("y")).start()

        @pl.when(self.valid(j - 1))
        def _():
            i = j - 1
            zz = self.place(i)
            k, total = self.with_core(x, zz, 1 - y)
            arrived(rx.at[zz], vn.at[zz, 0], me)
            rc[k, :, second] = total[:, half:].astype(BF)
            rc[k, :, first] = (total[:, :half] + rx[zz].astype(F32)).astype(BF)
            remote(rc.at[k], rn.at[0, zz], ss.at[i, 2], vn.at[zz, 2], me.near("y")).start()
            k, total = self.with_core(1 - x, zz, y)
            arrived(ry.at[zz], vn.at[zz, 1], me)
            rc[k, :, first] = total[:, :half].astype(BF)
            rc[k, :, second] = (total[:, half:] + ry[zz].astype(F32)).astype(BF)
            remote(rc.at[k], rn.at[1, zz], ss.at[i, 3], vn.at[zz, 3], me.near("x")).start()

        @pl.when(self.valid(j - 2))
        def _():
            i = j - 2
            zz = self.place(i)
            k, total = self.with_core(x, zz, y)
            arrived(rn.at[0, zz], vn.at[zz, 2], me)
            arrived(rn.at[1, zz], vn.at[zz, 3], me)
            self.acc[...] = total + rn[0, zz].astype(F32) + rn[1, zz].astype(F32)
            along_z(me, i, zz, self.acc, rc.at[k], self.rz, ss, 4, self.vz, self.causal)

            @pl.when(zz == me.z)
            def _():
                self.out[:, self.cols] = self.acc[...]

    def close(self):
        me = self.me
        whole = self.rc.at[0]
        first, second = self.rc.at[0, :, self.first], self.rc.at[0, :, self.second]

        def one(j, carry):
            @pl.when(self.valid(j))
            def _():
                zz = self.place(j)
                for xx in (1 - me.x, me.x):
                    for yy in (1 - me.y, me.y):
                        left(whole, self.sc.at[self.slot(xx, zz, yy)], me)
                left(first, self.ss.at[j, 0], me)
                left(second, self.ss.at[j, 1], me)
                for n in (2, 3):
                    left(whole, self.ss.at[j, n], me)
                if not self.causal:
                    pl.when(zz > me.z)(lambda: left(whole, self.ss.at[j, 4], me))
                pl.when(zz < me.z)(lambda: left(whole, self.ss.at[j, 5], me))

            return carry

        lax.fori_loop(0, 4, one, 0)


def along_z(me, i, zz, acc, room, rz, ss, n, vz, causal=False):
    z = me.z

    def add(slot):
        arrived(rz.at[slot], vz.at[slot], me)
        acc[...] += rz[slot].astype(F32)

    if not causal:
        pl.when((zz >= z) & (z > 0))(lambda: add(zz))
    pl.when((zz < z) & (z < NZ - 1))(lambda: add(zz))
    pl.when((zz == z) & (z < NZ - 1))(lambda: add(4))

    if not causal:

        @pl.when(zz > z)
        def _():
            room[...] = acc[...].astype(BF)
            remote(room, rz.at[zz], ss.at[i, n], vz.at[zz], me.near("up")).start()

    @pl.when(zz < z)
    def _():
        room[...] = acc[...].astype(BF)
        there = jnp.where(zz == z - 1, 4, zz)
        remote(room, rz.at[there], ss.at[i, n + 1], vz.at[there], me.near("down")).start()


def by_weight(x, z, y, c):
    return x * 16 + z * 4 + y * 2 + c


def by_token(x, z, y, c):
    return (z * 4 + y * 2 + c) * 2 + x


ANY = pl.BlockSpec(memory_space=pl.ANY)
VMEM = pl.BlockSpec(memory_space=pltpu.VMEM)
DMA = pltpu.SemaphoreType.DMA


def params(number, mib):
    return pltpu.CompilerParams(
        collective_id=number, has_side_effects=True, vmem_limit_bytes=mib << 20
    )


NT = (((1,), (1,)), ((), ()))
TN = (((0,), (0,)), ((), ()))
GROUP = QUERY_HEADS // KEY_VALUE_HEADS
LANES = GROUP * 128
SCALE = HEAD_SIZE ** (-0.5)
POWER = SCALE * 1.4426950408889634


def turned(u, cosine, sine):
    return u * cosine + pltpu.roll(u, 64, 1) * sine


def begin_of(place, doc):
    begin = jnp.zeros_like(place)
    for i in range(doc.shape[0]):
        begin = jnp.where(place >= doc[i], jnp.maximum(begin, doc[i]), begin)
    return begin


def rotary_tables(me, doc, freq):
    first = (me.b * 2 + me.x) * 128
    place = first + lax.broadcasted_iota(jnp.int32, (128, 128), 0)
    angle = (place - begin_of(place, doc)).astype(F32) * freq[...]
    sine = jnp.sin(angle)
    lane = lax.broadcasted_iota(jnp.int32, (128, 128), 1)
    return jnp.cos(angle), jnp.where(lane < 64, -sine, sine)


def query_bounds(me, doc):
    place = (me.b * 2 + me.x) * 128 + lax.broadcasted_iota(jnp.int32, (1, LANES), 1) % 128
    return begin_of(place, doc), place


def allowed_keys(start, bounds):
    key = start + lax.broadcasted_iota(jnp.int32, (256, LANES), 0)
    return (key >= bounds[0]) & (key <= bounds[1])


def eye(n):
    return lax.broadcasted_iota(jnp.int32, (n, n), 0) == lax.broadcasted_iota(jnp.int32, (n, n), 1)


def as_column(row):
    return jnp.sum(jnp.where(eye(row.shape[1]), row, 0.0), axis=1, keepdims=True)


def as_row(column):
    return jnp.sum(jnp.where(eye(column.shape[0]), column, 0.0), axis=0, keepdims=True)


QKV = 2048
WIDE = QKV + 128
PIECES = ((0, 1152), (1152, 1024))


def front_kernel(
    doc, freq, norm_one, norm_two, valid, states, down_in, wq, wk, wv, wo, up,
    gq_out, go_out, kv_out, win, wout, h_out, n2_out, n1_out, qs_out, o_out, lse, count,
    gq, go, kv, down, top, total, acc, low_rows, down_raw, cos, sin, n1, qs, o, h, n2,
    load_sem, own_sem, qsend, qrecv, gsend, grecv, ksend, krecv, asend, arecv, osend, orecv,
):
    me = Place()
    x, y, z, b, c = me.x, me.y, me.z, me.b, me.c
    here = by_weight(x, z, y, c)
    mine = [
        pltpu.make_async_copy(wq, gq.at[here, :, pl.ds(0, 1536)], own_sem.at[0]),
        pltpu.make_async_copy(wk, gq.at[here, :, pl.ds(1536, 256)], own_sem.at[1]),
        pltpu.make_async_copy(wv, gq.at[here, :, pl.ds(1792, 256)], own_sem.at[2]),
        pltpu.make_async_copy(wo, go.at[here], own_sem.at[3]),
    ]
    loads = [
        pltpu.make_async_copy(down_in, down_raw, load_sem.at[0]),
        pltpu.make_async_copy(states, low_rows, load_sem.at[1]),
    ]
    for copy in mine + loads:
        copy.start()

    lane = lax.broadcasted_iota(jnp.int32, (48, 128), 1)
    kept = jnp.sum(valid[...].astype(F32))
    extra = jnp.where(
        lane == 0,
        as_column(norm_one[...].astype(F32)),
        jnp.where(lane == 1, as_column(norm_two[...].astype(F32)), jnp.where(lane == 2, kept, 0.0)),
    )
    gq[here, :, pl.ds(QKV, 128)] = extra.astype(BF)
    loads[0].wait()
    for e in range(E):
        wide = down_raw[e].astype(F32)
        down[e] = jnp.concatenate([wide[:, :768], wide[:, 768:]], axis=0).astype(BF)
    greet_all(me)
    for copy in mine:
        copy.wait()

    def own_piece(n):
        col = pl.multiple_of(n * 768 + c * 384, 128)
        return pltpu.make_async_copy(
            up.at[b // 2, :, pl.ds(col, 384)], win.at[b, :, pl.ds(n * 384, 384)], own_sem.at[4 + n]
        )

    def own_down():
        return pltpu.make_async_copy(down.at[b // 2], wout.at[b], own_sem.at[6])

    def deal(k, carry):
        t = (b + k) % 16
        for n in range(2):
            col = pl.multiple_of(n * 768 + (t % 2) * 384, 128)
            remote(
                up.at[t // 2, :, pl.ds(col, 384)],
                win.at[b, :, pl.ds(n * 384, 384)],
                asend.at[k, n],
                arecv.at[b, n],
                (x, t),
            ).start()
        pl.when(t % 2 == x)(
            lambda: remote(down.at[t // 2], wout.at[b], osend.at[k], orecv.at[b], (x, t)).start()
        )
        return carry

    weights = [
        Gather(me, gq, by_weight, qsend.at[i], qrecv.at[i], PIECES[i]) for i in range(len(PIECES))
    ]

    def first_turn(j, carry):
        for piece in weights:
            piece.turn(j)
        lax.fori_loop(1 + j * 3, jnp.minimum(4 + j * 3, 16), deal, 0)

        @pl.when(j == 0)
        def _():
            cos[...], sin[...] = rotary_tables(me, doc, freq)

        return carry

    lax.fori_loop(0, 6, first_turn, 0)
    for n in range(2):
        own_piece(n).start()
    pl.when(c == x)(lambda: own_down().start())
    bounds = query_bounds(me, doc)
    loads[1].wait()
    rows = low_rows[...].astype(F32)
    level = rows * lax.rsqrt(jnp.mean(rows * rows, axis=-1, keepdims=True) + 1e-06)
    for piece in weights:
        piece.close()
    keep = pltpu.make_async_copy(gq, gq_out, own_sem.at[0])
    keep.start()

    gains = gq[:, :, pl.ds(QKV, 128)].reshape(1536, 128).astype(F32).T
    n1[...] = (level * gains[0:1]).astype(BF)
    turns = cos[...], sin[...]
    at = by_token(x, z, y, c)
    keys = Gather(me, kv, by_token, ksend, krecv, causal=True)
    output = Gather(me, go, by_weight, gsend, grecv)
    both = jnp.dot(n1[...], gq[:, :, pl.ds(1536, 512)].reshape(1536, 512), preferred_element_type=F32)
    for i in range(2):
        kv[at, :, i * 128 : i * 128 + 128] = turned(both[:, i * 128 : i * 128 + 128], *turns).astype(BF)
    kv[at, :, 256:512] = both[:, 256:512].astype(BF)
    keys.turn(0)
    query = jnp.dot(n1[...], gq[:, :, pl.ds(0, 1536)].reshape(1536, 1536), preferred_element_type=F32)
    for i in range(QUERY_HEADS):
        r = (i % GROUP) * 128
        qs[i // GROUP, r : r + 128] = turned(query[:, i * 128 : i * 128 + 128], *turns).astype(BF)
    count[...] = jnp.zeros((8, 128), F32) + jnp.sum(gains[2:3]) / 48.0
    saved = [
        pltpu.make_async_copy(n1, n1_out, load_sem.at[0]),
        pltpu.make_async_copy(qs, qs_out, load_sem.at[1]),
    ]
    for copy in saved:
        copy.start()

    top[...] = jnp.full_like(top, FLOOR_SCORE)
    total[...] = jnp.zeros_like(total)
    acc[...] = jnp.zeros_like(acc)
    def block(n):
        ok = allowed_keys(n * 256, bounds)
        for i in range(2):
            k = kv[pl.ds(n * 2, 2), :, i * 128 : i * 128 + 128].reshape(256, 128)
            v = kv[pl.ds(n * 2, 2), :, 256 + i * 128 : 384 + i * 128].reshape(256, 128)
            s = lax.dot_general(k, qs[i], NT, preferred_element_type=F32)
            s = jnp.where(ok, s, FLOOR_SCORE)
            old = top[i]
            new = jnp.maximum(old, jnp.max(s, axis=0, keepdims=True))
            factor = jnp.exp2((old - new) * POWER)
            p = jnp.exp2((s - new) * POWER)
            top[i] = new
            total[i] = total[i] * factor + jnp.sum(p, axis=0, keepdims=True)
            acc[i] = acc[i] * factor + lax.dot_general(v, p.astype(BF), TN, preferred_element_type=F32)

    def turn(j, carry):
        pl.when(j > 0)(lambda: keys.turn(j))
        output.turn(j - 2)

        @pl.when(keys.valid(j - 2))
        def _():
            i = j - 2
            keys.from_core(i)
            zz = z - i
            last = jnp.where(i == 0, y * 2 + c, 3)

            def one(n, carry):
                block(zz * 4 + last - n)
                return carry

            lax.fori_loop(0, last + 1, one, 0)

        return carry

    lax.fori_loop(0, 8, turn, 0)
    output.close()
    keep_o = pltpu.make_async_copy(go, go_out, own_sem.at[1])
    keep_o.start()
    keep_k = pltpu.make_async_copy(kv, kv_out, own_sem.at[2])
    keep_k.start()
    for i in range(2):
        lse[i] = top[i] * POWER + jnp.log2(total[i])
        done = acc[i] / total[i]
        for r in range(GROUP):
            col = (i * GROUP + r) * 128
            o[:, col : col + 128] = done[:, r * 128 : r * 128 + 128].T
    saved.append(pltpu.make_async_copy(o, o_out, load_sem.at[2]))
    saved[2].start()
    res = low_rows[...].astype(F32) + jnp.dot(
        o[...].astype(BF), go[...].reshape(1536, 1536), preferred_element_type=F32
    )
    h[...] = res
    n2[...] = (
        res * lax.rsqrt(jnp.mean(res * res, axis=-1, keepdims=True) + 1e-06) * gains[1:2]
    ).astype(BF)
    saved.append(pltpu.make_async_copy(h, h_out, load_sem.at[3]))
    saved.append(pltpu.make_async_copy(n2, n2_out, load_sem.at[4]))
    saved[3].start()
    saved[4].start()

    keys.close(False)

    def close(k, carry):
        piece = win.at[b, :, pl.ds(0, 384)]
        f = (b + 16 - k) % 16
        for n in range(2):
            left(piece, asend.at[k, n], me)
            arrived(win.at[f, :, pl.ds(n * 384, 384)], arecv.at[f, n], me)
        pl.when((b + k) % 2 == x)(lambda: left(wout.at[b], osend.at[k], me))
        pl.when(c == x)(lambda: arrived(wout.at[f], orecv.at[f], me))
        return carry

    lax.fori_loop(1, 16, close, 0)
    for n in range(2):
        own_piece(n).wait()
    pl.when(c == x)(lambda: own_down().wait())
    for copy in [keep, keep_o, keep_k] + saved:
        copy.wait()


def run_front(*operands):
    shape = jax.ShapeDtypeStruct
    smem = pl.BlockSpec(memory_space=pltpu.SMEM)
    return pl.pallas_call(
        front_kernel,
        out_shape=(
            shape((32, 48, WIDE), BF),
            shape((32, 48, 1536), BF),
            shape((32, 128, 512), BF),
            shape((16, 48, 768), BF),
            shape((16, 48, 768), BF),
            shape((128, 1536), F32),
            shape((128, 1536), BF),
            shape((128, 1536), BF),
            shape((2, LANES, 128), BF),
            shape((128, 1536), F32),
            shape((2, 1, LANES), F32),
            shape((8, 128), F32),
        ),
        in_specs=[smem] + [VMEM] * 4 + [ANY] * 7,
        out_specs=(ANY,) * 10 + (VMEM,) * 2,
        scratch_shapes=[
            pltpu.VMEM((32, 48, WIDE), BF),
            pltpu.VMEM((32, 48, 1536), BF),
            pltpu.VMEM((32, 128, 512), BF),
            pltpu.VMEM((8, 48, 768), BF),
            pltpu.VMEM((2, 1, LANES), F32),
            pltpu.VMEM((2, 1, LANES), F32),
            pltpu.VMEM((2, 128, LANES), F32),
            pltpu.VMEM((128, 1536), BF),
            pltpu.VMEM((8, 24, 1536), BF),
            pltpu.VMEM((128, 128), F32),
            pltpu.VMEM((128, 128), F32),
            pltpu.VMEM((128, 1536), BF),
            pltpu.VMEM((2, LANES, 128), BF),
            pltpu.VMEM((128, 1536), F32),
            pltpu.VMEM((128, 1536), F32),
            pltpu.VMEM((128, 1536), BF),
            DMA((5,)),
            DMA((7,)),
            DMA((2, 4, 10)),
            DMA((2, 32, 2)),
            DMA((4, 10)),
            DMA((32, 2)),
            DMA((4, 10)),
            DMA((32, 2)),
            DMA((16, 2)),
            DMA((16, 2)),
            DMA((16,)),
            DMA((16,)),
        ],
        compiler_params=params(1, 62),
        name="front",
    )(*operands)


GELU_A = 0.7978845608028654
GELU_B = 0.044715


CUTS = 2
CUT = 128 // CUTS


def experts_kernel(
    routes, gates, valid, count, n2, h_in, teacher_in, win, wout,
    err, final_out, dn2_out, dy_out, dwin_out, dwout_out,
    h, teacher, final, dy, nall, dyall, pairs, zg, dpairs, part, rc, ry, rz, acc, errs, tables, gate,
    wfull, slab, wdown, dwin, dwin_in, dwout, dwout_in,
    load_sem, own_sem, gsend, grecv, csend, crecv, ysend, yrecv, zsend, zrecv, esend, erecv,
    tsend, trecv, xsend, xrecv,
):
    me = Place()
    x, y, z, b, c = me.x, me.y, me.z, me.b, me.c
    half = pltpu.make_async_copy(win, wfull.at[x], own_sem.at[0])
    half.start()
    loads = [
        pltpu.make_async_copy(n2, nall.at[b], load_sem.at[0]),
        pltpu.make_async_copy(h_in, h, load_sem.at[1]),
        pltpu.make_async_copy(teacher_in, teacher, load_sem.at[2]),
    ]
    for load in loads:
        load.start()
    held = pltpu.make_async_copy(wout, slab, own_sem.at[1])
    pl.when(c == x)(held.start)
    expert = lax.broadcasted_iota(jnp.int32, (8, 128), 0)
    table = jnp.zeros((8, 128), F32)
    for k in range(TOP):
        table = table + jnp.where(routes[k : k + 1, :] == expert, gates[k : k + 1, :], 0.0)
    tables[b] = table
    greet_all(me)

    def rows_of(p):
        return pl.ds(p * CUT, CUT)

    def over_weights(k):
        cut = pl.ds(k * 4, 4)
        return remote(win.at[cut], wfull.at[x, cut], xsend.at[k], xrecv.at[k], me.near("x"))

    def over_down():
        return remote(wout, slab, xsend.at[4], xrecv.at[4], me.near("x"))

    def gather(buf, way, between):
        def put(j, p, kind, n, s):
            ref = buf.at[s, rows_of(p)]
            remote(ref, ref, gsend.at[way, j, p, n], grecv.at[way, s, p], me.near(kind)).start()

        def turn(j, carry):
            for p in range(CUTS):
                zz = me.outward(j)
                own = me.blk(zz, y, c)

                @pl.when((j > 0) & (j < 4))
                def _():
                    arrived(buf.at[own, rows_of(p)], grecv.at[way, own, p], me)

                @pl.when(j < 4)
                def _():
                    pl.when((zz <= z) & (z < NZ - 1))(lambda: put(j, p, "up", 0, own))
                    pl.when((zz >= z) & (z > 0))(lambda: put(j, p, "down", 1, own))
                    put(j, p, "y", 2, own)
                    put(j, p, "c", 3, own)

                @pl.when((j > 0) & (j < 5))
                def _():
                    i = j - 1
                    s = me.blk(me.outward(i), 1 - y, c)
                    arrived(buf.at[s, rows_of(p)], grecv.at[way, s, p], me)
                    put(i, p, "c", 4, s)

                between(j, p)
            return carry

        lax.fori_loop(0, 6, turn, 0)

        def close(j, carry):
            zz = me.outward(j)
            whole = buf.at[b, rows_of(0)]
            for p in range(CUTS):
                pl.when((zz <= z) & (z < NZ - 1))(lambda: left(whole, gsend.at[way, j, p, 0], me))
                pl.when((zz >= z) & (z > 0))(lambda: left(whole, gsend.at[way, j, p, 1], me))
                for n in (2, 3, 4):
                    left(whole, gsend.at[way, j, p, n], me)
            return carry

        lax.fori_loop(0, 4, close, 0)

    def from_core(buf, way, zz, yy):
        s = me.blk(zz, yy, 1 - c)
        for p in range(CUTS):
            arrived(buf.at[s, rows_of(p)], grecv.at[way, s, p], me)

    def to_other_core(way, q):
        remote(part.at[q * 2 + 1 - c], rc.at[q], csend.at[way, q], crecv.at[way, q], me.near("c")).start()

    def lead(way, j):
        zz = me.inward(j)
        q = zz * 2 + 1 - y
        s = q * 2 + c
        arrived(rc.at[q], crecv.at[way, q], me)
        part[s] = (part[s].astype(F32) + rc[q].astype(F32)).astype(BF)
        for p in range(CUTS):
            remote(
                part.at[s, rows_of(p)], ry.at[zz, rows_of(p)], ysend.at[way, j, p], yrecv.at[way, zz, p], me.near("y")
            ).start()

    def follow(way, j):
        zz = me.inward(j)
        q = zz * 2 + y
        s = q * 2 + c
        arrived(rc.at[q], crecv.at[way, q], me)
        for p in range(CUTS):
            cut = rows_of(p)
            arrived(ry.at[zz, cut], yrecv.at[way, zz, p], me)
            piece = acc.at[cut]
            piece[...] = part[s, cut].astype(F32) + rc[q, cut].astype(F32) + ry[zz, cut].astype(F32)
            along_z(
                me, j, zz, piece, part.at[s, cut], rz.at[:, cut], zsend.at[way, :, p], 0, zrecv.at[way, :, p]
            )

    def close_sum(way):
        def close(j, carry):
            zz = me.inward(j)
            whole, piece = part.at[b], part.at[b, rows_of(0)]
            left(whole, csend.at[way, j], me)
            left(whole, csend.at[way, j + 4], me)
            for p in range(CUTS):
                left(piece, ysend.at[way, j, p], me)
                pl.when(zz > z)(lambda: left(piece, zsend.at[way, j, p, 0], me))
                pl.when(zz < z)(lambda: left(piece, zsend.at[way, j, p, 1], me))
            return carry

        lax.fori_loop(0, 4, close, 0)

    def gelu_parts(g):
        t = jnp.tanh(GELU_A * (g + GELU_B * g * g * g))
        return t, 0.5 * g * (1.0 + t)

    def forward(q):
        rows = nall[pl.ds(q * 2, 2)].reshape(256, 1536)
        pair = jnp.dot(rows, wfull[...].reshape(1536, 768), preferred_element_type=F32)
        pairs[q] = pair
        unused, a = gelu_parts(pair[:, :384])
        scale = gate[pl.ds(q * 2, 2)].reshape(256, 1)
        zq = (a * pair[:, 384:] * scale).astype(BF)
        zg[q] = zq
        out = jnp.dot(zq, wdown[...], preferred_element_type=F32)
        part[pl.ds(q * 2, 2)] = out.astype(BF).reshape(2, 128, 1536)
        to_other_core(0, q)

    def backward(q):
        rows = dyall[pl.ds(q * 2, 2)].reshape(256, 1536)
        scale = gate[pl.ds(q * 2, 2)].reshape(256, 1)
        dz = lax.dot_general(rows, wdown[...], NT, preferred_element_type=F32) * scale
        g, u = pairs[q, :, :384], pairs[q, :, 384:]
        t, a = gelu_parts(g)
        slope = 0.5 * (1.0 + t) + 0.5 * g * (1.0 - t * t) * (GELU_A * (1.0 + 3.0 * GELU_B * g * g))
        dpairs[q, :, :384] = (dz * u * slope).astype(BF)
        dpairs[q, :, 384:] = (dz * a).astype(BF)
        out = lax.dot_general(dpairs[q], wfull[...].reshape(1536, 768), NT, preferred_element_type=F32)
        part[pl.ds(q * 2, 2)] = out.astype(BF).reshape(2, 128, 1536)
        to_other_core(1, q)

    loads[0].wait()
    pl.when(c == x)(held.wait)

    def tell_gates(k, carry):
        to = (b + k) % 16
        remote(tables.at[b], tables.at[b], tsend.at[k], trecv.at[b], (x, to)).start()
        return carry

    def with_tokens(j, p):
        if p == 0:
            pl.when((j == 0) & (c == x))(lambda: over_down().start())
            for k in range(4):
                pl.when(j == k)(over_weights(k).start)
        elif p == 1:

            @pl.when(j == 0)
            def _():
                lax.fori_loop(1, 16, tell_gates, 0)

    gather(nall, 0, with_tokens)

    def all_cores(buf, way):
        def one(j, carry):
            from_core(buf, way, j, y)
            from_core(buf, way, j, 1 - y)
            return carry

        lax.fori_loop(0, 4, one, 0)

    all_cores(nall, 0)
    def hear_gates(k, carry):
        left(tables.at[0], tsend.at[k], me)
        arrived(tables.at[(b + 16 - k) % 16], trecv.at[(b + 16 - k) % 16], me)
        return carry

    lax.fori_loop(1, 16, hear_gates, 0)

    def gate_of(s, carry):
        row = lax.broadcasted_iota(jnp.int32, (8, 128), 0)
        picked = jnp.sum(jnp.where(row == b // 2, tables[s], 0.0), axis=0, keepdims=True)
        gate[s] = as_column(picked)
        return carry

    lax.fori_loop(0, 16, gate_of, 0)
    half.wait()
    for k in range(4):
        arrived(wfull.at[1 - x, pl.ds(k * 4, 4)], xrecv.at[k], me)
    pl.when(c != x)(lambda: arrived(slab, xrecv.at[4], me))
    wide = slab[...].astype(F32).reshape(16, 2, 24, 768)
    wdown[:, :768] = wide[:, 0].reshape(384, 768).astype(BF)
    wdown[:, 768:] = wide[:, 1].reshape(384, 768).astype(BF)

    def outputs(j, carry):
        @pl.when(j < 4)
        def _():
            forward(me.inward(j) * 2 + 1 - y)

        pl.when(j > 0)(lambda: follow(0, j - 1))

        @pl.when(j < 4)
        def _():
            lead(0, j)
            forward(me.inward(j) * 2 + y)

        return carry

    lax.fori_loop(0, 5, outputs, 0)
    close_sum(0)

    keep = as_column(valid[...].astype(F32))
    loads[1].wait()
    loads[2].wait()
    done = h[...] + acc[...]
    final[...] = done.astype(BF)
    diff = done - teacher[...].astype(F32)
    scaled = (keep * (SPAN / count[0:1, 0:1])) * diff
    dy[...] = scaled
    dyall[b] = scaled.astype(BF)
    saved = [
        pltpu.make_async_copy(final, final_out, load_sem.at[0]),
        pltpu.make_async_copy(dy, dy_out, load_sem.at[1]),
    ]
    for copy in saved:
        copy.start()
    kept = jnp.sum(keep * diff * diff)
    me_index = x * 16 + b
    errs[me_index] = jnp.zeros((8, 128), F32) + kept

    def tell(k, carry):
        to = ((x + k // 16) % 2, (b + k) % 16)
        remote(errs.at[me_index], errs.at[me_index], esend.at[k], erecv.at[me_index], to).start()
        return carry

    def with_dy(j, p):
        if p == 0:

            @pl.when((j > 0) & (j < 5))
            def _():
                zz = me.outward(j - 1)
                from_core(dyall, 1, zz, y)
                backward(zz * 2 + y)

        elif p == CUTS - 1:

            @pl.when(j == 0)
            def _():
                lax.fori_loop(1, 32, tell, 0)

            @pl.when(j > 1)
            def _():
                zz = me.outward(j - 2)
                from_core(dyall, 1, zz, 1 - y)
                backward(zz * 2 + 1 - y)

    gather(dyall, 1, with_dy)

    def in_grad(i):
        col = pl.ds(pl.multiple_of(i * 256, 256), 256)
        rows = nall[:, :, col].reshape(2048, 256)
        dwin[col, :] = lax.dot_general(
            rows, dpairs[...].reshape(2048, 768), TN, preferred_element_type=F32
        ).astype(BF)

    def out_grad(i):
        col = pl.ds(i * 256, 256)
        right = dyall[:, :, col].reshape(2048, 256)
        value = lax.dot_general(zg[...].reshape(2048, 384), right, TN, preferred_element_type=F32)
        there = i // 3 * 24
        dwout[:, there : there + 24, (i % 3) * 256 : (i % 3) * 256 + 256] = value.reshape(16, 24, 256)

    def over_in(k):
        src = dwin.at[pl.ds(pl.multiple_of((1 - x) * 768 + k * 256, 256), 256)]
        return remote(src, dwin_in.at[pl.ds(k * 256, 256)], xsend.at[5 + k], xrecv.at[5 + k], me.near("x"))

    def over_out():
        return remote(slab, dwout_in, xsend.at[8], xrecv.at[8], me.near("x"))

    def leads(j, carry):
        lead(1, j)
        return carry

    lax.fori_loop(0, 4, leads, 0)

    def sums(j, carry):
        @pl.when(j == 0)
        def _():
            for k in range(3):
                in_grad((1 - x) * 3 + k)
                over_in(k).start()

        @pl.when(j == 1)
        def _():
            for k in range(6):
                out_grad(k)
            slab[...] = dwout[...].astype(BF)
            pl.when(c != x)(lambda: over_out().start())

        @pl.when(j == 2)
        def _():
            for k in range(3):
                in_grad(x * 3 + k)

        follow(1, j)
        return carry

    for k in range(4):
        over_weights(k).wait_send()
    pl.when(c == x)(lambda: over_down().wait_send())
    lax.fori_loop(0, 4, sums, 0)
    saved.append(pltpu.make_async_copy(acc, dn2_out, load_sem.at[2]))
    saved[2].start()
    close_sum(1)

    def hear(k, carry):
        left(errs.at[0], esend.at[k], me)
        s = ((x + k // 16) % 2) * 16 + (b + k) % 16
        arrived(errs.at[s], erecv.at[s], me)
        return carry

    lax.fori_loop(1, 32, hear, 0)
    total = errs[0]
    for s in range(1, 32):
        total = total + errs[s]
    err[...] = total / (1536.0 * count[...])

    for k in range(3):
        over_in(k).wait_send()
        here = pl.ds(pl.multiple_of(x * 768 + k * 256, 256), 256)
        there = pl.ds(k * 256, 256)
        arrived(dwin_in.at[there], xrecv.at[5 + k], me)
        dwin_in[there] = (dwin_in[there].astype(F32) + dwin[here, :].astype(F32)).astype(BF)
    out = pltpu.make_async_copy(dwin_in, dwin_out, own_sem.at[0])
    out.start()

    @pl.when(c == x)
    def _():
        arrived(dwout_in, xrecv.at[8], me)
        dwout_in[...] = (dwout_in[...].astype(F32) + dwout[...]).astype(BF)
        copy = pltpu.make_async_copy(dwout_in, dwout_out, own_sem.at[1])
        copy.start()
        copy.wait()

    pl.when(c != x)(lambda: over_out().wait_send())
    for copy in saved + [out]:
        copy.wait()


def run_experts(*operands):
    wide = (128, 1536)
    shard = (16,) + wide
    shape = jax.ShapeDtypeStruct
    return pl.pallas_call(
        experts_kernel,
        out_shape=(
            shape((8, 128), F32),
            shape(wide, BF),
            shape(wide, F32),
            shape(wide, F32),
            shape((768, 768), BF),
            shape((16, 48, 768), BF),
        ),
        in_specs=[VMEM] * 4 + [ANY] * 5,
        out_specs=(VMEM,) + (ANY,) * 5,
        scratch_shapes=[
            pltpu.VMEM(wide, F32),
            pltpu.VMEM(wide, BF),
            pltpu.VMEM(wide, BF),
            pltpu.VMEM(wide, F32),
            pltpu.VMEM(shard, BF),
            pltpu.VMEM(shard, BF),
            pltpu.VMEM((8, 256, 768), F32),
            pltpu.VMEM((8, 256, 384), BF),
            pltpu.VMEM((8, 256, 768), BF),
            pltpu.VMEM(shard, BF),
            pltpu.VMEM((8,) + wide, BF),
            pltpu.VMEM((4,) + wide, BF),
            pltpu.VMEM((5,) + wide, BF),
            pltpu.VMEM(wide, F32),
            pltpu.VMEM((32, 8, 128), F32),
            pltpu.VMEM((16, 8, 128), F32),
            pltpu.VMEM((16, 128, 1), F32),
            pltpu.VMEM((2, 16, 48, 768), BF),
            pltpu.VMEM((16, 48, 768), BF),
            pltpu.VMEM((384, 1536), BF),
            pltpu.VMEM((1536, 768), BF),
            pltpu.VMEM((768, 768), BF),
            pltpu.VMEM((16, 48, 768), F32),
            pltpu.VMEM((16, 48, 768), BF),
            DMA((3,)),
            DMA((2,)),
            DMA((2, 4, CUTS, 5)),
            DMA((2, 16, CUTS)),
            DMA((2, 8)),
            DMA((2, 8)),
            DMA((2, 4, CUTS)),
            DMA((2, 4, CUTS)),
            DMA((2, 4, CUTS, 2)),
            DMA((2, 5, CUTS)),
            DMA((32,)),
            DMA((32,)),
            DMA((16,)),
            DMA((16,)),
            DMA((9,)),
            DMA((9,)),
        ],
        compiler_params=params(2, 62),
        name="experts",
    )(*operands)


def norm_back(values, gain, grad):
    scale = lax.rsqrt(jnp.mean(values * values, axis=-1, keepdims=True) + 1e-06)
    inner = grad * gain
    mean = jnp.mean(inner * values, axis=-1, keepdims=True)
    return scale * inner - values * (scale * scale * scale * mean), jnp.sum(
        grad * values * scale, axis=0, keepdims=True
    )


Q_PIECES = ((0, 768), (768, 768))
LAST = (1536, 640)


def back_kernel(
    doc, freq, states_in, h_in, n1_in, qs_in, o_in, lse_in, dn2_in, dy_in, dwin, dwout, gq, go, kv_in,
    gx_out, gqw, gkw, gvw, gnorm, gout_out, gup, gdown,
    states, h, n1, qs, o, lse, dn2, dy, gx, gout, gkv,
    wq, wo, kv, pk, pw, dos, delta, dh, dq, dkv, dqkv, gqkv, *rest,
):
    sums = [(rest[i * 11 : i * 11 + 6], rest[i * 11 + 6 : i * 11 + 11]) for i in range(5)]
    load_sem, own_sem, asend, arecv, osend, orecv = rest[55:]
    me = Place()
    x, y, z, b, c = me.x, me.y, me.z, me.b, me.c
    loads = [
        pltpu.make_async_copy(go, wo, own_sem.at[0]),
        pltpu.make_async_copy(kv_in, kv, own_sem.at[1]),
        pltpu.make_async_copy(gq, wq, own_sem.at[2]),
    ]
    small = [
        pltpu.make_async_copy(src, dst, load_sem.at[i])
        for i, (src, dst) in enumerate(
            (
                (h_in, h), (dn2_in, dn2), (dy_in, dy), (o_in, o), (qs_in, qs), (lse_in, lse),
                (n1_in, n1), (states_in, states),
            )
        )
    ]
    for load in [loads[2]] + small[:3] + loads[:2] + small[3:]:
        load.start()
    greet_all(me)

    def own_piece(n):
        col = pl.multiple_of(n * 768 + c * 384, 128)
        return pltpu.make_async_copy(
            dwin.at[b, :, pl.ds(n * 384, 384)], gup.at[b // 2, :, pl.ds(col, 384)], own_sem.at[3 + n]
        )

    def own_down():
        return pltpu.make_async_copy(dwout.at[b], gdown.at[b // 2], own_sem.at[5])

    def deal(k, carry):
        t = (b + k) % 16
        for n in range(2):
            col = pl.multiple_of(n * 768 + c * 384, 128)
            remote(
                dwin.at[t, :, pl.ds(n * 384, 384)],
                gup.at[b // 2, :, pl.ds(col, 384)],
                asend.at[k, n],
                arecv.at[b, n],
                (x, t),
            ).start()
        pl.when(c == x)(
            lambda: remote(dwout.at[t], gdown.at[b // 2], osend.at[k], orecv.at[b // 2], (x, t)).start()
        )
        return carry

    for n in range(2):
        own_piece(n).start()
    pl.when(c == x)(lambda: own_down().start())
    loads[2].wait()
    for load in small[:3]:
        load.wait()
    gains = wq[:, :, pl.ds(QKV, 128)].reshape(1536, 128).astype(F32).T
    res_grad, gain_two = norm_back(h[...], gains[1:2], dn2[...])
    dh[...] = dy[...] + res_grad
    da = dh[...].astype(BF)
    loads[0].wait()
    do = lax.dot_general(
        da, wo[...].reshape(1536, 1536), NT, preferred_element_type=F32
    ).astype(BF)
    small[3].wait()
    low = o[...].astype(BF)
    for i in range(4):
        part = lax.dot_general(low[:, i * 384 : i * 384 + 384], da, TN, preferred_element_type=F32)
        wo[i * 8 : i * 8 + 8] = part.astype(BF).reshape(8, 48, 1536)
    out_sum = Sum(me, wo, by_weight, gout, *sums[0])
    key_sum = Sum(me, pk, by_token, dkv, *sums[1], causal=True)

    def lead_all(which):
        def one(j, carry):
            which.lead(j)
            return carry

        lax.fori_loop(0, 4, one, 0)

    lead_all(out_sum)
    for i in range(QUERY_HEADS):
        col, r = i * 128, (i % GROUP) * 128
        dos[i // GROUP, r : r + 128] = do[:, col : col + 128]
        prod = do[:, col : col + 128].astype(F32) * o[:, col : col + 128]
        delta[i // GROUP, :, r : r + 128] = jnp.sum(prod.T, axis=0, keepdims=True)
    dq[...] = jnp.zeros_like(dq)
    bounds = query_bounds(me, doc)
    loads[1].wait()
    for load in small[4:6]:
        load.wait()

    def block(n):
        ok = allowed_keys(n * 256, bounds)
        for i in range(2):
            k = kv[pl.ds(n * 2, 2), :, i * 128 : i * 128 + 128].reshape(256, 128)
            v = kv[pl.ds(n * 2, 2), :, 256 + i * 128 : 384 + i * 128].reshape(256, 128)
            s = lax.dot_general(k, qs[i], NT, preferred_element_type=F32)
            p = jnp.where(ok, jnp.exp2(s * POWER - lse[i]), 0.0)
            dp = lax.dot_general(v, dos[i], NT, preferred_element_type=F32)
            ds = (p * (dp - delta[i])).astype(BF)
            dv = jnp.dot(p.astype(BF), dos[i], preferred_element_type=F32)
            dk = jnp.dot(ds, qs[i], preferred_element_type=F32) * SCALE
            pk[pl.ds(n * 2, 2), :, i * 128 : i * 128 + 128] = dk.astype(BF).reshape(2, 128, 128)
            pk[pl.ds(n * 2, 2), :, 256 + i * 128 : 384 + i * 128] = dv.astype(BF).reshape(2, 128, 128)
            dq[i] += lax.dot_general(k, ds, TN, preferred_element_type=F32)

    def turn(j, carry):
        out_sum.turn(j)
        lax.fori_loop(1 + j * 4, jnp.minimum(5 + j * 4, 16), deal, 0)

        @pl.when(key_sum.valid(j))
        def _():
            last = jnp.where(j == z, y * 2 + c, 3)

            def one(n, carry):
                block(j * 4 + n)
                return carry

            lax.fori_loop(0, last + 1, one, 0)

            def blank(n, carry):
                pk[pl.ds((j * 4 + n) * 2, 2)] = jnp.zeros((2, 128, 512), BF)
                return carry

            lax.fori_loop(last + 1, 4, blank, 0)
            key_sum.lead(j)

        key_sum.turn(j)
        return carry

    lax.fori_loop(0, 4, turn, 0)

    cos, sin = rotary_tables(me, doc, freq)
    for load in small[6:]:
        load.wait()
    for i in range(QUERY_HEADS):
        r = (i % GROUP) * 128
        head = dq[i // GROUP, :, r : r + 128].T * SCALE
        dqkv[:, i * 128 : i * 128 + 128] = turned(head, cos, -sin).astype(BF)

    def weight_grad(start, width):
        for i in range(4):
            part = lax.dot_general(
                n1[:, i * 384 : i * 384 + 384], dqkv[:, start : start + width], TN, preferred_element_type=F32
            )
            pw[i * 8 : i * 8 + 8, :, start : start + width] = part.astype(BF).reshape(8, 48, width)

    weight_grad(0, 1536)
    proj = [Sum(me, pw, by_weight, gqkv, *sums[2 + i], Q_PIECES[i]) for i in range(2)]
    rest_sum = Sum(me, pw, by_weight, gqkv, *sums[4], LAST)
    for piece in proj:
        lead_all(piece)

    def last_turn(j, carry):
        for piece in proj:
            piece.turn(j)
        out_sum.turn(j + 4)
        pl.when(j < 2)(lambda: key_sum.turn(j + 4))

        @pl.when(j == 1)
        def _():
            for i in range(2):
                part = dkv[:, i * 128 : i * 128 + 128]
                dqkv[:, 1536 + i * 128 : 1664 + i * 128] = turned(part, cos, -sin).astype(BF)
            dqkv[:, 1792:2048] = dkv[:, 256:512].astype(BF)
            weight_grad(1536, 512)
            dn1 = lax.dot_general(
                dqkv[...], wq[:, :, pl.ds(0, QKV)].reshape(1536, QKV), NT, preferred_element_type=F32
            )
            in_grad, gain_one = norm_back(states[...].astype(F32), gains[0:1], dn1)
            rows = lax.broadcasted_iota(jnp.int32, (128, 1536), 0)
            tail = jnp.where(rows == 0, gain_one, jnp.where(rows == 1, gain_two, 0.0)).T
            pw[:, :, pl.ds(QKV, 128)] = tail.astype(BF).reshape(32, 48, 128)
            lead_all(rest_sum)
            gx[...] = dh[...] + in_grad

        rest_sum.turn(j - 2)
        return carry

    lax.fori_loop(0, 8, last_turn, 0)
    gkv[...] = gqkv[:, 1536:2048]
    stores = [
        pltpu.make_async_copy(gx, gx_out, load_sem.at[0]),
        pltpu.make_async_copy(gout, gout_out, load_sem.at[1]),
        pltpu.make_async_copy(gqkv.at[:, pl.ds(0, 1536)], gqw, load_sem.at[2]),
        pltpu.make_async_copy(gkv.at[:, pl.ds(0, 256)], gkw, load_sem.at[3]),
        pltpu.make_async_copy(gkv.at[:, pl.ds(256, 256)], gvw, load_sem.at[4]),
    ]
    for store in stores:
        store.start()
    gnorm[0:1, :] = as_row(gqkv[:, 2048:2049])
    gnorm[1:2, :] = as_row(gqkv[:, 2049:2050])
    out_sum.close()
    key_sum.close()
    rest_sum.close()
    for piece in proj:
        piece.close()

    def close(k, carry):
        f = (b + 16 - k) % 16
        for n in range(2):
            left(dwin.at[0, :, pl.ds(0, 384)], asend.at[k, n], me)
            col = pl.multiple_of(n * 768 + (f % 2) * 384, 128)
            arrived(gup.at[f // 2, :, pl.ds(col, 384)], arecv.at[f, n], me)
        pl.when(c == x)(lambda: left(dwout.at[0], osend.at[k], me))
        pl.when(f % 2 == x)(lambda: arrived(gdown.at[f // 2], orecv.at[f // 2], me))
        return carry

    lax.fori_loop(1, 16, close, 0)
    for n in range(2):
        own_piece(n).wait()
    pl.when(c == x)(lambda: own_down().wait())
    for store in stores:
        store.wait()


def run_back(*operands):
    shape = jax.ShapeDtypeStruct
    smem = pl.BlockSpec(memory_space=pltpu.SMEM)
    return pl.pallas_call(
        back_kernel,
        out_shape=(
            shape((128, 1536), F32),
            shape((48, 1536), F32),
            shape((48, 256), F32),
            shape((48, 256), F32),
            shape((2, 48), F32),
            shape((48, 1536), F32),
            shape((8, 48, 1536), BF),
            shape((8, 48, 768), BF),
        ),
        in_specs=[smem, VMEM] + [ANY] * 13,
        out_specs=(ANY,) * 4 + (VMEM,) + (ANY,) * 3,
        scratch_shapes=[
            pltpu.VMEM((128, 1536), BF),
            pltpu.VMEM((128, 1536), F32),
            pltpu.VMEM((128, 1536), BF),
            pltpu.VMEM((2, LANES, 128), BF),
            pltpu.VMEM((128, 1536), F32),
            pltpu.VMEM((2, 1, LANES), F32),
            pltpu.VMEM((128, 1536), F32),
            pltpu.VMEM((128, 1536), F32),
            pltpu.VMEM((128, 1536), F32),
            pltpu.VMEM((48, 1536), F32),
            pltpu.VMEM((48, 512), F32),
            pltpu.VMEM((32, 48, WIDE), BF),
            pltpu.VMEM((32, 48, 1536), BF),
            pltpu.VMEM((32, 128, 512), BF),
            pltpu.VMEM((32, 128, 512), BF),
            pltpu.VMEM((32, 48, WIDE), BF),
            pltpu.VMEM((2, LANES, 128), BF),
            pltpu.VMEM((2, 1, LANES), F32),
            pltpu.VMEM((128, 1536), F32),
            pltpu.VMEM((2, 128, LANES), F32),
            pltpu.VMEM((128, 512), F32),
            pltpu.VMEM((128, QKV), BF),
            pltpu.VMEM((48, WIDE), F32),
        ]
        + Sum.room(48, 1536)
        + Sum.room(128, 512)
        + Sum.room(48, 768)
        + Sum.room(48, 768)
        + Sum.room(48, LAST[1])
        + [DMA((8,)), DMA((6,)), DMA((16, 2)), DMA((16, 2)), DMA((16,)), DMA((8,))],
        compiler_params=params(3, 62),
        name="back",
    )(*operands)


def finish_kernel(
    err, gnorm, final, gx, gqw, gkw, gvw, gout, gup, gdown,
    loss, one, two, final_out, gx_out, gqw_out, gkw_out, gvw_out, gout_out, gup_out, gdown_out,
    low_up, low_down, wide_up, wide_down, *rest,
):
    rooms, sem, out_sem = rest[:6], rest[6], rest[7]
    whole = ((gup, low_up), (gdown, low_down), *zip((final, gx, gqw, gkw, gvw, gout), rooms))
    copies = [pltpu.make_async_copy(src, dst, sem.at[i]) for i, (src, dst) in enumerate(whole)]
    for copy in copies:
        copy.start()
    loss[...] = err[0:1, 0:1]
    one[...] = gnorm[0:1, :]
    two[...] = gnorm[1:2, :]
    outs = (final_out, gx_out, gqw_out, gkw_out, gvw_out, gout_out)
    last = []
    for i in range(6):
        copies[2 + i].wait()
        last.append(pltpu.make_async_copy(rooms[i], outs[i], out_sem.at[i]))
        last[i].start()
    copies[0].wait()
    wide_up[...] = low_up[...].astype(F32)
    last.append(pltpu.make_async_copy(wide_up, gup_out, out_sem.at[6]))
    last[6].start()
    copies[1].wait()
    for e in range(E):
        wide = low_down[e].astype(F32)
        wide_down[e, :, :768] = wide[:24]
        wide_down[e, :, 768:] = wide[24:]
    last.append(pltpu.make_async_copy(wide_down, gdown_out, out_sem.at[7]))
    last[7].start()
    for copy in last:
        copy.wait()


def run_finish(*operands):
    shape = jax.ShapeDtypeStruct
    up, down = (8, 48, 1536), (8, 24, 1536)
    return pl.pallas_call(
        finish_kernel,
        out_shape=(
            shape((1, 1), F32),
            shape((1, 48), F32),
            shape((1, 48), F32),
            shape((128, 1536), BF),
            shape((128, 1536), F32),
            shape((48, 1536), F32),
            shape((48, 256), F32),
            shape((48, 256), F32),
            shape((48, 1536), F32),
            shape(up, F32),
            shape(down, F32),
        ),
        in_specs=[VMEM] * 2 + [ANY] * 8,
        out_specs=(VMEM,) * 3 + (ANY,) * 8,
        scratch_shapes=[
            pltpu.VMEM(up, BF),
            pltpu.VMEM((8, 48, 768), BF),
            pltpu.VMEM(up, F32),
            pltpu.VMEM(down, F32),
            pltpu.VMEM((128, 1536), BF),
            pltpu.VMEM((128, 1536), F32),
            pltpu.VMEM((48, 1536), F32),
            pltpu.VMEM((48, 256), F32),
            pltpu.VMEM((48, 256), F32),
            pltpu.VMEM((48, 1536), F32),
            DMA((8,)),
            DMA((8,)),
        ],
        compiler_params=pltpu.CompilerParams(vmem_limit_bytes=60 << 20),
        name="finish",
    )(*operands)


def per_device(
    states, teacher, valid, routes, gates, doc_starts, norm_one,
    w_query, key_weight, value_weight, w_output, norm_two, expert_in, expert_out,
):
    tokens = states.shape[2]
    width = states.shape[3]
    half = HEAD_SIZE // 2
    freq = np.float32(ROTARY_BASE) ** (-np.arange(half).astype(np.float32) / np.float32(half))
    freq = jnp.asarray(np.concatenate([freq, freq])[None, :], F32)
    rows = states.reshape(tokens, width)
    kept = valid.reshape(1, tokens)
    gq, go, kv, win, wout, h, n2, n1, qs, o, lse, count = run_front(
        doc_starts, freq, norm_one.reshape(1, -1), norm_two.reshape(1, -1), kept, rows, expert_out,
        w_query, key_weight, value_weight, w_output, expert_in,
    )
    error, final, dn2, dy, dwin, dwout = run_experts(
        routes.reshape(tokens, TOP).T, gates.reshape(tokens, TOP).T, kept, count,
        n2, h, teacher.reshape(tokens, width), win, wout,
    )
    gx, gqw, gkw, gvw, gnorm, gout, gup, gdown = run_back(
        doc_starts, freq, rows, h, n1, qs, o, lse, dn2, dy, dwin.reshape(16, 48, 768), dwout, gq, go, kv
    )
    loss, one, two, final, gx, gqw, gkw, gvw, gout, gup, gdown = run_finish(
        error, gnorm, final, gx, gqw, gkw, gvw, gout, gup, gdown
    )
    shape = states.shape
    return (
        final.reshape(shape),
        loss.reshape(()),
        gx.reshape(shape),
        one.reshape(-1),
        gqw,
        gkw,
        gvw,
        gout,
        two.reshape(-1),
        gup,
        gdown,
    )


def solution(mesh):
    in_specs = (
        P("blk", "head", None, None),
        P("blk", "head", None, None),
        P("blk", "head", None),
        P("blk", "head", None, None),
        P("blk", "head", None, None),
        P(),
        P(("head", "blk")),
        P(("head", "blk"), None),
        P(("head", "blk"), None),
        P(("head", "blk"), None),
        P(("head", "blk"), None),
        P(("head", "blk")),
        P(None, ("head", "blk"), None),
        P(None, ("head", "blk"), None),
    )
    out_specs = (
        P("blk", "head", None, None),
        P(),
        P("blk", "head", None, None),
        P(("head", "blk")),
        P(("head", "blk"), None),
        P(("head", "blk"), None),
        P(("head", "blk"), None),
        P(("head", "blk"), None),
        P(("head", "blk")),
        P(None, ("head", "blk"), None),
        P(None, ("head", "blk"), None),
    )
    sizes = dict(mesh.shape)
    plan = per_device if sizes == {"head": 2, "blk": 4 * NZ} else per_device_plain
    return jax.shard_map(
        plan, mesh=mesh, in_specs=in_specs, out_specs=out_specs, check_vma=False
    )
```

```python
import functools

import jax
import jax.numpy as jnp
import numpy as np
from jax import lax
from jax.experimental import pallas as pl
from jax.experimental.pallas import tpu as pltpu
from jax.sharding import PartitionSpec as P

QUERY_HEADS = 12
KEY_VALUE_HEADS = 2
HEAD_SIZE = 128
TOP = 4
E = 8
CAP = 96

ROTARY_BASE = 10000.0
FLOOR_SCORE = -1e30

MESH = pl.DeviceIdType.MESH
NZ = 4
SPAN = 32 * 128.0
BF = jnp.bfloat16
F32 = jnp.float32

def product(left, right):
    return jnp.dot(left, right, preferred_element_type=jnp.float32)


def rms_norm(values, gain):
    scale = lax.rsqrt(jnp.mean(values * values, axis=-1, keepdims=True) + 1e-06)
    return values * scale * gain


def rotary_apply(values, where, sign):
    half = values.shape[-1] // 2
    freq = ROTARY_BASE ** (-jnp.arange(half).astype(jnp.float32) / half)
    angle = where.astype(jnp.float32)[:, None] * freq[None, :]
    cosine = jnp.cos(angle)[:, None, :]
    sine = jnp.sin(angle)[:, None, :] * sign
    first = values[..., :half]
    second = values[..., half:]
    return jnp.concatenate(
        [first * cosine - second * sine, second * cosine + first * sine], axis=-1
    )


def doc_layout(position_index, doc_starts):
    inside = (position_index[:, None] >= doc_starts[None, :]).astype(jnp.int32)
    document_segment = jnp.sum(inside, axis=-1) - 1
    begin = jnp.max(jnp.where(inside > 0, doc_starts[None, :], 0), axis=-1)
    return (document_segment, position_index - begin)


def gated(pair):
    half = pair.shape[-1] // 2
    return jax.nn.gelu(pair[..., :half], approximate=True) * pair[..., half:]


def in_blocks(step_fn, carry, piece, rows):
    count_blocks = piece[0].shape[0] // rows

    def turn(number, state):
        part = tuple((lax.dynamic_slice_in_dim(item, number * rows, rows, 0) for item in piece))
        return step_fn(state, part, number * rows)

    return lax.fori_loop(0, count_blocks, turn, carry)


def per_device_plain(
    states,
    teacher,
    valid,
    routes,
    gates,
    doc_starts,
    norm_one,
    w_query,
    key_weight,
    value_weight,
    w_output,
    norm_two,
    expert_in,
    expert_out,
):
    count_per_token = states.shape[2]
    width = states.shape[3]
    pairs = lax.axis_size("head")
    blocks = lax.axis_size("blk")
    rows = count_per_token * pairs
    span = rows * blocks
    head_group = QUERY_HEADS // KEY_VALUE_HEADS
    scale = HEAD_SIZE ** (-0.5)
    highest = lax.Precision.HIGHEST
    block_index = lax.axis_index("blk")
    pair_index = lax.axis_index("head")
    token_index = (block_index * pairs + pair_index) * count_per_token + jnp.arange(
        count_per_token, dtype=jnp.int32
    )
    unused_segment, token_position = doc_layout(token_index, doc_starts)
    query_index = block_index * rows + jnp.arange(rows, dtype=jnp.int32)
    query_segment, query_where = doc_layout(query_index, doc_starts)
    last_query = block_index * rows + rows - 1
    inputs = states.reshape(count_per_token, width).astype(jnp.float32)
    target = teacher.reshape(count_per_token, width).astype(jnp.float32)
    keep_mask = valid.reshape(count_per_token).astype(jnp.float32)
    route_rows = routes.reshape(count_per_token, TOP)
    gate_rows = gates.reshape(count_per_token, TOP)
    query_w, key_w, value_w, out_w, gain_low_one, gain_low_two = (
        lax.all_gather(w_query, ("head", "blk"), axis=0, tiled=True),
        lax.all_gather(key_weight, ("head", "blk"), axis=0, tiled=True),
        lax.all_gather(value_weight, ("head", "blk"), axis=0, tiled=True),
        lax.all_gather(w_output, ("head", "blk"), axis=0, tiled=True),
        lax.all_gather(norm_one, ("head", "blk"), axis=0, tiled=True),
        lax.all_gather(norm_two, ("head", "blk"), axis=0, tiled=True),
    )
    gain_one = gain_low_one.astype(jnp.float32)
    gain_two = gain_low_two.astype(jnp.float32)
    normed_one = rms_norm(inputs, gain_one)
    normed_low = normed_one.astype(jnp.bfloat16)
    query_lin = product(normed_low, query_w)
    key_linear = product(normed_low, key_w)
    value_linear = product(normed_low, value_w)
    query_rotated = rotary_apply(
        query_lin.reshape(count_per_token, QUERY_HEADS, HEAD_SIZE), token_position, 1.0
    )
    key_rotated = rotary_apply(
        key_linear.reshape(count_per_token, KEY_VALUE_HEADS, HEAD_SIZE), token_position, 1.0
    )
    query_outgoing = query_rotated.astype(jnp.bfloat16).reshape(
        count_per_token, KEY_VALUE_HEADS, head_group * HEAD_SIZE
    )
    key_send = key_rotated.astype(jnp.bfloat16)
    value_outgoing = value_linear.astype(jnp.bfloat16).reshape(
        count_per_token, KEY_VALUE_HEADS, HEAD_SIZE
    )
    query_grp, key_grp, value_grp = (
        lax.all_to_all(query_outgoing, "head", split_axis=1, concat_axis=0, tiled=True),
        lax.all_to_all(key_send, "head", split_axis=1, concat_axis=0, tiled=True),
        lax.all_to_all(value_outgoing, "head", split_axis=1, concat_axis=0, tiled=True),
    )
    query_heads = query_grp.reshape(rows, head_group, HEAD_SIZE)
    key_rows = key_grp.reshape(rows, HEAD_SIZE)
    value_rows = value_grp.reshape(rows, HEAD_SIZE)

    def scores_for(keys, start):
        block_size = keys.shape[0]
        key_index = start + jnp.arange(block_size, dtype=jnp.int32)
        key_segment, unused_where = doc_layout(key_index, doc_starts)
        allowed = (key_index[None, :] <= query_index[:, None]) & (
            key_segment[None, :] == query_segment[:, None]
        )
        raw = (
            jnp.einsum("qhd,kd->hqk", query_heads, keys, preferred_element_type=jnp.float32) * scale
        )
        return (raw, allowed[None])

    def attend(carry, piece, start):
        keys, values = piece

        def work(state):
            running, total, accum = state
            raw, allowed = scores_for(keys, start)
            masked = jnp.where(allowed, raw, FLOOR_SCORE)
            newest = jnp.maximum(running, jnp.max(masked, axis=-1))
            factor = jnp.exp(running - newest)
            weights = jnp.where(allowed, jnp.exp(masked - newest[..., None]), 0.0)
            total = total * factor + jnp.sum(weights, axis=-1)
            update = jnp.einsum(
                "hqk,kd->qhd",
                weights.astype(jnp.bfloat16),
                values,
                preferred_element_type=jnp.float32,
            )
            accum = accum * factor.T[:, :, None] + update
            return (newest, total, accum)

        return lax.cond(start <= last_query, work, lambda state: state, carry)

    start_state = (
        jnp.full((head_group, rows), FLOOR_SCORE, jnp.float32),
        jnp.zeros((head_group, rows), jnp.float32),
        jnp.zeros((rows, head_group, HEAD_SIZE), jnp.float32),
    )
    running, total, accum = in_blocks(
        attend,
        start_state,
        (
            lax.all_gather(key_rows, "blk", axis=0, tiled=True),
            lax.all_gather(value_rows, "blk", axis=0, tiled=True),
        ),
        rows,
    )
    attn_full = accum / total.T[:, :, None]
    log_total = running + jnp.log(total)
    out_send = attn_full.astype(jnp.bfloat16).reshape(rows, 1, head_group * HEAD_SIZE)
    out_tok = lax.all_to_all(out_send, "head", split_axis=0, concat_axis=1, tiled=True).reshape(
        count_per_token, QUERY_HEADS * HEAD_SIZE
    )
    residual = inputs + product(out_tok, out_w)
    normed_two = rms_norm(residual, gain_two)
    normed_two_low = normed_two.astype(jnp.bfloat16)
    up_w, down_w = (
        lax.all_gather(expert_in, ("head", "blk"), axis=1, tiled=True),
        lax.all_gather(expert_out, ("head", "blk"), axis=1, tiled=True),
    )
    route_hot = (route_rows[:, :, None] == jnp.arange(E, dtype=jnp.int32)[None, None, :]).astype(
        jnp.int32
    )
    flat_hot = route_hot.reshape(count_per_token * TOP, E)
    before = jnp.cumsum(flat_hot, axis=0) - flat_hot
    slot = jnp.sum(before * flat_hot, axis=-1).reshape(count_per_token, TOP)
    slot_hot = (slot[:, :, None] == jnp.arange(CAP, dtype=jnp.int32)[None, None, :]).astype(
        jnp.float32
    )
    route_float = route_hot.astype(jnp.float32)
    dispatch = jnp.einsum("tje,tjc->ect", route_float, slot_hot, precision=highest)
    combine = jnp.einsum("tje,tjc,tj->ect", route_float, slot_hot, gate_rows, precision=highest)
    expert_rows = jnp.einsum(
        "ect,td->ecd",
        dispatch.astype(jnp.bfloat16),
        normed_two_low,
        preferred_element_type=jnp.float32,
    ).astype(jnp.bfloat16)
    pair = jnp.einsum("ecd,edf->ecf", expert_rows, up_w, preferred_element_type=jnp.float32)
    hidden_low = gated(pair).astype(jnp.bfloat16)
    expert_result = jnp.einsum(
        "ecf,efd->ecd", hidden_low, down_w, preferred_element_type=jnp.float32
    )
    mixture = jnp.einsum("ect,ecd->td", combine, expert_result, precision=highest)
    final = residual + mixture
    diff = final - target
    local_count = jnp.sum(keep_mask)
    local_error = jnp.sum(keep_mask * jnp.sum(diff * diff, axis=-1))
    count_all, error_all = lax.psum((local_count, local_error), ("head", "blk"))
    loss = error_all / (width * count_all)
    grad_final = keep_mask[:, None] * diff * (span * 1.0 / count_all)
    up_back, down_back = (
        lax.all_gather(expert_in, ("head", "blk"), axis=1, tiled=True),
        lax.all_gather(expert_out, ("head", "blk"), axis=1, tiled=True),
    )
    grad_result = jnp.einsum("ect,td->ecd", combine, grad_final, precision=highest).astype(
        jnp.bfloat16
    )
    grad_down = jnp.einsum(
        "ecf,ecd->efd", hidden_low, grad_result, preferred_element_type=jnp.float32
    )
    grad_hidden = jnp.einsum(
        "ecd,efd->ecf", grad_result, down_back, preferred_element_type=jnp.float32
    )
    unused_value, pull_gate = jax.vjp(gated, pair)
    grad_pair = pull_gate(grad_hidden)[0].astype(jnp.bfloat16)
    grad_up = jnp.einsum("ecd,ecf->edf", expert_rows, grad_pair, preferred_element_type=jnp.float32)
    grad_rows = jnp.einsum("ecf,edf->ecd", grad_pair, up_back, preferred_element_type=jnp.float32)
    grad_normed_two = jnp.einsum("ect,ecd->td", dispatch, grad_rows, precision=highest)
    unused_value, pull_two = jax.vjp(rms_norm, residual, gain_two)
    grad_res_norm, grad_gain_two = pull_two(grad_normed_two)
    grad_residual = grad_final + grad_res_norm
    grad_attn_low = grad_residual.astype(jnp.bfloat16)
    grad_out_w = jnp.einsum("tk,td->kd", out_tok, grad_attn_low, preferred_element_type=jnp.float32)
    output_gradient_token = jnp.einsum(
        "td,kd->tk", grad_attn_low, out_w, preferred_element_type=jnp.float32
    ).astype(jnp.bfloat16)
    grad_out_grp = lax.all_to_all(
        output_gradient_token.reshape(count_per_token, KEY_VALUE_HEADS, head_group * HEAD_SIZE),
        "head",
        split_axis=1,
        concat_axis=0,
        tiled=True,
    ).reshape(rows, head_group, HEAD_SIZE)
    delta = jnp.einsum(
        "qhd,qhd->hq", grad_out_grp.astype(jnp.float32), attn_full, precision=highest
    )

    def attend_back(carry, piece, start):
        keys, values = piece

        def work(state):
            grad_query, grad_keys, grad_values = state
            raw, allowed = scores_for(keys, start)
            weights = jnp.where(allowed, jnp.exp(raw - log_total[..., None]), 0.0)
            grad_weights = jnp.einsum(
                "qhd,kd->hqk", grad_out_grp, values, preferred_element_type=jnp.float32
            )
            grad_raw = (weights * (grad_weights - delta[..., None])).astype(jnp.bfloat16)
            grad_query = (
                grad_query
                + jnp.einsum("hqk,kd->qhd", grad_raw, keys, preferred_element_type=jnp.float32)
                * scale
            )
            key_part = (
                jnp.einsum("hqk,qhd->kd", grad_raw, query_heads, preferred_element_type=jnp.float32)
                * scale
            )
            value_part = jnp.einsum(
                "hqk,qhd->kd",
                weights.astype(jnp.bfloat16),
                grad_out_grp,
                preferred_element_type=jnp.float32,
            )
            block_size = keys.shape[0]
            grad_keys = lax.dynamic_update_slice_in_dim(
                grad_keys,
                lax.dynamic_slice_in_dim(grad_keys, start, block_size, 0) + key_part,
                start,
                0,
            )
            grad_values = lax.dynamic_update_slice_in_dim(
                grad_values,
                lax.dynamic_slice_in_dim(grad_values, start, block_size, 0) + value_part,
                start,
                0,
            )
            return (grad_query, grad_keys, grad_values)

        return lax.cond(start <= last_query, work, lambda state: state, carry)

    back_state = (
        jnp.zeros((rows, head_group, HEAD_SIZE), jnp.float32),
        jnp.zeros((span, HEAD_SIZE), jnp.float32),
        jnp.zeros((span, HEAD_SIZE), jnp.float32),
    )
    grad_query, grad_keys_full, grad_values_full = in_blocks(
        attend_back,
        back_state,
        (
            lax.all_gather(key_rows, "blk", axis=0, tiled=True),
            lax.all_gather(value_rows, "blk", axis=0, tiled=True),
        ),
        rows,
    )
    grad_keys, grad_values = (
        lax.psum_scatter(grad_keys_full, "blk", scatter_dimension=0, tiled=True),
        lax.psum_scatter(grad_values_full, "blk", scatter_dimension=0, tiled=True),
    )
    grad_query_lin = (
        rotary_apply(grad_query, query_where, -1.0)
        .astype(jnp.bfloat16)
        .reshape(rows, 1, head_group * HEAD_SIZE)
    )
    grad_key_lin = rotary_apply(grad_keys.reshape(rows, 1, HEAD_SIZE), query_where, -1.0).astype(
        jnp.bfloat16
    )
    grad_value_lin = grad_values.astype(jnp.bfloat16).reshape(rows, 1, HEAD_SIZE)
    back_query, key_backward, value_backward = (
        lax.all_to_all(grad_query_lin, "head", split_axis=0, concat_axis=1, tiled=True),
        lax.all_to_all(grad_key_lin, "head", split_axis=0, concat_axis=1, tiled=True),
        lax.all_to_all(grad_value_lin, "head", split_axis=0, concat_axis=1, tiled=True),
    )
    back_query = back_query.reshape(count_per_token, QUERY_HEADS * HEAD_SIZE)
    key_backward = key_backward.reshape(count_per_token, KEY_VALUE_HEADS * HEAD_SIZE)
    value_backward = value_backward.reshape(count_per_token, KEY_VALUE_HEADS * HEAD_SIZE)
    grad_query_w = jnp.einsum(
        "td,tk->dk", normed_low, back_query, preferred_element_type=jnp.float32
    )
    grad_key_w = jnp.einsum(
        "td,tk->dk", normed_low, key_backward, preferred_element_type=jnp.float32
    )
    grad_value_w = jnp.einsum(
        "td,tk->dk", normed_low, value_backward, preferred_element_type=jnp.float32
    )
    grad_normed_one = jnp.einsum(
        "tk,dk->td", back_query, query_w, preferred_element_type=jnp.float32
    )
    grad_normed_one = grad_normed_one + jnp.einsum(
        "tk,dk->td", key_backward, key_w, preferred_element_type=jnp.float32
    )
    grad_normed_one = grad_normed_one + jnp.einsum(
        "tk,dk->td", value_backward, value_w, preferred_element_type=jnp.float32
    )
    unused_value, pull_one = jax.vjp(rms_norm, inputs, gain_one)
    grad_in_norm, grad_gain_one = pull_one(grad_normed_one)
    grad_inputs = grad_residual + grad_in_norm
    sums = (
        lax.psum_scatter(grad_query_w, ("head", "blk"), scatter_dimension=0, tiled=True),
        lax.psum_scatter(grad_key_w, ("head", "blk"), scatter_dimension=0, tiled=True),
        lax.psum_scatter(grad_value_w, ("head", "blk"), scatter_dimension=0, tiled=True),
        lax.psum_scatter(grad_out_w, ("head", "blk"), scatter_dimension=0, tiled=True),
        lax.psum_scatter(grad_gain_one, ("head", "blk"), scatter_dimension=0, tiled=True),
        lax.psum_scatter(grad_gain_two, ("head", "blk"), scatter_dimension=0, tiled=True),
        lax.psum_scatter(grad_up, ("head", "blk"), scatter_dimension=1, tiled=True),
        lax.psum_scatter(grad_down, ("head", "blk"), scatter_dimension=1, tiled=True),
    )
    shape = states.shape
    return (
        final.astype(jnp.bfloat16).reshape(shape),
        loss,
        grad_inputs.reshape(shape),
        sums[4],
        sums[0],
        sums[1],
        sums[2],
        sums[3],
        sums[5],
        sums[6],
        sums[7],
    )


class Place:
    def __init__(self):
        self.x = lax.axis_index("head")
        self.b = lax.axis_index("blk")
        self.c = self.b % 2
        self.y = (self.b // 2) % 2
        self.z = self.b // 4

    def near(self, kind):
        x, y, z, c = self.x, self.y, self.z, self.c
        if kind == "up":
            z = jnp.minimum(z + 1, NZ - 1)
        elif kind == "down":
            z = jnp.maximum(z - 1, 0)
        elif kind == "y":
            y = 1 - y
        elif kind == "x":
            x = 1 - x
        elif kind == "c":
            c = 1 - c
        return (x, z * 4 + y * 2 + c)

    def blk(self, z, y, c):
        return z * 4 + y * 2 + c

    def outward(self, j):
        inner = jnp.where(j < 2, 1 - j, j)
        order = jnp.where((self.z == 0) | (self.z == NZ - 1), j, inner)
        return jnp.where(self.z < 2, order, NZ - 1 - order)

    def inward(self, j):
        inner = jnp.where(j == 0, 3, jnp.where(j == 1, 0, jnp.where(j == 2, 2, 1)))
        order = jnp.where((self.z == 0) | (self.z == NZ - 1), NZ - 1 - j, inner)
        return jnp.where(self.z < 2, order, NZ - 1 - order)


def greet_all(me):
    barrier = pltpu.get_barrier_semaphore()

    def one(k, carry):
        pl.semaphore_signal(
            barrier, inc=1, device_id=((me.x + k // 16) % 2, (me.b + k) % 16), device_id_type=MESH
        )
        return carry

    lax.fori_loop(1, 32, one, 0)
    pl.semaphore_wait(barrier, 31)


def remote(src, dst, send, recv, to):
    return pltpu.make_async_remote_copy(
        src_ref=src, dst_ref=dst, send_sem=send, recv_sem=recv, device_id=to, device_id_type=MESH
    )


def arrived(ref, sem, me):
    remote(ref, ref, sem, sem, me.near("c")).wait_recv()


def left(ref, sem, me):
    remote(ref, ref, sem, sem, me.near("c")).wait_send()


class Gather:
    def __init__(self, me, g, index, send, recv, cols=None, causal=False):
        self.me, self.g, self.index, self.send, self.recv, self.causal = me, g, index, send, recv, causal
        start, width = cols or (0, g.shape[2])
        cut = (width // 2 + 127) // 128 * 128
        self.cols = pl.ds(start, width)
        self.first, self.second = pl.ds(start, cut), pl.ds(start + cut, width - cut)

    def place(self, j):
        return self.me.z - j if self.causal else self.me.outward(j)

    def valid(self, j):
        return (j >= 0) & (j <= (self.me.z if self.causal else NZ - 1))

    def ups(self, zz):
        if self.causal:
            return self.me.z < NZ - 1
        return (zz <= self.me.z) & (self.me.z < NZ - 1)

    def downs(self, zz):
        return (zz >= self.me.z) & (self.me.z > 0)

    def put(self, j, kind, n, s, cols=None, slot=0):
        ref = self.g.at[s, :, self.cols if cols is None else cols]
        remote(ref, ref, self.send.at[j, n], self.recv.at[s, slot], self.me.near(kind)).start()

    def wait(self, s):
        arrived(self.g.at[s, :, self.cols], self.recv.at[s, 0], self.me)

    def turn(self, j):
        me, index = self.me, self.index
        x, y, c = me.x, me.y, me.c

        @pl.when(self.valid(j) & (j > 0))
        def _():
            self.wait(index(x, self.place(j), y, c))

        @pl.when(self.valid(j))
        def _():
            zz = self.place(j)
            own = index(x, zz, y, c)
            pl.when(self.ups(zz))(lambda: self.put(j, "up", 0, own))
            if not self.causal:
                pl.when(self.downs(zz))(lambda: self.put(j, "down", 1, own))
            self.put(j, "y", 2, own)
            self.put(j, "x", 3, own)
            self.put(j, "c", 6, own)

        @pl.when(self.valid(j - 1))
        def _():
            i = j - 1
            zp = self.place(i)
            s = index(x, zp, 1 - y, c)
            self.wait(s)
            self.put(i, "x", 4, s, self.first, 0)
            self.put(i, "c", 7, s)
            t = index(1 - x, zp, y, c)
            self.wait(t)
            self.put(i, "y", 5, t, self.second, 1)
            self.put(i, "c", 8, t)

        @pl.when(self.valid(j - 2))
        def _():
            i = j - 2
            s = index(1 - x, self.place(i), 1 - y, c)
            arrived(self.g.at[s, :, self.first], self.recv.at[s, 0], me)
            arrived(self.g.at[s, :, self.second], self.recv.at[s, 1], me)
            self.put(i, "c", 9, s)

    def from_core(self, j):
        me = self.me
        for xx in (me.x, 1 - me.x):
            for yy in (me.y, 1 - me.y):
                self.wait(self.index(xx, self.place(j), yy, 1 - me.c))

    def close(self, cores=True):
        me = self.me

        def one(j, carry):
            @pl.when(self.valid(j))
            def _():
                zz = self.place(j)
                own = self.index(me.x, zz, me.y, me.c)
                whole = self.g.at[own, :, self.cols]
                first, second = self.g.at[own, :, self.first], self.g.at[own, :, self.second]
                pl.when(self.ups(zz))(lambda: left(whole, self.send.at[j, 0], me))
                if not self.causal:
                    pl.when(self.downs(zz))(lambda: left(whole, self.send.at[j, 1], me))
                for n in (2, 3, 6, 7, 8, 9):
                    left(whole, self.send.at[j, n], me)
                left(first, self.send.at[j, 4], me)
                left(second, self.send.at[j, 5], me)
                if cores:
                    self.from_core(j)

            return carry

        lax.fori_loop(0, 4, one, 0)


class Sum:
    def __init__(self, me, part, index, out, room, sems, cols=None, causal=False):
        self.me, self.part, self.index, self.out, self.causal = me, part, index, out, causal
        start, width = cols or (0, part.shape[2])
        self.cols = pl.ds(start, width)
        self.rc, self.rx, self.ry, self.rn, self.rz, self.acc = room
        self.sc, self.ss, self.vc, self.vn, self.vz = sems
        self.half = (width // 2 + 127) // 128 * 128
        self.first, self.second = pl.ds(0, self.half), pl.ds(self.half, width - self.half)

    @staticmethod
    def room(rows, columns):
        half = (columns // 2 + 127) // 128 * 128
        return [
            pltpu.VMEM((16, rows, columns), BF),
            pltpu.VMEM((4, rows, half), BF),
            pltpu.VMEM((4, rows, columns - half), BF),
            pltpu.VMEM((2, 4, rows, columns), BF),
            pltpu.VMEM((5, rows, columns), BF),
            pltpu.VMEM((rows, columns), F32),
            DMA((16,)),
            DMA((4, 6)),
            DMA((16,)),
            DMA((4, 4)),
            DMA((5,)),
        ]

    def place(self, j):
        return j if self.causal else self.me.inward(j)

    def valid(self, j):
        return (j >= 0) & (j <= (self.me.z if self.causal else NZ - 1))

    def slot(self, xx, zz, yy):
        return zz * 4 + xx * 2 + yy

    def lead(self, j):
        me = self.me
        zz = self.place(j)
        for xx in (1 - me.x, me.x):
            for yy in (1 - me.y, me.y):
                k = self.slot(xx, zz, yy)
                src = self.part.at[self.index(xx, zz, yy, 1 - me.c), :, self.cols]
                remote(src, self.rc.at[k], self.sc.at[k], self.vc.at[k], me.near("c")).start()

    def with_core(self, xx, zz, yy):
        k = self.slot(xx, zz, yy)
        arrived(self.rc.at[k], self.vc.at[k], self.me)
        own = self.part[self.index(xx, zz, yy, self.me.c), :, self.cols]
        return k, own.astype(F32) + self.rc[k].astype(F32)

    def turn(self, j):
        me, half, first, second = self.me, self.half, self.first, self.second
        rc, rx, ry, rn, ss, vn = self.rc, self.rx, self.ry, self.rn, self.ss, self.vn
        x, y = me.x, me.y

        @pl.when(self.valid(j))
        def _():
            zz = self.place(j)
            k, total = self.with_core(1 - x, zz, 1 - y)
            rc[k] = total.astype(BF)
            remote(rc.at[k, :, first], rx.at[zz], ss.at[j, 0], vn.at[zz, 0], me.near("x")).start()
            remote(rc.at[k, :, second], ry.at[zz], ss.at[j, 1], vn.at[zz, 1], me.near("y")).start()

        @pl.when(self.valid(j - 1))
        def _():
            i = j - 1
            zz = self.place(i)
            k, total = self.with_core(x, zz, 1 - y)
            arrived(rx.at[zz], vn.at[zz, 0], me)
            rc[k, :, second] = total[:, half:].astype(BF)
            rc[k, :, first] = (total[:, :half] + rx[zz].astype(F32)).astype(BF)
            remote(rc.at[k], rn.at[0, zz], ss.at[i, 2], vn.at[zz, 2], me.near("y")).start()
            k, total = self.with_core(1 - x, zz, y)
            arrived(ry.at[zz], vn.at[zz, 1], me)
            rc[k, :, first] = total[:, :half].astype(BF)
            rc[k, :, second] = (total[:, half:] + ry[zz].astype(F32)).astype(BF)
            remote(rc.at[k], rn.at[1, zz], ss.at[i, 3], vn.at[zz, 3], me.near("x")).start()

        @pl.when(self.valid(j - 2))
        def _():
            i = j - 2
            zz = self.place(i)
            k, total = self.with_core(x, zz, y)
            arrived(rn.at[0, zz], vn.at[zz, 2], me)
            arrived(rn.at[1, zz], vn.at[zz, 3], me)
            self.acc[...] = total + rn[0, zz].astype(F32) + rn[1, zz].astype(F32)
            along_z(me, i, zz, self.acc, rc.at[k], self.rz, ss, 4, self.vz, self.causal)

            @pl.when(zz == me.z)
            def _():
                self.out[:, self.cols] = self.acc[...]

    def close(self):
        me = self.me
        whole = self.rc.at[0]
        first, second = self.rc.at[0, :, self.first], self.rc.at[0, :, self.second]

        def one(j, carry):
            @pl.when(self.valid(j))
            def _():
                zz = self.place(j)
                for xx in (1 - me.x, me.x):
                    for yy in (1 - me.y, me.y):
                        left(whole, self.sc.at[self.slot(xx, zz, yy)], me)
                left(first, self.ss.at[j, 0], me)
                left(second, self.ss.at[j, 1], me)
                for n in (2, 3):
                    left(whole, self.ss.at[j, n], me)
                if not self.causal:
                    pl.when(zz > me.z)(lambda: left(whole, self.ss.at[j, 4], me))
                pl.when(zz < me.z)(lambda: left(whole, self.ss.at[j, 5], me))

            return carry

        lax.fori_loop(0, 4, one, 0)


def along_z(me, i, zz, acc, room, rz, ss, n, vz, causal=False):
    z = me.z

    def add(slot):
        arrived(rz.at[slot], vz.at[slot], me)
        acc[...] += rz[slot].astype(F32)

    if not causal:
        pl.when((zz >= z) & (z > 0))(lambda: add(zz))
    pl.when((zz < z) & (z < NZ - 1))(lambda: add(zz))
    pl.when((zz == z) & (z < NZ - 1))(lambda: add(4))

    if not causal:

        @pl.when(zz > z)
        def _():
            room[...] = acc[...].astype(BF)
            remote(room, rz.at[zz], ss.at[i, n], vz.at[zz], me.near("up")).start()

    @pl.when(zz < z)
    def _():
        room[...] = acc[...].astype(BF)
        there = jnp.where(zz == z - 1, 4, zz)
        remote(room, rz.at[there], ss.at[i, n + 1], vz.at[there], me.near("down")).start()


def by_weight(x, z, y, c):
    return x * 16 + z * 4 + y * 2 + c


def by_token(x, z, y, c):
    return (z * 4 + y * 2 + c) * 2 + x


ANY = pl.BlockSpec(memory_space=pl.ANY)
VMEM = pl.BlockSpec(memory_space=pltpu.VMEM)
DMA = pltpu.SemaphoreType.DMA


def params(number, mib):
    return pltpu.CompilerParams(
        collective_id=number, has_side_effects=True, vmem_limit_bytes=mib << 20
    )


NT = (((1,), (1,)), ((), ()))
TN = (((0,), (0,)), ((), ()))
GROUP = QUERY_HEADS // KEY_VALUE_HEADS
LANES = GROUP * 128
SCALE = HEAD_SIZE ** (-0.5)
POWER = SCALE * 1.4426950408889634


def turned(u, cosine, sine):
    return u * cosine + pltpu.roll(u, 64, 1) * sine


def begin_of(place, doc):
    begin = jnp.zeros_like(place)
    for i in range(doc.shape[1]):
        start = doc[0:1, i : i + 1]
        begin = jnp.where(place >= start, jnp.maximum(begin, start), begin)
    return begin


def rotary_tables(me, doc, freq):
    first = (me.b * 2 + me.x) * 128
    place = first + lax.broadcasted_iota(jnp.int32, (128, 128), 0)
    angle = (place - begin_of(place, doc)).astype(F32) * freq[...]
    sine = jnp.sin(angle)
    lane = lax.broadcasted_iota(jnp.int32, (128, 128), 1)
    return jnp.cos(angle), jnp.where(lane < 64, -sine, sine)


def query_bounds(me, doc):
    place = (me.b * 2 + me.x) * 128 + lax.broadcasted_iota(jnp.int32, (1, LANES), 1) % 128
    return begin_of(place, doc), place


def allowed_keys(start, bounds):
    key = start + lax.broadcasted_iota(jnp.int32, (256, LANES), 0)
    return (key >= bounds[0]) & (key <= bounds[1])


def eye(n):
    return lax.broadcasted_iota(jnp.int32, (n, n), 0) == lax.broadcasted_iota(jnp.int32, (n, n), 1)


def as_column(row):
    return jnp.sum(jnp.where(eye(row.shape[1]), row, 0.0), axis=1, keepdims=True)


def as_row(column):
    return jnp.sum(jnp.where(eye(column.shape[0]), column, 0.0), axis=0, keepdims=True)


QKV = 2048
WIDE = QKV + 128
PIECES = ((0, 1152), (1152, 1024))


def front_kernel(
    doc_in, freq_in, one_in, two_in, valid_in, states, down_in, wq, wk, wv, wo, up,
    gq_out, go_out, kv_out, win, wout, h_out, n2_out, n1_out, qs_out, o_out, lse_out, count_out, gains_out,
    doc, freq, norm_one, norm_two, valid, lse, count, gains_row, gq, go, kv, down, top, total, acc, low_rows, down_raw, cos, sin, n1, qs, o, h, n2,
    load_sem, own_sem, qsend, qrecv, gsend, grecv, ksend, krecv, asend, arecv, osend, orecv,
):
    me = Place()
    x, y, z, b, c = me.x, me.y, me.z, me.b, me.c
    here = by_weight(x, z, y, c)
    mine = [
        pltpu.make_async_copy(wq, gq.at[here, :, pl.ds(0, 1536)], own_sem.at[0]),
        pltpu.make_async_copy(wk, gq.at[here, :, pl.ds(1536, 256)], own_sem.at[1]),
        pltpu.make_async_copy(wv, gq.at[here, :, pl.ds(1792, 256)], own_sem.at[2]),
        pltpu.make_async_copy(wo, go.at[here], own_sem.at[3]),
    ]
    pairs = (
        (down_in, down_raw), (states, low_rows), (doc_in, doc), (freq_in, freq),
        (one_in, norm_one), (two_in, norm_two), (valid_in, valid),
    )
    loads = [pltpu.make_async_copy(src, dst, load_sem.at[i]) for i, (src, dst) in enumerate(pairs)]
    for copy in loads[4:] + mine + loads[:4]:
        copy.start()
    for load in loads[4:]:
        load.wait()

    lane = lax.broadcasted_iota(jnp.int32, (48, 128), 1)
    kept = jnp.sum(valid[...].astype(F32))
    extra = jnp.where(
        lane == 0,
        as_column(norm_one[...].astype(F32)),
        jnp.where(lane == 1, as_column(norm_two[...].astype(F32)), jnp.where(lane == 2, kept, 0.0)),
    )
    gq[here, :, pl.ds(QKV, 128)] = extra.astype(BF)
    greet_all(me)
    for copy in mine:
        copy.wait()

    def own_piece(n):
        col = pl.multiple_of(n * 768 + c * 384, 128)
        return pltpu.make_async_copy(
            up.at[b // 2, :, pl.ds(col, 384)], win.at[b, :, pl.ds(n * 384, 384)], own_sem.at[4 + n]
        )

    def own_down():
        return pltpu.make_async_copy(down.at[b // 2], wout.at[b], own_sem.at[6])

    def deal(k, carry):
        t = (b + k) % 16
        for n in range(2):
            col = pl.multiple_of(n * 768 + (t % 2) * 384, 128)
            remote(
                up.at[t // 2, :, pl.ds(col, 384)],
                win.at[b, :, pl.ds(n * 384, 384)],
                asend.at[k, n],
                arecv.at[b, n],
                (x, t),
            ).start()
        pl.when(t % 2 == x)(
            lambda: remote(down.at[t // 2], wout.at[b], osend.at[k], orecv.at[b], (x, t)).start()
        )
        return carry

    weights = [
        Gather(me, gq, by_weight, qsend.at[i], qrecv.at[i], PIECES[i]) for i in range(len(PIECES))
    ]

    def first_turn(j, carry):
        for piece in weights:
            piece.turn(j)

        @pl.when(j == 0)
        def _():
            for load in loads[:4]:
                load.wait()
            for e in range(E):
                wide = down_raw[e].astype(F32)
                down[e] = jnp.concatenate([wide[:, :768], wide[:, 768:]], axis=0).astype(BF)
            cos[...], sin[...] = rotary_tables(me, doc, freq)

        lax.fori_loop(1 + j * 3, jnp.minimum(4 + j * 3, 16), deal, 0)
        return carry

    lax.fori_loop(0, 6, first_turn, 0)
    for n in range(2):
        own_piece(n).start()
    pl.when(c == x)(lambda: own_down().start())
    bounds = query_bounds(me, doc)
    rows = low_rows[...].astype(F32)
    level = rows * lax.rsqrt(jnp.mean(rows * rows, axis=-1, keepdims=True) + 1e-06)
    for piece in weights:
        piece.close()
    keep = pltpu.make_async_copy(gq, gq_out, own_sem.at[0])
    keep.start()

    gains = gq[:, :, pl.ds(QKV, 128)].reshape(1536, 128).astype(F32).T
    n1[...] = (level * gains[0:1]).astype(BF)
    turns = cos[...], sin[...]
    at = by_token(x, z, y, c)
    keys = Gather(me, kv, by_token, ksend, krecv, causal=True)
    output = Gather(me, go, by_weight, gsend, grecv)
    both = jnp.dot(n1[...], gq[:, :, pl.ds(1536, 512)].reshape(1536, 512), preferred_element_type=F32)
    for i in range(2):
        kv[at, :, i * 128 : i * 128 + 128] = turned(both[:, i * 128 : i * 128 + 128], *turns).astype(BF)
    kv[at, :, 256:512] = both[:, 256:512].astype(BF)
    keys.turn(0)
    query = jnp.dot(n1[...], gq[:, :, pl.ds(0, 1536)].reshape(1536, 1536), preferred_element_type=F32)
    for i in range(QUERY_HEADS):
        r = (i % GROUP) * 128
        qs[i // GROUP, r : r + 128] = turned(query[:, i * 128 : i * 128 + 128], *turns).astype(BF)
    count[...] = jnp.zeros((8, 128), F32) + jnp.sum(gains[2:3]) / 48.0
    gains_row[...] = gains[0:8]
    saved = [
        pltpu.make_async_copy(count, count_out, load_sem.at[5]),
        pltpu.make_async_copy(gains_row, gains_out, load_sem.at[6]),
        pltpu.make_async_copy(n1, n1_out, load_sem.at[0]),
        pltpu.make_async_copy(qs, qs_out, load_sem.at[1]),
    ]
    for copy in saved:
        copy.start()

    top[...] = jnp.full_like(top, FLOOR_SCORE)
    total[...] = jnp.zeros_like(total)
    acc[...] = jnp.zeros_like(acc)
    def block(n):
        ok = allowed_keys(n * 256, bounds)
        for i in range(2):
            k = kv[pl.ds(n * 2, 2), :, i * 128 : i * 128 + 128].reshape(256, 128)
            v = kv[pl.ds(n * 2, 2), :, 256 + i * 128 : 384 + i * 128].reshape(256, 128)
            s = lax.dot_general(k, qs[i], NT, preferred_element_type=F32)
            s = jnp.where(ok, s, FLOOR_SCORE)
            old = top[i]
            new = jnp.maximum(old, jnp.max(s, axis=0, keepdims=True))
            factor = jnp.exp2((old - new) * POWER)
            p = jnp.exp2((s - new) * POWER)
            top[i] = new
            total[i] = total[i] * factor + jnp.sum(p, axis=0, keepdims=True)
            acc[i] = acc[i] * factor + lax.dot_general(v, p.astype(BF), TN, preferred_element_type=F32)

    def turn(j, carry):
        pl.when(j > 0)(lambda: keys.turn(j))
        output.turn(j - 2)

        @pl.when(keys.valid(j - 2))
        def _():
            i = j - 2
            keys.from_core(i)
            zz = z - i
            last = jnp.where(i == 0, y * 2 + c, 3)

            def one(n, carry):
                block(zz * 4 + last - n)
                return carry

            lax.fori_loop(0, last + 1, one, 0)

        return carry

    lax.fori_loop(0, 8, turn, 0)
    output.close()
    keep_o = pltpu.make_async_copy(go, go_out, own_sem.at[1])
    keep_o.start()
    keep_k = pltpu.make_async_copy(kv, kv_out, own_sem.at[2])
    keep_k.start()
    for i in range(2):
        lse[i] = top[i] * POWER + jnp.log2(total[i])
        done = acc[i] / total[i]
        for r in range(GROUP):
            col = (i * GROUP + r) * 128
            o[:, col : col + 128] = done[:, r * 128 : r * 128 + 128].T
    more = [pltpu.make_async_copy(o, o_out, load_sem.at[2]), pltpu.make_async_copy(lse, lse_out, load_sem.at[7])]
    for copy in more:
        copy.start()
    res = low_rows[...].astype(F32) + jnp.dot(
        o[...].astype(BF), go[...].reshape(1536, 1536), preferred_element_type=F32
    )
    h[...] = res
    n2[...] = (
        res * lax.rsqrt(jnp.mean(res * res, axis=-1, keepdims=True) + 1e-06) * gains[1:2]
    ).astype(BF)
    more.append(pltpu.make_async_copy(h, h_out, load_sem.at[3]))
    more.append(pltpu.make_async_copy(n2, n2_out, load_sem.at[4]))
    more[2].start()
    more[3].start()

    keys.close(False)

    def close(k, carry):
        piece = win.at[b, :, pl.ds(0, 384)]
        f = (b + 16 - k) % 16
        for n in range(2):
            left(piece, asend.at[k, n], me)
            arrived(win.at[f, :, pl.ds(n * 384, 384)], arecv.at[f, n], me)
        pl.when((b + k) % 2 == x)(lambda: left(wout.at[b], osend.at[k], me))
        pl.when(c == x)(lambda: arrived(wout.at[f], orecv.at[f], me))
        return carry

    lax.fori_loop(1, 16, close, 0)
    for n in range(2):
        own_piece(n).wait()
    pl.when(c == x)(lambda: own_down().wait())
    for copy in [keep, keep_o, keep_k] + saved + more:
        copy.wait()


def run_front(*operands):
    shape = jax.ShapeDtypeStruct
    return pl.pallas_call(
        front_kernel,
        out_shape=(
            shape((32, 48, WIDE), BF),
            shape((32, 48, 1536), BF),
            shape((32, 128, 512), BF),
            shape((16, 48, 768), BF),
            shape((16, 48, 768), BF),
            shape((128, 1536), F32),
            shape((128, 1536), BF),
            shape((128, 1536), BF),
            shape((2, LANES, 128), BF),
            shape((128, 1536), F32),
            shape((2, 1, LANES), F32),
            shape((8, 128), F32),
            shape((8, 1536), F32),
        ),
        in_specs=[ANY] * 12,
        out_specs=(ANY,) * 13,
        scratch_shapes=[
            pltpu.VMEM(operands[0].shape, jnp.int32),
            pltpu.VMEM((1, 128), F32),
            pltpu.VMEM((1, 48), BF),
            pltpu.VMEM((1, 48), BF),
            pltpu.VMEM((1, 128), jnp.int32),
            pltpu.VMEM((2, 1, LANES), F32),
            pltpu.VMEM((8, 128), F32),
            pltpu.VMEM((8, 1536), F32),
            pltpu.VMEM((32, 48, WIDE), BF),
            pltpu.VMEM((32, 48, 1536), BF),
            pltpu.VMEM((32, 128, 512), BF),
            pltpu.VMEM((8, 48, 768), BF),
            pltpu.VMEM((2, 1, LANES), F32),
            pltpu.VMEM((2, 1, LANES), F32),
            pltpu.VMEM((2, 128, LANES), F32),
            pltpu.VMEM((128, 1536), BF),
            pltpu.VMEM((8, 24, 1536), BF),
            pltpu.VMEM((128, 128), F32),
            pltpu.VMEM((128, 128), F32),
            pltpu.VMEM((128, 1536), BF),
            pltpu.VMEM((2, LANES, 128), BF),
            pltpu.VMEM((128, 1536), F32),
            pltpu.VMEM((128, 1536), F32),
            pltpu.VMEM((128, 1536), BF),
            DMA((8,)),
            DMA((7,)),
            DMA((2, 4, 10)),
            DMA((2, 32, 2)),
            DMA((4, 10)),
            DMA((32, 2)),
            DMA((4, 10)),
            DMA((32, 2)),
            DMA((16, 2)),
            DMA((16, 2)),
            DMA((16,)),
            DMA((16,)),
        ],
        compiler_params=params(1, 62),
        name="front",
    )(*operands)


GELU_A = 0.7978845608028654
GELU_B = 0.044715


CUTS = 2
CUT = 128 // CUTS


def experts_kernel(
    routes_in, gates_in, valid_in, count_in, n2, h_in, teacher_in, win, wout,
    err_out, final_out, dn2_out, dy_out, dwin_out, dwout_out,
    routes, gates, valid, count, err, h, teacher, final, dy, nall, dyall, pairs, zg, dpairs, part, rc, ry, rz, acc, errs, tables, gate,
    wfull, slab, wdown, dwin, dwin_in, dwout, dwout_in,
    load_sem, own_sem, gsend, grecv, csend, crecv, ysend, yrecv, zsend, zrecv, esend, erecv,
    tsend, trecv, xsend, xrecv,
):
    me = Place()
    x, y, z, b, c = me.x, me.y, me.z, me.b, me.c
    half = pltpu.make_async_copy(win, wfull.at[x], own_sem.at[0])
    half.start()
    loads = [
        pltpu.make_async_copy(n2, nall.at[b], load_sem.at[0]),
        pltpu.make_async_copy(h_in, h, load_sem.at[1]),
        pltpu.make_async_copy(teacher_in, teacher, load_sem.at[2]),
        pltpu.make_async_copy(routes_in, routes, load_sem.at[3]),
        pltpu.make_async_copy(gates_in, gates, load_sem.at[4]),
        pltpu.make_async_copy(valid_in, valid, load_sem.at[5]),
        pltpu.make_async_copy(count_in, count, load_sem.at[6]),
    ]
    for load in loads:
        load.start()
    held = pltpu.make_async_copy(wout, slab, own_sem.at[1])
    pl.when(c == x)(held.start)
    greet_all(me)

    def rows_of(p):
        return pl.ds(p * CUT, CUT)

    def over_weights(k):
        cut = pl.ds(k * 4, 4)
        return remote(win.at[cut], wfull.at[x, cut], xsend.at[k], xrecv.at[k], me.near("x"))

    def over_down():
        return remote(wout, slab, xsend.at[4], xrecv.at[4], me.near("x"))

    def gather(buf, way, between):
        def put(j, p, kind, n, s):
            ref = buf.at[s, rows_of(p)]
            remote(ref, ref, gsend.at[way, j, p, n], grecv.at[way, s, p], me.near(kind)).start()

        def turn(j, carry):
            for p in range(CUTS):
                zz = me.outward(j)
                own = me.blk(zz, y, c)

                @pl.when((j > 0) & (j < 4))
                def _():
                    arrived(buf.at[own, rows_of(p)], grecv.at[way, own, p], me)

                @pl.when(j < 4)
                def _():
                    pl.when((zz <= z) & (z < NZ - 1))(lambda: put(j, p, "up", 0, own))
                    pl.when((zz >= z) & (z > 0))(lambda: put(j, p, "down", 1, own))
                    put(j, p, "y", 2, own)
                    put(j, p, "c", 3, own)

                @pl.when((j > 0) & (j < 5))
                def _():
                    i = j - 1
                    s = me.blk(me.outward(i), 1 - y, c)
                    arrived(buf.at[s, rows_of(p)], grecv.at[way, s, p], me)
                    put(i, p, "c", 4, s)

                between(j, p)
            return carry

        lax.fori_loop(0, 6, turn, 0)

        def close(j, carry):
            zz = me.outward(j)
            whole = buf.at[b, rows_of(0)]
            for p in range(CUTS):
                pl.when((zz <= z) & (z < NZ - 1))(lambda: left(whole, gsend.at[way, j, p, 0], me))
                pl.when((zz >= z) & (z > 0))(lambda: left(whole, gsend.at[way, j, p, 1], me))
                for n in (2, 3, 4):
                    left(whole, gsend.at[way, j, p, n], me)
            return carry

        lax.fori_loop(0, 4, close, 0)

    def from_core(buf, way, zz, yy):
        s = me.blk(zz, yy, 1 - c)
        for p in range(CUTS):
            arrived(buf.at[s, rows_of(p)], grecv.at[way, s, p], me)

    def to_other_core(way, q):
        remote(part.at[q * 2 + 1 - c], rc.at[q], csend.at[way, q], crecv.at[way, q], me.near("c")).start()

    def lead(way, j):
        zz = me.inward(j)
        q = zz * 2 + 1 - y
        s = q * 2 + c
        arrived(rc.at[q], crecv.at[way, q], me)
        part[s] = (part[s].astype(F32) + rc[q].astype(F32)).astype(BF)
        for p in range(CUTS):
            remote(
                part.at[s, rows_of(p)], ry.at[zz, rows_of(p)], ysend.at[way, j, p], yrecv.at[way, zz, p], me.near("y")
            ).start()

    def follow(way, j):
        zz = me.inward(j)
        q = zz * 2 + y
        s = q * 2 + c
        arrived(rc.at[q], crecv.at[way, q], me)
        for p in range(CUTS):
            cut = rows_of(p)
            arrived(ry.at[zz, cut], yrecv.at[way, zz, p], me)
            piece = acc.at[cut]
            piece[...] = part[s, cut].astype(F32) + rc[q, cut].astype(F32) + ry[zz, cut].astype(F32)
            along_z(
                me, j, zz, piece, part.at[s, cut], rz.at[:, cut], zsend.at[way, :, p], 0, zrecv.at[way, :, p]
            )

    def close_sum(way):
        def close(j, carry):
            zz = me.inward(j)
            whole, piece = part.at[b], part.at[b, rows_of(0)]
            left(whole, csend.at[way, j], me)
            left(whole, csend.at[way, j + 4], me)
            for p in range(CUTS):
                left(piece, ysend.at[way, j, p], me)
                pl.when(zz > z)(lambda: left(piece, zsend.at[way, j, p, 0], me))
                pl.when(zz < z)(lambda: left(piece, zsend.at[way, j, p, 1], me))
            return carry

        lax.fori_loop(0, 4, close, 0)

    def gelu_parts(g):
        t = jnp.tanh(GELU_A * (g + GELU_B * g * g * g))
        return t, 0.5 * g * (1.0 + t)

    def forward(q):
        rows = nall[pl.ds(q * 2, 2)].reshape(256, 1536)
        pair = jnp.dot(rows, wfull[...].reshape(1536, 768), preferred_element_type=F32)
        pairs[q] = pair
        unused, a = gelu_parts(pair[:, :384])
        scale = gate[pl.ds(q * 2, 2)].reshape(256, 1)
        zq = (a * pair[:, 384:] * scale).astype(BF)
        zg[q] = zq
        out = jnp.dot(zq, wdown[...], preferred_element_type=F32)
        part[pl.ds(q * 2, 2)] = out.astype(BF).reshape(2, 128, 1536)
        to_other_core(0, q)

    def backward(q):
        rows = dyall[pl.ds(q * 2, 2)].reshape(256, 1536)
        scale = gate[pl.ds(q * 2, 2)].reshape(256, 1)
        dz = lax.dot_general(rows, wdown[...], NT, preferred_element_type=F32) * scale
        g, u = pairs[q, :, :384], pairs[q, :, 384:]
        t, a = gelu_parts(g)
        slope = 0.5 * (1.0 + t) + 0.5 * g * (1.0 - t * t) * (GELU_A * (1.0 + 3.0 * GELU_B * g * g))
        dpairs[q, :, :384] = (dz * u * slope).astype(BF)
        dpairs[q, :, 384:] = (dz * a).astype(BF)
        out = lax.dot_general(dpairs[q], wfull[...].reshape(1536, 768), NT, preferred_element_type=F32)
        part[pl.ds(q * 2, 2)] = out.astype(BF).reshape(2, 128, 1536)
        to_other_core(1, q)

    loads[0].wait()
    pl.when(c == x)(held.wait)

    def tell_gates(k, carry):
        to = (b + k) % 16
        remote(tables.at[b], tables.at[b], tsend.at[k], trecv.at[b], (x, to)).start()
        return carry

    def with_tokens(j, p):
        if p == 0:
            pl.when((j == 0) & (c == x))(lambda: over_down().start())
            for k in range(4):
                pl.when(j == k)(over_weights(k).start)
        elif p == 1:

            @pl.when(j == 0)
            def _():
                for load in loads[3:]:
                    load.wait()
                expert = lax.broadcasted_iota(jnp.int32, (8, 128), 0)
                table = jnp.zeros((8, 128), F32)
                for k in range(TOP):
                    table = table + jnp.where(routes[k : k + 1, :] == expert, gates[k : k + 1, :], 0.0)
                tables[b] = table
                lax.fori_loop(1, 16, tell_gates, 0)

    gather(nall, 0, with_tokens)

    def all_cores(buf, way):
        def one(j, carry):
            from_core(buf, way, j, y)
            from_core(buf, way, j, 1 - y)
            return carry

        lax.fori_loop(0, 4, one, 0)

    all_cores(nall, 0)
    def hear_gates(k, carry):
        left(tables.at[0], tsend.at[k], me)
        arrived(tables.at[(b + 16 - k) % 16], trecv.at[(b + 16 - k) % 16], me)
        return carry

    lax.fori_loop(1, 16, hear_gates, 0)

    def gate_of(s, carry):
        row = lax.broadcasted_iota(jnp.int32, (8, 128), 0)
        picked = jnp.sum(jnp.where(row == b // 2, tables[s], 0.0), axis=0, keepdims=True)
        gate[s] = as_column(picked)
        return carry

    lax.fori_loop(0, 16, gate_of, 0)
    half.wait()
    for k in range(4):
        arrived(wfull.at[1 - x, pl.ds(k * 4, 4)], xrecv.at[k], me)
    pl.when(c != x)(lambda: arrived(slab, xrecv.at[4], me))
    wide = slab[...].astype(F32).reshape(16, 2, 24, 768)
    wdown[:, :768] = wide[:, 0].reshape(384, 768).astype(BF)
    wdown[:, 768:] = wide[:, 1].reshape(384, 768).astype(BF)

    def outputs(j, carry):
        @pl.when(j < 4)
        def _():
            forward(me.inward(j) * 2 + 1 - y)

        pl.when(j > 0)(lambda: follow(0, j - 1))

        @pl.when(j < 4)
        def _():
            lead(0, j)
            forward(me.inward(j) * 2 + y)

        return carry

    lax.fori_loop(0, 5, outputs, 0)

    keep = as_column(valid[...].astype(F32))
    loads[1].wait()
    loads[2].wait()
    done = h[...] + acc[...]
    final[...] = done.astype(BF)
    diff = done - teacher[...].astype(F32)
    scaled = (keep * (SPAN / count[0:1, 0:1])) * diff
    dy[...] = scaled
    dyall[b] = scaled.astype(BF)
    saved = [
        pltpu.make_async_copy(final, final_out, load_sem.at[0]),
        pltpu.make_async_copy(dy, dy_out, load_sem.at[1]),
        pltpu.make_async_copy(acc, dn2_out, load_sem.at[2]),
        pltpu.make_async_copy(err, err_out, load_sem.at[3]),
    ]
    for copy in saved[:2]:
        copy.start()
    kept = jnp.sum(keep * diff * diff)
    me_index = x * 16 + b
    errs[me_index] = jnp.zeros((8, 128), F32) + kept

    def tell(k, carry):
        to = ((x + k // 16) % 2, (b + k) % 16)
        remote(errs.at[me_index], errs.at[me_index], esend.at[k], erecv.at[me_index], to).start()
        return carry

    def with_dy(j, p):
        if p == 0:

            @pl.when((j > 0) & (j < 5))
            def _():
                zz = me.outward(j - 1)
                from_core(dyall, 1, zz, y)
                backward(zz * 2 + y)

        elif p == CUTS - 1:

            @pl.when(j == 0)
            def _():
                lax.fori_loop(1, 32, tell, 0)
                close_sum(0)

            @pl.when(j > 1)
            def _():
                zz = me.outward(j - 2)
                from_core(dyall, 1, zz, 1 - y)
                backward(zz * 2 + 1 - y)

    gather(dyall, 1, with_dy)

    def in_grad(i):
        col = pl.ds(pl.multiple_of(i * 256, 256), 256)
        rows = nall[:, :, col].reshape(2048, 256)
        dwin[col, :] = lax.dot_general(
            rows, dpairs[...].reshape(2048, 768), TN, preferred_element_type=F32
        ).astype(BF)

    def out_grad(i):
        col = pl.ds(i * 256, 256)
        right = dyall[:, :, col].reshape(2048, 256)
        value = lax.dot_general(zg[...].reshape(2048, 384), right, TN, preferred_element_type=F32)
        there = i // 3 * 24
        dwout[:, there : there + 24, (i % 3) * 256 : (i % 3) * 256 + 256] = value.reshape(16, 24, 256)

    def over_in(k):
        src = dwin.at[pl.ds(pl.multiple_of((1 - x) * 768 + k * 256, 256), 256)]
        return remote(src, dwin_in.at[pl.ds(k * 256, 256)], xsend.at[5 + k], xrecv.at[5 + k], me.near("x"))

    def over_out():
        return remote(slab, dwout_in, xsend.at[8], xrecv.at[8], me.near("x"))

    def leads(j, carry):
        lead(1, j)
        return carry

    lax.fori_loop(0, 4, leads, 0)

    def sums(j, carry):
        @pl.when(j == 0)
        def _():
            for k in range(3):
                in_grad((1 - x) * 3 + k)
                over_in(k).start()

        @pl.when(j == 1)
        def _():
            for k in range(6):
                out_grad(k)
            slab[...] = dwout[...].astype(BF)
            pl.when(c != x)(lambda: over_out().start())

        @pl.when(j == 2)
        def _():
            for k in range(3):
                in_grad(x * 3 + k)

        follow(1, j)
        return carry

    for k in range(4):
        over_weights(k).wait_send()
    pl.when(c == x)(lambda: over_down().wait_send())
    lax.fori_loop(0, 4, sums, 0)
    saved[2].start()
    close_sum(1)

    def hear(k, carry):
        left(errs.at[0], esend.at[k], me)
        s = ((x + k // 16) % 2) * 16 + (b + k) % 16
        arrived(errs.at[s], erecv.at[s], me)
        return carry

    lax.fori_loop(1, 32, hear, 0)
    total = errs[0]
    for s in range(1, 32):
        total = total + errs[s]
    err[...] = total / (1536.0 * count[...])
    saved[3].start()

    for k in range(3):
        over_in(k).wait_send()
        here = pl.ds(pl.multiple_of(x * 768 + k * 256, 256), 256)
        there = pl.ds(k * 256, 256)
        arrived(dwin_in.at[there], xrecv.at[5 + k], me)
        dwin_in[there] = (dwin_in[there].astype(F32) + dwin[here, :].astype(F32)).astype(BF)
    out = pltpu.make_async_copy(dwin_in, dwin_out, own_sem.at[0])
    out.start()

    @pl.when(c == x)
    def _():
        arrived(dwout_in, xrecv.at[8], me)
        dwout_in[...] = (dwout_in[...].astype(F32) + dwout[...]).astype(BF)
        copy = pltpu.make_async_copy(dwout_in, dwout_out, own_sem.at[1])
        copy.start()
        copy.wait()

    pl.when(c != x)(lambda: over_out().wait_send())
    for copy in saved + [out]:
        copy.wait()


def run_experts(*operands):
    wide = (128, 1536)
    shard = (16,) + wide
    shape = jax.ShapeDtypeStruct
    return pl.pallas_call(
        experts_kernel,
        out_shape=(
            shape((8, 128), F32),
            shape(wide, BF),
            shape(wide, F32),
            shape(wide, F32),
            shape((768, 768), BF),
            shape((16, 48, 768), BF),
        ),
        in_specs=[ANY] * 9,
        out_specs=(ANY,) * 6,
        scratch_shapes=[
            pltpu.VMEM((TOP, 128), jnp.int32),
            pltpu.VMEM((TOP, 128), F32),
            pltpu.VMEM((1, 128), jnp.int32),
            pltpu.VMEM((8, 128), F32),
            pltpu.VMEM((8, 128), F32),
            pltpu.VMEM(wide, F32),
            pltpu.VMEM(wide, BF),
            pltpu.VMEM(wide, BF),
            pltpu.VMEM(wide, F32),
            pltpu.VMEM(shard, BF),
            pltpu.VMEM(shard, BF),
            pltpu.VMEM((8, 256, 768), F32),
            pltpu.VMEM((8, 256, 384), BF),
            pltpu.VMEM((8, 256, 768), BF),
            pltpu.VMEM(shard, BF),
            pltpu.VMEM((8,) + wide, BF),
            pltpu.VMEM((4,) + wide, BF),
            pltpu.VMEM((5,) + wide, BF),
            pltpu.VMEM(wide, F32),
            pltpu.VMEM((32, 8, 128), F32),
            pltpu.VMEM((16, 8, 128), F32),
            pltpu.VMEM((16, 128, 1), F32),
            pltpu.VMEM((2, 16, 48, 768), BF),
            pltpu.VMEM((16, 48, 768), BF),
            pltpu.VMEM((384, 1536), BF),
            pltpu.VMEM((1536, 768), BF),
            pltpu.VMEM((768, 768), BF),
            pltpu.VMEM((16, 48, 768), F32),
            pltpu.VMEM((16, 48, 768), BF),
            DMA((7,)),
            DMA((2,)),
            DMA((2, 4, CUTS, 5)),
            DMA((2, 16, CUTS)),
            DMA((2, 8)),
            DMA((2, 8)),
            DMA((2, 4, CUTS)),
            DMA((2, 4, CUTS)),
            DMA((2, 4, CUTS, 2)),
            DMA((2, 5, CUTS)),
            DMA((32,)),
            DMA((32,)),
            DMA((16,)),
            DMA((16,)),
            DMA((9,)),
            DMA((9,)),
        ],
        compiler_params=params(2, 62),
        name="experts",
    )(*operands)


def norm_back(values, gain, grad):
    scale = lax.rsqrt(jnp.mean(values * values, axis=-1, keepdims=True) + 1e-06)
    inner = grad * gain
    mean = jnp.mean(inner * values, axis=-1, keepdims=True)
    return scale * inner - values * (scale * scale * scale * mean), jnp.sum(
        grad * values * scale, axis=0, keepdims=True
    )


Q_PIECES = ((0, 768), (768, 768))
LAST = (1536, 640)


def back_kernel(
    doc_in, freq_in, gains_in, states_in, h_in, n1_in, qs_in, o_in, lse_in, dn2_in, dy_in, dwin, dwout, gq, go, kv_in,
    gx_out, gqw, gkw, gvw, gnorm_out, gout_out, gup, gdown,
    doc, freq, gains, gnorm, states, h, n1, qs, o, lse, dn2, dy, gx, gout, gkv,
    wq, wo, kv, pk, pw, dos, delta, dh, dq, dkv, dqkv, gqkv, *rest,
):
    sums = [(rest[i * 11 : i * 11 + 6], rest[i * 11 + 6 : i * 11 + 11]) for i in range(5)]
    load_sem, own_sem, asend, arecv, osend, orecv = rest[55:]
    me = Place()
    x, y, z, b, c = me.x, me.y, me.z, me.b, me.c
    loads = [
        pltpu.make_async_copy(go, wo, own_sem.at[0]),
        pltpu.make_async_copy(kv_in, kv, own_sem.at[1]),
        pltpu.make_async_copy(gq, wq, own_sem.at[2]),
    ]
    small = [
        pltpu.make_async_copy(src, dst, load_sem.at[i])
        for i, (src, dst) in enumerate(
            (
                (h_in, h), (dn2_in, dn2), (dy_in, dy), (o_in, o), (qs_in, qs), (lse_in, lse),
                (n1_in, n1), (states_in, states), (doc_in, doc), (freq_in, freq), (gains_in, gains),
            )
        )
    ]
    for load in small[:3] + [small[10], loads[0]] + small[3:10] + [loads[1], loads[2]]:
        load.start()
    greet_all(me)

    def own_piece(n):
        col = pl.multiple_of(n * 768 + c * 384, 128)
        return pltpu.make_async_copy(
            dwin.at[b, :, pl.ds(n * 384, 384)], gup.at[b // 2, :, pl.ds(col, 384)], own_sem.at[3 + n]
        )

    def own_down():
        return pltpu.make_async_copy(dwout.at[b], gdown.at[b // 2], own_sem.at[5])

    def deal(k, carry):
        t = (b + k) % 16
        for n in range(2):
            col = pl.multiple_of(n * 768 + c * 384, 128)
            remote(
                dwin.at[t, :, pl.ds(n * 384, 384)],
                gup.at[b // 2, :, pl.ds(col, 384)],
                asend.at[k, n],
                arecv.at[b, n],
                (x, t),
            ).start()
        pl.when(c == x)(
            lambda: remote(dwout.at[t], gdown.at[b // 2], osend.at[k], orecv.at[b // 2], (x, t)).start()
        )
        return carry

    for n in range(2):
        own_piece(n).start()
    pl.when(c == x)(lambda: own_down().start())
    lax.fori_loop(1, 16, deal, 0)
    for load in small[:3] + small[8:]:
        load.wait()
    res_grad, gain_two = norm_back(h[...], gains[1:2], dn2[...])
    dh[...] = dy[...] + res_grad
    da = dh[...].astype(BF)
    loads[0].wait()
    do = lax.dot_general(
        da, wo[...].reshape(1536, 1536), NT, preferred_element_type=F32
    ).astype(BF)
    small[3].wait()
    low = o[...].astype(BF)
    for i in range(4):
        part = lax.dot_general(low[:, i * 384 : i * 384 + 384], da, TN, preferred_element_type=F32)
        wo[i * 8 : i * 8 + 8] = part.astype(BF).reshape(8, 48, 1536)
    out_sum = Sum(me, wo, by_weight, gout, *sums[0])
    key_sum = Sum(me, pk, by_token, dkv, *sums[1], causal=True)

    def lead_all(which):
        def one(j, carry):
            which.lead(j)
            return carry

        lax.fori_loop(0, 4, one, 0)

    lead_all(out_sum)
    for i in range(QUERY_HEADS):
        col, r = i * 128, (i % GROUP) * 128
        dos[i // GROUP, r : r + 128] = do[:, col : col + 128]
        prod = do[:, col : col + 128].astype(F32) * o[:, col : col + 128]
        delta[i // GROUP, :, r : r + 128] = jnp.sum(prod.T, axis=0, keepdims=True)
    dq[...] = jnp.zeros_like(dq)
    bounds = query_bounds(me, doc)
    loads[1].wait()
    for load in small[4:6]:
        load.wait()

    def block(n):
        ok = allowed_keys(n * 256, bounds)
        for i in range(2):
            k = kv[pl.ds(n * 2, 2), :, i * 128 : i * 128 + 128].reshape(256, 128)
            v = kv[pl.ds(n * 2, 2), :, 256 + i * 128 : 384 + i * 128].reshape(256, 128)
            s = lax.dot_general(k, qs[i], NT, preferred_element_type=F32)
            p = jnp.where(ok, jnp.exp2(s * POWER - lse[i]), 0.0)
            dp = lax.dot_general(v, dos[i], NT, preferred_element_type=F32)
            ds = (p * (dp - delta[i])).astype(BF)
            dv = jnp.dot(p.astype(BF), dos[i], preferred_element_type=F32)
            dk = jnp.dot(ds, qs[i], preferred_element_type=F32) * SCALE
            pk[pl.ds(n * 2, 2), :, i * 128 : i * 128 + 128] = dk.astype(BF).reshape(2, 128, 128)
            pk[pl.ds(n * 2, 2), :, 256 + i * 128 : 384 + i * 128] = dv.astype(BF).reshape(2, 128, 128)
            dq[i] += lax.dot_general(k, ds, TN, preferred_element_type=F32)

    def turn(j, carry):
        out_sum.turn(j)

        @pl.when(key_sum.valid(j))
        def _():
            last = jnp.where(j == z, y * 2 + c, 3)

            def one(n, carry):
                block(j * 4 + n)
                return carry

            lax.fori_loop(0, last + 1, one, 0)

            def blank(n, carry):
                pk[pl.ds((j * 4 + n) * 2, 2)] = jnp.zeros((2, 128, 512), BF)
                return carry

            lax.fori_loop(last + 1, 4, blank, 0)
            key_sum.lead(j)

        key_sum.turn(j)
        return carry

    lax.fori_loop(0, 4, turn, 0)

    cos, sin = rotary_tables(me, doc, freq)
    for load in small[6:8] + [loads[2]]:
        load.wait()
    for i in range(QUERY_HEADS):
        r = (i % GROUP) * 128
        head = dq[i // GROUP, :, r : r + 128].T * SCALE
        dqkv[:, i * 128 : i * 128 + 128] = turned(head, cos, -sin).astype(BF)

    def weight_grad(start, width):
        for i in range(4):
            part = lax.dot_general(
                n1[:, i * 384 : i * 384 + 384], dqkv[:, start : start + width], TN, preferred_element_type=F32
            )
            pw[i * 8 : i * 8 + 8, :, start : start + width] = part.astype(BF).reshape(8, 48, width)

    weight_grad(0, 1536)
    proj = [Sum(me, pw, by_weight, gqkv, *sums[2 + i], Q_PIECES[i]) for i in range(2)]
    rest_sum = Sum(me, pw, by_weight, gqkv, *sums[4], LAST)
    for piece in proj:
        lead_all(piece)

    def last_turn(j, carry):
        for piece in proj:
            piece.turn(j)
        out_sum.turn(j + 4)
        pl.when(j < 2)(lambda: key_sum.turn(j + 4))

        @pl.when(j == 1)
        def _():
            for i in range(2):
                part = dkv[:, i * 128 : i * 128 + 128]
                dqkv[:, 1536 + i * 128 : 1664 + i * 128] = turned(part, cos, -sin).astype(BF)
            dqkv[:, 1792:2048] = dkv[:, 256:512].astype(BF)
            weight_grad(1536, 512)
            dn1 = lax.dot_general(
                dqkv[...], wq[:, :, pl.ds(0, QKV)].reshape(1536, QKV), NT, preferred_element_type=F32
            )
            in_grad, gain_one = norm_back(states[...].astype(F32), gains[0:1], dn1)
            rows = lax.broadcasted_iota(jnp.int32, (128, 1536), 0)
            tail = jnp.where(rows == 0, gain_one, jnp.where(rows == 1, gain_two, 0.0)).T
            pw[:, :, pl.ds(QKV, 128)] = tail.astype(BF).reshape(32, 48, 128)
            lead_all(rest_sum)
            gx[...] = dh[...] + in_grad

        rest_sum.turn(j - 2)
        return carry

    lax.fori_loop(0, 8, last_turn, 0)
    gkv[...] = gqkv[:, 1536:2048]
    stores = [
        pltpu.make_async_copy(gx, gx_out, load_sem.at[0]),
        pltpu.make_async_copy(gout, gout_out, load_sem.at[1]),
        pltpu.make_async_copy(gqkv.at[:, pl.ds(0, 1536)], gqw, load_sem.at[2]),
        pltpu.make_async_copy(gkv.at[:, pl.ds(0, 256)], gkw, load_sem.at[3]),
        pltpu.make_async_copy(gkv.at[:, pl.ds(256, 256)], gvw, load_sem.at[4]),
    ]
    for store in stores:
        store.start()
    gnorm[0:1, 0:48] = as_row(gqkv[:, 2048:2049])
    gnorm[1:2, 0:48] = as_row(gqkv[:, 2049:2050])
    stores.append(pltpu.make_async_copy(gnorm, gnorm_out, load_sem.at[5]))
    stores[5].start()
    out_sum.close()
    key_sum.close()
    rest_sum.close()
    for piece in proj:
        piece.close()

    def close(k, carry):
        f = (b + 16 - k) % 16
        for n in range(2):
            left(dwin.at[0, :, pl.ds(0, 384)], asend.at[k, n], me)
            col = pl.multiple_of(n * 768 + (f % 2) * 384, 128)
            arrived(gup.at[f // 2, :, pl.ds(col, 384)], arecv.at[f, n], me)
        pl.when(c == x)(lambda: left(dwout.at[0], osend.at[k], me))
        pl.when(f % 2 == x)(lambda: arrived(gdown.at[f // 2], orecv.at[f // 2], me))
        return carry

    lax.fori_loop(1, 16, close, 0)
    for n in range(2):
        own_piece(n).wait()
    pl.when(c == x)(lambda: own_down().wait())
    for store in stores:
        store.wait()


def run_back(*operands):
    shape = jax.ShapeDtypeStruct
    return pl.pallas_call(
        back_kernel,
        out_shape=(
            shape((128, 1536), F32),
            shape((48, 1536), F32),
            shape((48, 256), F32),
            shape((48, 256), F32),
            shape((8, 128), F32),
            shape((48, 1536), F32),
            shape((8, 48, 1536), BF),
            shape((8, 48, 768), BF),
        ),
        in_specs=[ANY] * 16,
        out_specs=(ANY,) * 8,
        scratch_shapes=[
            pltpu.VMEM(operands[0].shape, jnp.int32),
            pltpu.VMEM((1, 128), F32),
            pltpu.VMEM((8, 1536), F32),
            pltpu.VMEM((8, 128), F32),
            pltpu.VMEM((128, 1536), BF),
            pltpu.VMEM((128, 1536), F32),
            pltpu.VMEM((128, 1536), BF),
            pltpu.VMEM((2, LANES, 128), BF),
            pltpu.VMEM((128, 1536), F32),
            pltpu.VMEM((2, 1, LANES), F32),
            pltpu.VMEM((128, 1536), F32),
            pltpu.VMEM((128, 1536), F32),
            pltpu.VMEM((128, 1536), F32),
            pltpu.VMEM((48, 1536), F32),
            pltpu.VMEM((48, 512), F32),
            pltpu.VMEM((32, 48, WIDE), BF),
            pltpu.VMEM((32, 48, 1536), BF),
            pltpu.VMEM((32, 128, 512), BF),
            pltpu.VMEM((32, 128, 512), BF),
            pltpu.VMEM((32, 48, WIDE), BF),
            pltpu.VMEM((2, LANES, 128), BF),
            pltpu.VMEM((2, 1, LANES), F32),
            pltpu.VMEM((128, 1536), F32),
            pltpu.VMEM((2, 128, LANES), F32),
            pltpu.VMEM((128, 512), F32),
            pltpu.VMEM((128, QKV), BF),
            pltpu.VMEM((48, WIDE), F32),
        ]
        + Sum.room(48, 1536)
        + Sum.room(128, 512)
        + Sum.room(48, 768)
        + Sum.room(48, 768)
        + Sum.room(48, LAST[1])
        + [DMA((11,)), DMA((6,)), DMA((16, 2)), DMA((16, 2)), DMA((16,)), DMA((8,))],
        compiler_params=params(3, 62),
        name="back",
    )(*operands)


def finish_kernel(
    err_in, gnorm_in, final, gx, gqw, gkw, gvw, gout, gup, gdown,
    loss_out, one_out, two_out, final_out, gx_out, gqw_out, gkw_out, gvw_out, gout_out, gup_out, gdown_out,
    low_up, low_down, wide_up, wide_down, *rest,
):
    rooms, (err, gnorm, loss, one, two, sem, out_sem) = rest[:6], rest[6:]
    whole = (
        (gup, low_up), (gdown, low_down), *zip((final, gx, gqw, gkw, gvw, gout), rooms), (err_in, err), (gnorm_in, gnorm)
    )
    copies = [pltpu.make_async_copy(src, dst, sem.at[i]) for i, (src, dst) in enumerate(whole)]
    for copy in copies:
        copy.start()
    outs = (final_out, gx_out, gqw_out, gkw_out, gvw_out, gout_out)
    last = []
    for i in range(6):
        copies[2 + i].wait()
        last.append(pltpu.make_async_copy(rooms[i], outs[i], out_sem.at[i]))
        last[i].start()
    copies[0].wait()
    wide_up[...] = low_up[...].astype(F32)
    last.append(pltpu.make_async_copy(wide_up, gup_out, out_sem.at[6]))
    last[6].start()
    copies[1].wait()
    for e in range(E):
        wide = low_down[e].astype(F32)
        wide_down[e, :, :768] = wide[:24]
        wide_down[e, :, 768:] = wide[24:]
    last.append(pltpu.make_async_copy(wide_down, gdown_out, out_sem.at[7]))
    last[7].start()
    copies[8].wait()
    copies[9].wait()
    loss[...] = err[0:1, 0:1]
    one[...] = gnorm[0:1, 0:48]
    two[...] = gnorm[1:2, 0:48]
    for i, (src, dst) in enumerate(((loss, loss_out), (one, one_out), (two, two_out))):
        last.append(pltpu.make_async_copy(src, dst, out_sem.at[8 + i]))
        last[8 + i].start()
    for copy in last:
        copy.wait()


def run_finish(*operands):
    shape = jax.ShapeDtypeStruct
    up, down = (8, 48, 1536), (8, 24, 1536)
    return pl.pallas_call(
        finish_kernel,
        out_shape=(
            shape((1, 1), F32),
            shape((1, 48), F32),
            shape((1, 48), F32),
            shape((128, 1536), BF),
            shape((128, 1536), F32),
            shape((48, 1536), F32),
            shape((48, 256), F32),
            shape((48, 256), F32),
            shape((48, 1536), F32),
            shape(up, F32),
            shape(down, F32),
        ),
        in_specs=[ANY] * 10,
        out_specs=(ANY,) * 11,
        scratch_shapes=[
            pltpu.VMEM(up, BF),
            pltpu.VMEM((8, 48, 768), BF),
            pltpu.VMEM(up, F32),
            pltpu.VMEM(down, F32),
            pltpu.VMEM((128, 1536), BF),
            pltpu.VMEM((128, 1536), F32),
            pltpu.VMEM((48, 1536), F32),
            pltpu.VMEM((48, 256), F32),
            pltpu.VMEM((48, 256), F32),
            pltpu.VMEM((48, 1536), F32),
            pltpu.VMEM((8, 128), F32),
            pltpu.VMEM((8, 128), F32),
            pltpu.VMEM((1, 1), F32),
            pltpu.VMEM((1, 48), F32),
            pltpu.VMEM((1, 48), F32),
            DMA((10,)),
            DMA((11,)),
        ],
        compiler_params=pltpu.CompilerParams(vmem_limit_bytes=60 << 20),
        name="finish",
    )(*operands)


def per_device(
    states, teacher, valid, routes, gates, doc_starts, norm_one,
    w_query, key_weight, value_weight, w_output, norm_two, expert_in, expert_out,
):
    tokens = states.shape[2]
    width = states.shape[3]
    half = HEAD_SIZE // 2
    freq = np.float32(ROTARY_BASE) ** (-np.arange(half).astype(np.float32) / np.float32(half))
    freq = jnp.asarray(np.concatenate([freq, freq])[None, :], F32)
    rows = states.reshape(tokens, width)
    kept = valid.reshape(1, tokens)
    doc = doc_starts.reshape(1, -1)
    gq, go, kv, win, wout, h, n2, n1, qs, o, lse, count, gains = run_front(
        doc, freq, norm_one.reshape(1, -1), norm_two.reshape(1, -1), kept, rows, expert_out,
        w_query, key_weight, value_weight, w_output, expert_in,
    )
    error, final, dn2, dy, dwin, dwout = run_experts(
        routes.reshape(tokens, TOP).T, gates.reshape(tokens, TOP).T, kept, count,
        n2, h, teacher.reshape(tokens, width), win, wout,
    )
    gx, gqw, gkw, gvw, gnorm, gout, gup, gdown = run_back(
        doc, freq, gains, rows, h, n1, qs, o, lse, dn2, dy, dwin.reshape(16, 48, 768), dwout, gq, go, kv
    )
    loss, one, two, final, gx, gqw, gkw, gvw, gout, gup, gdown = run_finish(
        error, gnorm, final, gx, gqw, gkw, gvw, gout, gup, gdown
    )
    shape = states.shape
    return (
        final.reshape(shape),
        loss.reshape(()),
        gx.reshape(shape),
        one.reshape(-1),
        gqw,
        gkw,
        gvw,
        gout,
        two.reshape(-1),
        gup,
        gdown,
    )


def solution(mesh):
    in_specs = (
        P("blk", "head", None, None),
        P("blk", "head", None, None),
        P("blk", "head", None),
        P("blk", "head", None, None),
        P("blk", "head", None, None),
        P(),
        P(("head", "blk")),
        P(("head", "blk"), None),
        P(("head", "blk"), None),
        P(("head", "blk"), None),
        P(("head", "blk"), None),
        P(("head", "blk")),
        P(None, ("head", "blk"), None),
        P(None, ("head", "blk"), None),
    )
    out_specs = (
        P("blk", "head", None, None),
        P(),
        P("blk", "head", None, None),
        P(("head", "blk")),
        P(("head", "blk"), None),
        P(("head", "blk"), None),
        P(("head", "blk"), None),
        P(("head", "blk"), None),
        P(("head", "blk")),
        P(None, ("head", "blk"), None),
        P(None, ("head", "blk"), None),
    )
    sizes = dict(mesh.shape)
    plan = per_device if sizes == {"head": 2, "blk": 4 * NZ} else per_device_plain
    return jax.shard_map(
        plan, mesh=mesh, in_specs=in_specs, out_specs=out_specs, check_vma=False
    )
```

```python
import functools

import jax
import jax.numpy as jnp
import numpy as np
from jax import lax
from jax.experimental import pallas as pl
from jax.experimental.pallas import tpu as pltpu
from jax.sharding import PartitionSpec as P

QUERY_HEADS = 12
KEY_VALUE_HEADS = 2
HEAD_SIZE = 128
TOP = 4
E = 8
CAP = 96

ROTARY_BASE = 10000.0
FLOOR_SCORE = -1e30

MESH = pl.DeviceIdType.MESH
NZ = 4
SPAN = 32 * 128.0
BF = jnp.bfloat16
F32 = jnp.float32

def product(left, right):
    return jnp.dot(left, right, preferred_element_type=jnp.float32)


def rms_norm(values, gain):
    scale = lax.rsqrt(jnp.mean(values * values, axis=-1, keepdims=True) + 1e-06)
    return values * scale * gain


def rotary_apply(values, where, sign):
    half = values.shape[-1] // 2
    freq = ROTARY_BASE ** (-jnp.arange(half).astype(jnp.float32) / half)
    angle = where.astype(jnp.float32)[:, None] * freq[None, :]
    cosine = jnp.cos(angle)[:, None, :]
    sine = jnp.sin(angle)[:, None, :] * sign
    first = values[..., :half]
    second = values[..., half:]
    return jnp.concatenate(
        [first * cosine - second * sine, second * cosine + first * sine], axis=-1
    )


def doc_layout(position_index, doc_starts):
    inside = (position_index[:, None] >= doc_starts[None, :]).astype(jnp.int32)
    document_segment = jnp.sum(inside, axis=-1) - 1
    begin = jnp.max(jnp.where(inside > 0, doc_starts[None, :], 0), axis=-1)
    return (document_segment, position_index - begin)


def gated(pair):
    half = pair.shape[-1] // 2
    return jax.nn.gelu(pair[..., :half], approximate=True) * pair[..., half:]


def in_blocks(step_fn, carry, piece, rows):
    count_blocks = piece[0].shape[0] // rows

    def turn(number, state):
        part = tuple((lax.dynamic_slice_in_dim(item, number * rows, rows, 0) for item in piece))
        return step_fn(state, part, number * rows)

    return lax.fori_loop(0, count_blocks, turn, carry)


def per_device_plain(
    states,
    teacher,
    valid,
    routes,
    gates,
    doc_starts,
    norm_one,
    w_query,
    key_weight,
    value_weight,
    w_output,
    norm_two,
    expert_in,
    expert_out,
):
    count_per_token = states.shape[2]
    width = states.shape[3]
    pairs = lax.axis_size("head")
    blocks = lax.axis_size("blk")
    rows = count_per_token * pairs
    span = rows * blocks
    head_group = QUERY_HEADS // KEY_VALUE_HEADS
    scale = HEAD_SIZE ** (-0.5)
    highest = lax.Precision.HIGHEST
    block_index = lax.axis_index("blk")
    pair_index = lax.axis_index("head")
    token_index = (block_index * pairs + pair_index) * count_per_token + jnp.arange(
        count_per_token, dtype=jnp.int32
    )
    unused_segment, token_position = doc_layout(token_index, doc_starts)
    query_index = block_index * rows + jnp.arange(rows, dtype=jnp.int32)
    query_segment, query_where = doc_layout(query_index, doc_starts)
    last_query = block_index * rows + rows - 1
    inputs = states.reshape(count_per_token, width).astype(jnp.float32)
    target = teacher.reshape(count_per_token, width).astype(jnp.float32)
    keep_mask = valid.reshape(count_per_token).astype(jnp.float32)
    route_rows = routes.reshape(count_per_token, TOP)
    gate_rows = gates.reshape(count_per_token, TOP)
    query_w, key_w, value_w, out_w, gain_low_one, gain_low_two = (
        lax.all_gather(w_query, ("head", "blk"), axis=0, tiled=True),
        lax.all_gather(key_weight, ("head", "blk"), axis=0, tiled=True),
        lax.all_gather(value_weight, ("head", "blk"), axis=0, tiled=True),
        lax.all_gather(w_output, ("head", "blk"), axis=0, tiled=True),
        lax.all_gather(norm_one, ("head", "blk"), axis=0, tiled=True),
        lax.all_gather(norm_two, ("head", "blk"), axis=0, tiled=True),
    )
    gain_one = gain_low_one.astype(jnp.float32)
    gain_two = gain_low_two.astype(jnp.float32)
    normed_one = rms_norm(inputs, gain_one)
    normed_low = normed_one.astype(jnp.bfloat16)
    query_lin = product(normed_low, query_w)
    key_linear = product(normed_low, key_w)
    value_linear = product(normed_low, value_w)
    query_rotated = rotary_apply(
        query_lin.reshape(count_per_token, QUERY_HEADS, HEAD_SIZE), token_position, 1.0
    )
    key_rotated = rotary_apply(
        key_linear.reshape(count_per_token, KEY_VALUE_HEADS, HEAD_SIZE), token_position, 1.0
    )
    query_outgoing = query_rotated.astype(jnp.bfloat16).reshape(
        count_per_token, KEY_VALUE_HEADS, head_group * HEAD_SIZE
    )
    key_send = key_rotated.astype(jnp.bfloat16)
    value_outgoing = value_linear.astype(jnp.bfloat16).reshape(
        count_per_token, KEY_VALUE_HEADS, HEAD_SIZE
    )
    query_grp, key_grp, value_grp = (
        lax.all_to_all(query_outgoing, "head", split_axis=1, concat_axis=0, tiled=True),
        lax.all_to_all(key_send, "head", split_axis=1, concat_axis=0, tiled=True),
        lax.all_to_all(value_outgoing, "head", split_axis=1, concat_axis=0, tiled=True),
    )
    query_heads = query_grp.reshape(rows, head_group, HEAD_SIZE)
    key_rows = key_grp.reshape(rows, HEAD_SIZE)
    value_rows = value_grp.reshape(rows, HEAD_SIZE)

    def scores_for(keys, start):
        block_size = keys.shape[0]
        key_index = start + jnp.arange(block_size, dtype=jnp.int32)
        key_segment, unused_where = doc_layout(key_index, doc_starts)
        allowed = (key_index[None, :] <= query_index[:, None]) & (
            key_segment[None, :] == query_segment[:, None]
        )
        raw = (
            jnp.einsum("qhd,kd->hqk", query_heads, keys, preferred_element_type=jnp.float32) * scale
        )
        return (raw, allowed[None])

    def attend(carry, piece, start):
        keys, values = piece

        def work(state):
            running, total, accum = state
            raw, allowed = scores_for(keys, start)
            masked = jnp.where(allowed, raw, FLOOR_SCORE)
            newest = jnp.maximum(running, jnp.max(masked, axis=-1))
            factor = jnp.exp(running - newest)
            weights = jnp.where(allowed, jnp.exp(masked - newest[..., None]), 0.0)
            total = total * factor + jnp.sum(weights, axis=-1)
            update = jnp.einsum(
                "hqk,kd->qhd",
                weights.astype(jnp.bfloat16),
                values,
                preferred_element_type=jnp.float32,
            )
            accum = accum * factor.T[:, :, None] + update
            return (newest, total, accum)

        return lax.cond(start <= last_query, work, lambda state: state, carry)

    start_state = (
        jnp.full((head_group, rows), FLOOR_SCORE, jnp.float32),
        jnp.zeros((head_group, rows), jnp.float32),
        jnp.zeros((rows, head_group, HEAD_SIZE), jnp.float32),
    )
    running, total, accum = in_blocks(
        attend,
        start_state,
        (
            lax.all_gather(key_rows, "blk", axis=0, tiled=True),
            lax.all_gather(value_rows, "blk", axis=0, tiled=True),
        ),
        rows,
    )
    attn_full = accum / total.T[:, :, None]
    log_total = running + jnp.log(total)
    out_send = attn_full.astype(jnp.bfloat16).reshape(rows, 1, head_group * HEAD_SIZE)
    out_tok = lax.all_to_all(out_send, "head", split_axis=0, concat_axis=1, tiled=True).reshape(
        count_per_token, QUERY_HEADS * HEAD_SIZE
    )
    residual = inputs + product(out_tok, out_w)
    normed_two = rms_norm(residual, gain_two)
    normed_two_low = normed_two.astype(jnp.bfloat16)
    up_w, down_w = (
        lax.all_gather(expert_in, ("head", "blk"), axis=1, tiled=True),
        lax.all_gather(expert_out, ("head", "blk"), axis=1, tiled=True),
    )
    route_hot = (route_rows[:, :, None] == jnp.arange(E, dtype=jnp.int32)[None, None, :]).astype(
        jnp.int32
    )
    flat_hot = route_hot.reshape(count_per_token * TOP, E)
    before = jnp.cumsum(flat_hot, axis=0) - flat_hot
    slot = jnp.sum(before * flat_hot, axis=-1).reshape(count_per_token, TOP)
    slot_hot = (slot[:, :, None] == jnp.arange(CAP, dtype=jnp.int32)[None, None, :]).astype(
        jnp.float32
    )
    route_float = route_hot.astype(jnp.float32)
    dispatch = jnp.einsum("tje,tjc->ect", route_float, slot_hot, precision=highest)
    combine = jnp.einsum("tje,tjc,tj->ect", route_float, slot_hot, gate_rows, precision=highest)
    expert_rows = jnp.einsum(
        "ect,td->ecd",
        dispatch.astype(jnp.bfloat16),
        normed_two_low,
        preferred_element_type=jnp.float32,
    ).astype(jnp.bfloat16)
    pair = jnp.einsum("ecd,edf->ecf", expert_rows, up_w, preferred_element_type=jnp.float32)
    hidden_low = gated(pair).astype(jnp.bfloat16)
    expert_result = jnp.einsum(
        "ecf,efd->ecd", hidden_low, down_w, preferred_element_type=jnp.float32
    )
    mixture = jnp.einsum("ect,ecd->td", combine, expert_result, precision=highest)
    final = residual + mixture
    diff = final - target
    local_count = jnp.sum(keep_mask)
    local_error = jnp.sum(keep_mask * jnp.sum(diff * diff, axis=-1))
    count_all, error_all = lax.psum((local_count, local_error), ("head", "blk"))
    loss = error_all / (width * count_all)
    grad_final = keep_mask[:, None] * diff * (span * 1.0 / count_all)
    up_back, down_back = (
        lax.all_gather(expert_in, ("head", "blk"), axis=1, tiled=True),
        lax.all_gather(expert_out, ("head", "blk"), axis=1, tiled=True),
    )
    grad_result = jnp.einsum("ect,td->ecd", combine, grad_final, precision=highest).astype(
        jnp.bfloat16
    )
    grad_down = jnp.einsum(
        "ecf,ecd->efd", hidden_low, grad_result, preferred_element_type=jnp.float32
    )
    grad_hidden = jnp.einsum(
        "ecd,efd->ecf", grad_result, down_back, preferred_element_type=jnp.float32
    )
    unused_value, pull_gate = jax.vjp(gated, pair)
    grad_pair = pull_gate(grad_hidden)[0].astype(jnp.bfloat16)
    grad_up = jnp.einsum("ecd,ecf->edf", expert_rows, grad_pair, preferred_element_type=jnp.float32)
    grad_rows = jnp.einsum("ecf,edf->ecd", grad_pair, up_back, preferred_element_type=jnp.float32)
    grad_normed_two = jnp.einsum("ect,ecd->td", dispatch, grad_rows, precision=highest)
    unused_value, pull_two = jax.vjp(rms_norm, residual, gain_two)
    grad_res_norm, grad_gain_two = pull_two(grad_normed_two)
    grad_residual = grad_final + grad_res_norm
    grad_attn_low = grad_residual.astype(jnp.bfloat16)
    grad_out_w = jnp.einsum("tk,td->kd", out_tok, grad_attn_low, preferred_element_type=jnp.float32)
    output_gradient_token = jnp.einsum(
        "td,kd->tk", grad_attn_low, out_w, preferred_element_type=jnp.float32
    ).astype(jnp.bfloat16)
    grad_out_grp = lax.all_to_all(
        output_gradient_token.reshape(count_per_token, KEY_VALUE_HEADS, head_group * HEAD_SIZE),
        "head",
        split_axis=1,
        concat_axis=0,
        tiled=True,
    ).reshape(rows, head_group, HEAD_SIZE)
    delta = jnp.einsum(
        "qhd,qhd->hq", grad_out_grp.astype(jnp.float32), attn_full, precision=highest
    )

    def attend_back(carry, piece, start):
        keys, values = piece

        def work(state):
            grad_query, grad_keys, grad_values = state
            raw, allowed = scores_for(keys, start)
            weights = jnp.where(allowed, jnp.exp(raw - log_total[..., None]), 0.0)
            grad_weights = jnp.einsum(
                "qhd,kd->hqk", grad_out_grp, values, preferred_element_type=jnp.float32
            )
            grad_raw = (weights * (grad_weights - delta[..., None])).astype(jnp.bfloat16)
            grad_query = (
                grad_query
                + jnp.einsum("hqk,kd->qhd", grad_raw, keys, preferred_element_type=jnp.float32)
                * scale
            )
            key_part = (
                jnp.einsum("hqk,qhd->kd", grad_raw, query_heads, preferred_element_type=jnp.float32)
                * scale
            )
            value_part = jnp.einsum(
                "hqk,qhd->kd",
                weights.astype(jnp.bfloat16),
                grad_out_grp,
                preferred_element_type=jnp.float32,
            )
            block_size = keys.shape[0]
            grad_keys = lax.dynamic_update_slice_in_dim(
                grad_keys,
                lax.dynamic_slice_in_dim(grad_keys, start, block_size, 0) + key_part,
                start,
                0,
            )
            grad_values = lax.dynamic_update_slice_in_dim(
                grad_values,
                lax.dynamic_slice_in_dim(grad_values, start, block_size, 0) + value_part,
                start,
                0,
            )
            return (grad_query, grad_keys, grad_values)

        return lax.cond(start <= last_query, work, lambda state: state, carry)

    back_state = (
        jnp.zeros((rows, head_group, HEAD_SIZE), jnp.float32),
        jnp.zeros((span, HEAD_SIZE), jnp.float32),
        jnp.zeros((span, HEAD_SIZE), jnp.float32),
    )
    grad_query, grad_keys_full, grad_values_full = in_blocks(
        attend_back,
        back_state,
        (
            lax.all_gather(key_rows, "blk", axis=0, tiled=True),
            lax.all_gather(value_rows, "blk", axis=0, tiled=True),
        ),
        rows,
    )
    grad_keys, grad_values = (
        lax.psum_scatter(grad_keys_full, "blk", scatter_dimension=0, tiled=True),
        lax.psum_scatter(grad_values_full, "blk", scatter_dimension=0, tiled=True),
    )
    grad_query_lin = (
        rotary_apply(grad_query, query_where, -1.0)
        .astype(jnp.bfloat16)
        .reshape(rows, 1, head_group * HEAD_SIZE)
    )
    grad_key_lin = rotary_apply(grad_keys.reshape(rows, 1, HEAD_SIZE), query_where, -1.0).astype(
        jnp.bfloat16
    )
    grad_value_lin = grad_values.astype(jnp.bfloat16).reshape(rows, 1, HEAD_SIZE)
    back_query, key_backward, value_backward = (
        lax.all_to_all(grad_query_lin, "head", split_axis=0, concat_axis=1, tiled=True),
        lax.all_to_all(grad_key_lin, "head", split_axis=0, concat_axis=1, tiled=True),
        lax.all_to_all(grad_value_lin, "head", split_axis=0, concat_axis=1, tiled=True),
    )
    back_query = back_query.reshape(count_per_token, QUERY_HEADS * HEAD_SIZE)
    key_backward = key_backward.reshape(count_per_token, KEY_VALUE_HEADS * HEAD_SIZE)
    value_backward = value_backward.reshape(count_per_token, KEY_VALUE_HEADS * HEAD_SIZE)
    grad_query_w = jnp.einsum(
        "td,tk->dk", normed_low, back_query, preferred_element_type=jnp.float32
    )
    grad_key_w = jnp.einsum(
        "td,tk->dk", normed_low, key_backward, preferred_element_type=jnp.float32
    )
    grad_value_w = jnp.einsum(
        "td,tk->dk", normed_low, value_backward, preferred_element_type=jnp.float32
    )
    grad_normed_one = jnp.einsum(
        "tk,dk->td", back_query, query_w, preferred_element_type=jnp.float32
    )
    grad_normed_one = grad_normed_one + jnp.einsum(
        "tk,dk->td", key_backward, key_w, preferred_element_type=jnp.float32
    )
    grad_normed_one = grad_normed_one + jnp.einsum(
        "tk,dk->td", value_backward, value_w, preferred_element_type=jnp.float32
    )
    unused_value, pull_one = jax.vjp(rms_norm, inputs, gain_one)
    grad_in_norm, grad_gain_one = pull_one(grad_normed_one)
    grad_inputs = grad_residual + grad_in_norm
    sums = (
        lax.psum_scatter(grad_query_w, ("head", "blk"), scatter_dimension=0, tiled=True),
        lax.psum_scatter(grad_key_w, ("head", "blk"), scatter_dimension=0, tiled=True),
        lax.psum_scatter(grad_value_w, ("head", "blk"), scatter_dimension=0, tiled=True),
        lax.psum_scatter(grad_out_w, ("head", "blk"), scatter_dimension=0, tiled=True),
        lax.psum_scatter(grad_gain_one, ("head", "blk"), scatter_dimension=0, tiled=True),
        lax.psum_scatter(grad_gain_two, ("head", "blk"), scatter_dimension=0, tiled=True),
        lax.psum_scatter(grad_up, ("head", "blk"), scatter_dimension=1, tiled=True),
        lax.psum_scatter(grad_down, ("head", "blk"), scatter_dimension=1, tiled=True),
    )
    shape = states.shape
    return (
        final.astype(jnp.bfloat16).reshape(shape),
        loss,
        grad_inputs.reshape(shape),
        sums[4],
        sums[0],
        sums[1],
        sums[2],
        sums[3],
        sums[5],
        sums[6],
        sums[7],
    )


class Place:
    def __init__(self):
        self.x = lax.axis_index("head")
        self.b = lax.axis_index("blk")
        self.c = self.b % 2
        self.y = (self.b // 2) % 2
        self.z = self.b // 4

    def near(self, kind):
        x, y, z, c = self.x, self.y, self.z, self.c
        if kind == "up":
            z = jnp.minimum(z + 1, NZ - 1)
        elif kind == "down":
            z = jnp.maximum(z - 1, 0)
        elif kind == "y":
            y = 1 - y
        elif kind == "x":
            x = 1 - x
        elif kind == "c":
            c = 1 - c
        return (x, z * 4 + y * 2 + c)

    def blk(self, z, y, c):
        return z * 4 + y * 2 + c

    def outward(self, j):
        inner = jnp.where(j < 2, 1 - j, j)
        order = jnp.where((self.z == 0) | (self.z == NZ - 1), j, inner)
        return jnp.where(self.z < 2, order, NZ - 1 - order)

    def inward(self, j):
        inner = jnp.where(j == 0, 3, jnp.where(j == 1, 0, jnp.where(j == 2, 2, 1)))
        order = jnp.where((self.z == 0) | (self.z == NZ - 1), NZ - 1 - j, inner)
        return jnp.where(self.z < 2, order, NZ - 1 - order)


def greet_all(me):
    barrier = pltpu.get_barrier_semaphore()

    def one(k, carry):
        pl.semaphore_signal(
            barrier, inc=1, device_id=((me.x + k // 16) % 2, (me.b + k) % 16), device_id_type=MESH
        )
        return carry

    lax.fori_loop(1, 32, one, 0)


def all_greeted():
    pl.semaphore_wait(pltpu.get_barrier_semaphore(), 31)


def remote(src, dst, send, recv, to):
    return pltpu.make_async_remote_copy(
        src_ref=src, dst_ref=dst, send_sem=send, recv_sem=recv, device_id=to, device_id_type=MESH
    )


def arrived(ref, sem, me):
    remote(ref, ref, sem, sem, me.near("c")).wait_recv()


def left(ref, sem, me):
    remote(ref, ref, sem, sem, me.near("c")).wait_send()


class Gather:
    def __init__(self, me, g, index, send, recv, cols=None, causal=False):
        self.me, self.g, self.index, self.send, self.recv, self.causal = me, g, index, send, recv, causal
        start, width = cols or (0, g.shape[2])
        cut = (width // 2 + 127) // 128 * 128
        self.cols = pl.ds(start, width)
        self.first, self.second = pl.ds(start, cut), pl.ds(start + cut, width - cut)

    def place(self, j):
        return self.me.z - j if self.causal else self.me.outward(j)

    def valid(self, j):
        return (j >= 0) & (j <= (self.me.z if self.causal else NZ - 1))

    def ups(self, zz):
        if self.causal:
            return self.me.z < NZ - 1
        return (zz <= self.me.z) & (self.me.z < NZ - 1)

    def downs(self, zz):
        return (zz >= self.me.z) & (self.me.z > 0)

    def put(self, j, kind, n, s, cols=None, slot=0):
        ref = self.g.at[s, :, self.cols if cols is None else cols]
        remote(ref, ref, self.send.at[j, n], self.recv.at[s, slot], self.me.near(kind)).start()

    def wait(self, s):
        arrived(self.g.at[s, :, self.cols], self.recv.at[s, 0], self.me)

    def turn(self, j):
        me, index = self.me, self.index
        x, y, c = me.x, me.y, me.c

        @pl.when(self.valid(j) & (j > 0))
        def _():
            self.wait(index(x, self.place(j), y, c))

        @pl.when(self.valid(j))
        def _():
            zz = self.place(j)
            own = index(x, zz, y, c)
            pl.when(self.ups(zz))(lambda: self.put(j, "up", 0, own))
            if not self.causal:
                pl.when(self.downs(zz))(lambda: self.put(j, "down", 1, own))
            self.put(j, "y", 2, own)
            self.put(j, "x", 3, own)
            self.put(j, "c", 6, own)

        @pl.when(self.valid(j - 1))
        def _():
            i = j - 1
            zp = self.place(i)
            s = index(x, zp, 1 - y, c)
            self.wait(s)
            self.put(i, "x", 4, s, self.first, 0)
            self.put(i, "c", 7, s)
            t = index(1 - x, zp, y, c)
            self.wait(t)
            self.put(i, "y", 5, t, self.second, 1)
            self.put(i, "c", 8, t)

        @pl.when(self.valid(j - 2))
        def _():
            i = j - 2
            s = index(1 - x, self.place(i), 1 - y, c)
            arrived(self.g.at[s, :, self.first], self.recv.at[s, 0], me)
            arrived(self.g.at[s, :, self.second], self.recv.at[s, 1], me)
            self.put(i, "c", 9, s)

    def from_core(self, j):
        me = self.me
        for xx in (me.x, 1 - me.x):
            for yy in (me.y, 1 - me.y):
                self.wait(self.index(xx, self.place(j), yy, 1 - me.c))

    def close(self, cores=True):
        me = self.me

        def one(j, carry):
            @pl.when(self.valid(j))
            def _():
                zz = self.place(j)
                own = self.index(me.x, zz, me.y, me.c)
                whole = self.g.at[own, :, self.cols]
                first, second = self.g.at[own, :, self.first], self.g.at[own, :, self.second]
                pl.when(self.ups(zz))(lambda: left(whole, self.send.at[j, 0], me))
                if not self.causal:
                    pl.when(self.downs(zz))(lambda: left(whole, self.send.at[j, 1], me))
                for n in (2, 3, 6, 7, 8, 9):
                    left(whole, self.send.at[j, n], me)
                left(first, self.send.at[j, 4], me)
                left(second, self.send.at[j, 5], me)
                if cores:
                    self.from_core(j)

            return carry

        lax.fori_loop(0, 4, one, 0)


class Sum:
    def __init__(self, me, part, index, out, room, sems, cols=None, causal=False):
        self.me, self.part, self.index, self.out, self.causal = me, part, index, out, causal
        start, width = cols or (0, part.shape[2])
        self.cols = pl.ds(start, width)
        self.rc, self.rx, self.ry, self.rn, self.rz, self.acc = room
        self.sc, self.ss, self.vc, self.vn, self.vz = sems
        self.half = (width // 2 + 127) // 128 * 128
        self.first, self.second = pl.ds(0, self.half), pl.ds(self.half, width - self.half)

    @staticmethod
    def room(rows, columns):
        half = (columns // 2 + 127) // 128 * 128
        return [
            pltpu.VMEM((16, rows, columns), BF),
            pltpu.VMEM((4, rows, half), BF),
            pltpu.VMEM((4, rows, columns - half), BF),
            pltpu.VMEM((2, 4, rows, columns), BF),
            pltpu.VMEM((5, rows, columns), BF),
            pltpu.VMEM((rows, columns), F32),
            DMA((16,)),
            DMA((4, 6)),
            DMA((16,)),
            DMA((4, 4)),
            DMA((5,)),
        ]

    def place(self, j):
        return j if self.causal else self.me.inward(j)

    def valid(self, j):
        return (j >= 0) & (j <= (self.me.z if self.causal else NZ - 1))

    def slot(self, xx, zz, yy):
        return zz * 4 + xx * 2 + yy

    def lead(self, j):
        me = self.me
        zz = self.place(j)
        for xx in (1 - me.x, me.x):
            for yy in (1 - me.y, me.y):
                k = self.slot(xx, zz, yy)
                src = self.part.at[self.index(xx, zz, yy, 1 - me.c), :, self.cols]
                remote(src, self.rc.at[k], self.sc.at[k], self.vc.at[k], me.near("c")).start()

    def with_core(self, xx, zz, yy):
        k = self.slot(xx, zz, yy)
        arrived(self.rc.at[k], self.vc.at[k], self.me)
        own = self.part[self.index(xx, zz, yy, self.me.c), :, self.cols]
        return k, own.astype(F32) + self.rc[k].astype(F32)

    def first_leg(self, i):
        me, half, first, second = self.me, self.half, self.first, self.second
        rc, rx, ry, rn, ss, vn = self.rc, self.rx, self.ry, self.rn, self.ss, self.vn
        x, y = me.x, me.y

        @pl.when(self.valid(i))
        def _():
            zz = self.place(i)
            k, total = self.with_core(1 - x, zz, 1 - y)
            rc[k] = total.astype(BF)
            remote(rc.at[k, :, first], rx.at[zz], ss.at[i, 0], vn.at[zz, 0], me.near("x")).start()
            remote(rc.at[k, :, second], ry.at[zz], ss.at[i, 1], vn.at[zz, 1], me.near("y")).start()

    def second_leg(self, i):
        me, half, first, second = self.me, self.half, self.first, self.second
        rc, rx, ry, rn, ss, vn = self.rc, self.rx, self.ry, self.rn, self.ss, self.vn
        x, y = me.x, me.y

        @pl.when(self.valid(i))
        def _():
            zz = self.place(i)
            k, total = self.with_core(x, zz, 1 - y)
            arrived(rx.at[zz], vn.at[zz, 0], me)
            rc[k, :, second] = total[:, half:].astype(BF)
            rc[k, :, first] = (total[:, :half] + rx[zz].astype(F32)).astype(BF)
            remote(rc.at[k], rn.at[0, zz], ss.at[i, 2], vn.at[zz, 2], me.near("y")).start()
            k, total = self.with_core(1 - x, zz, y)
            arrived(ry.at[zz], vn.at[zz, 1], me)
            rc[k, :, first] = total[:, :half].astype(BF)
            rc[k, :, second] = (total[:, half:] + ry[zz].astype(F32)).astype(BF)
            remote(rc.at[k], rn.at[1, zz], ss.at[i, 3], vn.at[zz, 3], me.near("x")).start()

    def third_leg(self, i):
        me, half, first, second = self.me, self.half, self.first, self.second
        rc, rx, ry, rn, ss, vn = self.rc, self.rx, self.ry, self.rn, self.ss, self.vn
        x, y = me.x, me.y

        @pl.when(self.valid(i))
        def _():
            zz = self.place(i)
            k, total = self.with_core(x, zz, y)
            arrived(rn.at[0, zz], vn.at[zz, 2], me)
            arrived(rn.at[1, zz], vn.at[zz, 3], me)
            self.acc[...] = total + rn[0, zz].astype(F32) + rn[1, zz].astype(F32)
            along_z(me, i, zz, self.acc, rc.at[k], self.rz, ss, 4, self.vz, self.causal)

            @pl.when(zz == me.z)
            def _():
                self.out[:, self.cols] = self.acc[...]

    def turn(self, j):
        self.first_leg(j)
        self.second_leg(j - 1)
        self.third_leg(j - 2)

    def first_legs(self):
        def one(j, carry):
            self.first_leg(j)
            return carry

        lax.fori_loop(0, 4, one, 0)

    def rest(self, j):
        self.second_leg(j)
        self.third_leg(j - 1)

    def close(self):
        me = self.me
        whole = self.rc.at[0]
        first, second = self.rc.at[0, :, self.first], self.rc.at[0, :, self.second]

        def one(j, carry):
            @pl.when(self.valid(j))
            def _():
                zz = self.place(j)
                for xx in (1 - me.x, me.x):
                    for yy in (1 - me.y, me.y):
                        left(whole, self.sc.at[self.slot(xx, zz, yy)], me)
                left(first, self.ss.at[j, 0], me)
                left(second, self.ss.at[j, 1], me)
                for n in (2, 3):
                    left(whole, self.ss.at[j, n], me)
                if not self.causal:
                    pl.when(zz > me.z)(lambda: left(whole, self.ss.at[j, 4], me))
                pl.when(zz < me.z)(lambda: left(whole, self.ss.at[j, 5], me))

            return carry

        lax.fori_loop(0, 4, one, 0)


def along_z(me, i, zz, acc, room, rz, ss, n, vz, causal=False):
    z = me.z

    def add(slot):
        arrived(rz.at[slot], vz.at[slot], me)
        acc[...] += rz[slot].astype(F32)

    if not causal:
        pl.when((zz >= z) & (z > 0))(lambda: add(zz))
    pl.when((zz < z) & (z < NZ - 1))(lambda: add(zz))
    pl.when((zz == z) & (z < NZ - 1))(lambda: add(4))

    if not causal:

        @pl.when(zz > z)
        def _():
            room[...] = acc[...].astype(BF)
            remote(room, rz.at[zz], ss.at[i, n], vz.at[zz], me.near("up")).start()

    @pl.when(zz < z)
    def _():
        room[...] = acc[...].astype(BF)
        there = jnp.where(zz == z - 1, 4, zz)
        remote(room, rz.at[there], ss.at[i, n + 1], vz.at[there], me.near("down")).start()


def by_weight(x, z, y, c):
    return x * 16 + z * 4 + y * 2 + c


def by_token(x, z, y, c):
    return (z * 4 + y * 2 + c) * 2 + x


ANY = pl.BlockSpec(memory_space=pl.ANY)
VMEM = pl.BlockSpec(memory_space=pltpu.VMEM)
DMA = pltpu.SemaphoreType.DMA


def params(number, mib):
    return pltpu.CompilerParams(
        collective_id=number, has_side_effects=True, vmem_limit_bytes=mib << 20
    )


NT = (((1,), (1,)), ((), ()))
TN = (((0,), (0,)), ((), ()))
GROUP = QUERY_HEADS // KEY_VALUE_HEADS
LANES = GROUP * 128
SCALE = HEAD_SIZE ** (-0.5)
POWER = SCALE * 1.4426950408889634


def turned(u, cosine, sine):
    return u * cosine + pltpu.roll(u, 64, 1) * sine


def begin_of(place, doc):
    begin = jnp.zeros_like(place)
    for i in range(doc.shape[1]):
        start = doc[0:1, i : i + 1]
        begin = jnp.where(place >= start, jnp.maximum(begin, start), begin)
    return begin


def rotary_tables(me, doc, freq):
    first = (me.b * 2 + me.x) * 128
    place = first + lax.broadcasted_iota(jnp.int32, (128, 128), 0)
    angle = (place - begin_of(place, doc)).astype(F32) * freq[...]
    sine = jnp.sin(angle)
    lane = lax.broadcasted_iota(jnp.int32, (128, 128), 1)
    return jnp.cos(angle), jnp.where(lane < 64, -sine, sine)


def query_bounds(me, doc):
    place = (me.b * 2 + me.x) * 128 + lax.broadcasted_iota(jnp.int32, (1, LANES), 1) % 128
    return begin_of(place, doc), place


def allowed_keys(start, bounds):
    key = start + lax.broadcasted_iota(jnp.int32, (256, LANES), 0)
    return (key >= bounds[0]) & (key <= bounds[1])


def eye(n):
    return lax.broadcasted_iota(jnp.int32, (n, n), 0) == lax.broadcasted_iota(jnp.int32, (n, n), 1)


def as_column(row):
    return jnp.sum(jnp.where(eye(row.shape[1]), row, 0.0), axis=1, keepdims=True)


def as_row(column):
    return jnp.sum(jnp.where(eye(column.shape[0]), column, 0.0), axis=0, keepdims=True)


QKV = 2048
WIDE = QKV + 128
PIECES = ((0, 1152), (1152, 1024))


def front_kernel(
    doc_in, freq_in, one_in, two_in, valid_in, states, down_in, wq, wk, wv, wo, up,
    gq_out, go_out, kv_out, win, wout, h_out, n2_out, n1_out, qs_out, o_out, lse_out, count_out, gains_out,
    doc, freq, norm_one, norm_two, valid, lse, count, gains_row, gq, go, kv, down, top, total, acc, low_rows, down_raw, cos, sin, n1, qs, o, h, n2,
    load_sem, own_sem, qsend, qrecv, gsend, grecv, ksend, krecv, asend, arecv, osend, orecv,
):
    me = Place()
    greet_all(me)
    x, y, z, b, c = me.x, me.y, me.z, me.b, me.c
    here = by_weight(x, z, y, c)
    mine = [
        pltpu.make_async_copy(wq, gq.at[here, :, pl.ds(0, 1536)], own_sem.at[0]),
        pltpu.make_async_copy(wk, gq.at[here, :, pl.ds(1536, 256)], own_sem.at[1]),
        pltpu.make_async_copy(wv, gq.at[here, :, pl.ds(1792, 256)], own_sem.at[2]),
        pltpu.make_async_copy(wo, go.at[here], own_sem.at[3]),
    ]
    pairs = (
        (down_in, down_raw), (states, low_rows), (doc_in, doc), (freq_in, freq),
        (one_in, norm_one), (two_in, norm_two), (valid_in, valid),
    )
    loads = [pltpu.make_async_copy(src, dst, load_sem.at[i]) for i, (src, dst) in enumerate(pairs)]
    for copy in loads[4:] + mine + loads[:4]:
        copy.start()
    for load in loads[4:]:
        load.wait()

    lane = lax.broadcasted_iota(jnp.int32, (48, 128), 1)
    kept = jnp.sum(valid[...].astype(F32))
    extra = jnp.where(
        lane == 0,
        as_column(norm_one[...].astype(F32)),
        jnp.where(lane == 1, as_column(norm_two[...].astype(F32)), jnp.where(lane == 2, kept, 0.0)),
    )
    gq[here, :, pl.ds(QKV, 128)] = extra.astype(BF)
    all_greeted()
    for copy in mine:
        copy.wait()

    def own_piece(n):
        col = pl.multiple_of(n * 768 + c * 384, 128)
        return pltpu.make_async_copy(
            up.at[b // 2, :, pl.ds(col, 384)], win.at[b, :, pl.ds(n * 384, 384)], own_sem.at[4 + n]
        )

    def own_down():
        return pltpu.make_async_copy(down.at[b // 2], wout.at[b], own_sem.at[6])

    def deal(k, carry):
        t = (b + k) % 16
        for n in range(2):
            col = pl.multiple_of(n * 768 + (t % 2) * 384, 128)
            remote(
                up.at[t // 2, :, pl.ds(col, 384)],
                win.at[b, :, pl.ds(n * 384, 384)],
                asend.at[k, n],
                arecv.at[b, n],
                (x, t),
            ).start()
        pl.when(t % 2 == x)(
            lambda: remote(down.at[t // 2], wout.at[b], osend.at[k], orecv.at[b], (x, t)).start()
        )
        return carry

    weights = [
        Gather(me, gq, by_weight, qsend.at[i], qrecv.at[i], PIECES[i]) for i in range(len(PIECES))
    ]

    def first_turn(j, carry):
        for piece in weights:
            piece.turn(j)

        @pl.when(j == 0)
        def _():
            for load in loads[:4]:
                load.wait()
            for e in range(E):
                wide = down_raw[e].astype(F32)
                down[e] = jnp.concatenate([wide[:, :768], wide[:, 768:]], axis=0).astype(BF)
            cos[...], sin[...] = rotary_tables(me, doc, freq)

        lax.fori_loop(1 + j * 3, jnp.minimum(4 + j * 3, 16), deal, 0)
        return carry

    lax.fori_loop(0, 6, first_turn, 0)
    for n in range(2):
        own_piece(n).start()
    pl.when(c == x)(lambda: own_down().start())
    bounds = query_bounds(me, doc)
    rows = low_rows[...].astype(F32)
    level = rows * lax.rsqrt(jnp.mean(rows * rows, axis=-1, keepdims=True) + 1e-06)
    for piece in weights:
        piece.close()
    keep = pltpu.make_async_copy(gq, gq_out, own_sem.at[0])
    keep.start()

    gains = gq[:, :, pl.ds(QKV, 128)].reshape(1536, 128).astype(F32).T
    n1[...] = (level * gains[0:1]).astype(BF)
    turns = cos[...], sin[...]
    at = by_token(x, z, y, c)
    keys = Gather(me, kv, by_token, ksend, krecv, causal=True)
    output = Gather(me, go, by_weight, gsend, grecv)
    both = jnp.dot(n1[...], gq[:, :, pl.ds(1536, 512)].reshape(1536, 512), preferred_element_type=F32)
    for i in range(2):
        kv[at, :, i * 128 : i * 128 + 128] = turned(both[:, i * 128 : i * 128 + 128], *turns).astype(BF)
    kv[at, :, 256:512] = both[:, 256:512].astype(BF)
    keys.turn(0)
    query = jnp.dot(n1[...], gq[:, :, pl.ds(0, 1536)].reshape(1536, 1536), preferred_element_type=F32)
    for i in range(QUERY_HEADS):
        r = (i % GROUP) * 128
        qs[i // GROUP, r : r + 128] = turned(query[:, i * 128 : i * 128 + 128], *turns).astype(BF)
    count[...] = jnp.zeros((8, 128), F32) + jnp.sum(gains[2:3]) / 48.0
    gains_row[...] = gains[0:8]
    saved = [
        pltpu.make_async_copy(count, count_out, load_sem.at[5]),
        pltpu.make_async_copy(gains_row, gains_out, load_sem.at[6]),
        pltpu.make_async_copy(n1, n1_out, load_sem.at[0]),
        pltpu.make_async_copy(qs, qs_out, load_sem.at[1]),
    ]
    for copy in saved:
        copy.start()

    top[...] = jnp.full_like(top, FLOOR_SCORE)
    total[...] = jnp.zeros_like(total)
    acc[...] = jnp.zeros_like(acc)
    def block(n):
        ok = allowed_keys(n * 256, bounds)
        for i in range(2):
            k = kv[pl.ds(n * 2, 2), :, i * 128 : i * 128 + 128].reshape(256, 128)
            v = kv[pl.ds(n * 2, 2), :, 256 + i * 128 : 384 + i * 128].reshape(256, 128)
            s = lax.dot_general(k, qs[i], NT, preferred_element_type=F32)
            s = jnp.where(ok, s, FLOOR_SCORE)
            old = top[i]
            new = jnp.maximum(old, jnp.max(s, axis=0, keepdims=True))
            factor = jnp.exp2((old - new) * POWER)
            p = jnp.exp2((s - new) * POWER)
            top[i] = new
            total[i] = total[i] * factor + jnp.sum(p, axis=0, keepdims=True)
            acc[i] = acc[i] * factor + lax.dot_general(v, p.astype(BF), TN, preferred_element_type=F32)

    def turn(j, carry):
        pl.when(j > 0)(lambda: keys.turn(j))
        output.turn(j - 2)

        @pl.when(keys.valid(j - 2))
        def _():
            i = j - 2
            keys.from_core(i)
            zz = z - i
            last = jnp.where(i == 0, y * 2 + c, 3)

            def one(n, carry):
                block(zz * 4 + last - n)
                return carry

            lax.fori_loop(0, last + 1, one, 0)

        return carry

    lax.fori_loop(0, 8, turn, 0)
    output.close()
    keep_o = pltpu.make_async_copy(go, go_out, own_sem.at[1])
    keep_o.start()
    keep_k = pltpu.make_async_copy(kv, kv_out, own_sem.at[2])
    keep_k.start()
    for i in range(2):
        lse[i] = top[i] * POWER + jnp.log2(total[i])
        done = acc[i] / total[i]
        for r in range(GROUP):
            col = (i * GROUP + r) * 128
            o[:, col : col + 128] = done[:, r * 128 : r * 128 + 128].T
    more = [pltpu.make_async_copy(o, o_out, load_sem.at[2]), pltpu.make_async_copy(lse, lse_out, load_sem.at[7])]
    for copy in more:
        copy.start()
    res = low_rows[...].astype(F32) + jnp.dot(
        o[...].astype(BF), go[...].reshape(1536, 1536), preferred_element_type=F32
    )
    h[...] = res
    n2[...] = (
        res * lax.rsqrt(jnp.mean(res * res, axis=-1, keepdims=True) + 1e-06) * gains[1:2]
    ).astype(BF)
    more.append(pltpu.make_async_copy(h, h_out, load_sem.at[3]))
    more.append(pltpu.make_async_copy(n2, n2_out, load_sem.at[4]))
    more[2].start()
    more[3].start()

    keys.close(False)

    def close(k, carry):
        piece = win.at[b, :, pl.ds(0, 384)]
        f = (b + 16 - k) % 16
        for n in range(2):
            left(piece, asend.at[k, n], me)
            arrived(win.at[f, :, pl.ds(n * 384, 384)], arecv.at[f, n], me)
        pl.when((b + k) % 2 == x)(lambda: left(wout.at[b], osend.at[k], me))
        pl.when(c == x)(lambda: arrived(wout.at[f], orecv.at[f], me))
        return carry

    lax.fori_loop(1, 16, close, 0)
    for n in range(2):
        own_piece(n).wait()
    pl.when(c == x)(lambda: own_down().wait())
    for copy in [keep, keep_o, keep_k] + saved + more:
        copy.wait()


def run_front(*operands):
    shape = jax.ShapeDtypeStruct
    return pl.pallas_call(
        front_kernel,
        out_shape=(
            shape((32, 48, WIDE), BF),
            shape((32, 48, 1536), BF),
            shape((32, 128, 512), BF),
            shape((16, 48, 768), BF),
            shape((16, 48, 768), BF),
            shape((128, 1536), F32),
            shape((128, 1536), BF),
            shape((128, 1536), BF),
            shape((2, LANES, 128), BF),
            shape((128, 1536), F32),
            shape((2, 1, LANES), F32),
            shape((8, 128), F32),
            shape((8, 1536), F32),
        ),
        in_specs=[ANY] * 12,
        out_specs=(ANY,) * 13,
        scratch_shapes=[
            pltpu.VMEM(operands[0].shape, jnp.int32),
            pltpu.VMEM((1, 128), F32),
            pltpu.VMEM((1, 48), BF),
            pltpu.VMEM((1, 48), BF),
            pltpu.VMEM((1, 128), jnp.int32),
            pltpu.VMEM((2, 1, LANES), F32),
            pltpu.VMEM((8, 128), F32),
            pltpu.VMEM((8, 1536), F32),
            pltpu.VMEM((32, 48, WIDE), BF),
            pltpu.VMEM((32, 48, 1536), BF),
            pltpu.VMEM((32, 128, 512), BF),
            pltpu.VMEM((8, 48, 768), BF),
            pltpu.VMEM((2, 1, LANES), F32),
            pltpu.VMEM((2, 1, LANES), F32),
            pltpu.VMEM((2, 128, LANES), F32),
            pltpu.VMEM((128, 1536), BF),
            pltpu.VMEM((8, 24, 1536), BF),
            pltpu.VMEM((128, 128), F32),
            pltpu.VMEM((128, 128), F32),
            pltpu.VMEM((128, 1536), BF),
            pltpu.VMEM((2, LANES, 128), BF),
            pltpu.VMEM((128, 1536), F32),
            pltpu.VMEM((128, 1536), F32),
            pltpu.VMEM((128, 1536), BF),
            DMA((8,)),
            DMA((7,)),
            DMA((2, 4, 10)),
            DMA((2, 32, 2)),
            DMA((4, 10)),
            DMA((32, 2)),
            DMA((4, 10)),
            DMA((32, 2)),
            DMA((16, 2)),
            DMA((16, 2)),
            DMA((16,)),
            DMA((16,)),
        ],
        compiler_params=params(1, 62),
        name="front",
    )(*operands)


GELU_A = 0.7978845608028654
GELU_B = 0.044715


PARTS = ((0, 64), (64, 48), (112, 16))
CUTS = 2


def experts_kernel(
    routes_in, gates_in, valid_in, count_in, n2, h_in, teacher_in, win, wout,
    err_out, final_out, dn2_out, dy_out, dwin_out, dwout_out,
    routes, gates, valid, count, err, h, teacher, final, dy, nall, dyall, pairs, zg, dpairs, part, rc, ry, rz, rzt, ryt, tail, acc, errs, tables, gate,
    wfull, slab, wdown, dwin, dwin_in, dwout, dwout_in,
    load_sem, own_sem, gsend, grecv, csend, crecv, ysend, yrecv, zsend, zrecv, esend, erecv,
    tsend, trecv, xsend, xrecv,
):
    me = Place()
    greet_all(me)
    x, y, z, b, c = me.x, me.y, me.z, me.b, me.c
    half = pltpu.make_async_copy(win, wfull.at[x], own_sem.at[0])
    half.start()
    loads = [
        pltpu.make_async_copy(n2, nall.at[b], load_sem.at[0]),
        pltpu.make_async_copy(h_in, h, load_sem.at[1]),
        pltpu.make_async_copy(teacher_in, teacher, load_sem.at[2]),
        pltpu.make_async_copy(routes_in, routes, load_sem.at[3]),
        pltpu.make_async_copy(gates_in, gates, load_sem.at[4]),
        pltpu.make_async_copy(valid_in, valid, load_sem.at[5]),
        pltpu.make_async_copy(count_in, count, load_sem.at[6]),
    ]
    for load in loads:
        load.start()
    held = pltpu.make_async_copy(wout, slab, own_sem.at[1])
    pl.when(c == x)(held.start)
    all_greeted()

    def rows_of(p):
        return pl.ds(*PARTS[p])

    def over_weights(k):
        cut = pl.ds(k * 4, 4)
        return remote(win.at[cut], wfull.at[x, cut], xsend.at[k], xrecv.at[k], me.near("x"))

    def over_down():
        return remote(wout, slab, xsend.at[4], xrecv.at[4], me.near("x"))

    def put(buf, way, j, p, kind, n, s):
        ref = buf.at[s, rows_of(p)]
        remote(ref, ref, gsend.at[way, j, p, n], grecv.at[way, s, p], me.near(kind)).start()

    def along(buf, way, j, p, n, s, zz):
        pl.when((zz <= z) & (z < NZ - 1))(lambda: put(buf, way, j, p, "up", n, s))
        pl.when((zz >= z) & (z > 0))(lambda: put(buf, way, j, p, "down", n + 1, s))

    def begin(buf, way, p):
        along(buf, way, 0, p, 0, b, z)
        put(buf, way, 0, p, "y", 2, b)
        put(buf, way, 0, p, "c", 3, b)

    def gather(buf, way, between):
        def turn(j, carry):
            between(j, -1)
            for p in range(CUTS + 1):
                zz = me.outward(j)
                own = me.blk(zz, y, c)

                @pl.when((j > 0) & (j < 4))
                def _():
                    arrived(buf.at[own, rows_of(p)], grecv.at[way, own, p], me)

                @pl.when((j > 0) & (j < 4))
                def _():
                    along(buf, way, j, p, 0, own, zz)
                    if p < CUTS:
                        put(buf, way, j, p, "y", 2, own)
                    put(buf, way, j, p, "c", 3, own)

                @pl.when((j > 0) & (j < 5))
                def _():
                    i = j - 1
                    zp = me.outward(i)
                    s = me.blk(zp, 1 - y, c)
                    arrived(buf.at[s, rows_of(p)], grecv.at[way, s, p], me)
                    if p == CUTS:
                        along(buf, way, i, p, 5, s, zp)
                    put(buf, way, i, p, "c", 4, s)

                between(j, p)
            return carry

        lax.fori_loop(0, 6, turn, 0)

        def close(j, carry):
            zz = me.outward(j)
            for p in range(CUTS + 1):
                whole = buf.at[b, rows_of(p)]
                ends = (0, 1) if p < CUTS else (0, 1, 5, 6)
                for n in ends:
                    ok = (zz <= z) & (z < NZ - 1) if n in (0, 5) else (zz >= z) & (z > 0)
                    pl.when(ok)(lambda: left(whole, gsend.at[way, j, p, n], me))
                if p < CUTS:
                    left(whole, gsend.at[way, j, p, 2], me)
                else:
                    pl.when(j == 0)(lambda: left(whole, gsend.at[way, j, p, 2], me))
                for n in (3, 4):
                    left(whole, gsend.at[way, j, p, n], me)
            return carry

        lax.fori_loop(0, 4, close, 0)

    def from_core(buf, way, zz, yy):
        s = me.blk(zz, yy, 1 - c)
        for p in range(CUTS + 1):
            arrived(buf.at[s, rows_of(p)], grecv.at[way, s, p], me)

    def to_other_core(way, q):
        remote(part.at[q * 2 + 1 - c], rc.at[q], csend.at[way, q], crecv.at[way, q], me.near("c")).start()

    def lead(way, j):
        zz = me.inward(j)
        q = zz * 2 + 1 - y
        s = q * 2 + c
        arrived(rc.at[q], crecv.at[way, q], me)
        part[s] = (part[s].astype(F32) + rc[q].astype(F32)).astype(BF)
        for p in range(CUTS):
            remote(
                part.at[s, rows_of(p)], ry.at[zz, rows_of(p)], ysend.at[way, j, p], yrecv.at[way, zz, p], me.near("y")
            ).start()

    def follow(way, j, done=None):
        zz = me.inward(j)
        q = zz * 2 + y
        s = q * 2 + c
        arrived(rc.at[q], crecv.at[way, q], me)
        cut = rows_of(CUTS)
        for n, yy in enumerate((1 - y, y)):
            k = zz * 2 + yy
            room = part.at[k * 2 + c, cut]
            if n:
                tail[...] = room[...].astype(F32) + rc[k, cut].astype(F32)
            else:
                tail[...] = room[...].astype(F32)
            along_z(
                me, j, zz, tail, room, rzt.at[n], zsend.at[way, :, CUTS + n], 0, zrecv.at[way, :, CUTS + n]
            )
            if n == 0:

                @pl.when(zz == z)
                def _():
                    room[...] = tail[...].astype(BF)
                    remote(room, ryt, ysend.at[way, 3, CUTS], yrecv.at[way, 0, CUTS], me.near("y")).start()

        for p in range(CUTS):
            cut = rows_of(p)
            arrived(ry.at[zz, cut], yrecv.at[way, zz, p], me)
            piece = acc.at[cut]
            piece[...] = part[s, cut].astype(F32) + rc[q, cut].astype(F32) + ry[zz, cut].astype(F32)
            along_z(
                me, j, zz, piece, part.at[s, cut], rz.at[:, cut], zsend.at[way, :, p], 0, zrecv.at[way, :, p]
            )
            if done is not None:
                pl.when(zz == z)(functools.partial(done, p))

        @pl.when(zz == z)
        def _():
            arrived(ryt, yrecv.at[way, 0, CUTS], me)
            acc[rows_of(CUTS)] = tail[...] + ryt[...].astype(F32)
            if done is not None:
                done(CUTS)

    def close_sum(way):
        def close(j, carry):
            zz = me.inward(j)
            whole = part.at[b]
            left(whole, csend.at[way, j], me)
            left(whole, csend.at[way, j + 4], me)
            for p in range(CUTS + 2):
                piece = part.at[b, rows_of(min(p, CUTS))]
                if p < CUTS:
                    left(piece, ysend.at[way, j, p], me)
                elif p == CUTS:
                    pl.when(j == 3)(lambda: left(piece, ysend.at[way, j, p], me))
                pl.when(zz > z)(lambda: left(piece, zsend.at[way, j, p, 0], me))
                pl.when(zz < z)(lambda: left(piece, zsend.at[way, j, p, 1], me))
            return carry

        lax.fori_loop(0, 4, close, 0)

    def gelu_parts(g):
        t = jnp.tanh(GELU_A * (g + GELU_B * g * g * g))
        return t, 0.5 * g * (1.0 + t)

    def forward(q):
        rows = nall[pl.ds(q * 2, 2)].reshape(256, 1536)
        pair = jnp.dot(rows, wfull[...].reshape(1536, 768), preferred_element_type=F32)
        pairs[q] = pair
        unused, a = gelu_parts(pair[:, :384])
        scale = gate[pl.ds(q * 2, 2)].reshape(256, 1)
        zq = (a * pair[:, 384:] * scale).astype(BF)
        zg[q] = zq
        out = jnp.dot(zq, wdown[...], preferred_element_type=F32)
        part[pl.ds(q * 2, 2)] = out.astype(BF).reshape(2, 128, 1536)
        to_other_core(0, q)

    def backward(q):
        rows = dyall[pl.ds(q * 2, 2)].reshape(256, 1536)
        scale = gate[pl.ds(q * 2, 2)].reshape(256, 1)
        dz = lax.dot_general(rows, wdown[...], NT, preferred_element_type=F32) * scale
        g, u = pairs[q, :, :384], pairs[q, :, 384:]
        t, a = gelu_parts(g)
        slope = 0.5 * (1.0 + t) + 0.5 * g * (1.0 - t * t) * (GELU_A * (1.0 + 3.0 * GELU_B * g * g))
        dpairs[q, :, :384] = (dz * u * slope).astype(BF)
        dpairs[q, :, 384:] = (dz * a).astype(BF)
        out = lax.dot_general(dpairs[q], wfull[...].reshape(1536, 768), NT, preferred_element_type=F32)
        part[pl.ds(q * 2, 2)] = out.astype(BF).reshape(2, 128, 1536)
        to_other_core(1, q)

    loads[0].wait()
    pl.when(c == x)(held.wait)

    def tell_gates(k, carry):
        to = (b + k) % 16
        remote(tables.at[b], tables.at[b], tsend.at[k], trecv.at[b], (x, to)).start()
        return carry

    def with_tokens(j, p):
        if p == 0:
            pl.when((j == 0) & (c == x))(lambda: over_down().start())
            for k in range(4):
                pl.when(j == k)(over_weights(k).start)
        elif p == 1:

            @pl.when(j == 0)
            def _():
                for load in loads[3:]:
                    load.wait()
                expert = lax.broadcasted_iota(jnp.int32, (8, 128), 0)
                table = jnp.zeros((8, 128), F32)
                for k in range(TOP):
                    table = table + jnp.where(routes[k : k + 1, :] == expert, gates[k : k + 1, :], 0.0)
                tables[b] = table
                lax.fori_loop(1, 16, tell_gates, 0)

    for p in range(CUTS + 1):
        begin(nall, 0, p)
    gather(nall, 0, with_tokens)

    def all_cores(buf, way):
        def one(j, carry):
            from_core(buf, way, j, y)
            from_core(buf, way, j, 1 - y)
            return carry

        lax.fori_loop(0, 4, one, 0)

    all_cores(nall, 0)
    def hear_gates(k, carry):
        left(tables.at[0], tsend.at[k], me)
        arrived(tables.at[(b + 16 - k) % 16], trecv.at[(b + 16 - k) % 16], me)
        return carry

    lax.fori_loop(1, 16, hear_gates, 0)

    def gate_of(s, carry):
        row = lax.broadcasted_iota(jnp.int32, (8, 128), 0)
        picked = jnp.sum(jnp.where(row == b // 2, tables[s], 0.0), axis=0, keepdims=True)
        gate[s] = as_column(picked)
        return carry

    lax.fori_loop(0, 16, gate_of, 0)
    half.wait()
    for k in range(4):
        arrived(wfull.at[1 - x, pl.ds(k * 4, 4)], xrecv.at[k], me)
    pl.when(c != x)(lambda: arrived(slab, xrecv.at[4], me))
    wide = slab[...].astype(F32).reshape(16, 2, 24, 768)
    wdown[:, :768] = wide[:, 0].reshape(384, 768).astype(BF)
    wdown[:, 768:] = wide[:, 1].reshape(384, 768).astype(BF)

    keep = as_column(valid[...].astype(F32))
    factor = keep * (SPAN / count[0:1, 0:1])
    loads[1].wait()
    loads[2].wait()
    me_index = x * 16 + b
    errs[me_index] = jnp.zeros((8, 128), F32)

    def loss_and_dy(p):
        cut, at = rows_of(p), slice(PARTS[p][0], PARTS[p][0] + PARTS[p][1])
        done = h[cut] + acc[cut]
        final[cut] = done.astype(BF)
        diff = done - teacher[cut].astype(F32)
        scaled = factor[at] * diff
        dy[cut] = scaled
        dyall[b, cut] = scaled.astype(BF)
        begin(dyall, 1, p)
        errs[me_index] += jnp.zeros((8, 128), F32) + jnp.sum(keep[at] * diff * diff)

    def outputs(j, carry):
        @pl.when(j < 4)
        def _():
            forward(me.inward(j) * 2 + 1 - y)

        @pl.when((j > 0) & (j < 5))
        def _():
            forward(me.inward(j - 1) * 2 + y)

        pl.when(j < 4)(lambda: lead(0, j))
        pl.when(j > 1)(lambda: follow(0, j - 2, loss_and_dy))
        return carry

    lax.fori_loop(0, 6, outputs, 0)

    saved = [
        pltpu.make_async_copy(final, final_out, load_sem.at[0]),
        pltpu.make_async_copy(dy, dy_out, load_sem.at[1]),
        pltpu.make_async_copy(acc, dn2_out, load_sem.at[2]),
        pltpu.make_async_copy(err, err_out, load_sem.at[3]),
    ]
    for copy in saved[:2]:
        copy.start()
    def tell(k, carry):
        to = ((x + k // 16) % 2, (b + k) % 16)
        remote(errs.at[me_index], errs.at[me_index], esend.at[k], erecv.at[me_index], to).start()
        return carry

    def inputs(i, yy):
        zz = me.outward(i)
        from_core(dyall, 1, zz, yy)
        backward(zz * 2 + yy)

    def with_dy(j, p):
        if p == -1:

            @pl.when(j == 4)
            def _():
                inputs(2, 1 - y)
                inputs(3, y)

            @pl.when(j == 5)
            def _():
                lead(1, 3)
                inputs(3, 1 - y)

        elif p == 0:
            pl.when((j > 0) & (j < 4))(lambda: inputs(j - 1, y))
        elif p == CUTS - 1:

            @pl.when(j == 0)
            def _():
                lax.fori_loop(1, 32, tell, 0)
                close_sum(0)

            pl.when((j > 1) & (j < 4))(lambda: inputs(j - 2, 1 - y))

    gather(dyall, 1, with_dy)

    def in_grad(i):
        col = pl.ds(pl.multiple_of(i * 256, 256), 256)
        rows = nall[:, :, col].reshape(2048, 256)
        dwin[col, :] = lax.dot_general(
            rows, dpairs[...].reshape(2048, 768), TN, preferred_element_type=F32
        ).astype(BF)

    def out_grad(i):
        col = pl.ds(i * 256, 256)
        right = dyall[:, :, col].reshape(2048, 256)
        value = lax.dot_general(zg[...].reshape(2048, 384), right, TN, preferred_element_type=F32)
        there = i // 3 * 24
        dwout[:, there : there + 24, (i % 3) * 256 : (i % 3) * 256 + 256] = value.reshape(16, 24, 256)

    def over_in(k):
        src = dwin.at[pl.ds(pl.multiple_of((1 - x) * 768 + k * 256, 256), 256)]
        return remote(src, dwin_in.at[pl.ds(k * 256, 256)], xsend.at[5 + k], xrecv.at[5 + k], me.near("x"))

    def over_out():
        return remote(slab, dwout_in, xsend.at[8], xrecv.at[8], me.near("x"))

    def leads(j, carry):
        lead(1, j)
        return carry

    lax.fori_loop(0, 3, leads, 0)

    def sums(j, carry):
        @pl.when(j == 0)
        def _():
            for k in range(3):
                in_grad((1 - x) * 3 + k)
                over_in(k).start()

        @pl.when(j == 1)
        def _():
            for k in range(6):
                out_grad(k)
            slab[...] = dwout[...].astype(BF)
            pl.when(c != x)(lambda: over_out().start())

        @pl.when(j == 2)
        def _():
            for k in range(3):
                in_grad(x * 3 + k)

        follow(1, j)
        return carry

    for k in range(4):
        over_weights(k).wait_send()
    pl.when(c == x)(lambda: over_down().wait_send())
    lax.fori_loop(0, 4, sums, 0)
    saved[2].start()
    close_sum(1)

    def hear(k, carry):
        left(errs.at[0], esend.at[k], me)
        s = ((x + k // 16) % 2) * 16 + (b + k) % 16
        arrived(errs.at[s], erecv.at[s], me)
        return carry

    lax.fori_loop(1, 32, hear, 0)
    total = errs[0]
    for s in range(1, 32):
        total = total + errs[s]
    err[...] = total / (1536.0 * count[...])
    saved[3].start()

    for k in range(3):
        over_in(k).wait_send()
        here = pl.ds(pl.multiple_of(x * 768 + k * 256, 256), 256)
        there = pl.ds(k * 256, 256)
        arrived(dwin_in.at[there], xrecv.at[5 + k], me)
        dwin_in[there] = (dwin_in[there].astype(F32) + dwin[here, :].astype(F32)).astype(BF)
    out = pltpu.make_async_copy(dwin_in, dwin_out, own_sem.at[0])
    out.start()

    @pl.when(c == x)
    def _():
        arrived(dwout_in, xrecv.at[8], me)
        dwout_in[...] = (dwout_in[...].astype(F32) + dwout[...]).astype(BF)
        copy = pltpu.make_async_copy(dwout_in, dwout_out, own_sem.at[1])
        copy.start()
        copy.wait()

    pl.when(c != x)(lambda: over_out().wait_send())
    for copy in saved + [out]:
        copy.wait()


def run_experts(*operands):
    wide = (128, 1536)
    shard = (16,) + wide
    shape = jax.ShapeDtypeStruct
    return pl.pallas_call(
        experts_kernel,
        out_shape=(
            shape((8, 128), F32),
            shape(wide, BF),
            shape(wide, F32),
            shape(wide, F32),
            shape((768, 768), BF),
            shape((16, 48, 768), BF),
        ),
        in_specs=[ANY] * 9,
        out_specs=(ANY,) * 6,
        scratch_shapes=[
            pltpu.VMEM((TOP, 128), jnp.int32),
            pltpu.VMEM((TOP, 128), F32),
            pltpu.VMEM((1, 128), jnp.int32),
            pltpu.VMEM((8, 128), F32),
            pltpu.VMEM((8, 128), F32),
            pltpu.VMEM(wide, F32),
            pltpu.VMEM(wide, BF),
            pltpu.VMEM(wide, BF),
            pltpu.VMEM(wide, F32),
            pltpu.VMEM(shard, BF),
            pltpu.VMEM(shard, BF),
            pltpu.VMEM((8, 256, 768), F32),
            pltpu.VMEM((8, 256, 384), BF),
            pltpu.VMEM((8, 256, 768), BF),
            pltpu.VMEM(shard, BF),
            pltpu.VMEM((8,) + wide, BF),
            pltpu.VMEM((4,) + wide, BF),
            pltpu.VMEM((5,) + wide, BF),
            pltpu.VMEM((2, 5, PARTS[CUTS][1], 1536), BF),
            pltpu.VMEM((PARTS[CUTS][1], 1536), BF),
            pltpu.VMEM((PARTS[CUTS][1], 1536), F32),
            pltpu.VMEM(wide, F32),
            pltpu.VMEM((32, 8, 128), F32),
            pltpu.VMEM((16, 8, 128), F32),
            pltpu.VMEM((16, 128, 1), F32),
            pltpu.VMEM((2, 16, 48, 768), BF),
            pltpu.VMEM((16, 48, 768), BF),
            pltpu.VMEM((384, 1536), BF),
            pltpu.VMEM((1536, 768), BF),
            pltpu.VMEM((768, 768), BF),
            pltpu.VMEM((16, 48, 768), F32),
            pltpu.VMEM((16, 48, 768), BF),
            DMA((7,)),
            DMA((2,)),
            DMA((2, 4, CUTS + 1, 7)),
            DMA((2, 16, CUTS + 1)),
            DMA((2, 8)),
            DMA((2, 8)),
            DMA((2, 4, CUTS + 1)),
            DMA((2, 4, CUTS + 1)),
            DMA((2, 4, CUTS + 2, 2)),
            DMA((2, 5, CUTS + 2)),
            DMA((32,)),
            DMA((32,)),
            DMA((16,)),
            DMA((16,)),
            DMA((9,)),
            DMA((9,)),
        ],
        compiler_params=params(2, 62),
        name="experts",
    )(*operands)


def norm_back(values, gain, grad):
    scale = lax.rsqrt(jnp.mean(values * values, axis=-1, keepdims=True) + 1e-06)
    inner = grad * gain
    mean = jnp.mean(inner * values, axis=-1, keepdims=True)
    return scale * inner - values * (scale * scale * scale * mean), jnp.sum(
        grad * values * scale, axis=0, keepdims=True
    )


Q_PIECES = ((0, 768), (768, 768))
LAST = (1536, 640)


def back_kernel(
    doc_in, freq_in, gains_in, states_in, h_in, n1_in, qs_in, o_in, lse_in, dn2_in, dy_in, dwin, dwout, gq, go, kv_in,
    gx_out, gqw, gkw, gvw, gnorm_out, gout_out, gup, gdown,
    doc, freq, gains, gnorm, states, h, n1, qs, o, lse, dn2, dy, gx, gout, gkv,
    wq, wo, kv, pk, pw, dos, delta, dh, dq, dkv, dqkv, gqkv, *rest,
):
    sums = [(rest[i * 11 : i * 11 + 6], rest[i * 11 + 6 : i * 11 + 11]) for i in range(5)]
    load_sem, own_sem, asend, arecv, osend, orecv = rest[55:]
    me = Place()
    greet_all(me)
    x, y, z, b, c = me.x, me.y, me.z, me.b, me.c
    loads = [
        pltpu.make_async_copy(go, wo, own_sem.at[0]),
        pltpu.make_async_copy(kv_in, kv, own_sem.at[1]),
        pltpu.make_async_copy(gq, wq, own_sem.at[2]),
    ]
    small = [
        pltpu.make_async_copy(src, dst, load_sem.at[i])
        for i, (src, dst) in enumerate(
            (
                (h_in, h), (dn2_in, dn2), (dy_in, dy), (o_in, o), (qs_in, qs), (lse_in, lse),
                (n1_in, n1), (states_in, states), (doc_in, doc), (freq_in, freq), (gains_in, gains),
            )
        )
    ]
    for load in small[:3] + [small[10], loads[0]] + small[3:10] + [loads[1], loads[2]]:
        load.start()
    all_greeted()

    def own_piece(n):
        col = pl.multiple_of(n * 768 + c * 384, 128)
        return pltpu.make_async_copy(
            dwin.at[b, :, pl.ds(n * 384, 384)], gup.at[b // 2, :, pl.ds(col, 384)], own_sem.at[3 + n]
        )

    def own_down():
        return pltpu.make_async_copy(dwout.at[b], gdown.at[b // 2], own_sem.at[5])

    def deal(k, carry):
        t = (b + k) % 16
        for n in range(2):
            col = pl.multiple_of(n * 768 + c * 384, 128)
            remote(
                dwin.at[t, :, pl.ds(n * 384, 384)],
                gup.at[b // 2, :, pl.ds(col, 384)],
                asend.at[k, n],
                arecv.at[b, n],
                (x, t),
            ).start()
        pl.when(c == x)(
            lambda: remote(dwout.at[t], gdown.at[b // 2], osend.at[k], orecv.at[b // 2], (x, t)).start()
        )
        return carry

    for n in range(2):
        own_piece(n).start()
    pl.when(c == x)(lambda: own_down().start())
    lax.fori_loop(1, 16, deal, 0)
    for load in small[:3] + small[8:]:
        load.wait()
    res_grad, gain_two = norm_back(h[...], gains[1:2], dn2[...])
    dh[...] = dy[...] + res_grad
    da = dh[...].astype(BF)
    loads[0].wait()
    do = lax.dot_general(
        da, wo[...].reshape(1536, 1536), NT, preferred_element_type=F32
    ).astype(BF)
    small[3].wait()
    low = o[...].astype(BF)
    for i in range(4):
        part = lax.dot_general(low[:, i * 384 : i * 384 + 384], da, TN, preferred_element_type=F32)
        wo[i * 8 : i * 8 + 8] = part.astype(BF).reshape(8, 48, 1536)
    out_sum = Sum(me, wo, by_weight, gout, *sums[0])
    key_sum = Sum(me, pk, by_token, dkv, *sums[1], causal=True)

    def lead_all(which):
        def one(j, carry):
            which.lead(j)
            return carry

        lax.fori_loop(0, 4, one, 0)

    lead_all(out_sum)
    for i in range(QUERY_HEADS):
        col, r = i * 128, (i % GROUP) * 128
        dos[i // GROUP, r : r + 128] = do[:, col : col + 128]
        prod = do[:, col : col + 128].astype(F32) * o[:, col : col + 128]
        delta[i // GROUP, :, r : r + 128] = jnp.sum(prod.T, axis=0, keepdims=True)
    dq[...] = jnp.zeros_like(dq)
    bounds = query_bounds(me, doc)
    loads[1].wait()
    for load in small[4:6]:
        load.wait()

    def block(n):
        ok = allowed_keys(n * 256, bounds)
        for i in range(2):
            k = kv[pl.ds(n * 2, 2), :, i * 128 : i * 128 + 128].reshape(256, 128)
            v = kv[pl.ds(n * 2, 2), :, 256 + i * 128 : 384 + i * 128].reshape(256, 128)
            s = lax.dot_general(k, qs[i], NT, preferred_element_type=F32)
            p = jnp.where(ok, jnp.exp2(s * POWER - lse[i]), 0.0)
            dp = lax.dot_general(v, dos[i], NT, preferred_element_type=F32)
            ds = (p * (dp - delta[i])).astype(BF)
            dv = jnp.dot(p.astype(BF), dos[i], preferred_element_type=F32)
            dk = jnp.dot(ds, qs[i], preferred_element_type=F32) * SCALE
            pk[pl.ds(n * 2, 2), :, i * 128 : i * 128 + 128] = dk.astype(BF).reshape(2, 128, 128)
            pk[pl.ds(n * 2, 2), :, 256 + i * 128 : 384 + i * 128] = dv.astype(BF).reshape(2, 128, 128)
            dq[i] += lax.dot_general(k, ds, TN, preferred_element_type=F32)

    def turn(j, carry):
        out_sum.turn(j)

        @pl.when(key_sum.valid(j))
        def _():
            last = jnp.where(j == z, y * 2 + c, 3)

            def one(n, carry):
                block(j * 4 + n)
                return carry

            lax.fori_loop(0, last + 1, one, 0)

            def blank(n, carry):
                pk[pl.ds((j * 4 + n) * 2, 2)] = jnp.zeros((2, 128, 512), BF)
                return carry

            lax.fori_loop(last + 1, 4, blank, 0)
            key_sum.lead(j)

        key_sum.turn(j)
        return carry

    lax.fori_loop(0, 4, turn, 0)

    cos, sin = rotary_tables(me, doc, freq)
    for load in small[6:8] + [loads[2]]:
        load.wait()
    for i in range(QUERY_HEADS):
        r = (i % GROUP) * 128
        head = dq[i // GROUP, :, r : r + 128].T * SCALE
        dqkv[:, i * 128 : i * 128 + 128] = turned(head, cos, -sin).astype(BF)

    def weight_grad(start, width):
        for i in range(4):
            part = lax.dot_general(
                n1[:, i * 384 : i * 384 + 384], dqkv[:, start : start + width], TN, preferred_element_type=F32
            )
            pw[i * 8 : i * 8 + 8, :, start : start + width] = part.astype(BF).reshape(8, 48, width)

    weight_grad(0, 1536)
    proj = [Sum(me, pw, by_weight, gqkv, *sums[2 + i], Q_PIECES[i]) for i in range(2)]
    rest_sum = Sum(me, pw, by_weight, gqkv, *sums[4], LAST)
    for piece in proj:
        lead_all(piece)

    def last_turn(j, carry):
        out_sum.turn(j + 4)
        pl.when(j < 2)(lambda: key_sum.turn(j + 4))
        for piece in proj:
            piece.turn(j)

        @pl.when(j == 1)
        def _():
            for i in range(2):
                part = dkv[:, i * 128 : i * 128 + 128]
                dqkv[:, 1536 + i * 128 : 1664 + i * 128] = turned(part, cos, -sin).astype(BF)
            dqkv[:, 1792:2048] = dkv[:, 256:512].astype(BF)
            weight_grad(1536, 512)
            dn1 = lax.dot_general(
                dqkv[...], wq[:, :, pl.ds(0, QKV)].reshape(1536, QKV), NT, preferred_element_type=F32
            )
            in_grad, gain_one = norm_back(states[...].astype(F32), gains[0:1], dn1)
            rows = lax.broadcasted_iota(jnp.int32, (128, 1536), 0)
            tail = jnp.where(rows == 0, gain_one, jnp.where(rows == 1, gain_two, 0.0)).T
            pw[:, :, pl.ds(QKV, 128)] = tail.astype(BF).reshape(32, 48, 128)
            lead_all(rest_sum)
            gx[...] = dh[...] + in_grad
            rest_sum.first_legs()

        rest_sum.rest(j - 2)
        return carry

    lax.fori_loop(0, 7, last_turn, 0)
    gkv[...] = gqkv[:, 1536:2048]
    stores = [
        pltpu.make_async_copy(gx, gx_out, load_sem.at[0]),
        pltpu.make_async_copy(gout, gout_out, load_sem.at[1]),
        pltpu.make_async_copy(gqkv.at[:, pl.ds(0, 1536)], gqw, load_sem.at[2]),
        pltpu.make_async_copy(gkv.at[:, pl.ds(0, 256)], gkw, load_sem.at[3]),
        pltpu.make_async_copy(gkv.at[:, pl.ds(256, 256)], gvw, load_sem.at[4]),
    ]
    for store in stores:
        store.start()
    gnorm[0:1, 0:48] = as_row(gqkv[:, 2048:2049])
    gnorm[1:2, 0:48] = as_row(gqkv[:, 2049:2050])
    stores.append(pltpu.make_async_copy(gnorm, gnorm_out, load_sem.at[5]))
    stores[5].start()
    out_sum.close()
    key_sum.close()
    rest_sum.close()
    for piece in proj:
        piece.close()

    def close(k, carry):
        f = (b + 16 - k) % 16
        for n in range(2):
            left(dwin.at[0, :, pl.ds(0, 384)], asend.at[k, n], me)
            col = pl.multiple_of(n * 768 + (f % 2) * 384, 128)
            arrived(gup.at[f // 2, :, pl.ds(col, 384)], arecv.at[f, n], me)
        pl.when(c == x)(lambda: left(dwout.at[0], osend.at[k], me))
        pl.when(f % 2 == x)(lambda: arrived(gdown.at[f // 2], orecv.at[f // 2], me))
        return carry

    lax.fori_loop(1, 16, close, 0)
    for n in range(2):
        own_piece(n).wait()
    pl.when(c == x)(lambda: own_down().wait())
    for store in stores:
        store.wait()


def run_back(*operands):
    shape = jax.ShapeDtypeStruct
    return pl.pallas_call(
        back_kernel,
        out_shape=(
            shape((128, 1536), F32),
            shape((48, 1536), F32),
            shape((48, 256), F32),
            shape((48, 256), F32),
            shape((8, 128), F32),
            shape((48, 1536), F32),
            shape((8, 48, 1536), BF),
            shape((8, 48, 768), BF),
        ),
        in_specs=[ANY] * 16,
        out_specs=(ANY,) * 8,
        scratch_shapes=[
            pltpu.VMEM(operands[0].shape, jnp.int32),
            pltpu.VMEM((1, 128), F32),
            pltpu.VMEM((8, 1536), F32),
            pltpu.VMEM((8, 128), F32),
            pltpu.VMEM((128, 1536), BF),
            pltpu.VMEM((128, 1536), F32),
            pltpu.VMEM((128, 1536), BF),
            pltpu.VMEM((2, LANES, 128), BF),
            pltpu.VMEM((128, 1536), F32),
            pltpu.VMEM((2, 1, LANES), F32),
            pltpu.VMEM((128, 1536), F32),
            pltpu.VMEM((128, 1536), F32),
            pltpu.VMEM((128, 1536), F32),
            pltpu.VMEM((48, 1536), F32),
            pltpu.VMEM((48, 512), F32),
            pltpu.VMEM((32, 48, WIDE), BF),
            pltpu.VMEM((32, 48, 1536), BF),
            pltpu.VMEM((32, 128, 512), BF),
            pltpu.VMEM((32, 128, 512), BF),
            pltpu.VMEM((32, 48, WIDE), BF),
            pltpu.VMEM((2, LANES, 128), BF),
            pltpu.VMEM((2, 1, LANES), F32),
            pltpu.VMEM((128, 1536), F32),
            pltpu.VMEM((2, 128, LANES), F32),
            pltpu.VMEM((128, 512), F32),
            pltpu.VMEM((128, QKV), BF),
            pltpu.VMEM((48, WIDE), F32),
        ]
        + Sum.room(48, 1536)
        + Sum.room(128, 512)
        + Sum.room(48, 768)
        + Sum.room(48, 768)
        + Sum.room(48, LAST[1])
        + [DMA((11,)), DMA((6,)), DMA((16, 2)), DMA((16, 2)), DMA((16,)), DMA((8,))],
        compiler_params=params(3, 62),
        name="back",
    )(*operands)


def finish_kernel(
    err_in, gnorm_in, final, gx, gqw, gkw, gvw, gout, gup, gdown,
    loss_out, one_out, two_out, final_out, gx_out, gqw_out, gkw_out, gvw_out, gout_out, gup_out, gdown_out,
    low_up, low_down, wide_up, wide_down, *rest,
):
    rooms, (err, gnorm, loss, one, two, sem, out_sem) = rest[:6], rest[6:]
    whole = (
        (gup, low_up), (gdown, low_down), *zip((final, gx, gqw, gkw, gvw, gout), rooms), (err_in, err), (gnorm_in, gnorm)
    )
    copies = [pltpu.make_async_copy(src, dst, sem.at[i]) for i, (src, dst) in enumerate(whole)]
    for copy in copies:
        copy.start()
    outs = (final_out, gx_out, gqw_out, gkw_out, gvw_out, gout_out)
    last = []
    for i in range(6):
        copies[2 + i].wait()
        last.append(pltpu.make_async_copy(rooms[i], outs[i], out_sem.at[i]))
        last[i].start()
    copies[0].wait()
    wide_up[...] = low_up[...].astype(F32)
    last.append(pltpu.make_async_copy(wide_up, gup_out, out_sem.at[6]))
    last[6].start()
    copies[1].wait()
    for e in range(E):
        wide = low_down[e].astype(F32)
        wide_down[e, :, :768] = wide[:24]
        wide_down[e, :, 768:] = wide[24:]
    last.append(pltpu.make_async_copy(wide_down, gdown_out, out_sem.at[7]))
    last[7].start()
    copies[8].wait()
    copies[9].wait()
    loss[...] = err[0:1, 0:1]
    one[...] = gnorm[0:1, 0:48]
    two[...] = gnorm[1:2, 0:48]
    for i, (src, dst) in enumerate(((loss, loss_out), (one, one_out), (two, two_out))):
        last.append(pltpu.make_async_copy(src, dst, out_sem.at[8 + i]))
        last[8 + i].start()
    for copy in last:
        copy.wait()


def run_finish(*operands):
    shape = jax.ShapeDtypeStruct
    up, down = (8, 48, 1536), (8, 24, 1536)
    return pl.pallas_call(
        finish_kernel,
        out_shape=(
            shape((1, 1), F32),
            shape((1, 48), F32),
            shape((1, 48), F32),
            shape((128, 1536), BF),
            shape((128, 1536), F32),
            shape((48, 1536), F32),
            shape((48, 256), F32),
            shape((48, 256), F32),
            shape((48, 1536), F32),
            shape(up, F32),
            shape(down, F32),
        ),
        in_specs=[ANY] * 10,
        out_specs=(ANY,) * 11,
        scratch_shapes=[
            pltpu.VMEM(up, BF),
            pltpu.VMEM((8, 48, 768), BF),
            pltpu.VMEM(up, F32),
            pltpu.VMEM(down, F32),
            pltpu.VMEM((128, 1536), BF),
            pltpu.VMEM((128, 1536), F32),
            pltpu.VMEM((48, 1536), F32),
            pltpu.VMEM((48, 256), F32),
            pltpu.VMEM((48, 256), F32),
            pltpu.VMEM((48, 1536), F32),
            pltpu.VMEM((8, 128), F32),
            pltpu.VMEM((8, 128), F32),
            pltpu.VMEM((1, 1), F32),
            pltpu.VMEM((1, 48), F32),
            pltpu.VMEM((1, 48), F32),
            DMA((10,)),
            DMA((11,)),
        ],
        compiler_params=pltpu.CompilerParams(vmem_limit_bytes=60 << 20),
        name="finish",
    )(*operands)


def per_device(
    states, teacher, valid, routes, gates, doc_starts, norm_one,
    w_query, key_weight, value_weight, w_output, norm_two, expert_in, expert_out,
):
    tokens = states.shape[2]
    width = states.shape[3]
    half = HEAD_SIZE // 2
    freq = np.float32(ROTARY_BASE) ** (-np.arange(half).astype(np.float32) / np.float32(half))
    freq = jnp.asarray(np.concatenate([freq, freq])[None, :], F32)
    rows = states.reshape(tokens, width)
    kept = valid.reshape(1, tokens)
    doc = doc_starts.reshape(1, -1)
    gq, go, kv, win, wout, h, n2, n1, qs, o, lse, count, gains = run_front(
        doc, freq, norm_one.reshape(1, -1), norm_two.reshape(1, -1), kept, rows, expert_out,
        w_query, key_weight, value_weight, w_output, expert_in,
    )
    error, final, dn2, dy, dwin, dwout = run_experts(
        routes.reshape(tokens, TOP).T, gates.reshape(tokens, TOP).T, kept, count,
        n2, h, teacher.reshape(tokens, width), win, wout,
    )
    gx, gqw, gkw, gvw, gnorm, gout, gup, gdown = run_back(
        doc, freq, gains, rows, h, n1, qs, o, lse, dn2, dy, dwin.reshape(16, 48, 768), dwout, gq, go, kv
    )
    loss, one, two, final, gx, gqw, gkw, gvw, gout, gup, gdown = run_finish(
        error, gnorm, final, gx, gqw, gkw, gvw, gout, gup, gdown
    )
    shape = states.shape
    return (
        final.reshape(shape),
        loss.reshape(()),
        gx.reshape(shape),
        one.reshape(-1),
        gqw,
        gkw,
        gvw,
        gout,
        two.reshape(-1),
        gup,
        gdown,
    )


def solution(mesh):
    in_specs = (
        P("blk", "head", None, None),
        P("blk", "head", None, None),
        P("blk", "head", None),
        P("blk", "head", None, None),
        P("blk", "head", None, None),
        P(),
        P(("head", "blk")),
        P(("head", "blk"), None),
        P(("head", "blk"), None),
        P(("head", "blk"), None),
        P(("head", "blk"), None),
        P(("head", "blk")),
        P(None, ("head", "blk"), None),
        P(None, ("head", "blk"), None),
    )
    out_specs = (
        P("blk", "head", None, None),
        P(),
        P("blk", "head", None, None),
        P(("head", "blk")),
        P(("head", "blk"), None),
        P(("head", "blk"), None),
        P(("head", "blk"), None),
        P(("head", "blk"), None),
        P(("head", "blk")),
        P(None, ("head", "blk"), None),
        P(None, ("head", "blk"), None),
    )
    sizes = dict(mesh.shape)
    plan = per_device if sizes == {"head": 2, "blk": 4 * NZ} else per_device_plain
    return jax.shard_map(
        plan, mesh=mesh, in_specs=in_specs, out_specs=out_specs, check_vma=False
    )
```

```python
import functools

import jax
import jax.numpy as jnp
import numpy as np
from jax import lax
from jax.experimental import pallas as pl
from jax.experimental.pallas import tpu as pltpu
from jax.sharding import PartitionSpec as P

QUERY_HEADS = 12
KEY_VALUE_HEADS = 2
HEAD_SIZE = 128
TOP = 4
E = 8
CAP = 96

ROTARY_BASE = 10000.0
FLOOR_SCORE = -1e30

MESH = pl.DeviceIdType.MESH
NZ = 4
SPAN = 32 * 128.0
BF = jnp.bfloat16
F32 = jnp.float32

def product(left, right):
    return jnp.dot(left, right, preferred_element_type=jnp.float32)


def rms_norm(values, gain):
    scale = lax.rsqrt(jnp.mean(values * values, axis=-1, keepdims=True) + 1e-06)
    return values * scale * gain


def rotary_apply(values, where, sign):
    half = values.shape[-1] // 2
    freq = ROTARY_BASE ** (-jnp.arange(half).astype(jnp.float32) / half)
    angle = where.astype(jnp.float32)[:, None] * freq[None, :]
    cosine = jnp.cos(angle)[:, None, :]
    sine = jnp.sin(angle)[:, None, :] * sign
    first = values[..., :half]
    second = values[..., half:]
    return jnp.concatenate(
        [first * cosine - second * sine, second * cosine + first * sine], axis=-1
    )


def doc_layout(position_index, doc_starts):
    inside = (position_index[:, None] >= doc_starts[None, :]).astype(jnp.int32)
    document_segment = jnp.sum(inside, axis=-1) - 1
    begin = jnp.max(jnp.where(inside > 0, doc_starts[None, :], 0), axis=-1)
    return (document_segment, position_index - begin)


def gated(pair):
    half = pair.shape[-1] // 2
    return jax.nn.gelu(pair[..., :half], approximate=True) * pair[..., half:]


def in_blocks(step_fn, carry, piece, rows):
    count_blocks = piece[0].shape[0] // rows

    def turn(number, state):
        part = tuple((lax.dynamic_slice_in_dim(item, number * rows, rows, 0) for item in piece))
        return step_fn(state, part, number * rows)

    return lax.fori_loop(0, count_blocks, turn, carry)


def per_device_plain(
    states,
    teacher,
    valid,
    routes,
    gates,
    doc_starts,
    norm_one,
    w_query,
    key_weight,
    value_weight,
    w_output,
    norm_two,
    expert_in,
    expert_out,
):
    count_per_token = states.shape[2]
    width = states.shape[3]
    pairs = lax.axis_size("head")
    blocks = lax.axis_size("blk")
    rows = count_per_token * pairs
    span = rows * blocks
    head_group = QUERY_HEADS // KEY_VALUE_HEADS
    scale = HEAD_SIZE ** (-0.5)
    highest = lax.Precision.HIGHEST
    block_index = lax.axis_index("blk")
    pair_index = lax.axis_index("head")
    token_index = (block_index * pairs + pair_index) * count_per_token + jnp.arange(
        count_per_token, dtype=jnp.int32
    )
    unused_segment, token_position = doc_layout(token_index, doc_starts)
    query_index = block_index * rows + jnp.arange(rows, dtype=jnp.int32)
    query_segment, query_where = doc_layout(query_index, doc_starts)
    last_query = block_index * rows + rows - 1
    inputs = states.reshape(count_per_token, width).astype(jnp.float32)
    target = teacher.reshape(count_per_token, width).astype(jnp.float32)
    keep_mask = valid.reshape(count_per_token).astype(jnp.float32)
    route_rows = routes.reshape(count_per_token, TOP)
    gate_rows = gates.reshape(count_per_token, TOP)
    query_w, key_w, value_w, out_w, gain_low_one, gain_low_two = (
        lax.all_gather(w_query, ("head", "blk"), axis=0, tiled=True),
        lax.all_gather(key_weight, ("head", "blk"), axis=0, tiled=True),
        lax.all_gather(value_weight, ("head", "blk"), axis=0, tiled=True),
        lax.all_gather(w_output, ("head", "blk"), axis=0, tiled=True),
        lax.all_gather(norm_one, ("head", "blk"), axis=0, tiled=True),
        lax.all_gather(norm_two, ("head", "blk"), axis=0, tiled=True),
    )
    gain_one = gain_low_one.astype(jnp.float32)
    gain_two = gain_low_two.astype(jnp.float32)
    normed_one = rms_norm(inputs, gain_one)
    normed_low = normed_one.astype(jnp.bfloat16)
    query_lin = product(normed_low, query_w)
    key_linear = product(normed_low, key_w)
    value_linear = product(normed_low, value_w)
    query_rotated = rotary_apply(
        query_lin.reshape(count_per_token, QUERY_HEADS, HEAD_SIZE), token_position, 1.0
    )
    key_rotated = rotary_apply(
        key_linear.reshape(count_per_token, KEY_VALUE_HEADS, HEAD_SIZE), token_position, 1.0
    )
    query_outgoing = query_rotated.astype(jnp.bfloat16).reshape(
        count_per_token, KEY_VALUE_HEADS, head_group * HEAD_SIZE
    )
    key_send = key_rotated.astype(jnp.bfloat16)
    value_outgoing = value_linear.astype(jnp.bfloat16).reshape(
        count_per_token, KEY_VALUE_HEADS, HEAD_SIZE
    )
    query_grp, key_grp, value_grp = (
        lax.all_to_all(query_outgoing, "head", split_axis=1, concat_axis=0, tiled=True),
        lax.all_to_all(key_send, "head", split_axis=1, concat_axis=0, tiled=True),
        lax.all_to_all(value_outgoing, "head", split_axis=1, concat_axis=0, tiled=True),
    )
    query_heads = query_grp.reshape(rows, head_group, HEAD_SIZE)
    key_rows = key_grp.reshape(rows, HEAD_SIZE)
    value_rows = value_grp.reshape(rows, HEAD_SIZE)

    def scores_for(keys, start):
        block_size = keys.shape[0]
        key_index = start + jnp.arange(block_size, dtype=jnp.int32)
        key_segment, unused_where = doc_layout(key_index, doc_starts)
        allowed = (key_index[None, :] <= query_index[:, None]) & (
            key_segment[None, :] == query_segment[:, None]
        )
        raw = (
            jnp.einsum("qhd,kd->hqk", query_heads, keys, preferred_element_type=jnp.float32) * scale
        )
        return (raw, allowed[None])

    def attend(carry, piece, start):
        keys, values = piece

        def work(state):
            running, total, accum = state
            raw, allowed = scores_for(keys, start)
            masked = jnp.where(allowed, raw, FLOOR_SCORE)
            newest = jnp.maximum(running, jnp.max(masked, axis=-1))
            factor = jnp.exp(running - newest)
            weights = jnp.where(allowed, jnp.exp(masked - newest[..., None]), 0.0)
            total = total * factor + jnp.sum(weights, axis=-1)
            update = jnp.einsum(
                "hqk,kd->qhd",
                weights.astype(jnp.bfloat16),
                values,
                preferred_element_type=jnp.float32,
            )
            accum = accum * factor.T[:, :, None] + update
            return (newest, total, accum)

        return lax.cond(start <= last_query, work, lambda state: state, carry)

    start_state = (
        jnp.full((head_group, rows), FLOOR_SCORE, jnp.float32),
        jnp.zeros((head_group, rows), jnp.float32),
        jnp.zeros((rows, head_group, HEAD_SIZE), jnp.float32),
    )
    running, total, accum = in_blocks(
        attend,
        start_state,
        (
            lax.all_gather(key_rows, "blk", axis=0, tiled=True),
            lax.all_gather(value_rows, "blk", axis=0, tiled=True),
        ),
        rows,
    )
    attn_full = accum / total.T[:, :, None]
    log_total = running + jnp.log(total)
    out_send = attn_full.astype(jnp.bfloat16).reshape(rows, 1, head_group * HEAD_SIZE)
    out_tok = lax.all_to_all(out_send, "head", split_axis=0, concat_axis=1, tiled=True).reshape(
        count_per_token, QUERY_HEADS * HEAD_SIZE
    )
    residual = inputs + product(out_tok, out_w)
    normed_two = rms_norm(residual, gain_two)
    normed_two_low = normed_two.astype(jnp.bfloat16)
    up_w, down_w = (
        lax.all_gather(expert_in, ("head", "blk"), axis=1, tiled=True),
        lax.all_gather(expert_out, ("head", "blk"), axis=1, tiled=True),
    )
    route_hot = (route_rows[:, :, None] == jnp.arange(E, dtype=jnp.int32)[None, None, :]).astype(
        jnp.int32
    )
    flat_hot = route_hot.reshape(count_per_token * TOP, E)
    before = jnp.cumsum(flat_hot, axis=0) - flat_hot
    slot = jnp.sum(before * flat_hot, axis=-1).reshape(count_per_token, TOP)
    slot_hot = (slot[:, :, None] == jnp.arange(CAP, dtype=jnp.int32)[None, None, :]).astype(
        jnp.float32
    )
    route_float = route_hot.astype(jnp.float32)
    dispatch = jnp.einsum("tje,tjc->ect", route_float, slot_hot, precision=highest)
    combine = jnp.einsum("tje,tjc,tj->ect", route_float, slot_hot, gate_rows, precision=highest)
    expert_rows = jnp.einsum(
        "ect,td->ecd",
        dispatch.astype(jnp.bfloat16),
        normed_two_low,
        preferred_element_type=jnp.float32,
    ).astype(jnp.bfloat16)
    pair = jnp.einsum("ecd,edf->ecf", expert_rows, up_w, preferred_element_type=jnp.float32)
    hidden_low = gated(pair).astype(jnp.bfloat16)
    expert_result = jnp.einsum(
        "ecf,efd->ecd", hidden_low, down_w, preferred_element_type=jnp.float32
    )
    mixture = jnp.einsum("ect,ecd->td", combine, expert_result, precision=highest)
    final = residual + mixture
    diff = final - target
    local_count = jnp.sum(keep_mask)
    local_error = jnp.sum(keep_mask * jnp.sum(diff * diff, axis=-1))
    count_all, error_all = lax.psum((local_count, local_error), ("head", "blk"))
    loss = error_all / (width * count_all)
    grad_final = keep_mask[:, None] * diff * (span * 1.0 / count_all)
    up_back, down_back = (
        lax.all_gather(expert_in, ("head", "blk"), axis=1, tiled=True),
        lax.all_gather(expert_out, ("head", "blk"), axis=1, tiled=True),
    )
    grad_result = jnp.einsum("ect,td->ecd", combine, grad_final, precision=highest).astype(
        jnp.bfloat16
    )
    grad_down = jnp.einsum(
        "ecf,ecd->efd", hidden_low, grad_result, preferred_element_type=jnp.float32
    )
    grad_hidden = jnp.einsum(
        "ecd,efd->ecf", grad_result, down_back, preferred_element_type=jnp.float32
    )
    unused_value, pull_gate = jax.vjp(gated, pair)
    grad_pair = pull_gate(grad_hidden)[0].astype(jnp.bfloat16)
    grad_up = jnp.einsum("ecd,ecf->edf", expert_rows, grad_pair, preferred_element_type=jnp.float32)
    grad_rows = jnp.einsum("ecf,edf->ecd", grad_pair, up_back, preferred_element_type=jnp.float32)
    grad_normed_two = jnp.einsum("ect,ecd->td", dispatch, grad_rows, precision=highest)
    unused_value, pull_two = jax.vjp(rms_norm, residual, gain_two)
    grad_res_norm, grad_gain_two = pull_two(grad_normed_two)
    grad_residual = grad_final + grad_res_norm
    grad_attn_low = grad_residual.astype(jnp.bfloat16)
    grad_out_w = jnp.einsum("tk,td->kd", out_tok, grad_attn_low, preferred_element_type=jnp.float32)
    output_gradient_token = jnp.einsum(
        "td,kd->tk", grad_attn_low, out_w, preferred_element_type=jnp.float32
    ).astype(jnp.bfloat16)
    grad_out_grp = lax.all_to_all(
        output_gradient_token.reshape(count_per_token, KEY_VALUE_HEADS, head_group * HEAD_SIZE),
        "head",
        split_axis=1,
        concat_axis=0,
        tiled=True,
    ).reshape(rows, head_group, HEAD_SIZE)
    delta = jnp.einsum(
        "qhd,qhd->hq", grad_out_grp.astype(jnp.float32), attn_full, precision=highest
    )

    def attend_back(carry, piece, start):
        keys, values = piece

        def work(state):
            grad_query, grad_keys, grad_values = state
            raw, allowed = scores_for(keys, start)
            weights = jnp.where(allowed, jnp.exp(raw - log_total[..., None]), 0.0)
            grad_weights = jnp.einsum(
                "qhd,kd->hqk", grad_out_grp, values, preferred_element_type=jnp.float32
            )
            grad_raw = (weights * (grad_weights - delta[..., None])).astype(jnp.bfloat16)
            grad_query = (
                grad_query
                + jnp.einsum("hqk,kd->qhd", grad_raw, keys, preferred_element_type=jnp.float32)
                * scale
            )
            key_part = (
                jnp.einsum("hqk,qhd->kd", grad_raw, query_heads, preferred_element_type=jnp.float32)
                * scale
            )
            value_part = jnp.einsum(
                "hqk,qhd->kd",
                weights.astype(jnp.bfloat16),
                grad_out_grp,
                preferred_element_type=jnp.float32,
            )
            block_size = keys.shape[0]
            grad_keys = lax.dynamic_update_slice_in_dim(
                grad_keys,
                lax.dynamic_slice_in_dim(grad_keys, start, block_size, 0) + key_part,
                start,
                0,
            )
            grad_values = lax.dynamic_update_slice_in_dim(
                grad_values,
                lax.dynamic_slice_in_dim(grad_values, start, block_size, 0) + value_part,
                start,
                0,
            )
            return (grad_query, grad_keys, grad_values)

        return lax.cond(start <= last_query, work, lambda state: state, carry)

    back_state = (
        jnp.zeros((rows, head_group, HEAD_SIZE), jnp.float32),
        jnp.zeros((span, HEAD_SIZE), jnp.float32),
        jnp.zeros((span, HEAD_SIZE), jnp.float32),
    )
    grad_query, grad_keys_full, grad_values_full = in_blocks(
        attend_back,
        back_state,
        (
            lax.all_gather(key_rows, "blk", axis=0, tiled=True),
            lax.all_gather(value_rows, "blk", axis=0, tiled=True),
        ),
        rows,
    )
    grad_keys, grad_values = (
        lax.psum_scatter(grad_keys_full, "blk", scatter_dimension=0, tiled=True),
        lax.psum_scatter(grad_values_full, "blk", scatter_dimension=0, tiled=True),
    )
    grad_query_lin = (
        rotary_apply(grad_query, query_where, -1.0)
        .astype(jnp.bfloat16)
        .reshape(rows, 1, head_group * HEAD_SIZE)
    )
    grad_key_lin = rotary_apply(grad_keys.reshape(rows, 1, HEAD_SIZE), query_where, -1.0).astype(
        jnp.bfloat16
    )
    grad_value_lin = grad_values.astype(jnp.bfloat16).reshape(rows, 1, HEAD_SIZE)
    back_query, key_backward, value_backward = (
        lax.all_to_all(grad_query_lin, "head", split_axis=0, concat_axis=1, tiled=True),
        lax.all_to_all(grad_key_lin, "head", split_axis=0, concat_axis=1, tiled=True),
        lax.all_to_all(grad_value_lin, "head", split_axis=0, concat_axis=1, tiled=True),
    )
    back_query = back_query.reshape(count_per_token, QUERY_HEADS * HEAD_SIZE)
    key_backward = key_backward.reshape(count_per_token, KEY_VALUE_HEADS * HEAD_SIZE)
    value_backward = value_backward.reshape(count_per_token, KEY_VALUE_HEADS * HEAD_SIZE)
    grad_query_w = jnp.einsum(
        "td,tk->dk", normed_low, back_query, preferred_element_type=jnp.float32
    )
    grad_key_w = jnp.einsum(
        "td,tk->dk", normed_low, key_backward, preferred_element_type=jnp.float32
    )
    grad_value_w = jnp.einsum(
        "td,tk->dk", normed_low, value_backward, preferred_element_type=jnp.float32
    )
    grad_normed_one = jnp.einsum(
        "tk,dk->td", back_query, query_w, preferred_element_type=jnp.float32
    )
    grad_normed_one = grad_normed_one + jnp.einsum(
        "tk,dk->td", key_backward, key_w, preferred_element_type=jnp.float32
    )
    grad_normed_one = grad_normed_one + jnp.einsum(
        "tk,dk->td", value_backward, value_w, preferred_element_type=jnp.float32
    )
    unused_value, pull_one = jax.vjp(rms_norm, inputs, gain_one)
    grad_in_norm, grad_gain_one = pull_one(grad_normed_one)
    grad_inputs = grad_residual + grad_in_norm
    sums = (
        lax.psum_scatter(grad_query_w, ("head", "blk"), scatter_dimension=0, tiled=True),
        lax.psum_scatter(grad_key_w, ("head", "blk"), scatter_dimension=0, tiled=True),
        lax.psum_scatter(grad_value_w, ("head", "blk"), scatter_dimension=0, tiled=True),
        lax.psum_scatter(grad_out_w, ("head", "blk"), scatter_dimension=0, tiled=True),
        lax.psum_scatter(grad_gain_one, ("head", "blk"), scatter_dimension=0, tiled=True),
        lax.psum_scatter(grad_gain_two, ("head", "blk"), scatter_dimension=0, tiled=True),
        lax.psum_scatter(grad_up, ("head", "blk"), scatter_dimension=1, tiled=True),
        lax.psum_scatter(grad_down, ("head", "blk"), scatter_dimension=1, tiled=True),
    )
    shape = states.shape
    return (
        final.astype(jnp.bfloat16).reshape(shape),
        loss,
        grad_inputs.reshape(shape),
        sums[4],
        sums[0],
        sums[1],
        sums[2],
        sums[3],
        sums[5],
        sums[6],
        sums[7],
    )


class Place:
    def __init__(self):
        self.x = lax.axis_index("head")
        self.b = lax.axis_index("blk")
        self.c = self.b % 2
        self.y = (self.b // 2) % 2
        self.z = self.b // 4

    def near(self, kind):
        x, y, z, c = self.x, self.y, self.z, self.c
        if kind == "up":
            z = jnp.minimum(z + 1, NZ - 1)
        elif kind == "down":
            z = jnp.maximum(z - 1, 0)
        elif kind == "y":
            y = 1 - y
        elif kind == "x":
            x = 1 - x
        elif kind == "c":
            c = 1 - c
        return (x, z * 4 + y * 2 + c)

    def blk(self, z, y, c):
        return z * 4 + y * 2 + c

    def outward(self, j):
        inner = jnp.where(j < 2, 1 - j, j)
        order = jnp.where((self.z == 0) | (self.z == NZ - 1), j, inner)
        return jnp.where(self.z < 2, order, NZ - 1 - order)

    def inward(self, j):
        inner = jnp.where(j == 0, 3, jnp.where(j == 1, 0, jnp.where(j == 2, 2, 1)))
        order = jnp.where((self.z == 0) | (self.z == NZ - 1), NZ - 1 - j, inner)
        return jnp.where(self.z < 2, order, NZ - 1 - order)


def greet_all(me):
    barrier = pltpu.get_barrier_semaphore()

    def one(k, carry):
        pl.semaphore_signal(
            barrier, inc=1, device_id=((me.x + k // 16) % 2, (me.b + k) % 16), device_id_type=MESH
        )
        return carry

    lax.fori_loop(1, 32, one, 0)


def all_greeted():
    pl.semaphore_wait(pltpu.get_barrier_semaphore(), 31)


def remote(src, dst, send, recv, to):
    return pltpu.make_async_remote_copy(
        src_ref=src, dst_ref=dst, send_sem=send, recv_sem=recv, device_id=to, device_id_type=MESH
    )


def arrived(ref, sem, me):
    remote(ref, ref, sem, sem, me.near("c")).wait_recv()


def left(ref, sem, me):
    remote(ref, ref, sem, sem, me.near("c")).wait_send()


class Gather:
    def __init__(self, me, g, index, send, recv, cols=None, causal=False):
        self.me, self.g, self.index, self.send, self.recv, self.causal = me, g, index, send, recv, causal
        start, width = cols or (0, g.shape[2])
        cut = (width // 2 + 127) // 128 * 128
        self.cols = pl.ds(start, width)
        self.first, self.second = pl.ds(start, cut), pl.ds(start + cut, width - cut)

    def place(self, j):
        return self.me.z - j if self.causal else self.me.outward(j)

    def valid(self, j):
        return (j >= 0) & (j <= (self.me.z if self.causal else NZ - 1))

    def ups(self, zz):
        if self.causal:
            return self.me.z < NZ - 1
        return (zz <= self.me.z) & (self.me.z < NZ - 1)

    def downs(self, zz):
        return (zz >= self.me.z) & (self.me.z > 0)

    def put(self, j, kind, n, s, cols=None, slot=0):
        ref = self.g.at[s, :, self.cols if cols is None else cols]
        remote(ref, ref, self.send.at[j, n], self.recv.at[s, slot], self.me.near(kind)).start()

    def wait(self, s):
        arrived(self.g.at[s, :, self.cols], self.recv.at[s, 0], self.me)

    def turn(self, j):
        me, index = self.me, self.index
        x, y, c = me.x, me.y, me.c

        @pl.when(self.valid(j) & (j > 0))
        def _():
            self.wait(index(x, self.place(j), y, c))

        @pl.when(self.valid(j))
        def _():
            zz = self.place(j)
            own = index(x, zz, y, c)
            pl.when(self.ups(zz))(lambda: self.put(j, "up", 0, own))
            if not self.causal:
                pl.when(self.downs(zz))(lambda: self.put(j, "down", 1, own))
            self.put(j, "y", 2, own)
            self.put(j, "x", 3, own)
            self.put(j, "c", 6, own)

        @pl.when(self.valid(j - 1))
        def _():
            i = j - 1
            zp = self.place(i)
            s = index(x, zp, 1 - y, c)
            self.wait(s)
            self.put(i, "x", 4, s, self.first, 0)
            self.put(i, "c", 7, s)
            t = index(1 - x, zp, y, c)
            self.wait(t)
            self.put(i, "y", 5, t, self.second, 1)
            self.put(i, "c", 8, t)

        @pl.when(self.valid(j - 2))
        def _():
            i = j - 2
            s = index(1 - x, self.place(i), 1 - y, c)
            arrived(self.g.at[s, :, self.first], self.recv.at[s, 0], me)
            arrived(self.g.at[s, :, self.second], self.recv.at[s, 1], me)
            self.put(i, "c", 9, s)

    def from_core(self, j):
        me = self.me
        for xx in (me.x, 1 - me.x):
            for yy in (me.y, 1 - me.y):
                self.wait(self.index(xx, self.place(j), yy, 1 - me.c))

    def from_cores(self):
        def one(j, carry):
            self.from_core(j)
            return carry

        lax.fori_loop(0, 4, one, 0)

    def close(self):
        me = self.me

        def one(j, carry):
            @pl.when(self.valid(j))
            def _():
                zz = self.place(j)
                own = self.index(me.x, zz, me.y, me.c)
                whole = self.g.at[own, :, self.cols]
                first, second = self.g.at[own, :, self.first], self.g.at[own, :, self.second]
                pl.when(self.ups(zz))(lambda: left(whole, self.send.at[j, 0], me))
                if not self.causal:
                    pl.when(self.downs(zz))(lambda: left(whole, self.send.at[j, 1], me))
                for n in (2, 3, 6, 7, 8, 9):
                    left(whole, self.send.at[j, n], me)
                left(first, self.send.at[j, 4], me)
                left(second, self.send.at[j, 5], me)

            return carry

        lax.fori_loop(0, 4, one, 0)


class Sum:
    def __init__(self, me, part, index, out, room, sems, cols=None, causal=False):
        self.me, self.part, self.index, self.out, self.causal = me, part, index, out, causal
        start, width = cols or (0, part.shape[2])
        self.cols = pl.ds(start, width)
        self.rc, self.rx, self.ry, self.rn, self.rz, self.acc = room
        self.sc, self.ss, self.vc, self.vn, self.vz = sems
        self.half = (width // 2 + 127) // 128 * 128
        self.first, self.second = pl.ds(0, self.half), pl.ds(self.half, width - self.half)

    @staticmethod
    def room(rows, columns):
        half = (columns // 2 + 127) // 128 * 128
        return [
            pltpu.VMEM((16, rows, columns), BF),
            pltpu.VMEM((4, rows, half), BF),
            pltpu.VMEM((4, rows, columns - half), BF),
            pltpu.VMEM((2, 4, rows, columns), BF),
            pltpu.VMEM((5, rows, columns), BF),
            pltpu.VMEM((rows, columns), F32),
            DMA((16,)),
            DMA((4, 6)),
            DMA((16,)),
            DMA((4, 4)),
            DMA((5,)),
        ]

    def place(self, j):
        return j if self.causal else self.me.inward(j)

    def valid(self, j):
        return (j >= 0) & (j <= (self.me.z if self.causal else NZ - 1))

    def slot(self, xx, zz, yy):
        return zz * 4 + xx * 2 + yy

    def lead(self, j):
        me = self.me
        zz = self.place(j)
        for xx in (1 - me.x, me.x):
            for yy in (1 - me.y, me.y):
                k = self.slot(xx, zz, yy)
                src = self.part.at[self.index(xx, zz, yy, 1 - me.c), :, self.cols]
                remote(src, self.rc.at[k], self.sc.at[k], self.vc.at[k], me.near("c")).start()

    def with_core(self, xx, zz, yy):
        k = self.slot(xx, zz, yy)
        arrived(self.rc.at[k], self.vc.at[k], self.me)
        own = self.part[self.index(xx, zz, yy, self.me.c), :, self.cols]
        return k, own.astype(F32) + self.rc[k].astype(F32)

    def first_leg(self, i):
        me, half, first, second = self.me, self.half, self.first, self.second
        rc, rx, ry, rn, ss, vn = self.rc, self.rx, self.ry, self.rn, self.ss, self.vn
        x, y = me.x, me.y

        @pl.when(self.valid(i))
        def _():
            zz = self.place(i)
            k, total = self.with_core(1 - x, zz, 1 - y)
            rc[k] = total.astype(BF)
            remote(rc.at[k, :, first], rx.at[zz], ss.at[i, 0], vn.at[zz, 0], me.near("x")).start()
            remote(rc.at[k, :, second], ry.at[zz], ss.at[i, 1], vn.at[zz, 1], me.near("y")).start()

    def second_leg(self, i):
        me, half, first, second = self.me, self.half, self.first, self.second
        rc, rx, ry, rn, ss, vn = self.rc, self.rx, self.ry, self.rn, self.ss, self.vn
        x, y = me.x, me.y

        @pl.when(self.valid(i))
        def _():
            zz = self.place(i)
            k, total = self.with_core(x, zz, 1 - y)
            arrived(rx.at[zz], vn.at[zz, 0], me)
            rc[k, :, second] = total[:, half:].astype(BF)
            rc[k, :, first] = (total[:, :half] + rx[zz].astype(F32)).astype(BF)
            remote(rc.at[k], rn.at[0, zz], ss.at[i, 2], vn.at[zz, 2], me.near("y")).start()
            k, total = self.with_core(1 - x, zz, y)
            arrived(ry.at[zz], vn.at[zz, 1], me)
            rc[k, :, first] = total[:, :half].astype(BF)
            rc[k, :, second] = (total[:, half:] + ry[zz].astype(F32)).astype(BF)
            remote(rc.at[k], rn.at[1, zz], ss.at[i, 3], vn.at[zz, 3], me.near("x")).start()

    def third_leg(self, i):
        me, half, first, second = self.me, self.half, self.first, self.second
        rc, rx, ry, rn, ss, vn = self.rc, self.rx, self.ry, self.rn, self.ss, self.vn
        x, y = me.x, me.y

        @pl.when(self.valid(i))
        def _():
            zz = self.place(i)
            k, total = self.with_core(x, zz, y)
            arrived(rn.at[0, zz], vn.at[zz, 2], me)
            arrived(rn.at[1, zz], vn.at[zz, 3], me)
            self.acc[...] = total + rn[0, zz].astype(F32) + rn[1, zz].astype(F32)
            along_z(me, i, zz, self.acc, rc.at[k], self.rz, ss, 4, self.vz, self.causal)

            @pl.when(zz == me.z)
            def _():
                self.out[:, self.cols] = self.acc[...]

    def turn(self, j):
        self.first_leg(j)
        self.second_leg(j - 1)
        self.third_leg(j - 2)

    def first_legs(self):
        def one(j, carry):
            self.first_leg(j)
            return carry

        lax.fori_loop(0, 4, one, 0)

    def rest(self, j):
        self.second_leg(j)
        self.third_leg(j - 1)

    def close(self):
        me = self.me
        whole = self.rc.at[0]
        first, second = self.rc.at[0, :, self.first], self.rc.at[0, :, self.second]

        def one(j, carry):
            @pl.when(self.valid(j))
            def _():
                zz = self.place(j)
                for xx in (1 - me.x, me.x):
                    for yy in (1 - me.y, me.y):
                        left(whole, self.sc.at[self.slot(xx, zz, yy)], me)
                left(first, self.ss.at[j, 0], me)
                left(second, self.ss.at[j, 1], me)
                for n in (2, 3):
                    left(whole, self.ss.at[j, n], me)
                if not self.causal:
                    pl.when(zz > me.z)(lambda: left(whole, self.ss.at[j, 4], me))
                pl.when(zz < me.z)(lambda: left(whole, self.ss.at[j, 5], me))

            return carry

        lax.fori_loop(0, 4, one, 0)


def along_z(me, i, zz, acc, room, rz, ss, n, vz, causal=False):
    z = me.z

    def add(slot):
        arrived(rz.at[slot], vz.at[slot], me)
        acc[...] += rz[slot].astype(F32)

    if not causal:
        pl.when((zz >= z) & (z > 0))(lambda: add(zz))
    pl.when((zz < z) & (z < NZ - 1))(lambda: add(zz))
    pl.when((zz == z) & (z < NZ - 1))(lambda: add(4))

    if not causal:

        @pl.when(zz > z)
        def _():
            room[...] = acc[...].astype(BF)
            remote(room, rz.at[zz], ss.at[i, n], vz.at[zz], me.near("up")).start()

    @pl.when(zz < z)
    def _():
        room[...] = acc[...].astype(BF)
        there = jnp.where(zz == z - 1, 4, zz)
        remote(room, rz.at[there], ss.at[i, n + 1], vz.at[there], me.near("down")).start()


def by_weight(x, z, y, c):
    return x * 16 + z * 4 + y * 2 + c


def by_token(x, z, y, c):
    return (z * 4 + y * 2 + c) * 2 + x


ANY = pl.BlockSpec(memory_space=pl.ANY)
VMEM = pl.BlockSpec(memory_space=pltpu.VMEM)
DMA = pltpu.SemaphoreType.DMA


def params(number, mib):
    return pltpu.CompilerParams(
        collective_id=number, has_side_effects=True, vmem_limit_bytes=mib << 20
    )


NT = (((1,), (1,)), ((), ()))
TN = (((0,), (0,)), ((), ()))
GROUP = QUERY_HEADS // KEY_VALUE_HEADS
LANES = GROUP * 128
SCALE = HEAD_SIZE ** (-0.5)
POWER = SCALE * 1.4426950408889634


def turned(u, cosine, sine):
    return u * cosine + pltpu.roll(u, 64, 1) * sine


def begin_of(place, doc):
    begin = jnp.zeros_like(place)
    for i in range(doc.shape[1]):
        start = doc[0:1, i : i + 1]
        begin = jnp.where(place >= start, jnp.maximum(begin, start), begin)
    return begin


def rotary_tables(me, doc, freq):
    first = (me.b * 2 + me.x) * 128
    place = first + lax.broadcasted_iota(jnp.int32, (128, 128), 0)
    angle = (place - begin_of(place, doc)).astype(F32) * freq[...]
    sine = jnp.sin(angle)
    lane = lax.broadcasted_iota(jnp.int32, (128, 128), 1)
    return jnp.cos(angle), jnp.where(lane < 64, -sine, sine)


def query_bounds(me, doc):
    place = (me.b * 2 + me.x) * 128 + lax.broadcasted_iota(jnp.int32, (1, LANES), 1) % 128
    return begin_of(place, doc), place


def allowed_keys(start, bounds):
    key = start + lax.broadcasted_iota(jnp.int32, (256, LANES), 0)
    return (key >= bounds[0]) & (key <= bounds[1])


def eye(n):
    return lax.broadcasted_iota(jnp.int32, (n, n), 0) == lax.broadcasted_iota(jnp.int32, (n, n), 1)


def as_column(row):
    return jnp.sum(jnp.where(eye(row.shape[1]), row, 0.0), axis=1, keepdims=True)


def as_row(column):
    return jnp.sum(jnp.where(eye(column.shape[0]), column, 0.0), axis=0, keepdims=True)


QKV = 2048
WIDE = QKV + 128
PIECES = ((0, 1152), (1152, 1024))


def front_kernel(
    doc_in, freq_in, one_in, two_in, valid_in, states, down_in, wq, wk, wv, wo, up,
    gq_out, go_out, kv_out, win, wout, h_out, n2_out, n1_out, qs_out, o_out, lse_out, count_out, gains_out,
    doc, freq, norm_one, norm_two, valid, lse, count, gains_row, gq, go, kv, down, top, total, acc, low_rows, down_raw, cos, sin, n1, qs, o, h, n2,
    load_sem, own_sem, qsend, qrecv, gsend, grecv, ksend, krecv, asend, arecv, osend, orecv,
):
    me = Place()
    greet_all(me)
    x, y, z, b, c = me.x, me.y, me.z, me.b, me.c
    here = by_weight(x, z, y, c)
    mine = [
        pltpu.make_async_copy(wq, gq.at[here, :, pl.ds(0, 1536)], own_sem.at[0]),
        pltpu.make_async_copy(wk, gq.at[here, :, pl.ds(1536, 256)], own_sem.at[1]),
        pltpu.make_async_copy(wv, gq.at[here, :, pl.ds(1792, 256)], own_sem.at[2]),
        pltpu.make_async_copy(wo, go.at[here], own_sem.at[3]),
    ]
    pairs = (
        (down_in, down_raw), (states, low_rows), (doc_in, doc), (freq_in, freq),
        (one_in, norm_one), (two_in, norm_two), (valid_in, valid),
    )
    loads = [pltpu.make_async_copy(src, dst, load_sem.at[i]) for i, (src, dst) in enumerate(pairs)]
    for copy in loads[4:] + mine + loads[:4]:
        copy.start()
    for load in loads[4:]:
        load.wait()

    lane = lax.broadcasted_iota(jnp.int32, (48, 128), 1)
    kept = jnp.sum(valid[...].astype(F32))
    extra = jnp.where(
        lane == 0,
        as_column(norm_one[...].astype(F32)),
        jnp.where(lane == 1, as_column(norm_two[...].astype(F32)), jnp.where(lane == 2, kept, 0.0)),
    )
    gq[here, :, pl.ds(QKV, 128)] = extra.astype(BF)
    all_greeted()
    for copy in mine:
        copy.wait()

    def own_piece(n):
        col = pl.multiple_of(n * 768 + c * 384, 128)
        return pltpu.make_async_copy(
            up.at[b // 2, :, pl.ds(col, 384)], win.at[b, :, pl.ds(n * 384, 384)], own_sem.at[4 + n]
        )

    def own_down():
        return pltpu.make_async_copy(down.at[b // 2], wout.at[b], own_sem.at[6])

    def deal(k, carry):
        t = (b + (k * 13) % 16) % 16
        for n in range(2):
            col = pl.multiple_of(n * 768 + (t % 2) * 384, 128)
            remote(
                up.at[t // 2, :, pl.ds(col, 384)],
                win.at[b, :, pl.ds(n * 384, 384)],
                asend.at[k, n],
                arecv.at[b, n],
                (x, t),
            ).start()
        pl.when(t % 2 == x)(
            lambda: remote(down.at[t // 2], wout.at[b], osend.at[k], orecv.at[b], (x, t)).start()
        )
        return carry

    weights = [
        Gather(me, gq, by_weight, qsend.at[i], qrecv.at[i], PIECES[i]) for i in range(len(PIECES))
    ]

    def first_turn(j, carry):
        for piece in weights:
            piece.turn(j)

        @pl.when(j == 0)
        def _():
            for load in loads[:4]:
                load.wait()
            for e in range(E):
                wide = down_raw[e].astype(F32)
                down[e] = jnp.concatenate([wide[:, :768], wide[:, 768:]], axis=0).astype(BF)
            cos[...], sin[...] = rotary_tables(me, doc, freq)

        lax.fori_loop(1 + j * 3, jnp.minimum(4 + j * 3, 16), deal, 0)
        return carry

    lax.fori_loop(0, 6, first_turn, 0)
    for n in range(2):
        own_piece(n).start()
    pl.when(c == x)(lambda: own_down().start())
    bounds = query_bounds(me, doc)
    rows = low_rows[...].astype(F32)
    level = rows * lax.rsqrt(jnp.mean(rows * rows, axis=-1, keepdims=True) + 1e-06)
    for piece in weights:
        piece.from_cores()
    keep = pltpu.make_async_copy(gq, gq_out, own_sem.at[0])
    keep.start()

    gains = gq[:, :, pl.ds(QKV, 128)].reshape(1536, 128).astype(F32).T
    n1[...] = (level * gains[0:1]).astype(BF)
    turns = cos[...], sin[...]
    at = by_token(x, z, y, c)
    keys = Gather(me, kv, by_token, ksend, krecv, causal=True)
    output = Gather(me, go, by_weight, gsend, grecv)
    both = jnp.dot(n1[...], gq[:, :, pl.ds(1536, 512)].reshape(1536, 512), preferred_element_type=F32)
    for i in range(2):
        kv[at, :, i * 128 : i * 128 + 128] = turned(both[:, i * 128 : i * 128 + 128], *turns).astype(BF)
    kv[at, :, 256:512] = both[:, 256:512].astype(BF)
    keys.turn(0)
    query = jnp.dot(n1[...], gq[:, :, pl.ds(0, 1536)].reshape(1536, 1536), preferred_element_type=F32)
    for i in range(QUERY_HEADS):
        r = (i % GROUP) * 128
        qs[i // GROUP, r : r + 128] = turned(query[:, i * 128 : i * 128 + 128], *turns).astype(BF)
    count[...] = jnp.zeros((8, 128), F32) + jnp.sum(gains[2:3]) / 48.0
    gains_row[...] = gains[0:8]
    saved = [
        pltpu.make_async_copy(count, count_out, load_sem.at[5]),
        pltpu.make_async_copy(gains_row, gains_out, load_sem.at[6]),
        pltpu.make_async_copy(n1, n1_out, load_sem.at[0]),
        pltpu.make_async_copy(qs, qs_out, load_sem.at[1]),
    ]
    for copy in saved:
        copy.start()

    top[...] = jnp.full_like(top, FLOOR_SCORE)
    total[...] = jnp.zeros_like(total)
    acc[...] = jnp.zeros_like(acc)
    def block(n):
        ok = allowed_keys(n * 256, bounds)
        for i in range(2):
            k = kv[pl.ds(n * 2, 2), :, i * 128 : i * 128 + 128].reshape(256, 128)
            v = kv[pl.ds(n * 2, 2), :, 256 + i * 128 : 384 + i * 128].reshape(256, 128)
            s = lax.dot_general(k, qs[i], NT, preferred_element_type=F32)
            s = jnp.where(ok, s, FLOOR_SCORE)
            old = top[i]
            new = jnp.maximum(old, jnp.max(s, axis=0, keepdims=True))
            factor = jnp.exp2((old - new) * POWER)
            p = jnp.exp2((s - new) * POWER)
            top[i] = new
            total[i] = total[i] * factor + jnp.sum(p, axis=0, keepdims=True)
            acc[i] = acc[i] * factor + lax.dot_general(v, p.astype(BF), TN, preferred_element_type=F32)

    def close_deal(k, carry):
        piece = win.at[b, :, pl.ds(0, 384)]
        f = (b + 16 - k) % 16
        for n in range(2):
            left(piece, asend.at[k, n], me)
            arrived(win.at[f, :, pl.ds(n * 384, 384)], arecv.at[f, n], me)
        pl.when((b + k) % 2 == x)(lambda: left(wout.at[b], osend.at[k], me))
        pl.when(c == x)(lambda: arrived(wout.at[f], orecv.at[f], me))
        return carry

    def turn(j, carry):
        pl.when(j > 0)(lambda: keys.turn(j))
        output.turn(j - 2)

        @pl.when(j == 1)
        def _():
            for piece in weights:
                piece.close()

        @pl.when(j == 6)
        def _():
            lax.fori_loop(1, 16, close_deal, 0)
            keys.close()


        @pl.when(keys.valid(j - 2))
        def _():
            i = j - 2
            keys.from_core(i)
            zz = z - i
            last = jnp.where(i == 0, y * 2 + c, 3)

            def one(n, carry):
                block(zz * 4 + last - n)
                return carry

            lax.fori_loop(0, last + 1, one, 0)

        return carry

    lax.fori_loop(0, 8, turn, 0)
    keep_k = pltpu.make_async_copy(kv, kv_out, own_sem.at[2])
    keep_k.start()
    for i in range(2):
        lse[i] = top[i] * POWER + jnp.log2(total[i])
        done = acc[i] / total[i]
        for r in range(GROUP):
            col = (i * GROUP + r) * 128
            o[:, col : col + 128] = done[:, r * 128 : r * 128 + 128].T
    more = [pltpu.make_async_copy(o, o_out, load_sem.at[2]), pltpu.make_async_copy(lse, lse_out, load_sem.at[7])]
    for copy in more:
        copy.start()
    output.from_cores()
    keep_o = pltpu.make_async_copy(go, go_out, own_sem.at[1])
    keep_o.start()
    res = low_rows[...].astype(F32) + jnp.dot(
        o[...].astype(BF), go[...].reshape(1536, 1536), preferred_element_type=F32
    )
    h[...] = res
    n2[...] = (
        res * lax.rsqrt(jnp.mean(res * res, axis=-1, keepdims=True) + 1e-06) * gains[1:2]
    ).astype(BF)
    more.append(pltpu.make_async_copy(h, h_out, load_sem.at[3]))
    more.append(pltpu.make_async_copy(n2, n2_out, load_sem.at[4]))
    more[2].start()
    more[3].start()

    output.close()
    for n in range(2):
        own_piece(n).wait()
    pl.when(c == x)(lambda: own_down().wait())
    for copy in [keep, keep_o, keep_k] + saved + more:
        copy.wait()


def run_front(*operands):
    shape = jax.ShapeDtypeStruct
    return pl.pallas_call(
        front_kernel,
        out_shape=(
            shape((32, 48, WIDE), BF),
            shape((32, 48, 1536), BF),
            shape((32, 128, 512), BF),
            shape((16, 48, 768), BF),
            shape((16, 48, 768), BF),
            shape((128, 1536), F32),
            shape((128, 1536), BF),
            shape((128, 1536), BF),
            shape((2, LANES, 128), BF),
            shape((128, 1536), F32),
            shape((2, 1, LANES), F32),
            shape((8, 128), F32),
            shape((8, 1536), F32),
        ),
        in_specs=[ANY] * 12,
        out_specs=(ANY,) * 13,
        scratch_shapes=[
            pltpu.VMEM(operands[0].shape, jnp.int32),
            pltpu.VMEM((1, 128), F32),
            pltpu.VMEM((1, 48), BF),
            pltpu.VMEM((1, 48), BF),
            pltpu.VMEM((1, 128), jnp.int32),
            pltpu.VMEM((2, 1, LANES), F32),
            pltpu.VMEM((8, 128), F32),
            pltpu.VMEM((8, 1536), F32),
            pltpu.VMEM((32, 48, WIDE), BF),
            pltpu.VMEM((32, 48, 1536), BF),
            pltpu.VMEM((32, 128, 512), BF),
            pltpu.VMEM((8, 48, 768), BF),
            pltpu.VMEM((2, 1, LANES), F32),
            pltpu.VMEM((2, 1, LANES), F32),
            pltpu.VMEM((2, 128, LANES), F32),
            pltpu.VMEM((128, 1536), BF),
            pltpu.VMEM((8, 24, 1536), BF),
            pltpu.VMEM((128, 128), F32),
            pltpu.VMEM((128, 128), F32),
            pltpu.VMEM((128, 1536), BF),
            pltpu.VMEM((2, LANES, 128), BF),
            pltpu.VMEM((128, 1536), F32),
            pltpu.VMEM((128, 1536), F32),
            pltpu.VMEM((128, 1536), BF),
            DMA((8,)),
            DMA((7,)),
            DMA((2, 4, 10)),
            DMA((2, 32, 2)),
            DMA((4, 10)),
            DMA((32, 2)),
            DMA((4, 10)),
            DMA((32, 2)),
            DMA((16, 2)),
            DMA((16, 2)),
            DMA((16,)),
            DMA((16,)),
        ],
        compiler_params=params(1, 62),
        name="front",
    )(*operands)


GELU_A = 0.7978845608028654
GELU_B = 0.044715


PARTS = ((0, 64), (64, 48), (112, 16))
CUTS = 2


def experts_kernel(
    routes_in, gates_in, valid_in, count_in, n2, h_in, teacher_in, win, wout,
    err_out, final_out, dn2_out, dy_out, dwin_out, dwout_out,
    routes, gates, valid, count, err, h, teacher, final, dy, nall, dyall, pairs, zg, dpairs, part, rc, ry, rz, rzt, ryt, tail, acc, errs, tables, gate,
    wfull, slab, wdown, dwin, dwin_in, dwout, dwout_in,
    load_sem, own_sem, gsend, grecv, csend, crecv, ysend, yrecv, zsend, zrecv, esend, erecv,
    tsend, trecv, xsend, xrecv,
):
    me = Place()
    greet_all(me)
    x, y, z, b, c = me.x, me.y, me.z, me.b, me.c
    half = pltpu.make_async_copy(win, wfull.at[x], own_sem.at[0])
    half.start()
    loads = [
        pltpu.make_async_copy(n2, nall.at[b], load_sem.at[0]),
        pltpu.make_async_copy(h_in, h, load_sem.at[1]),
        pltpu.make_async_copy(teacher_in, teacher, load_sem.at[2]),
        pltpu.make_async_copy(routes_in, routes, load_sem.at[3]),
        pltpu.make_async_copy(gates_in, gates, load_sem.at[4]),
        pltpu.make_async_copy(valid_in, valid, load_sem.at[5]),
        pltpu.make_async_copy(count_in, count, load_sem.at[6]),
    ]
    for load in loads:
        load.start()
    held = pltpu.make_async_copy(wout, slab, own_sem.at[1])
    pl.when(c == x)(held.start)
    all_greeted()

    def rows_of(p):
        return pl.ds(*PARTS[p])

    def over_weights(k):
        cut = pl.ds(k * 4, 4)
        return remote(win.at[cut], wfull.at[x, cut], xsend.at[k], xrecv.at[k], me.near("x"))

    def over_down():
        return remote(wout, slab, xsend.at[4], xrecv.at[4], me.near("x"))

    def put(buf, way, j, p, kind, n, s):
        ref = buf.at[s, rows_of(p)]
        remote(ref, ref, gsend.at[way, j, p, n], grecv.at[way, s, p], me.near(kind)).start()

    def along(buf, way, j, p, n, s, zz):
        pl.when((zz <= z) & (z < NZ - 1))(lambda: put(buf, way, j, p, "up", n, s))
        pl.when((zz >= z) & (z > 0))(lambda: put(buf, way, j, p, "down", n + 1, s))

    def begin(buf, way, p):
        along(buf, way, 0, p, 0, b, z)
        put(buf, way, 0, p, "y", 2, b)
        put(buf, way, 0, p, "c", 3, b)

    def gather(buf, way, between):
        def turn(j, carry):
            between(j, -1)
            for p in range(CUTS + 1):
                zz = me.outward(j)
                own = me.blk(zz, y, c)

                @pl.when((j > 0) & (j < 4))
                def _():
                    arrived(buf.at[own, rows_of(p)], grecv.at[way, own, p], me)

                @pl.when((j > 0) & (j < 4))
                def _():
                    along(buf, way, j, p, 0, own, zz)
                    if p < CUTS:
                        put(buf, way, j, p, "y", 2, own)
                    put(buf, way, j, p, "c", 3, own)

                @pl.when((j > 0) & (j < 5))
                def _():
                    i = j - 1
                    zp = me.outward(i)
                    s = me.blk(zp, 1 - y, c)
                    arrived(buf.at[s, rows_of(p)], grecv.at[way, s, p], me)
                    if p == CUTS:
                        along(buf, way, i, p, 5, s, zp)
                    put(buf, way, i, p, "c", 4, s)

                between(j, p)
            return carry

        lax.fori_loop(0, 6, turn, 0)

    def close_gather(buf, way):
        def close(j, carry):
            zz = me.outward(j)
            for p in range(CUTS + 1):
                whole = buf.at[b, rows_of(p)]
                ends = (0, 1) if p < CUTS else (0, 1, 5, 6)
                for n in ends:
                    ok = (zz <= z) & (z < NZ - 1) if n in (0, 5) else (zz >= z) & (z > 0)
                    pl.when(ok)(lambda: left(whole, gsend.at[way, j, p, n], me))
                if p < CUTS:
                    left(whole, gsend.at[way, j, p, 2], me)
                else:
                    pl.when(j == 0)(lambda: left(whole, gsend.at[way, j, p, 2], me))
                for n in (3, 4):
                    left(whole, gsend.at[way, j, p, n], me)
            return carry

        lax.fori_loop(0, 4, close, 0)

    def from_core(buf, way, zz, yy):
        s = me.blk(zz, yy, 1 - c)
        for p in range(CUTS + 1):
            arrived(buf.at[s, rows_of(p)], grecv.at[way, s, p], me)

    def to_other_core(way, q):
        remote(part.at[q * 2 + 1 - c], rc.at[q], csend.at[way, q], crecv.at[way, q], me.near("c")).start()

    def lead(way, j):
        zz = me.inward(j)
        q = zz * 2 + 1 - y
        s = q * 2 + c
        arrived(rc.at[q], crecv.at[way, q], me)
        part[s] = (part[s].astype(F32) + rc[q].astype(F32)).astype(BF)
        for p in range(CUTS):
            remote(
                part.at[s, rows_of(p)], ry.at[zz, rows_of(p)], ysend.at[way, j, p], yrecv.at[way, zz, p], me.near("y")
            ).start()

    def follow(way, j, done=None):
        zz = me.inward(j)
        q = zz * 2 + y
        s = q * 2 + c
        arrived(rc.at[q], crecv.at[way, q], me)
        cut = rows_of(CUTS)
        for n, yy in enumerate((1 - y, y)):
            k = zz * 2 + yy
            room = part.at[k * 2 + c, cut]
            if n:
                tail[...] = room[...].astype(F32) + rc[k, cut].astype(F32)
            else:
                tail[...] = room[...].astype(F32)
            along_z(
                me, j, zz, tail, room, rzt.at[n], zsend.at[way, :, CUTS + n], 0, zrecv.at[way, :, CUTS + n]
            )
            if n == 0:

                @pl.when(zz == z)
                def _():
                    room[...] = tail[...].astype(BF)
                    remote(room, ryt, ysend.at[way, 3, CUTS], yrecv.at[way, 0, CUTS], me.near("y")).start()

        for p in range(CUTS):
            cut = rows_of(p)
            arrived(ry.at[zz, cut], yrecv.at[way, zz, p], me)
            piece = acc.at[cut]
            piece[...] = part[s, cut].astype(F32) + rc[q, cut].astype(F32) + ry[zz, cut].astype(F32)
            along_z(
                me, j, zz, piece, part.at[s, cut], rz.at[:, cut], zsend.at[way, :, p], 0, zrecv.at[way, :, p]
            )
            if done is not None:
                pl.when(zz == z)(functools.partial(done, p))

        @pl.when(zz == z)
        def _():
            arrived(ryt, yrecv.at[way, 0, CUTS], me)
            acc[rows_of(CUTS)] = tail[...] + ryt[...].astype(F32)
            if done is not None:
                done(CUTS)

    def close_sum(way):
        def close(j, carry):
            zz = me.inward(j)
            whole = part.at[b]
            left(whole, csend.at[way, j], me)
            left(whole, csend.at[way, j + 4], me)
            for p in range(CUTS + 2):
                piece = part.at[b, rows_of(min(p, CUTS))]
                if p < CUTS:
                    left(piece, ysend.at[way, j, p], me)
                elif p == CUTS:
                    pl.when(j == 3)(lambda: left(piece, ysend.at[way, j, p], me))
                pl.when(zz > z)(lambda: left(piece, zsend.at[way, j, p, 0], me))
                pl.when(zz < z)(lambda: left(piece, zsend.at[way, j, p, 1], me))
            return carry

        lax.fori_loop(0, 4, close, 0)

    def gelu_parts(g):
        t = jnp.tanh(GELU_A * (g + GELU_B * g * g * g))
        return t, 0.5 * g * (1.0 + t)

    def forward(q):
        rows = nall[pl.ds(q * 2, 2)].reshape(256, 1536)
        pair = jnp.dot(rows, wfull[...].reshape(1536, 768), preferred_element_type=F32)
        pairs[q] = pair
        unused, a = gelu_parts(pair[:, :384])
        scale = gate[pl.ds(q * 2, 2)].reshape(256, 1)
        zq = (a * pair[:, 384:] * scale).astype(BF)
        zg[q] = zq
        out = jnp.dot(zq, wdown[...], preferred_element_type=F32)
        part[pl.ds(q * 2, 2)] = out.astype(BF).reshape(2, 128, 1536)
        to_other_core(0, q)

    def backward(q):
        rows = dyall[pl.ds(q * 2, 2)].reshape(256, 1536)
        scale = gate[pl.ds(q * 2, 2)].reshape(256, 1)
        dz = lax.dot_general(rows, wdown[...], NT, preferred_element_type=F32) * scale
        g, u = pairs[q, :, :384], pairs[q, :, 384:]
        t, a = gelu_parts(g)
        slope = 0.5 * (1.0 + t) + 0.5 * g * (1.0 - t * t) * (GELU_A * (1.0 + 3.0 * GELU_B * g * g))
        dpairs[q, :, :384] = (dz * u * slope).astype(BF)
        dpairs[q, :, 384:] = (dz * a).astype(BF)
        out = lax.dot_general(dpairs[q], wfull[...].reshape(1536, 768), NT, preferred_element_type=F32)
        part[pl.ds(q * 2, 2)] = out.astype(BF).reshape(2, 128, 1536)
        to_other_core(1, q)

    loads[0].wait()
    pl.when(c == x)(held.wait)

    def tell_gates(k, carry):
        to = (b + k) % 16
        remote(tables.at[b], tables.at[b], tsend.at[k], trecv.at[b], (x, to)).start()
        return carry

    def with_tokens(j, p):
        if p == 0:
            pl.when((j == 0) & (c == x))(lambda: over_down().start())
            for k in range(4):
                pl.when(j == k)(over_weights(k).start)
        elif p == 1:

            @pl.when(j == 0)
            def _():
                for load in loads[3:]:
                    load.wait()
                expert = lax.broadcasted_iota(jnp.int32, (8, 128), 0)
                table = jnp.zeros((8, 128), F32)
                for k in range(TOP):
                    table = table + jnp.where(routes[k : k + 1, :] == expert, gates[k : k + 1, :], 0.0)
                tables[b] = table
                lax.fori_loop(1, 16, tell_gates, 0)

    for p in range(CUTS + 1):
        begin(nall, 0, p)
    gather(nall, 0, with_tokens)

    def all_cores(buf, way):
        def one(j, carry):
            from_core(buf, way, j, y)
            from_core(buf, way, j, 1 - y)
            return carry

        lax.fori_loop(0, 4, one, 0)

    all_cores(nall, 0)
    def hear_gates(k, carry):
        left(tables.at[0], tsend.at[k], me)
        arrived(tables.at[(b + 16 - k) % 16], trecv.at[(b + 16 - k) % 16], me)
        return carry

    lax.fori_loop(1, 16, hear_gates, 0)

    def gate_of(s, carry):
        row = lax.broadcasted_iota(jnp.int32, (8, 128), 0)
        picked = jnp.sum(jnp.where(row == b // 2, tables[s], 0.0), axis=0, keepdims=True)
        gate[s] = as_column(picked)
        return carry

    lax.fori_loop(0, 16, gate_of, 0)
    half.wait()
    for k in range(4):
        arrived(wfull.at[1 - x, pl.ds(k * 4, 4)], xrecv.at[k], me)
    pl.when(c != x)(lambda: arrived(slab, xrecv.at[4], me))
    wide = slab[...].astype(F32).reshape(16, 2, 24, 768)
    wdown[:, :768] = wide[:, 0].reshape(384, 768).astype(BF)
    wdown[:, 768:] = wide[:, 1].reshape(384, 768).astype(BF)

    keep = as_column(valid[...].astype(F32))
    factor = keep * (SPAN / count[0:1, 0:1])
    loads[1].wait()
    loads[2].wait()
    me_index = x * 16 + b
    errs[me_index] = jnp.zeros((8, 128), F32)

    def loss_and_dy(p):
        cut, at = rows_of(p), slice(PARTS[p][0], PARTS[p][0] + PARTS[p][1])
        done = h[cut] + acc[cut]
        final[cut] = done.astype(BF)
        diff = done - teacher[cut].astype(F32)
        scaled = factor[at] * diff
        dy[cut] = scaled
        dyall[b, cut] = scaled.astype(BF)
        begin(dyall, 1, p)
        errs[me_index] += jnp.zeros((8, 128), F32) + jnp.sum(keep[at] * diff * diff)

    def outputs(j, carry):
        @pl.when(j < 4)
        def _():
            forward(me.inward(j) * 2 + 1 - y)

        @pl.when((j > 0) & (j < 5))
        def _():
            forward(me.inward(j - 1) * 2 + y)

        pl.when(j < 4)(lambda: lead(0, j))
        pl.when(j == 1)(lambda: close_gather(nall, 0))
        pl.when(j > 1)(lambda: follow(0, j - 2, loss_and_dy))
        return carry

    lax.fori_loop(0, 6, outputs, 0)

    saved = [
        pltpu.make_async_copy(final, final_out, load_sem.at[0]),
        pltpu.make_async_copy(dy, dy_out, load_sem.at[1]),
        pltpu.make_async_copy(acc, dn2_out, load_sem.at[2]),
        pltpu.make_async_copy(err, err_out, load_sem.at[3]),
    ]
    for copy in saved[:2]:
        copy.start()
    def tell(k, carry):
        to = ((x + k // 16) % 2, (b + k) % 16)
        remote(errs.at[me_index], errs.at[me_index], esend.at[k], erecv.at[me_index], to).start()
        return carry

    def inputs(i, yy):
        zz = me.outward(i)
        from_core(dyall, 1, zz, yy)
        backward(zz * 2 + yy)

    def with_dy(j, p):
        if p == -1:

            @pl.when(j == 4)
            def _():
                inputs(2, 1 - y)
                inputs(3, y)

            @pl.when(j == 5)
            def _():
                lead(1, 3)
                inputs(3, 1 - y)

        elif p == 0:
            pl.when((j > 0) & (j < 4))(lambda: inputs(j - 1, y))
        elif p == CUTS - 1:

            @pl.when(j == 0)
            def _():
                lax.fori_loop(1, 32, tell, 0)
                close_sum(0)

            pl.when((j > 1) & (j < 4))(lambda: inputs(j - 2, 1 - y))

    gather(dyall, 1, with_dy)

    def in_grad(i):
        col = pl.ds(pl.multiple_of(i * 256, 256), 256)
        rows = nall[:, :, col].reshape(2048, 256)
        dwin[col, :] = lax.dot_general(
            rows, dpairs[...].reshape(2048, 768), TN, preferred_element_type=F32
        ).astype(BF)

    def out_grad(i):
        col = pl.ds(i * 256, 256)
        right = dyall[:, :, col].reshape(2048, 256)
        value = lax.dot_general(zg[...].reshape(2048, 384), right, TN, preferred_element_type=F32)
        there = i // 3 * 24
        dwout[:, there : there + 24, (i % 3) * 256 : (i % 3) * 256 + 256] = value.reshape(16, 24, 256)

    def over_in(k):
        src = dwin.at[pl.ds(pl.multiple_of((1 - x) * 768 + k * 256, 256), 256)]
        return remote(src, dwin_in.at[pl.ds(k * 256, 256)], xsend.at[5 + k], xrecv.at[5 + k], me.near("x"))

    def over_out():
        return remote(slab, dwout_in, xsend.at[8], xrecv.at[8], me.near("x"))

    def leads(j, carry):
        lead(1, j)
        return carry

    lax.fori_loop(0, 3, leads, 0)

    def hear(k, carry):
        left(errs.at[0], esend.at[k], me)
        s = ((x + k // 16) % 2) * 16 + (b + k) % 16
        arrived(errs.at[s], erecv.at[s], me)
        return carry

    def sums(j, carry):
        @pl.when(j == 3)
        def _():
            close_gather(dyall, 1)
            lax.fori_loop(1, 32, hear, 0)
            total = errs[0]
            for s in range(1, 32):
                total = total + errs[s]
            err[...] = total / (1536.0 * count[...])

        @pl.when(j == 0)
        def _():
            for k in range(3):
                in_grad((1 - x) * 3 + k)
                over_in(k).start()

        @pl.when(j == 1)
        def _():
            for k in range(6):
                out_grad(k)
            slab[...] = dwout[...].astype(BF)
            pl.when(c != x)(lambda: over_out().start())

        @pl.when(j == 2)
        def _():
            for k in range(3):
                in_grad(x * 3 + k)

        follow(1, j)
        return carry

    for k in range(4):
        over_weights(k).wait_send()
    pl.when(c == x)(lambda: over_down().wait_send())
    lax.fori_loop(0, 4, sums, 0)
    saved[2].start()
    saved[3].start()
    close_sum(1)

    for k in range(3):
        over_in(k).wait_send()
        here = pl.ds(pl.multiple_of(x * 768 + k * 256, 256), 256)
        there = pl.ds(k * 256, 256)
        arrived(dwin_in.at[there], xrecv.at[5 + k], me)
        dwin_in[there] = (dwin_in[there].astype(F32) + dwin[here, :].astype(F32)).astype(BF)
    out = pltpu.make_async_copy(dwin_in, dwin_out, own_sem.at[0])
    out.start()

    @pl.when(c == x)
    def _():
        arrived(dwout_in, xrecv.at[8], me)
        dwout_in[...] = (dwout_in[...].astype(F32) + dwout[...]).astype(BF)
        copy = pltpu.make_async_copy(dwout_in, dwout_out, own_sem.at[1])
        copy.start()
        copy.wait()

    pl.when(c != x)(lambda: over_out().wait_send())
    for copy in saved + [out]:
        copy.wait()


def run_experts(*operands):
    wide = (128, 1536)
    shard = (16,) + wide
    shape = jax.ShapeDtypeStruct
    return pl.pallas_call(
        experts_kernel,
        out_shape=(
            shape((8, 128), F32),
            shape(wide, BF),
            shape(wide, F32),
            shape(wide, F32),
            shape((768, 768), BF),
            shape((16, 48, 768), BF),
        ),
        in_specs=[ANY] * 9,
        out_specs=(ANY,) * 6,
        scratch_shapes=[
            pltpu.VMEM((TOP, 128), jnp.int32),
            pltpu.VMEM((TOP, 128), F32),
            pltpu.VMEM((1, 128), jnp.int32),
            pltpu.VMEM((8, 128), F32),
            pltpu.VMEM((8, 128), F32),
            pltpu.VMEM(wide, F32),
            pltpu.VMEM(wide, BF),
            pltpu.VMEM(wide, BF),
            pltpu.VMEM(wide, F32),
            pltpu.VMEM(shard, BF),
            pltpu.VMEM(shard, BF),
            pltpu.VMEM((8, 256, 768), F32),
            pltpu.VMEM((8, 256, 384), BF),
            pltpu.VMEM((8, 256, 768), BF),
            pltpu.VMEM(shard, BF),
            pltpu.VMEM((8,) + wide, BF),
            pltpu.VMEM((4,) + wide, BF),
            pltpu.VMEM((5,) + wide, BF),
            pltpu.VMEM((2, 5, PARTS[CUTS][1], 1536), BF),
            pltpu.VMEM((PARTS[CUTS][1], 1536), BF),
            pltpu.VMEM((PARTS[CUTS][1], 1536), F32),
            pltpu.VMEM(wide, F32),
            pltpu.VMEM((32, 8, 128), F32),
            pltpu.VMEM((16, 8, 128), F32),
            pltpu.VMEM((16, 128, 1), F32),
            pltpu.VMEM((2, 16, 48, 768), BF),
            pltpu.VMEM((16, 48, 768), BF),
            pltpu.VMEM((384, 1536), BF),
            pltpu.VMEM((1536, 768), BF),
            pltpu.VMEM((768, 768), BF),
            pltpu.VMEM((16, 48, 768), F32),
            pltpu.VMEM((16, 48, 768), BF),
            DMA((7,)),
            DMA((2,)),
            DMA((2, 4, CUTS + 1, 7)),
            DMA((2, 16, CUTS + 1)),
            DMA((2, 8)),
            DMA((2, 8)),
            DMA((2, 4, CUTS + 1)),
            DMA((2, 4, CUTS + 1)),
            DMA((2, 4, CUTS + 2, 2)),
            DMA((2, 5, CUTS + 2)),
            DMA((32,)),
            DMA((32,)),
            DMA((16,)),
            DMA((16,)),
            DMA((9,)),
            DMA((9,)),
        ],
        compiler_params=params(2, 62),
        name="experts",
    )(*operands)


def norm_back(values, gain, grad):
    scale = lax.rsqrt(jnp.mean(values * values, axis=-1, keepdims=True) + 1e-06)
    inner = grad * gain
    mean = jnp.mean(inner * values, axis=-1, keepdims=True)
    return scale * inner - values * (scale * scale * scale * mean), jnp.sum(
        grad * values * scale, axis=0, keepdims=True
    )


Q_PIECES = ((0, 768), (768, 768))
LAST = (1536, 640)


def back_kernel(
    doc_in, freq_in, gains_in, states_in, h_in, n1_in, qs_in, o_in, lse_in, dn2_in, dy_in, dwin, dwout, gq, go, kv_in,
    gx_out, gqw, gkw, gvw, gnorm_out, gout_out, gup, gdown,
    doc, freq, gains, gnorm, states, h, n1, qs, o, lse, dn2, dy, gx, gout, gkv,
    wq, wo, kv, pk, pw, dos, delta, dh, dq, dkv, dqkv, gqkv, *rest,
):
    sums = [(rest[i * 11 : i * 11 + 6], rest[i * 11 + 6 : i * 11 + 11]) for i in range(5)]
    load_sem, own_sem, asend, arecv, osend, orecv = rest[55:]
    me = Place()
    greet_all(me)
    x, y, z, b, c = me.x, me.y, me.z, me.b, me.c
    loads = [
        pltpu.make_async_copy(go, wo, own_sem.at[0]),
        pltpu.make_async_copy(kv_in, kv, own_sem.at[1]),
        pltpu.make_async_copy(gq, wq, own_sem.at[2]),
    ]
    small = [
        pltpu.make_async_copy(src, dst, load_sem.at[i])
        for i, (src, dst) in enumerate(
            (
                (h_in, h), (dn2_in, dn2), (dy_in, dy), (o_in, o), (qs_in, qs), (lse_in, lse),
                (n1_in, n1), (states_in, states), (doc_in, doc), (freq_in, freq), (gains_in, gains),
            )
        )
    ]
    for load in small[:3] + [small[10], loads[0]] + small[3:10] + [loads[1], loads[2]]:
        load.start()
    all_greeted()

    def own_piece(n):
        col = pl.multiple_of(n * 768 + c * 384, 128)
        return pltpu.make_async_copy(
            dwin.at[b, :, pl.ds(n * 384, 384)], gup.at[b // 2, :, pl.ds(col, 384)], own_sem.at[3 + n]
        )

    def own_down():
        return pltpu.make_async_copy(dwout.at[b], gdown.at[b // 2], own_sem.at[5])

    def deal(k, carry):
        t = (b + (k * 9) % 16) % 16
        for n in range(2):
            col = pl.multiple_of(n * 768 + c * 384, 128)
            remote(
                dwin.at[t, :, pl.ds(n * 384, 384)],
                gup.at[b // 2, :, pl.ds(col, 384)],
                asend.at[k, n],
                arecv.at[b, n],
                (x, t),
            ).start()
        pl.when(c == x)(
            lambda: remote(dwout.at[t], gdown.at[b // 2], osend.at[k], orecv.at[b // 2], (x, t)).start()
        )
        return carry

    for n in range(2):
        own_piece(n).start()
    pl.when(c == x)(lambda: own_down().start())
    lax.fori_loop(1, 16, deal, 0)
    for load in small[:3] + small[8:]:
        load.wait()
    res_grad, gain_two = norm_back(h[...], gains[1:2], dn2[...])
    dh[...] = dy[...] + res_grad
    da = dh[...].astype(BF)
    loads[0].wait()
    do = lax.dot_general(
        da, wo[...].reshape(1536, 1536), NT, preferred_element_type=F32
    ).astype(BF)
    small[3].wait()
    low = o[...].astype(BF)
    for i in range(4):
        part = lax.dot_general(low[:, i * 384 : i * 384 + 384], da, TN, preferred_element_type=F32)
        wo[i * 8 : i * 8 + 8] = part.astype(BF).reshape(8, 48, 1536)
    out_sum = Sum(me, wo, by_weight, gout, *sums[0])
    key_sum = Sum(me, pk, by_token, dkv, *sums[1], causal=True)

    def lead_all(which):
        def one(j, carry):
            which.lead(j)
            return carry

        lax.fori_loop(0, 4, one, 0)

    lead_all(out_sum)
    for i in range(QUERY_HEADS):
        col, r = i * 128, (i % GROUP) * 128
        dos[i // GROUP, r : r + 128] = do[:, col : col + 128]
        prod = do[:, col : col + 128].astype(F32) * o[:, col : col + 128]
        delta[i // GROUP, :, r : r + 128] = jnp.sum(prod.T, axis=0, keepdims=True)
    dq[...] = jnp.zeros_like(dq)
    bounds = query_bounds(me, doc)
    loads[1].wait()
    for load in small[4:6]:
        load.wait()

    def block(n):
        ok = allowed_keys(n * 256, bounds)
        for i in range(2):
            k = kv[pl.ds(n * 2, 2), :, i * 128 : i * 128 + 128].reshape(256, 128)
            v = kv[pl.ds(n * 2, 2), :, 256 + i * 128 : 384 + i * 128].reshape(256, 128)
            s = lax.dot_general(k, qs[i], NT, preferred_element_type=F32)
            p = jnp.where(ok, jnp.exp2(s * POWER - lse[i]), 0.0)
            dp = lax.dot_general(v, dos[i], NT, preferred_element_type=F32)
            ds = (p * (dp - delta[i])).astype(BF)
            dv = jnp.dot(p.astype(BF), dos[i], preferred_element_type=F32)
            dk = jnp.dot(ds, qs[i], preferred_element_type=F32) * SCALE
            pk[pl.ds(n * 2, 2), :, i * 128 : i * 128 + 128] = dk.astype(BF).reshape(2, 128, 128)
            pk[pl.ds(n * 2, 2), :, 256 + i * 128 : 384 + i * 128] = dv.astype(BF).reshape(2, 128, 128)
            dq[i] += lax.dot_general(k, ds, TN, preferred_element_type=F32)

    def turn(j, carry):
        out_sum.turn(j)

        @pl.when(key_sum.valid(j))
        def _():
            last = jnp.where(j == z, y * 2 + c, 3)

            def one(n, carry):
                block(j * 4 + n)
                return carry

            lax.fori_loop(0, last + 1, one, 0)

            def blank(n, carry):
                pk[pl.ds((j * 4 + n) * 2, 2)] = jnp.zeros((2, 128, 512), BF)
                return carry

            lax.fori_loop(last + 1, 4, blank, 0)
            key_sum.lead(j)

        key_sum.turn(j)
        return carry

    lax.fori_loop(0, 4, turn, 0)

    cos, sin = rotary_tables(me, doc, freq)
    for load in small[6:8] + [loads[2]]:
        load.wait()
    for i in range(QUERY_HEADS):
        r = (i % GROUP) * 128
        head = dq[i // GROUP, :, r : r + 128].T * SCALE
        dqkv[:, i * 128 : i * 128 + 128] = turned(head, cos, -sin).astype(BF)

    def weight_grad(start, width):
        for i in range(4):
            part = lax.dot_general(
                n1[:, i * 384 : i * 384 + 384], dqkv[:, start : start + width], TN, preferred_element_type=F32
            )
            pw[i * 8 : i * 8 + 8, :, start : start + width] = part.astype(BF).reshape(8, 48, width)

    weight_grad(0, 1536)
    proj = [Sum(me, pw, by_weight, gqkv, *sums[2 + i], Q_PIECES[i]) for i in range(2)]
    rest_sum = Sum(me, pw, by_weight, gqkv, *sums[4], LAST)
    for piece in proj:
        lead_all(piece)

    stores = [
        pltpu.make_async_copy(gx, gx_out, load_sem.at[0]),
        pltpu.make_async_copy(gout, gout_out, load_sem.at[1]),
        pltpu.make_async_copy(gqkv.at[:, pl.ds(0, 1536)], gqw, load_sem.at[2]),
        pltpu.make_async_copy(gkv.at[:, pl.ds(0, 256)], gkw, load_sem.at[3]),
        pltpu.make_async_copy(gkv.at[:, pl.ds(256, 256)], gvw, load_sem.at[4]),
        pltpu.make_async_copy(gnorm, gnorm_out, load_sem.at[5]),
    ]

    def close_deal(k, carry):
        f = (b + 16 - k) % 16
        for n in range(2):
            left(dwin.at[0, :, pl.ds(0, 384)], asend.at[k, n], me)
            col = pl.multiple_of(n * 768 + (f % 2) * 384, 128)
            arrived(gup.at[f // 2, :, pl.ds(col, 384)], arecv.at[f, n], me)
        pl.when(c == x)(lambda: left(dwout.at[0], osend.at[k], me))
        pl.when(f % 2 == x)(lambda: arrived(gdown.at[f // 2], orecv.at[f // 2], me))
        return carry

    def last_turn(j, carry):
        out_sum.turn(j + 4)
        pl.when(j < 2)(lambda: key_sum.turn(j + 4))
        for piece in proj:
            piece.turn(j)

        @pl.when(j == 1)
        def _():
            for i in range(2):
                part = dkv[:, i * 128 : i * 128 + 128]
                dqkv[:, 1536 + i * 128 : 1664 + i * 128] = turned(part, cos, -sin).astype(BF)
            dqkv[:, 1792:2048] = dkv[:, 256:512].astype(BF)
            weight_grad(1536, 512)
            dn1 = lax.dot_general(
                dqkv[...], wq[:, :, pl.ds(0, QKV)].reshape(1536, QKV), NT, preferred_element_type=F32
            )
            in_grad, gain_one = norm_back(states[...].astype(F32), gains[0:1], dn1)
            rows = lax.broadcasted_iota(jnp.int32, (128, 1536), 0)
            tail = jnp.where(rows == 0, gain_one, jnp.where(rows == 1, gain_two, 0.0)).T
            pw[:, :, pl.ds(QKV, 128)] = tail.astype(BF).reshape(32, 48, 128)
            lead_all(rest_sum)
            gx[...] = dh[...] + in_grad
            rest_sum.first_legs()

        rest_sum.rest(j - 2)

        @pl.when(j == 2)
        def _():
            stores[0].start()
            stores[1].start()
            out_sum.close()

        @pl.when(j == 3)
        def _():
            key_sum.close()
            lax.fori_loop(1, 16, close_deal, 0)

        @pl.when(j == 5)
        def _():
            stores[2].start()
            for piece in proj:
                piece.close()

        return carry

    lax.fori_loop(0, 7, last_turn, 0)
    gkv[...] = gqkv[:, 1536:2048]
    for store in stores[3:5]:
        store.start()
    gnorm[0:1, 0:48] = as_row(gqkv[:, 2048:2049])
    gnorm[1:2, 0:48] = as_row(gqkv[:, 2049:2050])
    stores[5].start()
    rest_sum.close()

    for n in range(2):
        own_piece(n).wait()
    pl.when(c == x)(lambda: own_down().wait())
    for store in stores:
        store.wait()


def run_back(*operands):
    shape = jax.ShapeDtypeStruct
    return pl.pallas_call(
        back_kernel,
        out_shape=(
            shape((128, 1536), F32),
            shape((48, 1536), F32),
            shape((48, 256), F32),
            shape((48, 256), F32),
            shape((8, 128), F32),
            shape((48, 1536), F32),
            shape((8, 48, 1536), BF),
            shape((8, 48, 768), BF),
        ),
        in_specs=[ANY] * 16,
        out_specs=(ANY,) * 8,
        scratch_shapes=[
            pltpu.VMEM(operands[0].shape, jnp.int32),
            pltpu.VMEM((1, 128), F32),
            pltpu.VMEM((8, 1536), F32),
            pltpu.VMEM((8, 128), F32),
            pltpu.VMEM((128, 1536), BF),
            pltpu.VMEM((128, 1536), F32),
            pltpu.VMEM((128, 1536), BF),
            pltpu.VMEM((2, LANES, 128), BF),
            pltpu.VMEM((128, 1536), F32),
            pltpu.VMEM((2, 1, LANES), F32),
            pltpu.VMEM((128, 1536), F32),
            pltpu.VMEM((128, 1536), F32),
            pltpu.VMEM((128, 1536), F32),
            pltpu.VMEM((48, 1536), F32),
            pltpu.VMEM((48, 512), F32),
            pltpu.VMEM((32, 48, WIDE), BF),
            pltpu.VMEM((32, 48, 1536), BF),
            pltpu.VMEM((32, 128, 512), BF),
            pltpu.VMEM((32, 128, 512), BF),
            pltpu.VMEM((32, 48, WIDE), BF),
            pltpu.VMEM((2, LANES, 128), BF),
            pltpu.VMEM((2, 1, LANES), F32),
            pltpu.VMEM((128, 1536), F32),
            pltpu.VMEM((2, 128, LANES), F32),
            pltpu.VMEM((128, 512), F32),
            pltpu.VMEM((128, QKV), BF),
            pltpu.VMEM((48, WIDE), F32),
        ]
        + Sum.room(48, 1536)
        + Sum.room(128, 512)
        + Sum.room(48, 768)
        + Sum.room(48, 768)
        + Sum.room(48, LAST[1])
        + [DMA((11,)), DMA((6,)), DMA((16, 2)), DMA((16, 2)), DMA((16,)), DMA((8,))],
        compiler_params=params(3, 62),
        name="back",
    )(*operands)


def finish_kernel(
    err_in, gnorm_in, final, gx, gqw, gkw, gvw, gout, gup, gdown,
    loss_out, one_out, two_out, final_out, gx_out, gqw_out, gkw_out, gvw_out, gout_out, gup_out, gdown_out,
    low_up, low_down, wide_up, wide_down, *rest,
):
    rooms, (err, gnorm, loss, one, two, sem, out_sem) = rest[:6], rest[6:]
    whole = (
        (gup, low_up), (gdown, low_down), *zip((final, gx, gqw, gkw, gvw, gout), rooms), (err_in, err), (gnorm_in, gnorm)
    )
    copies = [pltpu.make_async_copy(src, dst, sem.at[i]) for i, (src, dst) in enumerate(whole)]
    for copy in copies:
        copy.start()
    outs = (final_out, gx_out, gqw_out, gkw_out, gvw_out, gout_out)
    last = []
    for i in range(6):
        copies[2 + i].wait()
        last.append(pltpu.make_async_copy(rooms[i], outs[i], out_sem.at[i]))
        last[i].start()
    copies[0].wait()
    wide_up[...] = low_up[...].astype(F32)
    last.append(pltpu.make_async_copy(wide_up, gup_out, out_sem.at[6]))
    last[6].start()
    copies[1].wait()
    for e in range(E):
        wide = low_down[e].astype(F32)
        wide_down[e, :, :768] = wide[:24]
        wide_down[e, :, 768:] = wide[24:]
    last.append(pltpu.make_async_copy(wide_down, gdown_out, out_sem.at[7]))
    last[7].start()
    copies[8].wait()
    copies[9].wait()
    loss[...] = err[0:1, 0:1]
    one[...] = gnorm[0:1, 0:48]
    two[...] = gnorm[1:2, 0:48]
    for i, (src, dst) in enumerate(((loss, loss_out), (one, one_out), (two, two_out))):
        last.append(pltpu.make_async_copy(src, dst, out_sem.at[8 + i]))
        last[8 + i].start()
    for copy in last:
        copy.wait()


def run_finish(*operands):
    shape = jax.ShapeDtypeStruct
    up, down = (8, 48, 1536), (8, 24, 1536)
    return pl.pallas_call(
        finish_kernel,
        out_shape=(
            shape((1, 1), F32),
            shape((1, 48), F32),
            shape((1, 48), F32),
            shape((128, 1536), BF),
            shape((128, 1536), F32),
            shape((48, 1536), F32),
            shape((48, 256), F32),
            shape((48, 256), F32),
            shape((48, 1536), F32),
            shape(up, F32),
            shape(down, F32),
        ),
        in_specs=[ANY] * 10,
        out_specs=(ANY,) * 11,
        scratch_shapes=[
            pltpu.VMEM(up, BF),
            pltpu.VMEM((8, 48, 768), BF),
            pltpu.VMEM(up, F32),
            pltpu.VMEM(down, F32),
            pltpu.VMEM((128, 1536), BF),
            pltpu.VMEM((128, 1536), F32),
            pltpu.VMEM((48, 1536), F32),
            pltpu.VMEM((48, 256), F32),
            pltpu.VMEM((48, 256), F32),
            pltpu.VMEM((48, 1536), F32),
            pltpu.VMEM((8, 128), F32),
            pltpu.VMEM((8, 128), F32),
            pltpu.VMEM((1, 1), F32),
            pltpu.VMEM((1, 48), F32),
            pltpu.VMEM((1, 48), F32),
            DMA((10,)),
            DMA((11,)),
        ],
        compiler_params=pltpu.CompilerParams(vmem_limit_bytes=60 << 20),
        name="finish",
    )(*operands)


def per_device(
    states, teacher, valid, routes, gates, doc_starts, norm_one,
    w_query, key_weight, value_weight, w_output, norm_two, expert_in, expert_out,
):
    tokens = states.shape[2]
    width = states.shape[3]
    half = HEAD_SIZE // 2
    freq = np.float32(ROTARY_BASE) ** (-np.arange(half).astype(np.float32) / np.float32(half))
    freq = jnp.asarray(np.concatenate([freq, freq])[None, :], F32)
    rows = states.reshape(tokens, width)
    kept = valid.reshape(1, tokens)
    doc = doc_starts.reshape(1, -1)
    gq, go, kv, win, wout, h, n2, n1, qs, o, lse, count, gains = run_front(
        doc, freq, norm_one.reshape(1, -1), norm_two.reshape(1, -1), kept, rows, expert_out,
        w_query, key_weight, value_weight, w_output, expert_in,
    )
    error, final, dn2, dy, dwin, dwout = run_experts(
        routes.reshape(tokens, TOP).T, gates.reshape(tokens, TOP).T, kept, count,
        n2, h, teacher.reshape(tokens, width), win, wout,
    )
    gx, gqw, gkw, gvw, gnorm, gout, gup, gdown = run_back(
        doc, freq, gains, rows, h, n1, qs, o, lse, dn2, dy, dwin.reshape(16, 48, 768), dwout, gq, go, kv
    )
    loss, one, two, final, gx, gqw, gkw, gvw, gout, gup, gdown = run_finish(
        error, gnorm, final, gx, gqw, gkw, gvw, gout, gup, gdown
    )
    shape = states.shape
    return (
        final.reshape(shape),
        loss.reshape(()),
        gx.reshape(shape),
        one.reshape(-1),
        gqw,
        gkw,
        gvw,
        gout,
        two.reshape(-1),
        gup,
        gdown,
    )


def solution(mesh):
    in_specs = (
        P("blk", "head", None, None),
        P("blk", "head", None, None),
        P("blk", "head", None),
        P("blk", "head", None, None),
        P("blk", "head", None, None),
        P(),
        P(("head", "blk")),
        P(("head", "blk"), None),
        P(("head", "blk"), None),
        P(("head", "blk"), None),
        P(("head", "blk"), None),
        P(("head", "blk")),
        P(None, ("head", "blk"), None),
        P(None, ("head", "blk"), None),
    )
    out_specs = (
        P("blk", "head", None, None),
        P(),
        P("blk", "head", None, None),
        P(("head", "blk")),
        P(("head", "blk"), None),
        P(("head", "blk"), None),
        P(("head", "blk"), None),
        P(("head", "blk"), None),
        P(("head", "blk")),
        P(None, ("head", "blk"), None),
        P(None, ("head", "blk"), None),
    )
    sizes = dict(mesh.shape)
    plan = per_device if sizes == {"head": 2, "blk": 4 * NZ} else per_device_plain
    return jax.shard_map(
        plan, mesh=mesh, in_specs=in_specs, out_specs=out_specs, check_vma=False
    )
```

```python
import functools

import jax
import jax.numpy as jnp
import numpy as np
from jax import lax
from jax.experimental import pallas as pl
from jax.experimental.pallas import tpu as pltpu
from jax.sharding import PartitionSpec as P

QUERY_HEADS = 12
KEY_VALUE_HEADS = 2
HEAD_SIZE = 128
TOP = 4
E = 8
CAP = 96

ROTARY_BASE = 10000.0
FLOOR_SCORE = -1e30

MESH = pl.DeviceIdType.MESH
NZ = 4
SPAN = 32 * 128.0
BF = jnp.bfloat16
F32 = jnp.float32

def product(left, right):
    return jnp.dot(left, right, preferred_element_type=jnp.float32)


def rms_norm(values, gain):
    scale = lax.rsqrt(jnp.mean(values * values, axis=-1, keepdims=True) + 1e-06)
    return values * scale * gain


def rotary_apply(values, where, sign):
    half = values.shape[-1] // 2
    freq = ROTARY_BASE ** (-jnp.arange(half).astype(jnp.float32) / half)
    angle = where.astype(jnp.float32)[:, None] * freq[None, :]
    cosine = jnp.cos(angle)[:, None, :]
    sine = jnp.sin(angle)[:, None, :] * sign
    first = values[..., :half]
    second = values[..., half:]
    return jnp.concatenate(
        [first * cosine - second * sine, second * cosine + first * sine], axis=-1
    )


def doc_layout(position_index, doc_starts):
    inside = (position_index[:, None] >= doc_starts[None, :]).astype(jnp.int32)
    document_segment = jnp.sum(inside, axis=-1) - 1
    begin = jnp.max(jnp.where(inside > 0, doc_starts[None, :], 0), axis=-1)
    return (document_segment, position_index - begin)


def gated(pair):
    half = pair.shape[-1] // 2
    return jax.nn.gelu(pair[..., :half], approximate=True) * pair[..., half:]


def in_blocks(step_fn, carry, piece, rows):
    count_blocks = piece[0].shape[0] // rows

    def turn(number, state):
        part = tuple((lax.dynamic_slice_in_dim(item, number * rows, rows, 0) for item in piece))
        return step_fn(state, part, number * rows)

    return lax.fori_loop(0, count_blocks, turn, carry)


def per_device_plain(
    states,
    teacher,
    valid,
    routes,
    gates,
    doc_starts,
    norm_one,
    w_query,
    key_weight,
    value_weight,
    w_output,
    norm_two,
    expert_in,
    expert_out,
):
    count_per_token = states.shape[2]
    width = states.shape[3]
    pairs = lax.axis_size("head")
    blocks = lax.axis_size("blk")
    rows = count_per_token * pairs
    span = rows * blocks
    head_group = QUERY_HEADS // KEY_VALUE_HEADS
    scale = HEAD_SIZE ** (-0.5)
    highest = lax.Precision.HIGHEST
    block_index = lax.axis_index("blk")
    pair_index = lax.axis_index("head")
    token_index = (block_index * pairs + pair_index) * count_per_token + jnp.arange(
        count_per_token, dtype=jnp.int32
    )
    unused_segment, token_position = doc_layout(token_index, doc_starts)
    query_index = block_index * rows + jnp.arange(rows, dtype=jnp.int32)
    query_segment, query_where = doc_layout(query_index, doc_starts)
    last_query = block_index * rows + rows - 1
    inputs = states.reshape(count_per_token, width).astype(jnp.float32)
    target = teacher.reshape(count_per_token, width).astype(jnp.float32)
    keep_mask = valid.reshape(count_per_token).astype(jnp.float32)
    route_rows = routes.reshape(count_per_token, TOP)
    gate_rows = gates.reshape(count_per_token, TOP)
    query_w, key_w, value_w, out_w, gain_low_one, gain_low_two = (
        lax.all_gather(w_query, ("head", "blk"), axis=0, tiled=True),
        lax.all_gather(key_weight, ("head", "blk"), axis=0, tiled=True),
        lax.all_gather(value_weight, ("head", "blk"), axis=0, tiled=True),
        lax.all_gather(w_output, ("head", "blk"), axis=0, tiled=True),
        lax.all_gather(norm_one, ("head", "blk"), axis=0, tiled=True),
        lax.all_gather(norm_two, ("head", "blk"), axis=0, tiled=True),
    )
    gain_one = gain_low_one.astype(jnp.float32)
    gain_two = gain_low_two.astype(jnp.float32)
    normed_one = rms_norm(inputs, gain_one)
    normed_low = normed_one.astype(jnp.bfloat16)
    query_lin = product(normed_low, query_w)
    key_linear = product(normed_low, key_w)
    value_linear = product(normed_low, value_w)
    query_rotated = rotary_apply(
        query_lin.reshape(count_per_token, QUERY_HEADS, HEAD_SIZE), token_position, 1.0
    )
    key_rotated = rotary_apply(
        key_linear.reshape(count_per_token, KEY_VALUE_HEADS, HEAD_SIZE), token_position, 1.0
    )
    query_outgoing = query_rotated.astype(jnp.bfloat16).reshape(
        count_per_token, KEY_VALUE_HEADS, head_group * HEAD_SIZE
    )
    key_send = key_rotated.astype(jnp.bfloat16)
    value_outgoing = value_linear.astype(jnp.bfloat16).reshape(
        count_per_token, KEY_VALUE_HEADS, HEAD_SIZE
    )
    query_grp, key_grp, value_grp = (
        lax.all_to_all(query_outgoing, "head", split_axis=1, concat_axis=0, tiled=True),
        lax.all_to_all(key_send, "head", split_axis=1, concat_axis=0, tiled=True),
        lax.all_to_all(value_outgoing, "head", split_axis=1, concat_axis=0, tiled=True),
    )
    query_heads = query_grp.reshape(rows, head_group, HEAD_SIZE)
    key_rows = key_grp.reshape(rows, HEAD_SIZE)
    value_rows = value_grp.reshape(rows, HEAD_SIZE)

    def scores_for(keys, start):
        block_size = keys.shape[0]
        key_index = start + jnp.arange(block_size, dtype=jnp.int32)
        key_segment, unused_where = doc_layout(key_index, doc_starts)
        allowed = (key_index[None, :] <= query_index[:, None]) & (
            key_segment[None, :] == query_segment[:, None]
        )
        raw = (
            jnp.einsum("qhd,kd->hqk", query_heads, keys, preferred_element_type=jnp.float32) * scale
        )
        return (raw, allowed[None])

    def attend(carry, piece, start):
        keys, values = piece

        def work(state):
            running, total, accum = state
            raw, allowed = scores_for(keys, start)
            masked = jnp.where(allowed, raw, FLOOR_SCORE)
            newest = jnp.maximum(running, jnp.max(masked, axis=-1))
            factor = jnp.exp(running - newest)
            weights = jnp.where(allowed, jnp.exp(masked - newest[..., None]), 0.0)
            total = total * factor + jnp.sum(weights, axis=-1)
            update = jnp.einsum(
                "hqk,kd->qhd",
                weights.astype(jnp.bfloat16),
                values,
                preferred_element_type=jnp.float32,
            )
            accum = accum * factor.T[:, :, None] + update
            return (newest, total, accum)

        return lax.cond(start <= last_query, work, lambda state: state, carry)

    start_state = (
        jnp.full((head_group, rows), FLOOR_SCORE, jnp.float32),
        jnp.zeros((head_group, rows), jnp.float32),
        jnp.zeros((rows, head_group, HEAD_SIZE), jnp.float32),
    )
    running, total, accum = in_blocks(
        attend,
        start_state,
        (
            lax.all_gather(key_rows, "blk", axis=0, tiled=True),
            lax.all_gather(value_rows, "blk", axis=0, tiled=True),
        ),
        rows,
    )
    attn_full = accum / total.T[:, :, None]
    log_total = running + jnp.log(total)
    out_send = attn_full.astype(jnp.bfloat16).reshape(rows, 1, head_group * HEAD_SIZE)
    out_tok = lax.all_to_all(out_send, "head", split_axis=0, concat_axis=1, tiled=True).reshape(
        count_per_token, QUERY_HEADS * HEAD_SIZE
    )
    residual = inputs + product(out_tok, out_w)
    normed_two = rms_norm(residual, gain_two)
    normed_two_low = normed_two.astype(jnp.bfloat16)
    up_w, down_w = (
        lax.all_gather(expert_in, ("head", "blk"), axis=1, tiled=True),
        lax.all_gather(expert_out, ("head", "blk"), axis=1, tiled=True),
    )
    route_hot = (route_rows[:, :, None] == jnp.arange(E, dtype=jnp.int32)[None, None, :]).astype(
        jnp.int32
    )
    flat_hot = route_hot.reshape(count_per_token * TOP, E)
    before = jnp.cumsum(flat_hot, axis=0) - flat_hot
    slot = jnp.sum(before * flat_hot, axis=-1).reshape(count_per_token, TOP)
    slot_hot = (slot[:, :, None] == jnp.arange(CAP, dtype=jnp.int32)[None, None, :]).astype(
        jnp.float32
    )
    route_float = route_hot.astype(jnp.float32)
    dispatch = jnp.einsum("tje,tjc->ect", route_float, slot_hot, precision=highest)
    combine = jnp.einsum("tje,tjc,tj->ect", route_float, slot_hot, gate_rows, precision=highest)
    expert_rows = jnp.einsum(
        "ect,td->ecd",
        dispatch.astype(jnp.bfloat16),
        normed_two_low,
        preferred_element_type=jnp.float32,
    ).astype(jnp.bfloat16)
    pair = jnp.einsum("ecd,edf->ecf", expert_rows, up_w, preferred_element_type=jnp.float32)
    hidden_low = gated(pair).astype(jnp.bfloat16)
    expert_result = jnp.einsum(
        "ecf,efd->ecd", hidden_low, down_w, preferred_element_type=jnp.float32
    )
    mixture = jnp.einsum("ect,ecd->td", combine, expert_result, precision=highest)
    final = residual + mixture
    diff = final - target
    local_count = jnp.sum(keep_mask)
    local_error = jnp.sum(keep_mask * jnp.sum(diff * diff, axis=-1))
    count_all, error_all = lax.psum((local_count, local_error), ("head", "blk"))
    loss = error_all / (width * count_all)
    grad_final = keep_mask[:, None] * diff * (span * 1.0 / count_all)
    up_back, down_back = (
        lax.all_gather(expert_in, ("head", "blk"), axis=1, tiled=True),
        lax.all_gather(expert_out, ("head", "blk"), axis=1, tiled=True),
    )
    grad_result = jnp.einsum("ect,td->ecd", combine, grad_final, precision=highest).astype(
        jnp.bfloat16
    )
    grad_down = jnp.einsum(
        "ecf,ecd->efd", hidden_low, grad_result, preferred_element_type=jnp.float32
    )
    grad_hidden = jnp.einsum(
        "ecd,efd->ecf", grad_result, down_back, preferred_element_type=jnp.float32
    )
    unused_value, pull_gate = jax.vjp(gated, pair)
    grad_pair = pull_gate(grad_hidden)[0].astype(jnp.bfloat16)
    grad_up = jnp.einsum("ecd,ecf->edf", expert_rows, grad_pair, preferred_element_type=jnp.float32)
    grad_rows = jnp.einsum("ecf,edf->ecd", grad_pair, up_back, preferred_element_type=jnp.float32)
    grad_normed_two = jnp.einsum("ect,ecd->td", dispatch, grad_rows, precision=highest)
    unused_value, pull_two = jax.vjp(rms_norm, residual, gain_two)
    grad_res_norm, grad_gain_two = pull_two(grad_normed_two)
    grad_residual = grad_final + grad_res_norm
    grad_attn_low = grad_residual.astype(jnp.bfloat16)
    grad_out_w = jnp.einsum("tk,td->kd", out_tok, grad_attn_low, preferred_element_type=jnp.float32)
    output_gradient_token = jnp.einsum(
        "td,kd->tk", grad_attn_low, out_w, preferred_element_type=jnp.float32
    ).astype(jnp.bfloat16)
    grad_out_grp = lax.all_to_all(
        output_gradient_token.reshape(count_per_token, KEY_VALUE_HEADS, head_group * HEAD_SIZE),
        "head",
        split_axis=1,
        concat_axis=0,
        tiled=True,
    ).reshape(rows, head_group, HEAD_SIZE)
    delta = jnp.einsum(
        "qhd,qhd->hq", grad_out_grp.astype(jnp.float32), attn_full, precision=highest
    )

    def attend_back(carry, piece, start):
        keys, values = piece

        def work(state):
            grad_query, grad_keys, grad_values = state
            raw, allowed = scores_for(keys, start)
            weights = jnp.where(allowed, jnp.exp(raw - log_total[..., None]), 0.0)
            grad_weights = jnp.einsum(
                "qhd,kd->hqk", grad_out_grp, values, preferred_element_type=jnp.float32
            )
            grad_raw = (weights * (grad_weights - delta[..., None])).astype(jnp.bfloat16)
            grad_query = (
                grad_query
                + jnp.einsum("hqk,kd->qhd", grad_raw, keys, preferred_element_type=jnp.float32)
                * scale
            )
            key_part = (
                jnp.einsum("hqk,qhd->kd", grad_raw, query_heads, preferred_element_type=jnp.float32)
                * scale
            )
            value_part = jnp.einsum(
                "hqk,qhd->kd",
                weights.astype(jnp.bfloat16),
                grad_out_grp,
                preferred_element_type=jnp.float32,
            )
            block_size = keys.shape[0]
            grad_keys = lax.dynamic_update_slice_in_dim(
                grad_keys,
                lax.dynamic_slice_in_dim(grad_keys, start, block_size, 0) + key_part,
                start,
                0,
            )
            grad_values = lax.dynamic_update_slice_in_dim(
                grad_values,
                lax.dynamic_slice_in_dim(grad_values, start, block_size, 0) + value_part,
                start,
                0,
            )
            return (grad_query, grad_keys, grad_values)

        return lax.cond(start <= last_query, work, lambda state: state, carry)

    back_state = (
        jnp.zeros((rows, head_group, HEAD_SIZE), jnp.float32),
        jnp.zeros((span, HEAD_SIZE), jnp.float32),
        jnp.zeros((span, HEAD_SIZE), jnp.float32),
    )
    grad_query, grad_keys_full, grad_values_full = in_blocks(
        attend_back,
        back_state,
        (
            lax.all_gather(key_rows, "blk", axis=0, tiled=True),
            lax.all_gather(value_rows, "blk", axis=0, tiled=True),
        ),
        rows,
    )
    grad_keys, grad_values = (
        lax.psum_scatter(grad_keys_full, "blk", scatter_dimension=0, tiled=True),
        lax.psum_scatter(grad_values_full, "blk", scatter_dimension=0, tiled=True),
    )
    grad_query_lin = (
        rotary_apply(grad_query, query_where, -1.0)
        .astype(jnp.bfloat16)
        .reshape(rows, 1, head_group * HEAD_SIZE)
    )
    grad_key_lin = rotary_apply(grad_keys.reshape(rows, 1, HEAD_SIZE), query_where, -1.0).astype(
        jnp.bfloat16
    )
    grad_value_lin = grad_values.astype(jnp.bfloat16).reshape(rows, 1, HEAD_SIZE)
    back_query, key_backward, value_backward = (
        lax.all_to_all(grad_query_lin, "head", split_axis=0, concat_axis=1, tiled=True),
        lax.all_to_all(grad_key_lin, "head", split_axis=0, concat_axis=1, tiled=True),
        lax.all_to_all(grad_value_lin, "head", split_axis=0, concat_axis=1, tiled=True),
    )
    back_query = back_query.reshape(count_per_token, QUERY_HEADS * HEAD_SIZE)
    key_backward = key_backward.reshape(count_per_token, KEY_VALUE_HEADS * HEAD_SIZE)
    value_backward = value_backward.reshape(count_per_token, KEY_VALUE_HEADS * HEAD_SIZE)
    grad_query_w = jnp.einsum(
        "td,tk->dk", normed_low, back_query, preferred_element_type=jnp.float32
    )
    grad_key_w = jnp.einsum(
        "td,tk->dk", normed_low, key_backward, preferred_element_type=jnp.float32
    )
    grad_value_w = jnp.einsum(
        "td,tk->dk", normed_low, value_backward, preferred_element_type=jnp.float32
    )
    grad_normed_one = jnp.einsum(
        "tk,dk->td", back_query, query_w, preferred_element_type=jnp.float32
    )
    grad_normed_one = grad_normed_one + jnp.einsum(
        "tk,dk->td", key_backward, key_w, preferred_element_type=jnp.float32
    )
    grad_normed_one = grad_normed_one + jnp.einsum(
        "tk,dk->td", value_backward, value_w, preferred_element_type=jnp.float32
    )
    unused_value, pull_one = jax.vjp(rms_norm, inputs, gain_one)
    grad_in_norm, grad_gain_one = pull_one(grad_normed_one)
    grad_inputs = grad_residual + grad_in_norm
    sums = (
        lax.psum_scatter(grad_query_w, ("head", "blk"), scatter_dimension=0, tiled=True),
        lax.psum_scatter(grad_key_w, ("head", "blk"), scatter_dimension=0, tiled=True),
        lax.psum_scatter(grad_value_w, ("head", "blk"), scatter_dimension=0, tiled=True),
        lax.psum_scatter(grad_out_w, ("head", "blk"), scatter_dimension=0, tiled=True),
        lax.psum_scatter(grad_gain_one, ("head", "blk"), scatter_dimension=0, tiled=True),
        lax.psum_scatter(grad_gain_two, ("head", "blk"), scatter_dimension=0, tiled=True),
        lax.psum_scatter(grad_up, ("head", "blk"), scatter_dimension=1, tiled=True),
        lax.psum_scatter(grad_down, ("head", "blk"), scatter_dimension=1, tiled=True),
    )
    shape = states.shape
    return (
        final.astype(jnp.bfloat16).reshape(shape),
        loss,
        grad_inputs.reshape(shape),
        sums[4],
        sums[0],
        sums[1],
        sums[2],
        sums[3],
        sums[5],
        sums[6],
        sums[7],
    )


class Place:
    def __init__(self):
        self.x = lax.axis_index("head")
        self.b = lax.axis_index("blk")
        self.c = self.b % 2
        self.y = (self.b // 2) % 2
        self.z = self.b // 4

    def near(self, kind):
        x, y, z, c = self.x, self.y, self.z, self.c
        if kind == "up":
            z = jnp.minimum(z + 1, NZ - 1)
        elif kind == "down":
            z = jnp.maximum(z - 1, 0)
        elif kind == "y":
            y = 1 - y
        elif kind == "x":
            x = 1 - x
        elif kind == "c":
            c = 1 - c
        return (x, z * 4 + y * 2 + c)

    def blk(self, z, y, c):
        return z * 4 + y * 2 + c

    def outward(self, j):
        inner = jnp.where(j < 2, 1 - j, j)
        order = jnp.where((self.z == 0) | (self.z == NZ - 1), j, inner)
        return jnp.where(self.z < 2, order, NZ - 1 - order)

    def inward(self, j):
        inner = jnp.where(j == 0, 3, jnp.where(j == 1, 0, jnp.where(j == 2, 2, 1)))
        order = jnp.where((self.z == 0) | (self.z == NZ - 1), NZ - 1 - j, inner)
        return jnp.where(self.z < 2, order, NZ - 1 - order)


def greet_all(me):
    barrier = pltpu.get_barrier_semaphore()

    def one(k, carry):
        pl.semaphore_signal(
            barrier, inc=1, device_id=((me.x + k // 16) % 2, (me.b + k) % 16), device_id_type=MESH
        )
        return carry

    lax.fori_loop(1, 32, one, 0)


def all_greeted():
    pl.semaphore_wait(pltpu.get_barrier_semaphore(), 31)


def remote(src, dst, send, recv, to):
    return pltpu.make_async_remote_copy(
        src_ref=src, dst_ref=dst, send_sem=send, recv_sem=recv, device_id=to, device_id_type=MESH
    )


def arrived(ref, sem, me):
    remote(ref, ref, sem, sem, me.near("c")).wait_recv()


def left(ref, sem, me):
    remote(ref, ref, sem, sem, me.near("c")).wait_send()


class Gather:
    def __init__(self, me, g, index, send, recv, cols=None, causal=False):
        self.me, self.g, self.index, self.send, self.recv, self.causal = me, g, index, send, recv, causal
        start, width = cols or (0, g.shape[2])
        cut = (width // 2 + 127) // 128 * 128
        self.cols = pl.ds(start, width)
        self.first, self.second = pl.ds(start, cut), pl.ds(start + cut, width - cut)

    def place(self, j):
        return self.me.z - j if self.causal else self.me.outward(j)

    def valid(self, j):
        return (j >= 0) & (j <= (self.me.z if self.causal else NZ - 1))

    def ups(self, zz):
        if self.causal:
            return self.me.z < NZ - 1
        return (zz <= self.me.z) & (self.me.z < NZ - 1)

    def downs(self, zz):
        return (zz >= self.me.z) & (self.me.z > 0)

    def put(self, j, kind, n, s, cols=None, slot=0):
        ref = self.g.at[s, :, self.cols if cols is None else cols]
        remote(ref, ref, self.send.at[j, n], self.recv.at[s, slot], self.me.near(kind)).start()

    def wait(self, s):
        arrived(self.g.at[s, :, self.cols], self.recv.at[s, 0], self.me)

    def turn(self, j):
        me, index = self.me, self.index
        x, y, c = me.x, me.y, me.c

        @pl.when(self.valid(j) & (j > 0))
        def _():
            self.wait(index(x, self.place(j), y, c))

        @pl.when(self.valid(j))
        def _():
            zz = self.place(j)
            own = index(x, zz, y, c)
            pl.when(self.ups(zz))(lambda: self.put(j, "up", 0, own))
            if not self.causal:
                pl.when(self.downs(zz))(lambda: self.put(j, "down", 1, own))
            self.put(j, "y", 2, own)
            self.put(j, "x", 3, own)
            self.put(j, "c", 6, own)

        @pl.when(self.valid(j - 1))
        def _():
            i = j - 1
            zp = self.place(i)
            s = index(x, zp, 1 - y, c)
            self.wait(s)
            self.put(i, "x", 4, s, self.first, 0)
            self.put(i, "c", 7, s)
            t = index(1 - x, zp, y, c)
            self.wait(t)
            self.put(i, "y", 5, t, self.second, 1)
            self.put(i, "c", 8, t)

        @pl.when(self.valid(j - 2))
        def _():
            i = j - 2
            s = index(1 - x, self.place(i), 1 - y, c)
            arrived(self.g.at[s, :, self.first], self.recv.at[s, 0], me)
            arrived(self.g.at[s, :, self.second], self.recv.at[s, 1], me)
            self.put(i, "c", 9, s)

    def from_core(self, j):
        me = self.me
        for xx in (me.x, 1 - me.x):
            for yy in (me.y, 1 - me.y):
                self.wait(self.index(xx, self.place(j), yy, 1 - me.c))

    def from_cores(self):
        def one(j, carry):
            self.from_core(j)
            return carry

        lax.fori_loop(0, 4, one, 0)

    def close(self):
        me = self.me

        def one(j, carry):
            @pl.when(self.valid(j))
            def _():
                zz = self.place(j)
                own = self.index(me.x, zz, me.y, me.c)
                whole = self.g.at[own, :, self.cols]
                first, second = self.g.at[own, :, self.first], self.g.at[own, :, self.second]
                pl.when(self.ups(zz))(lambda: left(whole, self.send.at[j, 0], me))
                if not self.causal:
                    pl.when(self.downs(zz))(lambda: left(whole, self.send.at[j, 1], me))
                for n in (2, 3, 6, 7, 8, 9):
                    left(whole, self.send.at[j, n], me)
                left(first, self.send.at[j, 4], me)
                left(second, self.send.at[j, 5], me)

            return carry

        lax.fori_loop(0, 4, one, 0)


class Sum:
    def __init__(self, me, part, index, out, room, sems, cols=None, causal=False):
        self.me, self.part, self.index, self.out, self.causal = me, part, index, out, causal
        start, width = cols or (0, part.shape[2])
        self.cols = pl.ds(start, width)
        self.rc, self.rx, self.ry, self.rn, self.rz, self.acc = room
        self.sc, self.ss, self.vc, self.vn, self.vz = sems
        self.half = (width // 2 + 127) // 128 * 128
        self.first, self.second = pl.ds(0, self.half), pl.ds(self.half, width - self.half)

    @staticmethod
    def room(rows, columns):
        half = (columns // 2 + 127) // 128 * 128
        return [
            pltpu.VMEM((16, rows, columns), BF),
            pltpu.VMEM((4, rows, half), BF),
            pltpu.VMEM((4, rows, columns - half), BF),
            pltpu.VMEM((2, 4, rows, columns), BF),
            pltpu.VMEM((5, rows, columns), BF),
            pltpu.VMEM((rows, columns), F32),
            DMA((16,)),
            DMA((4, 6)),
            DMA((16,)),
            DMA((4, 4)),
            DMA((5,)),
        ]

    def place(self, j):
        return j if self.causal else self.me.inward(j)

    def valid(self, j):
        return (j >= 0) & (j <= (self.me.z if self.causal else NZ - 1))

    def slot(self, xx, zz, yy):
        return zz * 4 + xx * 2 + yy

    def lead(self, j):
        me = self.me
        zz = self.place(j)
        for xx in (1 - me.x, me.x):
            for yy in (1 - me.y, me.y):
                k = self.slot(xx, zz, yy)
                src = self.part.at[self.index(xx, zz, yy, 1 - me.c), :, self.cols]
                remote(src, self.rc.at[k], self.sc.at[k], self.vc.at[k], me.near("c")).start()

    def with_core(self, xx, zz, yy):
        k = self.slot(xx, zz, yy)
        arrived(self.rc.at[k], self.vc.at[k], self.me)
        own = self.part[self.index(xx, zz, yy, self.me.c), :, self.cols]
        return k, own.astype(F32) + self.rc[k].astype(F32)

    def first_leg(self, i):
        me, half, first, second = self.me, self.half, self.first, self.second
        rc, rx, ry, rn, ss, vn = self.rc, self.rx, self.ry, self.rn, self.ss, self.vn
        x, y = me.x, me.y

        @pl.when(self.valid(i))
        def _():
            zz = self.place(i)
            k, total = self.with_core(1 - x, zz, 1 - y)
            rc[k] = total.astype(BF)
            remote(rc.at[k, :, first], rx.at[zz], ss.at[i, 0], vn.at[zz, 0], me.near("x")).start()
            remote(rc.at[k, :, second], ry.at[zz], ss.at[i, 1], vn.at[zz, 1], me.near("y")).start()

    def second_leg(self, i):
        me, half, first, second = self.me, self.half, self.first, self.second
        rc, rx, ry, rn, ss, vn = self.rc, self.rx, self.ry, self.rn, self.ss, self.vn
        x, y = me.x, me.y

        @pl.when(self.valid(i))
        def _():
            zz = self.place(i)
            k, total = self.with_core(x, zz, 1 - y)
            arrived(rx.at[zz], vn.at[zz, 0], me)
            rc[k, :, second] = total[:, half:].astype(BF)
            rc[k, :, first] = (total[:, :half] + rx[zz].astype(F32)).astype(BF)
            remote(rc.at[k], rn.at[0, zz], ss.at[i, 2], vn.at[zz, 2], me.near("y")).start()
            k, total = self.with_core(1 - x, zz, y)
            arrived(ry.at[zz], vn.at[zz, 1], me)
            rc[k, :, first] = total[:, :half].astype(BF)
            rc[k, :, second] = (total[:, half:] + ry[zz].astype(F32)).astype(BF)
            remote(rc.at[k], rn.at[1, zz], ss.at[i, 3], vn.at[zz, 3], me.near("x")).start()

    def third_leg(self, i):
        me, half, first, second = self.me, self.half, self.first, self.second
        rc, rx, ry, rn, ss, vn = self.rc, self.rx, self.ry, self.rn, self.ss, self.vn
        x, y = me.x, me.y

        @pl.when(self.valid(i))
        def _():
            zz = self.place(i)
            k, total = self.with_core(x, zz, y)
            arrived(rn.at[0, zz], vn.at[zz, 2], me)
            arrived(rn.at[1, zz], vn.at[zz, 3], me)
            self.acc[...] = total + rn[0, zz].astype(F32) + rn[1, zz].astype(F32)
            along_z(me, i, zz, self.acc, rc.at[k], self.rz, ss, 4, self.vz, self.causal)

            @pl.when(zz == me.z)
            def _():
                self.out[:, self.cols] = self.acc[...]

    def turn(self, j):
        self.first_leg(j)
        self.second_leg(j - 1)
        self.third_leg(j - 2)

    def first_legs(self):
        def one(j, carry):
            self.first_leg(j)
            return carry

        lax.fori_loop(0, 4, one, 0)

    def rest(self, j):
        self.second_leg(j)
        self.third_leg(j - 1)

    def close(self):
        me = self.me
        whole = self.rc.at[0]
        first, second = self.rc.at[0, :, self.first], self.rc.at[0, :, self.second]

        def one(j, carry):
            @pl.when(self.valid(j))
            def _():
                zz = self.place(j)
                for xx in (1 - me.x, me.x):
                    for yy in (1 - me.y, me.y):
                        left(whole, self.sc.at[self.slot(xx, zz, yy)], me)
                left(first, self.ss.at[j, 0], me)
                left(second, self.ss.at[j, 1], me)
                for n in (2, 3):
                    left(whole, self.ss.at[j, n], me)
                if not self.causal:
                    pl.when(zz > me.z)(lambda: left(whole, self.ss.at[j, 4], me))
                pl.when(zz < me.z)(lambda: left(whole, self.ss.at[j, 5], me))

            return carry

        lax.fori_loop(0, 4, one, 0)


def along_z(me, i, zz, acc, room, rz, ss, n, vz, causal=False):
    z = me.z

    def add(slot):
        arrived(rz.at[slot], vz.at[slot], me)
        acc[...] += rz[slot].astype(F32)

    if not causal:
        pl.when((zz >= z) & (z > 0))(lambda: add(zz))
    pl.when((zz < z) & (z < NZ - 1))(lambda: add(zz))
    pl.when((zz == z) & (z < NZ - 1))(lambda: add(4))

    if not causal:

        @pl.when(zz > z)
        def _():
            room[...] = acc[...].astype(BF)
            remote(room, rz.at[zz], ss.at[i, n], vz.at[zz], me.near("up")).start()

    @pl.when(zz < z)
    def _():
        room[...] = acc[...].astype(BF)
        there = jnp.where(zz == z - 1, 4, zz)
        remote(room, rz.at[there], ss.at[i, n + 1], vz.at[there], me.near("down")).start()


def by_weight(x, z, y, c):
    return x * 16 + z * 4 + y * 2 + c


def by_token(x, z, y, c):
    return (z * 4 + y * 2 + c) * 2 + x


ANY = pl.BlockSpec(memory_space=pl.ANY)
VMEM = pl.BlockSpec(memory_space=pltpu.VMEM)
DMA = pltpu.SemaphoreType.DMA


def params(number, mib):
    return pltpu.CompilerParams(
        collective_id=number, has_side_effects=True, vmem_limit_bytes=mib << 20
    )


NT = (((1,), (1,)), ((), ()))
TN = (((0,), (0,)), ((), ()))
GROUP = QUERY_HEADS // KEY_VALUE_HEADS
LANES = GROUP * 128
SCALE = HEAD_SIZE ** (-0.5)
POWER = SCALE * 1.4426950408889634


def turned(u, cosine, sine):
    return u * cosine + pltpu.roll(u, 64, 1) * sine


def begin_of(place, doc):
    begin = jnp.zeros_like(place)
    for i in range(doc.shape[1]):
        start = doc[0:1, i : i + 1]
        begin = jnp.where(place >= start, jnp.maximum(begin, start), begin)
    return begin


def rotary_tables(me, doc, freq):
    first = (me.b * 2 + me.x) * 128
    place = first + lax.broadcasted_iota(jnp.int32, (128, 128), 0)
    angle = (place - begin_of(place, doc)).astype(F32) * freq[...]
    sine = jnp.sin(angle)
    lane = lax.broadcasted_iota(jnp.int32, (128, 128), 1)
    return jnp.cos(angle), jnp.where(lane < 64, -sine, sine)


def query_bounds(me, doc):
    place = (me.b * 2 + me.x) * 128 + lax.broadcasted_iota(jnp.int32, (1, LANES), 1) % 128
    return begin_of(place, doc), place


def allowed_keys(start, bounds):
    key = start + lax.broadcasted_iota(jnp.int32, (256, LANES), 0)
    return (key >= bounds[0]) & (key <= bounds[1])


def eye(n):
    return lax.broadcasted_iota(jnp.int32, (n, n), 0) == lax.broadcasted_iota(jnp.int32, (n, n), 1)


def as_column(row):
    return jnp.sum(jnp.where(eye(row.shape[1]), row, 0.0), axis=1, keepdims=True)


def as_row(column):
    return jnp.sum(jnp.where(eye(column.shape[0]), column, 0.0), axis=0, keepdims=True)


QKV = 2048
WIDE = QKV + 128
PIECES = ((0, 1152), (1152, 1024))


def front_kernel(
    doc_in, freq_in, one_in, two_in, valid_in, states, down_in, wq, wk, wv, wo, up,
    gq_out, go_out, kv_out, win, wout, h_out, n2_out, n1_out, qs_out, o_out, lse_out, count_out, gains_out,
    doc, freq, norm_one, norm_two, valid, lse, count, gains_row, gq, go, kv, down, top, total, acc, low_rows, down_raw, cos, sin, n1, qs, o, h, n2,
    load_sem, own_sem, qsend, qrecv, gsend, grecv, ksend, krecv, asend, arecv, osend, orecv,
):
    me = Place()
    greet_all(me)
    x, y, z, b, c = me.x, me.y, me.z, me.b, me.c
    here = by_weight(x, z, y, c)
    mine = [
        pltpu.make_async_copy(wq, gq.at[here, :, pl.ds(0, 1536)], own_sem.at[0]),
        pltpu.make_async_copy(wk, gq.at[here, :, pl.ds(1536, 256)], own_sem.at[1]),
        pltpu.make_async_copy(wv, gq.at[here, :, pl.ds(1792, 256)], own_sem.at[2]),
        pltpu.make_async_copy(wo, go.at[here], own_sem.at[3]),
    ]
    pairs = (
        (down_in, down_raw), (states, low_rows), (doc_in, doc), (freq_in, freq),
        (one_in, norm_one), (two_in, norm_two), (valid_in, valid),
    )
    loads = [pltpu.make_async_copy(src, dst, load_sem.at[i]) for i, (src, dst) in enumerate(pairs)]
    for copy in loads[4:] + mine + loads[:4]:
        copy.start()
    for load in loads[4:]:
        load.wait()

    lane = lax.broadcasted_iota(jnp.int32, (48, 128), 1)
    kept = jnp.sum(valid[...].astype(F32))
    extra = jnp.where(
        lane == 0,
        as_column(norm_one[...].astype(F32)),
        jnp.where(lane == 1, as_column(norm_two[...].astype(F32)), jnp.where(lane == 2, kept, 0.0)),
    )
    gq[here, :, pl.ds(QKV, 128)] = extra.astype(BF)
    all_greeted()
    for copy in mine:
        copy.wait()

    def own_piece(n):
        col = pl.multiple_of(n * 768 + c * 384, 128)
        return pltpu.make_async_copy(
            up.at[b // 2, :, pl.ds(col, 384)], win.at[b, :, pl.ds(n * 384, 384)], own_sem.at[4 + n]
        )

    def own_down():
        return pltpu.make_async_copy(down.at[b // 2], wout.at[b], own_sem.at[6])

    def deal(k, carry):
        t = (b + (k * 13) % 16) % 16
        for n in range(2):
            col = pl.multiple_of(n * 768 + (t % 2) * 384, 128)
            remote(
                up.at[t // 2, :, pl.ds(col, 384)],
                win.at[b, :, pl.ds(n * 384, 384)],
                asend.at[k, n],
                arecv.at[b, n],
                (x, t),
            ).start()
        pl.when(t % 2 == x)(
            lambda: remote(down.at[t // 2], wout.at[b], osend.at[k], orecv.at[b], (x, t)).start()
        )
        return carry

    weights = [
        Gather(me, gq, by_weight, qsend.at[i], qrecv.at[i], PIECES[i]) for i in range(len(PIECES))
    ]

    def first_turn(j, carry):
        for piece in weights:
            piece.turn(j)

        @pl.when(j == 0)
        def _():
            for load in loads[:4]:
                load.wait()
            for e in range(E):
                wide = down_raw[e].astype(F32)
                down[e] = jnp.concatenate([wide[:, :768], wide[:, 768:]], axis=0).astype(BF)
            cos[...], sin[...] = rotary_tables(me, doc, freq)

        lax.fori_loop(1 + j * 3, jnp.minimum(4 + j * 3, 16), deal, 0)
        return carry

    lax.fori_loop(0, 6, first_turn, 0)
    for n in range(2):
        own_piece(n).start()
    pl.when(c == x)(lambda: own_down().start())
    bounds = query_bounds(me, doc)
    rows = low_rows[...].astype(F32)
    level = rows * lax.rsqrt(jnp.mean(rows * rows, axis=-1, keepdims=True) + 1e-06)
    for piece in weights:
        piece.from_cores()
    keep = pltpu.make_async_copy(gq, gq_out, own_sem.at[0])
    keep.start()

    gains = gq[:, :, pl.ds(QKV, 128)].reshape(1536, 128).astype(F32).T
    n1[...] = (level * gains[0:1]).astype(BF)
    turns = cos[...], sin[...]
    at = by_token(x, z, y, c)
    keys = Gather(me, kv, by_token, ksend, krecv, causal=True)
    output = Gather(me, go, by_weight, gsend, grecv)
    both = jnp.dot(n1[...], gq[:, :, pl.ds(1536, 512)].reshape(1536, 512), preferred_element_type=F32)
    for i in range(2):
        kv[at, :, i * 128 : i * 128 + 128] = turned(both[:, i * 128 : i * 128 + 128], *turns).astype(BF)
    kv[at, :, 256:512] = both[:, 256:512].astype(BF)
    keys.turn(0)
    query = jnp.dot(n1[...], gq[:, :, pl.ds(0, 1536)].reshape(1536, 1536), preferred_element_type=F32)
    for i in range(QUERY_HEADS):
        r = (i % GROUP) * 128
        qs[i // GROUP, r : r + 128] = turned(query[:, i * 128 : i * 128 + 128], *turns).astype(BF)
    count[...] = jnp.zeros((8, 128), F32) + jnp.sum(gains[2:3]) / 48.0
    gains_row[...] = gains[0:8]
    saved = [
        pltpu.make_async_copy(count, count_out, load_sem.at[5]),
        pltpu.make_async_copy(gains_row, gains_out, load_sem.at[6]),
        pltpu.make_async_copy(n1, n1_out, load_sem.at[0]),
        pltpu.make_async_copy(qs, qs_out, load_sem.at[1]),
    ]
    for copy in saved:
        copy.start()

    top[...] = jnp.full_like(top, FLOOR_SCORE)
    total[...] = jnp.zeros_like(total)
    acc[...] = jnp.zeros_like(acc)
    def block(n):
        ok = allowed_keys(n * 256, bounds)
        for i in range(2):
            k = kv[pl.ds(n * 2, 2), :, i * 128 : i * 128 + 128].reshape(256, 128)
            v = kv[pl.ds(n * 2, 2), :, 256 + i * 128 : 384 + i * 128].reshape(256, 128)
            s = lax.dot_general(k, qs[i], NT, preferred_element_type=F32)
            s = jnp.where(ok, s, FLOOR_SCORE)
            old = top[i]
            new = jnp.maximum(old, jnp.max(s, axis=0, keepdims=True))
            factor = jnp.exp2((old - new) * POWER)
            p = jnp.exp2((s - new) * POWER)
            top[i] = new
            total[i] = total[i] * factor + jnp.sum(p, axis=0, keepdims=True)
            acc[i] = acc[i] * factor + lax.dot_general(v, p.astype(BF), TN, preferred_element_type=F32)

    def close_deal(k, carry):
        piece = win.at[b, :, pl.ds(0, 384)]
        f = (b + 16 - k) % 16
        for n in range(2):
            left(piece, asend.at[k, n], me)
            arrived(win.at[f, :, pl.ds(n * 384, 384)], arecv.at[f, n], me)
        pl.when((b + k) % 2 == x)(lambda: left(wout.at[b], osend.at[k], me))
        pl.when(c == x)(lambda: arrived(wout.at[f], orecv.at[f], me))
        return carry

    def turn(j, carry):
        pl.when(j > 0)(lambda: keys.turn(j))
        output.turn(j - 2)

        @pl.when(j == 1)
        def _():
            for piece in weights:
                piece.close()

        @pl.when(j == 6)
        def _():
            lax.fori_loop(1, 16, close_deal, 0)
            keys.close()


        @pl.when(keys.valid(j - 2))
        def _():
            i = j - 2
            keys.from_core(i)
            zz = z - i
            last = jnp.where(i == 0, y * 2 + c, 3)

            def one(n, carry):
                block(zz * 4 + last - n)
                return carry

            lax.fori_loop(0, last + 1, one, 0)

        return carry

    lax.fori_loop(0, 8, turn, 0)
    keep_k = pltpu.make_async_copy(kv, kv_out, own_sem.at[2])
    keep_k.start()
    for i in range(2):
        lse[i] = top[i] * POWER + jnp.log2(total[i])
        done = acc[i] / total[i]
        for r in range(GROUP):
            col = (i * GROUP + r) * 128
            o[:, col : col + 128] = done[:, r * 128 : r * 128 + 128].T
    more = [pltpu.make_async_copy(o, o_out, load_sem.at[2]), pltpu.make_async_copy(lse, lse_out, load_sem.at[7])]
    for copy in more:
        copy.start()
    output.from_cores()
    keep_o = pltpu.make_async_copy(go, go_out, own_sem.at[1])
    keep_o.start()
    res = low_rows[...].astype(F32) + jnp.dot(
        o[...].astype(BF), go[...].reshape(1536, 1536), preferred_element_type=F32
    )
    h[...] = res
    n2[...] = (
        res * lax.rsqrt(jnp.mean(res * res, axis=-1, keepdims=True) + 1e-06) * gains[1:2]
    ).astype(BF)
    more.append(pltpu.make_async_copy(h, h_out, load_sem.at[3]))
    more.append(pltpu.make_async_copy(n2, n2_out, load_sem.at[4]))
    more[2].start()
    more[3].start()

    output.close()
    for n in range(2):
        own_piece(n).wait()
    pl.when(c == x)(lambda: own_down().wait())
    for copy in [keep, keep_o, keep_k] + saved + more:
        copy.wait()


def run_front(*operands):
    shape = jax.ShapeDtypeStruct
    return pl.pallas_call(
        front_kernel,
        out_shape=(
            shape((32, 48, WIDE), BF),
            shape((32, 48, 1536), BF),
            shape((32, 128, 512), BF),
            shape((16, 48, 768), BF),
            shape((16, 48, 768), BF),
            shape((128, 1536), F32),
            shape((128, 1536), BF),
            shape((128, 1536), BF),
            shape((2, LANES, 128), BF),
            shape((128, 1536), F32),
            shape((2, 1, LANES), F32),
            shape((8, 128), F32),
            shape((8, 1536), F32),
        ),
        in_specs=[ANY] * 12,
        out_specs=(ANY,) * 13,
        scratch_shapes=[
            pltpu.VMEM(operands[0].shape, jnp.int32),
            pltpu.VMEM((1, 128), F32),
            pltpu.VMEM((1, 48), BF),
            pltpu.VMEM((1, 48), BF),
            pltpu.VMEM((1, 128), jnp.int32),
            pltpu.VMEM((2, 1, LANES), F32),
            pltpu.VMEM((8, 128), F32),
            pltpu.VMEM((8, 1536), F32),
            pltpu.VMEM((32, 48, WIDE), BF),
            pltpu.VMEM((32, 48, 1536), BF),
            pltpu.VMEM((32, 128, 512), BF),
            pltpu.VMEM((8, 48, 768), BF),
            pltpu.VMEM((2, 1, LANES), F32),
            pltpu.VMEM((2, 1, LANES), F32),
            pltpu.VMEM((2, 128, LANES), F32),
            pltpu.VMEM((128, 1536), BF),
            pltpu.VMEM((8, 24, 1536), BF),
            pltpu.VMEM((128, 128), F32),
            pltpu.VMEM((128, 128), F32),
            pltpu.VMEM((128, 1536), BF),
            pltpu.VMEM((2, LANES, 128), BF),
            pltpu.VMEM((128, 1536), F32),
            pltpu.VMEM((128, 1536), F32),
            pltpu.VMEM((128, 1536), BF),
            DMA((8,)),
            DMA((7,)),
            DMA((2, 4, 10)),
            DMA((2, 32, 2)),
            DMA((4, 10)),
            DMA((32, 2)),
            DMA((4, 10)),
            DMA((32, 2)),
            DMA((16, 2)),
            DMA((16, 2)),
            DMA((16,)),
            DMA((16,)),
        ],
        compiler_params=params(1, 62),
        name="front",
    )(*operands)


GELU_A = 0.7978845608028654
GELU_B = 0.044715


READY_AT = 4
PARTS = ((0, 64), (64, 48), (112, 16))
CUTS = 2


def experts_kernel(
    routes_in, gates_in, valid_in, count_in, n2, h_in, teacher_in, win, wout,
    err_out, final_out, dn2_out, dy_out, dwin_out, dwout_out,
    routes, gates, valid, count, err, h, teacher, final, dy, nall, dyall, pairs, zg, dpairs, part, rc, ry, rz, rzt, ryt, tail, acc, errs, tables, gate,
    wfull, slab, wdown, dwin, dwin_in, dwout, dwout_in,
    load_sem, own_sem, gsend, grecv, csend, crecv, ysend, yrecv, zsend, zrecv, esend, erecv,
    tsend, trecv, xsend, xrecv,
):
    me = Place()
    greet_all(me)
    x, y, z, b, c = me.x, me.y, me.z, me.b, me.c
    half = pltpu.make_async_copy(win, wfull.at[x], own_sem.at[0])
    half.start()
    loads = [
        pltpu.make_async_copy(n2, nall.at[b], load_sem.at[0]),
        pltpu.make_async_copy(h_in, h, load_sem.at[1]),
        pltpu.make_async_copy(teacher_in, teacher, load_sem.at[2]),
        pltpu.make_async_copy(routes_in, routes, load_sem.at[3]),
        pltpu.make_async_copy(gates_in, gates, load_sem.at[4]),
        pltpu.make_async_copy(valid_in, valid, load_sem.at[5]),
        pltpu.make_async_copy(count_in, count, load_sem.at[6]),
    ]
    for load in loads:
        load.start()
    held = pltpu.make_async_copy(wout, slab, own_sem.at[1])
    pl.when(c == x)(held.start)
    all_greeted()

    def rows_of(p):
        return pl.ds(*PARTS[p])

    def over_weights(k):
        cut = pl.ds(k * 4, 4)
        return remote(win.at[cut], wfull.at[x, cut], xsend.at[k], xrecv.at[k], me.near("x"))

    def over_down():
        return remote(wout, slab, xsend.at[4], xrecv.at[4], me.near("x"))

    def put(buf, way, j, p, kind, n, s):
        ref = buf.at[s, rows_of(p)]
        remote(ref, ref, gsend.at[way, j, p, n], grecv.at[way, s, p], me.near(kind)).start()

    def along(buf, way, j, p, n, s, zz):
        pl.when((zz <= z) & (z < NZ - 1))(lambda: put(buf, way, j, p, "up", n, s))
        pl.when((zz >= z) & (z > 0))(lambda: put(buf, way, j, p, "down", n + 1, s))

    def begin(buf, way, p):
        along(buf, way, 0, p, 0, b, z)
        put(buf, way, 0, p, "y", 2, b)
        put(buf, way, 0, p, "c", 3, b)

    def gather(buf, way, between):
        def turn(j, carry):
            between(j, -1)
            for p in range(CUTS + 1):
                zz = me.outward(j)
                own = me.blk(zz, y, c)

                @pl.when((j > 0) & (j < 4))
                def _():
                    arrived(buf.at[own, rows_of(p)], grecv.at[way, own, p], me)

                @pl.when((j > 0) & (j < 4))
                def _():
                    along(buf, way, j, p, 0, own, zz)
                    if p < CUTS:
                        put(buf, way, j, p, "y", 2, own)
                    put(buf, way, j, p, "c", 3, own)

                @pl.when((j > 0) & (j < 5))
                def _():
                    i = j - 1
                    zp = me.outward(i)
                    s = me.blk(zp, 1 - y, c)
                    arrived(buf.at[s, rows_of(p)], grecv.at[way, s, p], me)
                    if p == CUTS:
                        along(buf, way, i, p, 5, s, zp)
                    put(buf, way, i, p, "c", 4, s)

                between(j, p)
            return carry

        lax.fori_loop(0, 6, turn, 0)

    def close_gather(buf, way):
        def close(j, carry):
            zz = me.outward(j)
            for p in range(CUTS + 1):
                whole = buf.at[b, rows_of(p)]
                ends = (0, 1) if p < CUTS else (0, 1, 5, 6)
                for n in ends:
                    ok = (zz <= z) & (z < NZ - 1) if n in (0, 5) else (zz >= z) & (z > 0)
                    pl.when(ok)(lambda: left(whole, gsend.at[way, j, p, n], me))
                if p < CUTS:
                    left(whole, gsend.at[way, j, p, 2], me)
                else:
                    pl.when(j == 0)(lambda: left(whole, gsend.at[way, j, p, 2], me))
                for n in (3, 4):
                    left(whole, gsend.at[way, j, p, n], me)
            return carry

        lax.fori_loop(0, 4, close, 0)

    def from_core(buf, way, zz, yy):
        s = me.blk(zz, yy, 1 - c)
        for p in range(CUTS + 1):
            arrived(buf.at[s, rows_of(p)], grecv.at[way, s, p], me)

    def to_other_core(way, q):
        remote(part.at[q * 2 + 1 - c], rc.at[q], csend.at[way, q], crecv.at[way, q], me.near("c")).start()

    def lead(way, j):
        zz = me.inward(j)
        q = zz * 2 + 1 - y
        s = q * 2 + c
        arrived(rc.at[q], crecv.at[way, q], me)
        part[s] = (part[s].astype(F32) + rc[q].astype(F32)).astype(BF)
        for p in range(CUTS):
            remote(
                part.at[s, rows_of(p)], ry.at[zz, rows_of(p)], ysend.at[way, j, p], yrecv.at[way, zz, p], me.near("y")
            ).start()

    def follow(way, j, done=None):
        zz = me.inward(j)
        q = zz * 2 + y
        s = q * 2 + c
        arrived(rc.at[q], crecv.at[way, q], me)
        cut = rows_of(CUTS)
        for n, yy in enumerate((1 - y, y)):
            k = zz * 2 + yy
            room = part.at[k * 2 + c, cut]
            if n:
                tail[...] = room[...].astype(F32) + rc[k, cut].astype(F32)
            else:
                tail[...] = room[...].astype(F32)
            along_z(
                me, j, zz, tail, room, rzt.at[n], zsend.at[way, :, CUTS + n], 0, zrecv.at[way, :, CUTS + n]
            )
            if n == 0:

                @pl.when(zz == z)
                def _():
                    room[...] = tail[...].astype(BF)
                    remote(room, ryt, ysend.at[way, 3, CUTS], yrecv.at[way, 0, CUTS], me.near("y")).start()

        for p in range(CUTS):
            cut = rows_of(p)
            arrived(ry.at[zz, cut], yrecv.at[way, zz, p], me)
            piece = acc.at[cut]
            piece[...] = part[s, cut].astype(F32) + rc[q, cut].astype(F32) + ry[zz, cut].astype(F32)
            along_z(
                me, j, zz, piece, part.at[s, cut], rz.at[:, cut], zsend.at[way, :, p], 0, zrecv.at[way, :, p]
            )
            if done is not None:
                pl.when(zz == z)(functools.partial(done, p))

        @pl.when(zz == z)
        def _():
            arrived(ryt, yrecv.at[way, 0, CUTS], me)
            acc[rows_of(CUTS)] = tail[...] + ryt[...].astype(F32)
            if done is not None:
                done(CUTS)

    def close_sum(way):
        def close(j, carry):
            zz = me.inward(j)
            whole = part.at[b]
            left(whole, csend.at[way, j], me)
            left(whole, csend.at[way, j + 4], me)
            for p in range(CUTS + 2):
                piece = part.at[b, rows_of(min(p, CUTS))]
                if p < CUTS:
                    left(piece, ysend.at[way, j, p], me)
                elif p == CUTS:
                    pl.when(j == 3)(lambda: left(piece, ysend.at[way, j, p], me))
                pl.when(zz > z)(lambda: left(piece, zsend.at[way, j, p, 0], me))
                pl.when(zz < z)(lambda: left(piece, zsend.at[way, j, p, 1], me))
            return carry

        lax.fori_loop(0, 4, close, 0)

    def gelu_parts(g):
        t = jnp.tanh(GELU_A * (g + GELU_B * g * g * g))
        return t, 0.5 * g * (1.0 + t)

    def forward(q):
        rows = nall[pl.ds(q * 2, 2)].reshape(256, 1536)
        pair = jnp.dot(rows, wfull[...].reshape(1536, 768), preferred_element_type=F32)
        pairs[q] = pair
        unused, a = gelu_parts(pair[:, :384])
        scale = gate[pl.ds(q * 2, 2)].reshape(256, 1)
        zq = (a * pair[:, 384:] * scale).astype(BF)
        zg[q] = zq
        out = jnp.dot(zq, wdown[...], preferred_element_type=F32)
        part[pl.ds(q * 2, 2)] = out.astype(BF).reshape(2, 128, 1536)
        to_other_core(0, q)

    def backward(q):
        rows = dyall[pl.ds(q * 2, 2)].reshape(256, 1536)
        scale = gate[pl.ds(q * 2, 2)].reshape(256, 1)
        dz = lax.dot_general(rows, wdown[...], NT, preferred_element_type=F32) * scale
        g, u = pairs[q, :, :384], pairs[q, :, 384:]
        t, a = gelu_parts(g)
        slope = 0.5 * (1.0 + t) + 0.5 * g * (1.0 - t * t) * (GELU_A * (1.0 + 3.0 * GELU_B * g * g))
        dpairs[q, :, :384] = (dz * u * slope).astype(BF)
        dpairs[q, :, 384:] = (dz * a).astype(BF)
        out = lax.dot_general(dpairs[q], wfull[...].reshape(1536, 768), NT, preferred_element_type=F32)
        part[pl.ds(q * 2, 2)] = out.astype(BF).reshape(2, 128, 1536)
        to_other_core(1, q)

    loads[0].wait()
    pl.when(c == x)(held.wait)

    def tell_gates(k, carry):
        to = (b + k) % 16
        remote(tables.at[b], tables.at[b], tsend.at[k], trecv.at[b], (x, to)).start()
        return carry

    def hear_gates(k, carry):
        left(tables.at[0], tsend.at[k], me)
        arrived(tables.at[(b + 16 - k) % 16], trecv.at[(b + 16 - k) % 16], me)
        return carry

    def gate_of(s, carry):
        row = lax.broadcasted_iota(jnp.int32, (8, 128), 0)
        picked = jnp.sum(jnp.where(row == b // 2, tables[s], 0.0), axis=0, keepdims=True)
        gate[s] = as_column(picked)
        return carry

    def ready():
        lax.fori_loop(1, 16, hear_gates, 0)
        lax.fori_loop(0, 16, gate_of, 0)
        pl.when(c != x)(lambda: arrived(slab, xrecv.at[4], me))
        wide = slab[...].astype(F32).reshape(16, 2, 24, 768)
        wdown[:, :768] = wide[:, 0].reshape(384, 768).astype(BF)
        wdown[:, 768:] = wide[:, 1].reshape(384, 768).astype(BF)

    def with_tokens(j, p):
        if p == 0:
            pl.when((j == 0) & (c == x))(lambda: over_down().start())
            for k in range(4):
                pl.when(j == k)(over_weights(k).start)
        elif p == 1:

            @pl.when(j == 0)
            def _():
                for load in loads[3:]:
                    load.wait()
                expert = lax.broadcasted_iota(jnp.int32, (8, 128), 0)
                table = jnp.zeros((8, 128), F32)
                for k in range(TOP):
                    table = table + jnp.where(routes[k : k + 1, :] == expert, gates[k : k + 1, :], 0.0)
                tables[b] = table
                lax.fori_loop(1, 16, tell_gates, 0)

            pl.when(j == READY_AT)(ready)

    for p in range(CUTS + 1):
        begin(nall, 0, p)
    gather(nall, 0, with_tokens)

    def all_cores(buf, way):
        def one(j, carry):
            from_core(buf, way, j, y)
            from_core(buf, way, j, 1 - y)
            return carry

        lax.fori_loop(0, 4, one, 0)

    all_cores(nall, 0)
    half.wait()
    for k in range(4):
        arrived(wfull.at[1 - x, pl.ds(k * 4, 4)], xrecv.at[k], me)
    keep = as_column(valid[...].astype(F32))
    factor = keep * (SPAN / count[0:1, 0:1])
    loads[1].wait()
    loads[2].wait()
    me_index = x * 16 + b
    errs[me_index] = jnp.zeros((8, 128), F32)

    def loss_and_dy(p):
        cut, at = rows_of(p), slice(PARTS[p][0], PARTS[p][0] + PARTS[p][1])
        done = h[cut] + acc[cut]
        final[cut] = done.astype(BF)
        diff = done - teacher[cut].astype(F32)
        scaled = factor[at] * diff
        dy[cut] = scaled
        dyall[b, cut] = scaled.astype(BF)
        begin(dyall, 1, p)
        errs[me_index] += jnp.zeros((8, 128), F32) + jnp.sum(keep[at] * diff * diff)

    def outputs(j, carry):
        @pl.when(j < 4)
        def _():
            forward(me.inward(j) * 2 + 1 - y)

        @pl.when((j > 0) & (j < 5))
        def _():
            forward(me.inward(j - 1) * 2 + y)

        pl.when(j < 4)(lambda: lead(0, j))
        pl.when(j == 1)(lambda: close_gather(nall, 0))
        pl.when(j > 1)(lambda: follow(0, j - 2, loss_and_dy))
        return carry

    lax.fori_loop(0, 6, outputs, 0)

    saved = [
        pltpu.make_async_copy(final, final_out, load_sem.at[0]),
        pltpu.make_async_copy(dy, dy_out, load_sem.at[1]),
        pltpu.make_async_copy(acc, dn2_out, load_sem.at[2]),
        pltpu.make_async_copy(err, err_out, load_sem.at[3]),
    ]
    for copy in saved[:2]:
        copy.start()
    def tell(k, carry):
        to = ((x + k // 16) % 2, (b + k) % 16)
        remote(errs.at[me_index], errs.at[me_index], esend.at[k], erecv.at[me_index], to).start()
        return carry

    def inputs(i, yy):
        zz = me.outward(i)
        from_core(dyall, 1, zz, yy)
        backward(zz * 2 + yy)

    def with_dy(j, p):
        if p == -1:

            pl.when(j == 5)(lambda: lead(1, 3))

            def late(n, carry):
                inputs(jnp.where(n == 0, 2, 3), jnp.where(n == 1, y, 1 - y))
                return carry

            @pl.when(j > 3)
            def _():
                lax.fori_loop((j - 4) * 2, j - 2, late, 0)

        elif p == 0:
            pl.when((j > 0) & (j < 4))(lambda: inputs(j - 1, y))
        elif p == CUTS - 1:

            @pl.when(j == 0)
            def _():
                lax.fori_loop(1, 32, tell, 0)
                close_sum(0)

            pl.when((j > 1) & (j < 4))(lambda: inputs(j - 2, 1 - y))

    gather(dyall, 1, with_dy)

    def in_grad(i):
        col = pl.ds(pl.multiple_of(i * 256, 256), 256)
        rows = nall[:, :, col].reshape(2048, 256)
        dwin[col, :] = lax.dot_general(
            rows, dpairs[...].reshape(2048, 768), TN, preferred_element_type=F32
        ).astype(BF)

    def out_grad(k, there):
        i = there // 24 * 3 + k
        col = pl.ds(pl.multiple_of(i * 256, 256), 256)
        right = dyall[:, :, col].reshape(2048, 256)
        value = lax.dot_general(zg[...].reshape(2048, 384), right, TN, preferred_element_type=F32)
        part_col = pl.ds(pl.multiple_of(k * 256, 256), 256)
        dwout[:, there : there + 24, part_col] = value.reshape(16, 24, 256)

    def over_in(k):
        src = dwin.at[pl.ds(pl.multiple_of((1 - x) * 768 + k * 256, 256), 256)]
        return remote(src, dwin_in.at[pl.ds(pl.multiple_of(k * 256, 256), 256)], xsend.at[5 + k], xrecv.at[5 + k], me.near("x"))

    def over_out():
        return remote(slab, dwout_in, xsend.at[8], xrecv.at[8], me.near("x"))

    def leads(j, carry):
        lead(1, j)
        return carry

    lax.fori_loop(0, 3, leads, 0)

    def hear(k, carry):
        left(errs.at[0], esend.at[k], me)
        s = ((x + k // 16) % 2) * 16 + (b + k) % 16
        arrived(errs.at[s], erecv.at[s], me)
        return carry

    def sums(j, carry):
        @pl.when(j == 3)
        def _():
            close_gather(dyall, 1)
            lax.fori_loop(1, 32, hear, 0)
            total = errs[0]
            for s in range(1, 32):
                total = total + errs[s]
            err[...] = total / (1536.0 * count[...])

        @pl.when(j == 0)
        def _():
            def one(k, carry):
                in_grad((1 - x) * 3 + k)
                over_in(k).start()
                return carry

            lax.fori_loop(0, 3, one, 0)

        @pl.when(j == 1)
        def _():
            def one(k, carry):
                out_grad(k, 0)
                out_grad(k, 24)
                return carry

            lax.fori_loop(0, 3, one, 0)
            slab[...] = dwout[...].astype(BF)
            pl.when(c != x)(lambda: over_out().start())

        @pl.when(j == 2)
        def _():
            def one(k, carry):
                in_grad(x * 3 + k)
                return carry

            lax.fori_loop(0, 3, one, 0)

        follow(1, j)
        return carry

    for k in range(4):
        over_weights(k).wait_send()
    pl.when(c == x)(lambda: over_down().wait_send())
    lax.fori_loop(0, 4, sums, 0)
    saved[2].start()
    saved[3].start()
    close_sum(1)

    for k in range(3):
        over_in(k).wait_send()
        here = pl.ds(pl.multiple_of(x * 768 + k * 256, 256), 256)
        there = pl.ds(k * 256, 256)
        arrived(dwin_in.at[there], xrecv.at[5 + k], me)
        dwin_in[there] = (dwin_in[there].astype(F32) + dwin[here, :].astype(F32)).astype(BF)
    out = pltpu.make_async_copy(dwin_in, dwin_out, own_sem.at[0])
    out.start()

    @pl.when(c == x)
    def _():
        arrived(dwout_in, xrecv.at[8], me)
        dwout_in[...] = (dwout_in[...].astype(F32) + dwout[...]).astype(BF)
        copy = pltpu.make_async_copy(dwout_in, dwout_out, own_sem.at[1])
        copy.start()
        copy.wait()

    pl.when(c != x)(lambda: over_out().wait_send())
    for copy in saved + [out]:
        copy.wait()


def run_experts(*operands):
    wide = (128, 1536)
    shard = (16,) + wide
    shape = jax.ShapeDtypeStruct
    return pl.pallas_call(
        experts_kernel,
        out_shape=(
            shape((8, 128), F32),
            shape(wide, BF),
            shape(wide, F32),
            shape(wide, F32),
            shape((768, 768), BF),
            shape((16, 48, 768), BF),
        ),
        in_specs=[ANY] * 9,
        out_specs=(ANY,) * 6,
        scratch_shapes=[
            pltpu.VMEM((TOP, 128), jnp.int32),
            pltpu.VMEM((TOP, 128), F32),
            pltpu.VMEM((1, 128), jnp.int32),
            pltpu.VMEM((8, 128), F32),
            pltpu.VMEM((8, 128), F32),
            pltpu.VMEM(wide, F32),
            pltpu.VMEM(wide, BF),
            pltpu.VMEM(wide, BF),
            pltpu.VMEM(wide, F32),
            pltpu.VMEM(shard, BF),
            pltpu.VMEM(shard, BF),
            pltpu.VMEM((8, 256, 768), F32),
            pltpu.VMEM((8, 256, 384), BF),
            pltpu.VMEM((8, 256, 768), BF),
            pltpu.VMEM(shard, BF),
            pltpu.VMEM((8,) + wide, BF),
            pltpu.VMEM((4,) + wide, BF),
            pltpu.VMEM((5,) + wide, BF),
            pltpu.VMEM((2, 5, PARTS[CUTS][1], 1536), BF),
            pltpu.VMEM((PARTS[CUTS][1], 1536), BF),
            pltpu.VMEM((PARTS[CUTS][1], 1536), F32),
            pltpu.VMEM(wide, F32),
            pltpu.VMEM((32, 8, 128), F32),
            pltpu.VMEM((16, 8, 128), F32),
            pltpu.VMEM((16, 128, 1), F32),
            pltpu.VMEM((2, 16, 48, 768), BF),
            pltpu.VMEM((16, 48, 768), BF),
            pltpu.VMEM((384, 1536), BF),
            pltpu.VMEM((1536, 768), BF),
            pltpu.VMEM((768, 768), BF),
            pltpu.VMEM((16, 48, 768), F32),
            pltpu.VMEM((16, 48, 768), BF),
            DMA((7,)),
            DMA((2,)),
            DMA((2, 4, CUTS + 1, 7)),
            DMA((2, 16, CUTS + 1)),
            DMA((2, 8)),
            DMA((2, 8)),
            DMA((2, 4, CUTS + 1)),
            DMA((2, 4, CUTS + 1)),
            DMA((2, 4, CUTS + 2, 2)),
            DMA((2, 5, CUTS + 2)),
            DMA((32,)),
            DMA((32,)),
            DMA((16,)),
            DMA((16,)),
            DMA((9,)),
            DMA((9,)),
        ],
        compiler_params=params(2, 62),
        name="experts",
    )(*operands)


def norm_back(values, gain, grad):
    scale = lax.rsqrt(jnp.mean(values * values, axis=-1, keepdims=True) + 1e-06)
    inner = grad * gain
    mean = jnp.mean(inner * values, axis=-1, keepdims=True)
    return scale * inner - values * (scale * scale * scale * mean), jnp.sum(
        grad * values * scale, axis=0, keepdims=True
    )


Q_PIECES = ((0, 768), (768, 768))
LAST = (1536, 640)


def back_kernel(
    doc_in, freq_in, gains_in, states_in, h_in, n1_in, qs_in, o_in, lse_in, dn2_in, dy_in, dwin, dwout, gq, go, kv_in,
    gx_out, gqw, gkw, gvw, gnorm_out, gout_out, gup, gdown,
    doc, freq, gains, gnorm, states, h, n1, qs, o, lse, dn2, dy, gx, gout, gkv,
    wq, wo, kv, pk, pw, dos, delta, dh, dq, dkv, dqkv, gqkv, *rest,
):
    sums = [(rest[i * 11 : i * 11 + 6], rest[i * 11 + 6 : i * 11 + 11]) for i in range(5)]
    load_sem, own_sem, asend, arecv, osend, orecv = rest[55:]
    me = Place()
    greet_all(me)
    x, y, z, b, c = me.x, me.y, me.z, me.b, me.c
    loads = [
        pltpu.make_async_copy(go, wo, own_sem.at[0]),
        pltpu.make_async_copy(kv_in, kv, own_sem.at[1]),
        pltpu.make_async_copy(gq, wq, own_sem.at[2]),
    ]
    small = [
        pltpu.make_async_copy(src, dst, load_sem.at[i])
        for i, (src, dst) in enumerate(
            (
                (h_in, h), (dn2_in, dn2), (dy_in, dy), (o_in, o), (qs_in, qs), (lse_in, lse),
                (n1_in, n1), (states_in, states), (doc_in, doc), (freq_in, freq), (gains_in, gains),
            )
        )
    ]
    for load in small[:3] + [small[10], loads[0]] + small[3:10] + [loads[1], loads[2]]:
        load.start()
    all_greeted()

    def own_piece(n):
        col = pl.multiple_of(n * 768 + c * 384, 128)
        return pltpu.make_async_copy(
            dwin.at[b, :, pl.ds(n * 384, 384)], gup.at[b // 2, :, pl.ds(col, 384)], own_sem.at[3 + n]
        )

    def own_down():
        return pltpu.make_async_copy(dwout.at[b], gdown.at[b // 2], own_sem.at[5])

    def deal(k, carry):
        t = (b + (k * 9) % 16) % 16
        for n in range(2):
            col = pl.multiple_of(n * 768 + c * 384, 128)
            remote(
                dwin.at[t, :, pl.ds(n * 384, 384)],
                gup.at[b // 2, :, pl.ds(col, 384)],
                asend.at[k, n],
                arecv.at[b, n],
                (x, t),
            ).start()
        pl.when(c == x)(
            lambda: remote(dwout.at[t], gdown.at[b // 2], osend.at[k], orecv.at[b // 2], (x, t)).start()
        )
        return carry

    for n in range(2):
        own_piece(n).start()
    pl.when(c == x)(lambda: own_down().start())
    lax.fori_loop(1, 16, deal, 0)
    for load in small[:3] + small[8:]:
        load.wait()
    res_grad, gain_two = norm_back(h[...], gains[1:2], dn2[...])
    dh[...] = dy[...] + res_grad
    da = dh[...].astype(BF)
    loads[0].wait()
    do = lax.dot_general(
        da, wo[...].reshape(1536, 1536), NT, preferred_element_type=F32
    ).astype(BF)
    small[3].wait()
    low = o[...].astype(BF)
    for i in range(4):
        part = lax.dot_general(low[:, i * 384 : i * 384 + 384], da, TN, preferred_element_type=F32)
        wo[i * 8 : i * 8 + 8] = part.astype(BF).reshape(8, 48, 1536)
    out_sum = Sum(me, wo, by_weight, gout, *sums[0])
    key_sum = Sum(me, pk, by_token, dkv, *sums[1], causal=True)

    def lead_all(which):
        def one(j, carry):
            which.lead(j)
            return carry

        lax.fori_loop(0, 4, one, 0)

    lead_all(out_sum)
    for i in range(QUERY_HEADS):
        col, r = i * 128, (i % GROUP) * 128
        dos[i // GROUP, r : r + 128] = do[:, col : col + 128]
        prod = do[:, col : col + 128].astype(F32) * o[:, col : col + 128]
        delta[i // GROUP, :, r : r + 128] = jnp.sum(prod.T, axis=0, keepdims=True)
    dq[...] = jnp.zeros_like(dq)
    bounds = query_bounds(me, doc)
    loads[1].wait()
    for load in small[4:6]:
        load.wait()

    def block(n):
        ok = allowed_keys(n * 256, bounds)
        for i in range(2):
            k = kv[pl.ds(n * 2, 2), :, i * 128 : i * 128 + 128].reshape(256, 128)
            v = kv[pl.ds(n * 2, 2), :, 256 + i * 128 : 384 + i * 128].reshape(256, 128)
            s = lax.dot_general(k, qs[i], NT, preferred_element_type=F32)
            p = jnp.where(ok, jnp.exp2(s * POWER - lse[i]), 0.0)
            dp = lax.dot_general(v, dos[i], NT, preferred_element_type=F32)
            ds = (p * (dp - delta[i])).astype(BF)
            dv = jnp.dot(p.astype(BF), dos[i], preferred_element_type=F32)
            dk = jnp.dot(ds, qs[i], preferred_element_type=F32) * SCALE
            pk[pl.ds(n * 2, 2), :, i * 128 : i * 128 + 128] = dk.astype(BF).reshape(2, 128, 128)
            pk[pl.ds(n * 2, 2), :, 256 + i * 128 : 384 + i * 128] = dv.astype(BF).reshape(2, 128, 128)
            dq[i] += lax.dot_general(k, ds, TN, preferred_element_type=F32)

    def turn(j, carry):
        out_sum.turn(j)

        @pl.when(key_sum.valid(j))
        def _():
            last = jnp.where(j == z, y * 2 + c, 3)

            def one(n, carry):
                block(j * 4 + n)
                return carry

            lax.fori_loop(0, last + 1, one, 0)

            def blank(n, carry):
                pk[pl.ds((j * 4 + n) * 2, 2)] = jnp.zeros((2, 128, 512), BF)
                return carry

            lax.fori_loop(last + 1, 4, blank, 0)
            key_sum.lead(j)

        key_sum.turn(j)
        return carry

    lax.fori_loop(0, 4, turn, 0)

    cos, sin = rotary_tables(me, doc, freq)
    for load in small[6:8] + [loads[2]]:
        load.wait()
    for i in range(QUERY_HEADS):
        r = (i % GROUP) * 128
        head = dq[i // GROUP, :, r : r + 128].T * SCALE
        dqkv[:, i * 128 : i * 128 + 128] = turned(head, cos, -sin).astype(BF)

    def weight_grad(start, width):
        for i in range(4):
            part = lax.dot_general(
                n1[:, i * 384 : i * 384 + 384], dqkv[:, start : start + width], TN, preferred_element_type=F32
            )
            pw[i * 8 : i * 8 + 8, :, start : start + width] = part.astype(BF).reshape(8, 48, width)

    weight_grad(0, 1536)
    proj = [Sum(me, pw, by_weight, gqkv, *sums[2 + i], Q_PIECES[i]) for i in range(2)]
    rest_sum = Sum(me, pw, by_weight, gqkv, *sums[4], LAST)
    for piece in proj:
        lead_all(piece)

    stores = [
        pltpu.make_async_copy(gx, gx_out, load_sem.at[0]),
        pltpu.make_async_copy(gout, gout_out, load_sem.at[1]),
        pltpu.make_async_copy(gqkv.at[:, pl.ds(0, 1536)], gqw, load_sem.at[2]),
        pltpu.make_async_copy(gkv.at[:, pl.ds(0, 256)], gkw, load_sem.at[3]),
        pltpu.make_async_copy(gkv.at[:, pl.ds(256, 256)], gvw, load_sem.at[4]),
        pltpu.make_async_copy(gnorm, gnorm_out, load_sem.at[5]),
    ]

    def close_deal(k, carry):
        f = (b + 16 - k) % 16
        for n in range(2):
            left(dwin.at[0, :, pl.ds(0, 384)], asend.at[k, n], me)
            col = pl.multiple_of(n * 768 + (f % 2) * 384, 128)
            arrived(gup.at[f // 2, :, pl.ds(col, 384)], arecv.at[f, n], me)
        pl.when(c == x)(lambda: left(dwout.at[0], osend.at[k], me))
        pl.when(f % 2 == x)(lambda: arrived(gdown.at[f // 2], orecv.at[f // 2], me))
        return carry

    def last_turn(j, carry):
        out_sum.turn(j + 4)
        pl.when(j < 2)(lambda: key_sum.turn(j + 4))
        for piece in proj:
            piece.turn(j)

        @pl.when(j == 1)
        def _():
            for i in range(2):
                part = dkv[:, i * 128 : i * 128 + 128]
                dqkv[:, 1536 + i * 128 : 1664 + i * 128] = turned(part, cos, -sin).astype(BF)
            dqkv[:, 1792:2048] = dkv[:, 256:512].astype(BF)
            weight_grad(1536, 512)
            dn1 = lax.dot_general(
                dqkv[...], wq[:, :, pl.ds(0, QKV)].reshape(1536, QKV), NT, preferred_element_type=F32
            )
            in_grad, gain_one = norm_back(states[...].astype(F32), gains[0:1], dn1)
            rows = lax.broadcasted_iota(jnp.int32, (128, 1536), 0)
            tail = jnp.where(rows == 0, gain_one, jnp.where(rows == 1, gain_two, 0.0)).T
            pw[:, :, pl.ds(QKV, 128)] = tail.astype(BF).reshape(32, 48, 128)
            lead_all(rest_sum)
            gx[...] = dh[...] + in_grad
            rest_sum.first_legs()

        rest_sum.rest(j - 2)

        @pl.when(j == 2)
        def _():
            stores[0].start()
            stores[1].start()
            out_sum.close()

        @pl.when(j == 3)
        def _():
            key_sum.close()
            lax.fori_loop(1, 16, close_deal, 0)

        @pl.when(j == 5)
        def _():
            stores[2].start()
            for piece in proj:
                piece.close()

        return carry

    lax.fori_loop(0, 7, last_turn, 0)
    gkv[...] = gqkv[:, 1536:2048]
    for store in stores[3:5]:
        store.start()
    gnorm[0:1, 0:48] = as_row(gqkv[:, 2048:2049])
    gnorm[1:2, 0:48] = as_row(gqkv[:, 2049:2050])
    stores[5].start()
    rest_sum.close()

    for n in range(2):
        own_piece(n).wait()
    pl.when(c == x)(lambda: own_down().wait())
    for store in stores:
        store.wait()


def run_back(*operands):
    shape = jax.ShapeDtypeStruct
    return pl.pallas_call(
        back_kernel,
        out_shape=(
            shape((128, 1536), F32),
            shape((48, 1536), F32),
            shape((48, 256), F32),
            shape((48, 256), F32),
            shape((8, 128), F32),
            shape((48, 1536), F32),
            shape((8, 48, 1536), BF),
            shape((8, 48, 768), BF),
        ),
        in_specs=[ANY] * 16,
        out_specs=(ANY,) * 8,
        scratch_shapes=[
            pltpu.VMEM(operands[0].shape, jnp.int32),
            pltpu.VMEM((1, 128), F32),
            pltpu.VMEM((8, 1536), F32),
            pltpu.VMEM((8, 128), F32),
            pltpu.VMEM((128, 1536), BF),
            pltpu.VMEM((128, 1536), F32),
            pltpu.VMEM((128, 1536), BF),
            pltpu.VMEM((2, LANES, 128), BF),
            pltpu.VMEM((128, 1536), F32),
            pltpu.VMEM((2, 1, LANES), F32),
            pltpu.VMEM((128, 1536), F32),
            pltpu.VMEM((128, 1536), F32),
            pltpu.VMEM((128, 1536), F32),
            pltpu.VMEM((48, 1536), F32),
            pltpu.VMEM((48, 512), F32),
            pltpu.VMEM((32, 48, WIDE), BF),
            pltpu.VMEM((32, 48, 1536), BF),
            pltpu.VMEM((32, 128, 512), BF),
            pltpu.VMEM((32, 128, 512), BF),
            pltpu.VMEM((32, 48, WIDE), BF),
            pltpu.VMEM((2, LANES, 128), BF),
            pltpu.VMEM((2, 1, LANES), F32),
            pltpu.VMEM((128, 1536), F32),
            pltpu.VMEM((2, 128, LANES), F32),
            pltpu.VMEM((128, 512), F32),
            pltpu.VMEM((128, QKV), BF),
            pltpu.VMEM((48, WIDE), F32),
        ]
        + Sum.room(48, 1536)
        + Sum.room(128, 512)
        + Sum.room(48, 768)
        + Sum.room(48, 768)
        + Sum.room(48, LAST[1])
        + [DMA((11,)), DMA((6,)), DMA((16, 2)), DMA((16, 2)), DMA((16,)), DMA((8,))],
        compiler_params=params(3, 62),
        name="back",
    )(*operands)


def finish_kernel(
    err_in, gnorm_in, final, gx, gqw, gkw, gvw, gout, gup, gdown,
    loss_out, one_out, two_out, final_out, gx_out, gqw_out, gkw_out, gvw_out, gout_out, gup_out, gdown_out,
    low_up, low_down, wide_up, wide_down, *rest,
):
    rooms, (err, gnorm, loss, one, two, sem, out_sem) = rest[:6], rest[6:]
    whole = (
        (gup, low_up), (gdown, low_down), *zip((final, gx, gqw, gkw, gvw, gout), rooms), (err_in, err), (gnorm_in, gnorm)
    )
    copies = [pltpu.make_async_copy(src, dst, sem.at[i]) for i, (src, dst) in enumerate(whole)]
    for copy in copies:
        copy.start()
    outs = (final_out, gx_out, gqw_out, gkw_out, gvw_out, gout_out)
    last = []
    for i in range(6):
        copies[2 + i].wait()
        last.append(pltpu.make_async_copy(rooms[i], outs[i], out_sem.at[i]))
        last[i].start()
    copies[0].wait()
    wide_up[...] = low_up[...].astype(F32)
    last.append(pltpu.make_async_copy(wide_up, gup_out, out_sem.at[6]))
    last[6].start()
    copies[1].wait()
    for e in range(E):
        wide = low_down[e].astype(F32)
        wide_down[e, :, :768] = wide[:24]
        wide_down[e, :, 768:] = wide[24:]
    last.append(pltpu.make_async_copy(wide_down, gdown_out, out_sem.at[7]))
    last[7].start()
    copies[8].wait()
    copies[9].wait()
    loss[...] = err[0:1, 0:1]
    one[...] = gnorm[0:1, 0:48]
    two[...] = gnorm[1:2, 0:48]
    for i, (src, dst) in enumerate(((loss, loss_out), (one, one_out), (two, two_out))):
        last.append(pltpu.make_async_copy(src, dst, out_sem.at[8 + i]))
        last[8 + i].start()
    for copy in last:
        copy.wait()


def run_finish(*operands):
    shape = jax.ShapeDtypeStruct
    up, down = (8, 48, 1536), (8, 24, 1536)
    return pl.pallas_call(
        finish_kernel,
        out_shape=(
            shape((1, 1), F32),
            shape((1, 48), F32),
            shape((1, 48), F32),
            shape((128, 1536), BF),
            shape((128, 1536), F32),
            shape((48, 1536), F32),
            shape((48, 256), F32),
            shape((48, 256), F32),
            shape((48, 1536), F32),
            shape(up, F32),
            shape(down, F32),
        ),
        in_specs=[ANY] * 10,
        out_specs=(ANY,) * 11,
        scratch_shapes=[
            pltpu.VMEM(up, BF),
            pltpu.VMEM((8, 48, 768), BF),
            pltpu.VMEM(up, F32),
            pltpu.VMEM(down, F32),
            pltpu.VMEM((128, 1536), BF),
            pltpu.VMEM((128, 1536), F32),
            pltpu.VMEM((48, 1536), F32),
            pltpu.VMEM((48, 256), F32),
            pltpu.VMEM((48, 256), F32),
            pltpu.VMEM((48, 1536), F32),
            pltpu.VMEM((8, 128), F32),
            pltpu.VMEM((8, 128), F32),
            pltpu.VMEM((1, 1), F32),
            pltpu.VMEM((1, 48), F32),
            pltpu.VMEM((1, 48), F32),
            DMA((10,)),
            DMA((11,)),
        ],
        compiler_params=pltpu.CompilerParams(vmem_limit_bytes=60 << 20),
        name="finish",
    )(*operands)


def per_device(
    states, teacher, valid, routes, gates, doc_starts, norm_one,
    w_query, key_weight, value_weight, w_output, norm_two, expert_in, expert_out,
):
    tokens = states.shape[2]
    width = states.shape[3]
    half = HEAD_SIZE // 2
    freq = np.float32(ROTARY_BASE) ** (-np.arange(half).astype(np.float32) / np.float32(half))
    freq = jnp.asarray(np.concatenate([freq, freq])[None, :], F32)
    rows = states.reshape(tokens, width)
    kept = valid.reshape(1, tokens)
    doc = doc_starts.reshape(1, -1)
    gq, go, kv, win, wout, h, n2, n1, qs, o, lse, count, gains = run_front(
        doc, freq, norm_one.reshape(1, -1), norm_two.reshape(1, -1), kept, rows, expert_out,
        w_query, key_weight, value_weight, w_output, expert_in,
    )
    error, final, dn2, dy, dwin, dwout = run_experts(
        routes.reshape(tokens, TOP).T, gates.reshape(tokens, TOP).T, kept, count,
        n2, h, teacher.reshape(tokens, width), win, wout,
    )
    gx, gqw, gkw, gvw, gnorm, gout, gup, gdown = run_back(
        doc, freq, gains, rows, h, n1, qs, o, lse, dn2, dy, dwin.reshape(16, 48, 768), dwout, gq, go, kv
    )
    loss, one, two, final, gx, gqw, gkw, gvw, gout, gup, gdown = run_finish(
        error, gnorm, final, gx, gqw, gkw, gvw, gout, gup, gdown
    )
    shape = states.shape
    return (
        final.reshape(shape),
        loss.reshape(()),
        gx.reshape(shape),
        one.reshape(-1),
        gqw,
        gkw,
        gvw,
        gout,
        two.reshape(-1),
        gup,
        gdown,
    )


def solution(mesh):
    in_specs = (
        P("blk", "head", None, None),
        P("blk", "head", None, None),
        P("blk", "head", None),
        P("blk", "head", None, None),
        P("blk", "head", None, None),
        P(),
        P(("head", "blk")),
        P(("head", "blk"), None),
        P(("head", "blk"), None),
        P(("head", "blk"), None),
        P(("head", "blk"), None),
        P(("head", "blk")),
        P(None, ("head", "blk"), None),
        P(None, ("head", "blk"), None),
    )
    out_specs = (
        P("blk", "head", None, None),
        P(),
        P("blk", "head", None, None),
        P(("head", "blk")),
        P(("head", "blk"), None),
        P(("head", "blk"), None),
        P(("head", "blk"), None),
        P(("head", "blk"), None),
        P(("head", "blk")),
        P(None, ("head", "blk"), None),
        P(None, ("head", "blk"), None),
    )
    sizes = dict(mesh.shape)
    plan = per_device if sizes == {"head": 2, "blk": 4 * NZ} else per_device_plain
    return jax.shard_map(
        plan, mesh=mesh, in_specs=in_specs, out_specs=out_specs, check_vma=False
    )
```

```python
import functools

import jax
import jax.numpy as jnp
import numpy as np
from jax import lax
from jax.experimental import pallas as pl
from jax.experimental.pallas import tpu as pltpu
from jax.sharding import PartitionSpec as P

QUERY_HEADS = 12
KEY_VALUE_HEADS = 2
HEAD_SIZE = 128
TOP = 4
E = 8
CAP = 96

ROTARY_BASE = 10000.0
FLOOR_SCORE = -1e30

MESH = pl.DeviceIdType.MESH
NZ = 4
SPAN = 32 * 128.0
BF = jnp.bfloat16
F32 = jnp.float32

def product(left, right):
    return jnp.dot(left, right, preferred_element_type=jnp.float32)


def rms_norm(values, gain):
    scale = lax.rsqrt(jnp.mean(values * values, axis=-1, keepdims=True) + 1e-06)
    return values * scale * gain


def rotary_apply(values, where, sign):
    half = values.shape[-1] // 2
    freq = ROTARY_BASE ** (-jnp.arange(half).astype(jnp.float32) / half)
    angle = where.astype(jnp.float32)[:, None] * freq[None, :]
    cosine = jnp.cos(angle)[:, None, :]
    sine = jnp.sin(angle)[:, None, :] * sign
    first = values[..., :half]
    second = values[..., half:]
    return jnp.concatenate(
        [first * cosine - second * sine, second * cosine + first * sine], axis=-1
    )


def doc_layout(position_index, doc_starts):
    inside = (position_index[:, None] >= doc_starts[None, :]).astype(jnp.int32)
    document_segment = jnp.sum(inside, axis=-1) - 1
    begin = jnp.max(jnp.where(inside > 0, doc_starts[None, :], 0), axis=-1)
    return (document_segment, position_index - begin)


def gated(pair):
    half = pair.shape[-1] // 2
    return jax.nn.gelu(pair[..., :half], approximate=True) * pair[..., half:]


def in_blocks(step_fn, carry, piece, rows):
    count_blocks = piece[0].shape[0] // rows

    def turn(number, state):
        part = tuple((lax.dynamic_slice_in_dim(item, number * rows, rows, 0) for item in piece))
        return step_fn(state, part, number * rows)

    return lax.fori_loop(0, count_blocks, turn, carry)


def per_device_plain(
    states,
    teacher,
    valid,
    routes,
    gates,
    doc_starts,
    norm_one,
    w_query,
    key_weight,
    value_weight,
    w_output,
    norm_two,
    expert_in,
    expert_out,
):
    count_per_token = states.shape[2]
    width = states.shape[3]
    pairs = lax.axis_size("head")
    blocks = lax.axis_size("blk")
    rows = count_per_token * pairs
    span = rows * blocks
    head_group = QUERY_HEADS // KEY_VALUE_HEADS
    scale = HEAD_SIZE ** (-0.5)
    highest = lax.Precision.HIGHEST
    block_index = lax.axis_index("blk")
    pair_index = lax.axis_index("head")
    token_index = (block_index * pairs + pair_index) * count_per_token + jnp.arange(
        count_per_token, dtype=jnp.int32
    )
    unused_segment, token_position = doc_layout(token_index, doc_starts)
    query_index = block_index * rows + jnp.arange(rows, dtype=jnp.int32)
    query_segment, query_where = doc_layout(query_index, doc_starts)
    last_query = block_index * rows + rows - 1
    inputs = states.reshape(count_per_token, width).astype(jnp.float32)
    target = teacher.reshape(count_per_token, width).astype(jnp.float32)
    keep_mask = valid.reshape(count_per_token).astype(jnp.float32)
    route_rows = routes.reshape(count_per_token, TOP)
    gate_rows = gates.reshape(count_per_token, TOP)
    query_w, key_w, value_w, out_w, gain_low_one, gain_low_two = (
        lax.all_gather(w_query, ("head", "blk"), axis=0, tiled=True),
        lax.all_gather(key_weight, ("head", "blk"), axis=0, tiled=True),
        lax.all_gather(value_weight, ("head", "blk"), axis=0, tiled=True),
        lax.all_gather(w_output, ("head", "blk"), axis=0, tiled=True),
        lax.all_gather(norm_one, ("head", "blk"), axis=0, tiled=True),
        lax.all_gather(norm_two, ("head", "blk"), axis=0, tiled=True),
    )
    gain_one = gain_low_one.astype(jnp.float32)
    gain_two = gain_low_two.astype(jnp.float32)
    normed_one = rms_norm(inputs, gain_one)
    normed_low = normed_one.astype(jnp.bfloat16)
    query_lin = product(normed_low, query_w)
    key_linear = product(normed_low, key_w)
    value_linear = product(normed_low, value_w)
    query_rotated = rotary_apply(
        query_lin.reshape(count_per_token, QUERY_HEADS, HEAD_SIZE), token_position, 1.0
    )
    key_rotated = rotary_apply(
        key_linear.reshape(count_per_token, KEY_VALUE_HEADS, HEAD_SIZE), token_position, 1.0
    )
    query_outgoing = query_rotated.astype(jnp.bfloat16).reshape(
        count_per_token, KEY_VALUE_HEADS, head_group * HEAD_SIZE
    )
    key_send = key_rotated.astype(jnp.bfloat16)
    value_outgoing = value_linear.astype(jnp.bfloat16).reshape(
        count_per_token, KEY_VALUE_HEADS, HEAD_SIZE
    )
    query_grp, key_grp, value_grp = (
        lax.all_to_all(query_outgoing, "head", split_axis=1, concat_axis=0, tiled=True),
        lax.all_to_all(key_send, "head", split_axis=1, concat_axis=0, tiled=True),
        lax.all_to_all(value_outgoing, "head", split_axis=1, concat_axis=0, tiled=True),
    )
    query_heads = query_grp.reshape(rows, head_group, HEAD_SIZE)
    key_rows = key_grp.reshape(rows, HEAD_SIZE)
    value_rows = value_grp.reshape(rows, HEAD_SIZE)

    def scores_for(keys, start):
        block_size = keys.shape[0]
        key_index = start + jnp.arange(block_size, dtype=jnp.int32)
        key_segment, unused_where = doc_layout(key_index, doc_starts)
        allowed = (key_index[None, :] <= query_index[:, None]) & (
            key_segment[None, :] == query_segment[:, None]
        )
        raw = (
            jnp.einsum("qhd,kd->hqk", query_heads, keys, preferred_element_type=jnp.float32) * scale
        )
        return (raw, allowed[None])

    def attend(carry, piece, start):
        keys, values = piece

        def work(state):
            running, total, accum = state
            raw, allowed = scores_for(keys, start)
            masked = jnp.where(allowed, raw, FLOOR_SCORE)
            newest = jnp.maximum(running, jnp.max(masked, axis=-1))
            factor = jnp.exp(running - newest)
            weights = jnp.where(allowed, jnp.exp(masked - newest[..., None]), 0.0)
            total = total * factor + jnp.sum(weights, axis=-1)
            update = jnp.einsum(
                "hqk,kd->qhd",
                weights.astype(jnp.bfloat16),
                values,
                preferred_element_type=jnp.float32,
            )
            accum = accum * factor.T[:, :, None] + update
            return (newest, total, accum)

        return lax.cond(start <= last_query, work, lambda state: state, carry)

    start_state = (
        jnp.full((head_group, rows), FLOOR_SCORE, jnp.float32),
        jnp.zeros((head_group, rows), jnp.float32),
        jnp.zeros((rows, head_group, HEAD_SIZE), jnp.float32),
    )
    running, total, accum = in_blocks(
        attend,
        start_state,
        (
            lax.all_gather(key_rows, "blk", axis=0, tiled=True),
            lax.all_gather(value_rows, "blk", axis=0, tiled=True),
        ),
        rows,
    )
    attn_full = accum / total.T[:, :, None]
    log_total = running + jnp.log(total)
    out_send = attn_full.astype(jnp.bfloat16).reshape(rows, 1, head_group * HEAD_SIZE)
    out_tok = lax.all_to_all(out_send, "head", split_axis=0, concat_axis=1, tiled=True).reshape(
        count_per_token, QUERY_HEADS * HEAD_SIZE
    )
    residual = inputs + product(out_tok, out_w)
    normed_two = rms_norm(residual, gain_two)
    normed_two_low = normed_two.astype(jnp.bfloat16)
    up_w, down_w = (
        lax.all_gather(expert_in, ("head", "blk"), axis=1, tiled=True),
        lax.all_gather(expert_out, ("head", "blk"), axis=1, tiled=True),
    )
    route_hot = (route_rows[:, :, None] == jnp.arange(E, dtype=jnp.int32)[None, None, :]).astype(
        jnp.int32
    )
    flat_hot = route_hot.reshape(count_per_token * TOP, E)
    before = jnp.cumsum(flat_hot, axis=0) - flat_hot
    slot = jnp.sum(before * flat_hot, axis=-1).reshape(count_per_token, TOP)
    slot_hot = (slot[:, :, None] == jnp.arange(CAP, dtype=jnp.int32)[None, None, :]).astype(
        jnp.float32
    )
    route_float = route_hot.astype(jnp.float32)
    dispatch = jnp.einsum("tje,tjc->ect", route_float, slot_hot, precision=highest)
    combine = jnp.einsum("tje,tjc,tj->ect", route_float, slot_hot, gate_rows, precision=highest)
    expert_rows = jnp.einsum(
        "ect,td->ecd",
        dispatch.astype(jnp.bfloat16),
        normed_two_low,
        preferred_element_type=jnp.float32,
    ).astype(jnp.bfloat16)
    pair = jnp.einsum("ecd,edf->ecf", expert_rows, up_w, preferred_element_type=jnp.float32)
    hidden_low = gated(pair).astype(jnp.bfloat16)
    expert_result = jnp.einsum(
        "ecf,efd->ecd", hidden_low, down_w, preferred_element_type=jnp.float32
    )
    mixture = jnp.einsum("ect,ecd->td", combine, expert_result, precision=highest)
    final = residual + mixture
    diff = final - target
    local_count = jnp.sum(keep_mask)
    local_error = jnp.sum(keep_mask * jnp.sum(diff * diff, axis=-1))
    count_all, error_all = lax.psum((local_count, local_error), ("head", "blk"))
    loss = error_all / (width * count_all)
    grad_final = keep_mask[:, None] * diff * (span * 1.0 / count_all)
    up_back, down_back = (
        lax.all_gather(expert_in, ("head", "blk"), axis=1, tiled=True),
        lax.all_gather(expert_out, ("head", "blk"), axis=1, tiled=True),
    )
    grad_result = jnp.einsum("ect,td->ecd", combine, grad_final, precision=highest).astype(
        jnp.bfloat16
    )
    grad_down = jnp.einsum(
        "ecf,ecd->efd", hidden_low, grad_result, preferred_element_type=jnp.float32
    )
    grad_hidden = jnp.einsum(
        "ecd,efd->ecf", grad_result, down_back, preferred_element_type=jnp.float32
    )
    unused_value, pull_gate = jax.vjp(gated, pair)
    grad_pair = pull_gate(grad_hidden)[0].astype(jnp.bfloat16)
    grad_up = jnp.einsum("ecd,ecf->edf", expert_rows, grad_pair, preferred_element_type=jnp.float32)
    grad_rows = jnp.einsum("ecf,edf->ecd", grad_pair, up_back, preferred_element_type=jnp.float32)
    grad_normed_two = jnp.einsum("ect,ecd->td", dispatch, grad_rows, precision=highest)
    unused_value, pull_two = jax.vjp(rms_norm, residual, gain_two)
    grad_res_norm, grad_gain_two = pull_two(grad_normed_two)
    grad_residual = grad_final + grad_res_norm
    grad_attn_low = grad_residual.astype(jnp.bfloat16)
    grad_out_w = jnp.einsum("tk,td->kd", out_tok, grad_attn_low, preferred_element_type=jnp.float32)
    output_gradient_token = jnp.einsum(
        "td,kd->tk", grad_attn_low, out_w, preferred_element_type=jnp.float32
    ).astype(jnp.bfloat16)
    grad_out_grp = lax.all_to_all(
        output_gradient_token.reshape(count_per_token, KEY_VALUE_HEADS, head_group * HEAD_SIZE),
        "head",
        split_axis=1,
        concat_axis=0,
        tiled=True,
    ).reshape(rows, head_group, HEAD_SIZE)
    delta = jnp.einsum(
        "qhd,qhd->hq", grad_out_grp.astype(jnp.float32), attn_full, precision=highest
    )

    def attend_back(carry, piece, start):
        keys, values = piece

        def work(state):
            grad_query, grad_keys, grad_values = state
            raw, allowed = scores_for(keys, start)
            weights = jnp.where(allowed, jnp.exp(raw - log_total[..., None]), 0.0)
            grad_weights = jnp.einsum(
                "qhd,kd->hqk", grad_out_grp, values, preferred_element_type=jnp.float32
            )
            grad_raw = (weights * (grad_weights - delta[..., None])).astype(jnp.bfloat16)
            grad_query = (
                grad_query
                + jnp.einsum("hqk,kd->qhd", grad_raw, keys, preferred_element_type=jnp.float32)
                * scale
            )
            key_part = (
                jnp.einsum("hqk,qhd->kd", grad_raw, query_heads, preferred_element_type=jnp.float32)
                * scale
            )
            value_part = jnp.einsum(
                "hqk,qhd->kd",
                weights.astype(jnp.bfloat16),
                grad_out_grp,
                preferred_element_type=jnp.float32,
            )
            block_size = keys.shape[0]
            grad_keys = lax.dynamic_update_slice_in_dim(
                grad_keys,
                lax.dynamic_slice_in_dim(grad_keys, start, block_size, 0) + key_part,
                start,
                0,
            )
            grad_values = lax.dynamic_update_slice_in_dim(
                grad_values,
                lax.dynamic_slice_in_dim(grad_values, start, block_size, 0) + value_part,
                start,
                0,
            )
            return (grad_query, grad_keys, grad_values)

        return lax.cond(start <= last_query, work, lambda state: state, carry)

    back_state = (
        jnp.zeros((rows, head_group, HEAD_SIZE), jnp.float32),
        jnp.zeros((span, HEAD_SIZE), jnp.float32),
        jnp.zeros((span, HEAD_SIZE), jnp.float32),
    )
    grad_query, grad_keys_full, grad_values_full = in_blocks(
        attend_back,
        back_state,
        (
            lax.all_gather(key_rows, "blk", axis=0, tiled=True),
            lax.all_gather(value_rows, "blk", axis=0, tiled=True),
        ),
        rows,
    )
    grad_keys, grad_values = (
        lax.psum_scatter(grad_keys_full, "blk", scatter_dimension=0, tiled=True),
        lax.psum_scatter(grad_values_full, "blk", scatter_dimension=0, tiled=True),
    )
    grad_query_lin = (
        rotary_apply(grad_query, query_where, -1.0)
        .astype(jnp.bfloat16)
        .reshape(rows, 1, head_group * HEAD_SIZE)
    )
    grad_key_lin = rotary_apply(grad_keys.reshape(rows, 1, HEAD_SIZE), query_where, -1.0).astype(
        jnp.bfloat16
    )
    grad_value_lin = grad_values.astype(jnp.bfloat16).reshape(rows, 1, HEAD_SIZE)
    back_query, key_backward, value_backward = (
        lax.all_to_all(grad_query_lin, "head", split_axis=0, concat_axis=1, tiled=True),
        lax.all_to_all(grad_key_lin, "head", split_axis=0, concat_axis=1, tiled=True),
        lax.all_to_all(grad_value_lin, "head", split_axis=0, concat_axis=1, tiled=True),
    )
    back_query = back_query.reshape(count_per_token, QUERY_HEADS * HEAD_SIZE)
    key_backward = key_backward.reshape(count_per_token, KEY_VALUE_HEADS * HEAD_SIZE)
    value_backward = value_backward.reshape(count_per_token, KEY_VALUE_HEADS * HEAD_SIZE)
    grad_query_w = jnp.einsum(
        "td,tk->dk", normed_low, back_query, preferred_element_type=jnp.float32
    )
    grad_key_w = jnp.einsum(
        "td,tk->dk", normed_low, key_backward, preferred_element_type=jnp.float32
    )
    grad_value_w = jnp.einsum(
        "td,tk->dk", normed_low, value_backward, preferred_element_type=jnp.float32
    )
    grad_normed_one = jnp.einsum(
        "tk,dk->td", back_query, query_w, preferred_element_type=jnp.float32
    )
    grad_normed_one = grad_normed_one + jnp.einsum(
        "tk,dk->td", key_backward, key_w, preferred_element_type=jnp.float32
    )
    grad_normed_one = grad_normed_one + jnp.einsum(
        "tk,dk->td", value_backward, value_w, preferred_element_type=jnp.float32
    )
    unused_value, pull_one = jax.vjp(rms_norm, inputs, gain_one)
    grad_in_norm, grad_gain_one = pull_one(grad_normed_one)
    grad_inputs = grad_residual + grad_in_norm
    sums = (
        lax.psum_scatter(grad_query_w, ("head", "blk"), scatter_dimension=0, tiled=True),
        lax.psum_scatter(grad_key_w, ("head", "blk"), scatter_dimension=0, tiled=True),
        lax.psum_scatter(grad_value_w, ("head", "blk"), scatter_dimension=0, tiled=True),
        lax.psum_scatter(grad_out_w, ("head", "blk"), scatter_dimension=0, tiled=True),
        lax.psum_scatter(grad_gain_one, ("head", "blk"), scatter_dimension=0, tiled=True),
        lax.psum_scatter(grad_gain_two, ("head", "blk"), scatter_dimension=0, tiled=True),
        lax.psum_scatter(grad_up, ("head", "blk"), scatter_dimension=1, tiled=True),
        lax.psum_scatter(grad_down, ("head", "blk"), scatter_dimension=1, tiled=True),
    )
    shape = states.shape
    return (
        final.astype(jnp.bfloat16).reshape(shape),
        loss,
        grad_inputs.reshape(shape),
        sums[4],
        sums[0],
        sums[1],
        sums[2],
        sums[3],
        sums[5],
        sums[6],
        sums[7],
    )


class Place:
    def __init__(self):
        self.x = lax.axis_index("head")
        self.b = lax.axis_index("blk")
        self.c = self.b % 2
        self.y = (self.b // 2) % 2
        self.z = self.b // 4

    def near(self, kind):
        x, y, z, c = self.x, self.y, self.z, self.c
        if kind == "up":
            z = jnp.minimum(z + 1, NZ - 1)
        elif kind == "down":
            z = jnp.maximum(z - 1, 0)
        elif kind == "y":
            y = 1 - y
        elif kind == "x":
            x = 1 - x
        elif kind == "c":
            c = 1 - c
        return (x, z * 4 + y * 2 + c)

    def blk(self, z, y, c):
        return z * 4 + y * 2 + c

    def outward(self, j):
        inner = jnp.where(j < 2, 1 - j, j)
        order = jnp.where((self.z == 0) | (self.z == NZ - 1), j, inner)
        return jnp.where(self.z < 2, order, NZ - 1 - order)

    def inward(self, j):
        inner = jnp.where(j == 0, 3, jnp.where(j == 1, 0, jnp.where(j == 2, 2, 1)))
        order = jnp.where((self.z == 0) | (self.z == NZ - 1), NZ - 1 - j, inner)
        return jnp.where(self.z < 2, order, NZ - 1 - order)


def greet_all(me):
    barrier = pltpu.get_barrier_semaphore()

    def one(k, carry):
        pl.semaphore_signal(
            barrier, inc=1, device_id=((me.x + k // 16) % 2, (me.b + k) % 16), device_id_type=MESH
        )
        return carry

    lax.fori_loop(1, 32, one, 0)


def all_greeted():
    pl.semaphore_wait(pltpu.get_barrier_semaphore(), 31)


def remote(src, dst, send, recv, to):
    return pltpu.make_async_remote_copy(
        src_ref=src, dst_ref=dst, send_sem=send, recv_sem=recv, device_id=to, device_id_type=MESH
    )


def arrived(ref, sem, me):
    remote(ref, ref, sem, sem, me.near("c")).wait_recv()


def left(ref, sem, me):
    remote(ref, ref, sem, sem, me.near("c")).wait_send()


class Gather:
    def __init__(self, me, g, index, send, recv, cols=None, causal=False):
        self.me, self.g, self.index, self.send, self.recv, self.causal = me, g, index, send, recv, causal
        start, width = cols or (0, g.shape[2])
        cut = (width // 2 + 127) // 128 * 128
        self.cols = pl.ds(start, width)
        self.first, self.second = pl.ds(start, cut), pl.ds(start + cut, width - cut)

    def place(self, j):
        return self.me.z - j if self.causal else self.me.outward(j)

    def valid(self, j):
        return (j >= 0) & (j <= (self.me.z if self.causal else NZ - 1))

    def ups(self, zz):
        if self.causal:
            return self.me.z < NZ - 1
        return (zz <= self.me.z) & (self.me.z < NZ - 1)

    def downs(self, zz):
        return (zz >= self.me.z) & (self.me.z > 0)

    def put(self, j, kind, n, s, cols=None, slot=0):
        ref = self.g.at[s, :, self.cols if cols is None else cols]
        remote(ref, ref, self.send.at[j, n], self.recv.at[s, slot], self.me.near(kind)).start()

    def wait(self, s):
        arrived(self.g.at[s, :, self.cols], self.recv.at[s, 0], self.me)

    def turn(self, j):
        me, index = self.me, self.index
        x, y, c = me.x, me.y, me.c

        @pl.when(self.valid(j) & (j > 0))
        def _():
            self.wait(index(x, self.place(j), y, c))

        @pl.when(self.valid(j))
        def _():
            zz = self.place(j)
            own = index(x, zz, y, c)
            pl.when(self.ups(zz))(lambda: self.put(j, "up", 0, own))
            if not self.causal:
                pl.when(self.downs(zz))(lambda: self.put(j, "down", 1, own))
            self.put(j, "y", 2, own)
            self.put(j, "x", 3, own)
            self.put(j, "c", 6, own)

        @pl.when(self.valid(j - 1))
        def _():
            i = j - 1
            zp = self.place(i)
            s = index(x, zp, 1 - y, c)
            self.wait(s)
            self.put(i, "x", 4, s, self.first, 0)
            self.put(i, "c", 7, s)
            t = index(1 - x, zp, y, c)
            self.wait(t)
            self.put(i, "y", 5, t, self.second, 1)
            self.put(i, "c", 8, t)

        @pl.when(self.valid(j - 2))
        def _():
            i = j - 2
            s = index(1 - x, self.place(i), 1 - y, c)
            arrived(self.g.at[s, :, self.first], self.recv.at[s, 0], me)
            arrived(self.g.at[s, :, self.second], self.recv.at[s, 1], me)
            self.put(i, "c", 9, s)

    def from_core(self, j):
        me = self.me
        for xx in (me.x, 1 - me.x):
            for yy in (me.y, 1 - me.y):
                self.wait(self.index(xx, self.place(j), yy, 1 - me.c))

    def from_cores(self):
        def one(j, carry):
            self.from_core(j)
            return carry

        lax.fori_loop(0, 4, one, 0)

    def close(self):
        me = self.me

        def one(j, carry):
            @pl.when(self.valid(j))
            def _():
                zz = self.place(j)
                own = self.index(me.x, zz, me.y, me.c)
                whole = self.g.at[own, :, self.cols]
                first, second = self.g.at[own, :, self.first], self.g.at[own, :, self.second]
                pl.when(self.ups(zz))(lambda: left(whole, self.send.at[j, 0], me))
                if not self.causal:
                    pl.when(self.downs(zz))(lambda: left(whole, self.send.at[j, 1], me))
                for n in (2, 3, 6, 7, 8, 9):
                    left(whole, self.send.at[j, n], me)
                left(first, self.send.at[j, 4], me)
                left(second, self.send.at[j, 5], me)

            return carry

        lax.fori_loop(0, 4, one, 0)


class Sum:
    def __init__(self, me, part, index, out, room, sems, cols=None, causal=False):
        self.me, self.part, self.index, self.out, self.causal = me, part, index, out, causal
        start, width = cols or (0, part.shape[2])
        self.cols = pl.ds(start, width)
        self.rc, self.rx, self.ry, self.rn, self.rz, self.acc = room
        self.sc, self.ss, self.vc, self.vn, self.vz = sems
        self.half = (width // 2 + 127) // 128 * 128
        self.first, self.second = pl.ds(0, self.half), pl.ds(self.half, width - self.half)

    @staticmethod
    def room(rows, columns):
        half = (columns // 2 + 127) // 128 * 128
        return [
            pltpu.VMEM((16, rows, columns), BF),
            pltpu.VMEM((4, rows, half), BF),
            pltpu.VMEM((4, rows, columns - half), BF),
            pltpu.VMEM((2, 4, rows, columns), BF),
            pltpu.VMEM((5, rows, columns), BF),
            pltpu.VMEM((rows, columns), F32),
            DMA((16,)),
            DMA((4, 6)),
            DMA((16,)),
            DMA((4, 4)),
            DMA((5,)),
        ]

    def place(self, j):
        return j if self.causal else self.me.inward(j)

    def valid(self, j):
        return (j >= 0) & (j <= (self.me.z if self.causal else NZ - 1))

    def slot(self, xx, zz, yy):
        return zz * 4 + xx * 2 + yy

    def lead(self, j):
        me = self.me
        zz = self.place(j)
        for xx in (1 - me.x, me.x):
            for yy in (1 - me.y, me.y):
                k = self.slot(xx, zz, yy)
                src = self.part.at[self.index(xx, zz, yy, 1 - me.c), :, self.cols]
                remote(src, self.rc.at[k], self.sc.at[k], self.vc.at[k], me.near("c")).start()

    def with_core(self, xx, zz, yy):
        k = self.slot(xx, zz, yy)
        arrived(self.rc.at[k], self.vc.at[k], self.me)
        own = self.part[self.index(xx, zz, yy, self.me.c), :, self.cols]
        return k, own.astype(F32) + self.rc[k].astype(F32)

    def first_leg(self, i):
        me, half, first, second = self.me, self.half, self.first, self.second
        rc, rx, ry, rn, ss, vn = self.rc, self.rx, self.ry, self.rn, self.ss, self.vn
        x, y = me.x, me.y

        @pl.when(self.valid(i))
        def _():
            zz = self.place(i)
            k, total = self.with_core(1 - x, zz, 1 - y)
            rc[k] = total.astype(BF)
            remote(rc.at[k, :, first], rx.at[zz], ss.at[i, 0], vn.at[zz, 0], me.near("x")).start()
            remote(rc.at[k, :, second], ry.at[zz], ss.at[i, 1], vn.at[zz, 1], me.near("y")).start()

    def second_leg(self, i):
        me, half, first, second = self.me, self.half, self.first, self.second
        rc, rx, ry, rn, ss, vn = self.rc, self.rx, self.ry, self.rn, self.ss, self.vn
        x, y = me.x, me.y

        @pl.when(self.valid(i))
        def _():
            zz = self.place(i)
            k, total = self.with_core(x, zz, 1 - y)
            arrived(rx.at[zz], vn.at[zz, 0], me)
            rc[k, :, second] = total[:, half:].astype(BF)
            rc[k, :, first] = (total[:, :half] + rx[zz].astype(F32)).astype(BF)
            remote(rc.at[k], rn.at[0, zz], ss.at[i, 2], vn.at[zz, 2], me.near("y")).start()
            k, total = self.with_core(1 - x, zz, y)
            arrived(ry.at[zz], vn.at[zz, 1], me)
            rc[k, :, first] = total[:, :half].astype(BF)
            rc[k, :, second] = (total[:, half:] + ry[zz].astype(F32)).astype(BF)
            remote(rc.at[k], rn.at[1, zz], ss.at[i, 3], vn.at[zz, 3], me.near("x")).start()

    def third_leg(self, i):
        me, half, first, second = self.me, self.half, self.first, self.second
        rc, rx, ry, rn, ss, vn = self.rc, self.rx, self.ry, self.rn, self.ss, self.vn
        x, y = me.x, me.y

        @pl.when(self.valid(i))
        def _():
            zz = self.place(i)
            k, total = self.with_core(x, zz, y)
            arrived(rn.at[0, zz], vn.at[zz, 2], me)
            arrived(rn.at[1, zz], vn.at[zz, 3], me)
            self.acc[...] = total + rn[0, zz].astype(F32) + rn[1, zz].astype(F32)
            along_z(me, i, zz, self.acc, rc.at[k], self.rz, ss, 4, self.vz, self.causal)

            @pl.when(zz == me.z)
            def _():
                self.out[:, self.cols] = self.acc[...]

    def turn(self, j):
        self.first_leg(j)
        self.second_leg(j - 1)
        self.third_leg(j - 2)

    def first_legs(self):
        def one(j, carry):
            self.first_leg(j)
            return carry

        lax.fori_loop(0, 4, one, 0)

    def rest(self, j):
        self.second_leg(j)
        self.third_leg(j - 1)

    def close(self):
        me = self.me
        whole = self.rc.at[0]
        first, second = self.rc.at[0, :, self.first], self.rc.at[0, :, self.second]

        def one(j, carry):
            @pl.when(self.valid(j))
            def _():
                zz = self.place(j)
                for xx in (1 - me.x, me.x):
                    for yy in (1 - me.y, me.y):
                        left(whole, self.sc.at[self.slot(xx, zz, yy)], me)
                left(first, self.ss.at[j, 0], me)
                left(second, self.ss.at[j, 1], me)
                for n in (2, 3):
                    left(whole, self.ss.at[j, n], me)
                if not self.causal:
                    pl.when(zz > me.z)(lambda: left(whole, self.ss.at[j, 4], me))
                pl.when(zz < me.z)(lambda: left(whole, self.ss.at[j, 5], me))

            return carry

        lax.fori_loop(0, 4, one, 0)


def along_z(me, i, zz, acc, room, rz, ss, n, vz, causal=False):
    z = me.z

    def add(slot):
        arrived(rz.at[slot], vz.at[slot], me)
        acc[...] += rz[slot].astype(F32)

    if not causal:
        pl.when((zz >= z) & (z > 0))(lambda: add(zz))
    pl.when((zz < z) & (z < NZ - 1))(lambda: add(zz))
    pl.when((zz == z) & (z < NZ - 1))(lambda: add(4))

    if not causal:

        @pl.when(zz > z)
        def _():
            room[...] = acc[...].astype(BF)
            remote(room, rz.at[zz], ss.at[i, n], vz.at[zz], me.near("up")).start()

    @pl.when(zz < z)
    def _():
        room[...] = acc[...].astype(BF)
        there = jnp.where(zz == z - 1, 4, zz)
        remote(room, rz.at[there], ss.at[i, n + 1], vz.at[there], me.near("down")).start()


def by_weight(x, z, y, c):
    return x * 16 + z * 4 + y * 2 + c


def by_token(x, z, y, c):
    return (z * 4 + y * 2 + c) * 2 + x


ANY = pl.BlockSpec(memory_space=pl.ANY)
VMEM = pl.BlockSpec(memory_space=pltpu.VMEM)
DMA = pltpu.SemaphoreType.DMA


def params(number, mib):
    return pltpu.CompilerParams(
        collective_id=number, has_side_effects=True, vmem_limit_bytes=mib << 20
    )


NT = (((1,), (1,)), ((), ()))
TN = (((0,), (0,)), ((), ()))
GROUP = QUERY_HEADS // KEY_VALUE_HEADS
LANES = GROUP * 128
SCALE = HEAD_SIZE ** (-0.5)
POWER = SCALE * 1.4426950408889634


def turned(u, cosine, sine):
    return u * cosine + pltpu.roll(u, 64, 1) * sine


def begin_of(place, doc):
    begin = jnp.zeros_like(place)
    for i in range(doc.shape[1]):
        start = doc[0:1, i : i + 1]
        begin = jnp.where(place >= start, jnp.maximum(begin, start), begin)
    return begin


def rotary_tables(me, doc, freq):
    first = (me.b * 2 + me.x) * 128
    place = first + lax.broadcasted_iota(jnp.int32, (128, 128), 0)
    angle = (place - begin_of(place, doc)).astype(F32) * freq[...]
    sine = jnp.sin(angle)
    lane = lax.broadcasted_iota(jnp.int32, (128, 128), 1)
    return jnp.cos(angle), jnp.where(lane < 64, -sine, sine)


def query_bounds(me, doc):
    place = (me.b * 2 + me.x) * 128 + lax.broadcasted_iota(jnp.int32, (1, LANES), 1) % 128
    return begin_of(place, doc), place


def allowed_keys(start, bounds):
    key = start + lax.broadcasted_iota(jnp.int32, (256, LANES), 0)
    return (key >= bounds[0]) & (key <= bounds[1])


def eye(n):
    return lax.broadcasted_iota(jnp.int32, (n, n), 0) == lax.broadcasted_iota(jnp.int32, (n, n), 1)


def as_column(row):
    return jnp.sum(jnp.where(eye(row.shape[1]), row, 0.0), axis=1, keepdims=True)


def as_row(column):
    return jnp.sum(jnp.where(eye(column.shape[0]), column, 0.0), axis=0, keepdims=True)


QKV = 2048
WIDE = QKV + 128
PIECES = ((0, 1152), (1152, 1024))


def front_kernel(
    doc_in, freq_in, one_in, two_in, valid_in, states, down_in, wq, wk, wv, wo, up,
    gq_out, go_out, kv_out, win, wout, h_out, n2_out, n1_out, qs_out, o_out, lse_out, count_out, gains_out,
    doc, freq, norm_one, norm_two, valid, lse, count, gains_row, gq, go, kv, down, top, total, acc, low_rows, down_raw, cos, sin, n1, qs, o, h, n2,
    load_sem, own_sem, qsend, qrecv, gsend, grecv, ksend, krecv, asend, arecv, osend, orecv,
):
    me = Place()
    greet_all(me)
    x, y, z, b, c = me.x, me.y, me.z, me.b, me.c
    here = by_weight(x, z, y, c)
    mine = [
        pltpu.make_async_copy(wq, gq.at[here, :, pl.ds(0, 1536)], own_sem.at[0]),
        pltpu.make_async_copy(wk, gq.at[here, :, pl.ds(1536, 256)], own_sem.at[1]),
        pltpu.make_async_copy(wv, gq.at[here, :, pl.ds(1792, 256)], own_sem.at[2]),
        pltpu.make_async_copy(wo, go.at[here], own_sem.at[3]),
    ]
    pairs = (
        (down_in, down_raw), (states, low_rows), (doc_in, doc), (freq_in, freq),
        (one_in, norm_one), (two_in, norm_two), (valid_in, valid),
    )
    loads = [pltpu.make_async_copy(src, dst, load_sem.at[i]) for i, (src, dst) in enumerate(pairs)]
    for copy in loads[4:] + mine + loads[:4]:
        copy.start()
    for load in loads[4:]:
        load.wait()

    lane = lax.broadcasted_iota(jnp.int32, (48, 128), 1)
    kept = jnp.sum(valid[...].astype(F32))
    extra = jnp.where(
        lane == 0,
        as_column(norm_one[...].astype(F32)),
        jnp.where(lane == 1, as_column(norm_two[...].astype(F32)), jnp.where(lane == 2, kept, 0.0)),
    )
    gq[here, :, pl.ds(QKV, 128)] = extra.astype(BF)
    all_greeted()
    for copy in mine:
        copy.wait()

    def own_piece(n):
        col = pl.multiple_of(n * 768 + c * 384, 128)
        return pltpu.make_async_copy(
            up.at[b // 2, :, pl.ds(col, 384)], win.at[b, :, pl.ds(n * 384, 384)], own_sem.at[4 + n]
        )

    def own_down():
        return pltpu.make_async_copy(down.at[b // 2], wout.at[b], own_sem.at[6])

    def deal(k, carry):
        t = (b + (k * 13) % 16) % 16
        for n in range(2):
            col = pl.multiple_of(n * 768 + (t % 2) * 384, 128)
            remote(
                up.at[t // 2, :, pl.ds(col, 384)],
                win.at[b, :, pl.ds(n * 384, 384)],
                asend.at[k, n],
                arecv.at[b, n],
                (x, t),
            ).start()
        pl.when(t % 2 == x)(
            lambda: remote(down.at[t // 2], wout.at[b], osend.at[k], orecv.at[b], (x, t)).start()
        )
        return carry

    weights = [
        Gather(me, gq, by_weight, qsend.at[i], qrecv.at[i], PIECES[i]) for i in range(len(PIECES))
    ]

    def first_turn(j, carry):
        for piece in weights:
            piece.turn(j)

        @pl.when(j == 0)
        def _():
            for load in loads[:4]:
                load.wait()
            for e in range(E):
                wide = down_raw[e].astype(F32)
                down[e] = jnp.concatenate([wide[:, :768], wide[:, 768:]], axis=0).astype(BF)
            cos[...], sin[...] = rotary_tables(me, doc, freq)

        lax.fori_loop(1 + j * 3, jnp.minimum(4 + j * 3, 16), deal, 0)
        return carry

    lax.fori_loop(0, 6, first_turn, 0)
    for n in range(2):
        own_piece(n).start()
    pl.when(c == x)(lambda: own_down().start())
    bounds = query_bounds(me, doc)
    rows = low_rows[...].astype(F32)
    level = rows * lax.rsqrt(jnp.mean(rows * rows, axis=-1, keepdims=True) + 1e-06)
    for piece in weights:
        piece.from_cores()
    keep = pltpu.make_async_copy(gq, gq_out, own_sem.at[0])
    keep.start()

    gains = gq[:, :, pl.ds(QKV, 128)].reshape(1536, 128).astype(F32).T
    n1[...] = (level * gains[0:1]).astype(BF)
    turns = cos[...], sin[...]
    at = by_token(x, z, y, c)
    keys = Gather(me, kv, by_token, ksend, krecv, causal=True)
    output = Gather(me, go, by_weight, gsend, grecv)
    both = jnp.dot(n1[...], gq[:, :, pl.ds(1536, 512)].reshape(1536, 512), preferred_element_type=F32)
    for i in range(2):
        kv[at, :, i * 128 : i * 128 + 128] = turned(both[:, i * 128 : i * 128 + 128], *turns).astype(BF)
    kv[at, :, 256:512] = both[:, 256:512].astype(BF)
    keys.turn(0)
    query = jnp.dot(n1[...], gq[:, :, pl.ds(0, 1536)].reshape(1536, 1536), preferred_element_type=F32)
    for i in range(QUERY_HEADS):
        r = (i % GROUP) * 128
        qs[i // GROUP, r : r + 128] = turned(query[:, i * 128 : i * 128 + 128], *turns).astype(BF)
    count[...] = jnp.zeros((8, 128), F32) + jnp.sum(gains[2:3]) / 48.0
    gains_row[...] = gains[0:8]
    saved = [
        pltpu.make_async_copy(count, count_out, load_sem.at[5]),
        pltpu.make_async_copy(gains_row, gains_out, load_sem.at[6]),
        pltpu.make_async_copy(n1, n1_out, load_sem.at[0]),
        pltpu.make_async_copy(qs, qs_out, load_sem.at[1]),
    ]
    for copy in saved:
        copy.start()

    top[...] = jnp.full_like(top, FLOOR_SCORE)
    total[...] = jnp.zeros_like(total)
    acc[...] = jnp.zeros_like(acc)
    def block(n):
        ok = allowed_keys(n * 256, bounds)
        for i in range(2):
            k = kv[pl.ds(n * 2, 2), :, i * 128 : i * 128 + 128].reshape(256, 128)
            v = kv[pl.ds(n * 2, 2), :, 256 + i * 128 : 384 + i * 128].reshape(256, 128)
            s = lax.dot_general(k, qs[i], NT, preferred_element_type=F32)
            s = jnp.where(ok, s, FLOOR_SCORE)
            old = top[i]
            new = jnp.maximum(old, jnp.max(s, axis=0, keepdims=True))
            factor = jnp.exp2((old - new) * POWER)
            p = jnp.exp2((s - new) * POWER)
            top[i] = new
            total[i] = total[i] * factor + jnp.sum(p, axis=0, keepdims=True)
            acc[i] = acc[i] * factor + lax.dot_general(v, p.astype(BF), TN, preferred_element_type=F32)

    def close_deal(k, carry):
        piece = win.at[b, :, pl.ds(0, 384)]
        f = (b + 16 - k) % 16
        for n in range(2):
            left(piece, asend.at[k, n], me)
            arrived(win.at[f, :, pl.ds(n * 384, 384)], arecv.at[f, n], me)
        pl.when((b + k) % 2 == x)(lambda: left(wout.at[b], osend.at[k], me))
        pl.when(c == x)(lambda: arrived(wout.at[f], orecv.at[f], me))
        return carry

    def turn(j, carry):
        pl.when(j > 0)(lambda: keys.turn(j))
        output.turn(j - 2)

        @pl.when(j == 1)
        def _():
            for piece in weights:
                piece.close()

        @pl.when(j == 6)
        def _():
            lax.fori_loop(1, 16, close_deal, 0)
            keys.close()


        @pl.when(keys.valid(j - 2))
        def _():
            i = j - 2
            keys.from_core(i)
            zz = z - i
            last = jnp.where(i == 0, y * 2 + c, 3)

            def one(n, carry):
                block(zz * 4 + last - n)
                return carry

            lax.fori_loop(0, last + 1, one, 0)

        return carry

    lax.fori_loop(0, 8, turn, 0)
    keep_k = pltpu.make_async_copy(kv, kv_out, own_sem.at[2])
    keep_k.start()
    for i in range(2):
        lse[i] = top[i] * POWER + jnp.log2(total[i])
        done = acc[i] / total[i]
        for r in range(GROUP):
            col = (i * GROUP + r) * 128
            o[:, col : col + 128] = done[:, r * 128 : r * 128 + 128].T
    more = [pltpu.make_async_copy(o, o_out, load_sem.at[2]), pltpu.make_async_copy(lse, lse_out, load_sem.at[7])]
    for copy in more:
        copy.start()
    output.from_cores()
    keep_o = pltpu.make_async_copy(go, go_out, own_sem.at[1])
    keep_o.start()
    res = low_rows[...].astype(F32) + jnp.dot(
        o[...].astype(BF), go[...].reshape(1536, 1536), preferred_element_type=F32
    )
    h[...] = res
    n2[...] = (
        res * lax.rsqrt(jnp.mean(res * res, axis=-1, keepdims=True) + 1e-06) * gains[1:2]
    ).astype(BF)
    more.append(pltpu.make_async_copy(h, h_out, load_sem.at[3]))
    more.append(pltpu.make_async_copy(n2, n2_out, load_sem.at[4]))
    more[2].start()
    more[3].start()

    output.close()
    for n in range(2):
        own_piece(n).wait()
    pl.when(c == x)(lambda: own_down().wait())
    for copy in [keep, keep_o, keep_k] + saved + more:
        copy.wait()


def run_front(*operands):
    shape = jax.ShapeDtypeStruct
    return pl.pallas_call(
        front_kernel,
        out_shape=(
            shape((32, 48, WIDE), BF),
            shape((32, 48, 1536), BF),
            shape((32, 128, 512), BF),
            shape((16, 48, 768), BF),
            shape((16, 48, 768), BF),
            shape((128, 1536), F32),
            shape((128, 1536), BF),
            shape((128, 1536), BF),
            shape((2, LANES, 128), BF),
            shape((128, 1536), F32),
            shape((2, 1, LANES), F32),
            shape((8, 128), F32),
            shape((8, 1536), F32),
        ),
        in_specs=[ANY] * 12,
        out_specs=(ANY,) * 13,
        scratch_shapes=[
            pltpu.VMEM(operands[0].shape, jnp.int32),
            pltpu.VMEM((1, 128), F32),
            pltpu.VMEM((1, 48), BF),
            pltpu.VMEM((1, 48), BF),
            pltpu.VMEM((1, 128), jnp.int32),
            pltpu.VMEM((2, 1, LANES), F32),
            pltpu.VMEM((8, 128), F32),
            pltpu.VMEM((8, 1536), F32),
            pltpu.VMEM((32, 48, WIDE), BF),
            pltpu.VMEM((32, 48, 1536), BF),
            pltpu.VMEM((32, 128, 512), BF),
            pltpu.VMEM((8, 48, 768), BF),
            pltpu.VMEM((2, 1, LANES), F32),
            pltpu.VMEM((2, 1, LANES), F32),
            pltpu.VMEM((2, 128, LANES), F32),
            pltpu.VMEM((128, 1536), BF),
            pltpu.VMEM((8, 24, 1536), BF),
            pltpu.VMEM((128, 128), F32),
            pltpu.VMEM((128, 128), F32),
            pltpu.VMEM((128, 1536), BF),
            pltpu.VMEM((2, LANES, 128), BF),
            pltpu.VMEM((128, 1536), F32),
            pltpu.VMEM((128, 1536), F32),
            pltpu.VMEM((128, 1536), BF),
            DMA((8,)),
            DMA((7,)),
            DMA((2, 4, 10)),
            DMA((2, 32, 2)),
            DMA((4, 10)),
            DMA((32, 2)),
            DMA((4, 10)),
            DMA((32, 2)),
            DMA((16, 2)),
            DMA((16, 2)),
            DMA((16,)),
            DMA((16,)),
        ],
        compiler_params=params(1, 62),
        name="front",
    )(*operands)


GELU_A = 0.7978845608028654
GELU_B = 0.044715


READY_AT = 4
PARTS = ((0, 64), (64, 48), (112, 16))
CUTS = 2


def experts_kernel(
    routes_in, gates_in, valid_in, count_in, n2, h_in, teacher_in, win, wout,
    err_out, final_out, dn2_out, dy_out, dwin_out, dwout_out,
    routes, gates, valid, count, err, h, teacher, final, dy, nall, dyall, pairs, zg, dpairs, part, rc, ry, rz, rzt, ryt, tail, acc, errs, tables, gate,
    wfull, slab, wdown, dwin, dwin_in, dwout, dwout_in,
    load_sem, own_sem, gsend, grecv, csend, crecv, ysend, yrecv, zsend, zrecv, esend, erecv,
    tsend, trecv, xsend, xrecv,
):
    me = Place()
    greet_all(me)
    x, y, z, b, c = me.x, me.y, me.z, me.b, me.c
    half = pltpu.make_async_copy(win, wfull.at[x], own_sem.at[0])
    half.start()
    loads = [
        pltpu.make_async_copy(n2, nall.at[b], load_sem.at[0]),
        pltpu.make_async_copy(h_in, h, load_sem.at[1]),
        pltpu.make_async_copy(teacher_in, teacher, load_sem.at[2]),
        pltpu.make_async_copy(routes_in, routes, load_sem.at[3]),
        pltpu.make_async_copy(gates_in, gates, load_sem.at[4]),
        pltpu.make_async_copy(valid_in, valid, load_sem.at[5]),
        pltpu.make_async_copy(count_in, count, load_sem.at[6]),
    ]
    for load in loads:
        load.start()
    held = pltpu.make_async_copy(wout, slab, own_sem.at[1])
    pl.when(c == x)(held.start)
    all_greeted()

    def rows_of(p):
        return pl.ds(*PARTS[p])

    def over_weights(k):
        cut = pl.ds(k * 4, 4)
        return remote(win.at[cut], wfull.at[x, cut], xsend.at[k], xrecv.at[k], me.near("x"))

    def over_down():
        return remote(wout, slab, xsend.at[4], xrecv.at[4], me.near("x"))

    def put(buf, way, j, p, kind, n, s):
        ref = buf.at[s, rows_of(p)]
        remote(ref, ref, gsend.at[way, j, p, n], grecv.at[way, s, p], me.near(kind)).start()

    def along(buf, way, j, p, n, s, zz):
        pl.when((zz <= z) & (z < NZ - 1))(lambda: put(buf, way, j, p, "up", n, s))
        pl.when((zz >= z) & (z > 0))(lambda: put(buf, way, j, p, "down", n + 1, s))

    def begin(buf, way, p):
        along(buf, way, 0, p, 0, b, z)
        put(buf, way, 0, p, "y", 2, b)
        put(buf, way, 0, p, "c", 3, b)

    def gather(buf, way, between):
        def turn(j, carry):
            between(j, -1)
            for p in range(CUTS + 1):
                zz = me.outward(j)
                own = me.blk(zz, y, c)

                @pl.when((j > 0) & (j < 4))
                def _():
                    arrived(buf.at[own, rows_of(p)], grecv.at[way, own, p], me)

                @pl.when((j > 0) & (j < 4))
                def _():
                    along(buf, way, j, p, 0, own, zz)
                    if p < CUTS:
                        put(buf, way, j, p, "y", 2, own)
                    put(buf, way, j, p, "c", 3, own)

                @pl.when((j > 0) & (j < 5))
                def _():
                    i = j - 1
                    zp = me.outward(i)
                    s = me.blk(zp, 1 - y, c)
                    arrived(buf.at[s, rows_of(p)], grecv.at[way, s, p], me)
                    if p == CUTS:
                        along(buf, way, i, p, 5, s, zp)
                    put(buf, way, i, p, "c", 4, s)

                between(j, p)
            return carry

        lax.fori_loop(0, 6, turn, 0)

    def close_gather(buf, way):
        def close(j, carry):
            zz = me.outward(j)
            for p in range(CUTS + 1):
                whole = buf.at[b, rows_of(p)]
                ends = (0, 1) if p < CUTS else (0, 1, 5, 6)
                for n in ends:
                    ok = (zz <= z) & (z < NZ - 1) if n in (0, 5) else (zz >= z) & (z > 0)
                    pl.when(ok)(lambda: left(whole, gsend.at[way, j, p, n], me))
                if p < CUTS:
                    left(whole, gsend.at[way, j, p, 2], me)
                else:
                    pl.when(j == 0)(lambda: left(whole, gsend.at[way, j, p, 2], me))
                for n in (3, 4):
                    left(whole, gsend.at[way, j, p, n], me)
            return carry

        lax.fori_loop(0, 4, close, 0)

    def from_core(buf, way, zz, yy):
        s = me.blk(zz, yy, 1 - c)
        for p in range(CUTS + 1):
            arrived(buf.at[s, rows_of(p)], grecv.at[way, s, p], me)

    def to_other_core(way, q):
        remote(part.at[q * 2 + 1 - c], rc.at[q], csend.at[way, q], crecv.at[way, q], me.near("c")).start()

    def lead(way, j):
        zz = me.inward(j)
        q = zz * 2 + 1 - y
        s = q * 2 + c
        arrived(rc.at[q], crecv.at[way, q], me)
        part[s] = (part[s].astype(F32) + rc[q].astype(F32)).astype(BF)
        for p in range(CUTS):
            remote(
                part.at[s, rows_of(p)], ry.at[zz, rows_of(p)], ysend.at[way, j, p], yrecv.at[way, zz, p], me.near("y")
            ).start()

    def follow(way, j, done=None):
        zz = me.inward(j)
        q = zz * 2 + y
        s = q * 2 + c
        arrived(rc.at[q], crecv.at[way, q], me)
        cut = rows_of(CUTS)
        for n, yy in enumerate((1 - y, y)):
            k = zz * 2 + yy
            room = part.at[k * 2 + c, cut]
            if n:
                tail[...] = room[...].astype(F32) + rc[k, cut].astype(F32)
            else:
                tail[...] = room[...].astype(F32)
            along_z(
                me, j, zz, tail, room, rzt.at[n], zsend.at[way, :, CUTS + n], 0, zrecv.at[way, :, CUTS + n]
            )
            if n == 0:

                @pl.when(zz == z)
                def _():
                    room[...] = tail[...].astype(BF)
                    remote(room, ryt, ysend.at[way, 3, CUTS], yrecv.at[way, 0, CUTS], me.near("y")).start()

        for p in range(CUTS):
            cut = rows_of(p)
            arrived(ry.at[zz, cut], yrecv.at[way, zz, p], me)
            piece = acc.at[cut]
            piece[...] = part[s, cut].astype(F32) + rc[q, cut].astype(F32) + ry[zz, cut].astype(F32)
            along_z(
                me, j, zz, piece, part.at[s, cut], rz.at[:, cut], zsend.at[way, :, p], 0, zrecv.at[way, :, p]
            )
            if done is not None:
                pl.when(zz == z)(functools.partial(done, p))

        @pl.when(zz == z)
        def _():
            arrived(ryt, yrecv.at[way, 0, CUTS], me)
            acc[rows_of(CUTS)] = tail[...] + ryt[...].astype(F32)
            if done is not None:
                done(CUTS)

    def close_sum(way):
        def close(j, carry):
            zz = me.inward(j)
            whole = part.at[b]
            left(whole, csend.at[way, j], me)
            left(whole, csend.at[way, j + 4], me)
            for p in range(CUTS + 2):
                piece = part.at[b, rows_of(min(p, CUTS))]
                if p < CUTS:
                    left(piece, ysend.at[way, j, p], me)
                elif p == CUTS:
                    pl.when(j == 3)(lambda: left(piece, ysend.at[way, j, p], me))
                pl.when(zz > z)(lambda: left(piece, zsend.at[way, j, p, 0], me))
                pl.when(zz < z)(lambda: left(piece, zsend.at[way, j, p, 1], me))
            return carry

        lax.fori_loop(0, 4, close, 0)

    def gelu_parts(g):
        t = jnp.tanh(GELU_A * (g + GELU_B * g * g * g))
        return t, 0.5 * g * (1.0 + t)

    def forward(q):
        rows = nall[pl.ds(q * 2, 2)].reshape(256, 1536)
        pair = jnp.dot(rows, wfull[...].reshape(1536, 768), preferred_element_type=F32)
        pairs[q] = pair
        unused, a = gelu_parts(pair[:, :384])
        scale = gate[pl.ds(q * 2, 2)].reshape(256, 1)
        zq = (a * pair[:, 384:] * scale).astype(BF)
        zg[q] = zq
        out = jnp.dot(zq, wdown[...], preferred_element_type=F32)
        part[pl.ds(q * 2, 2)] = out.astype(BF).reshape(2, 128, 1536)
        to_other_core(0, q)

    def backward(q):
        rows = dyall[pl.ds(q * 2, 2)].reshape(256, 1536)
        scale = gate[pl.ds(q * 2, 2)].reshape(256, 1)
        dz = lax.dot_general(rows, wdown[...], NT, preferred_element_type=F32) * scale
        g, u = pairs[q, :, :384], pairs[q, :, 384:]
        t, a = gelu_parts(g)
        slope = 0.5 * (1.0 + t) + 0.5 * g * (1.0 - t * t) * (GELU_A * (1.0 + 3.0 * GELU_B * g * g))
        dpairs[q, :, :384] = (dz * u * slope).astype(BF)
        dpairs[q, :, 384:] = (dz * a).astype(BF)
        out = lax.dot_general(dpairs[q], wfull[...].reshape(1536, 768), NT, preferred_element_type=F32)
        part[pl.ds(q * 2, 2)] = out.astype(BF).reshape(2, 128, 1536)
        to_other_core(1, q)

    loads[0].wait()
    pl.when(c == x)(held.wait)

    def tell_gates(k, carry):
        to = (b + k) % 16
        remote(tables.at[b], tables.at[b], tsend.at[k], trecv.at[b], (x, to)).start()
        return carry

    def hear_gates(k, carry):
        left(tables.at[0], tsend.at[k], me)
        arrived(tables.at[(b + 16 - k) % 16], trecv.at[(b + 16 - k) % 16], me)
        return carry

    def gate_of(s, carry):
        row = lax.broadcasted_iota(jnp.int32, (8, 128), 0)
        picked = jnp.sum(jnp.where(row == b // 2, tables[s], 0.0), axis=0, keepdims=True)
        gate[s] = as_column(picked)
        return carry

    def ready():
        lax.fori_loop(1, 16, hear_gates, 0)
        lax.fori_loop(0, 16, gate_of, 0)
        pl.when(c != x)(lambda: arrived(slab, xrecv.at[4], me))
        wide = slab[...].astype(F32).reshape(16, 2, 24, 768)
        wdown[:, :768] = wide[:, 0].reshape(384, 768).astype(BF)
        wdown[:, 768:] = wide[:, 1].reshape(384, 768).astype(BF)

    def with_tokens(j, p):
        if p == 0:
            pl.when((j == 0) & (c == x))(lambda: over_down().start())
            for k in range(4):
                pl.when(j == k)(over_weights(k).start)
        elif p == 1:

            @pl.when(j == 0)
            def _():
                for load in loads[3:]:
                    load.wait()
                expert = lax.broadcasted_iota(jnp.int32, (8, 128), 0)
                table = jnp.zeros((8, 128), F32)
                for k in range(TOP):
                    table = table + jnp.where(routes[k : k + 1, :] == expert, gates[k : k + 1, :], 0.0)
                tables[b] = table
                lax.fori_loop(1, 16, tell_gates, 0)

            pl.when(j == READY_AT)(ready)

    for p in range(CUTS + 1):
        begin(nall, 0, p)
    gather(nall, 0, with_tokens)

    def all_cores(buf, way):
        def one(j, carry):
            from_core(buf, way, j, y)
            from_core(buf, way, j, 1 - y)
            return carry

        lax.fori_loop(0, 4, one, 0)

    all_cores(nall, 0)
    half.wait()
    for k in range(4):
        arrived(wfull.at[1 - x, pl.ds(k * 4, 4)], xrecv.at[k], me)
    keep = as_column(valid[...].astype(F32))
    factor = keep * (SPAN / count[0:1, 0:1])
    loads[1].wait()
    loads[2].wait()
    me_index = x * 16 + b
    errs[me_index] = jnp.zeros((8, 128), F32)

    def loss_and_dy(p):
        cut, at = rows_of(p), slice(PARTS[p][0], PARTS[p][0] + PARTS[p][1])
        done = h[cut] + acc[cut]
        final[cut] = done.astype(BF)
        diff = done - teacher[cut].astype(F32)
        scaled = factor[at] * diff
        dy[cut] = scaled
        dyall[b, cut] = scaled.astype(BF)
        begin(dyall, 1, p)
        errs[me_index] += jnp.zeros((8, 128), F32) + jnp.sum(keep[at] * diff * diff)

    def outputs(j, carry):
        @pl.when(j < 4)
        def _():
            forward(me.inward(j) * 2 + 1 - y)

        @pl.when((j > 0) & (j < 5))
        def _():
            forward(me.inward(j - 1) * 2 + y)

        pl.when(j < 4)(lambda: lead(0, j))
        pl.when(j == 1)(lambda: close_gather(nall, 0))
        pl.when(j > 1)(lambda: follow(0, j - 2, loss_and_dy))
        return carry

    lax.fori_loop(0, 6, outputs, 0)

    saved = [
        pltpu.make_async_copy(final, final_out, load_sem.at[0]),
        pltpu.make_async_copy(dy, dy_out, load_sem.at[1]),
        pltpu.make_async_copy(acc, dn2_out, load_sem.at[2]),
        pltpu.make_async_copy(err, err_out, load_sem.at[3]),
    ]
    for copy in saved[:2]:
        copy.start()
    def tell(k, carry):
        to = ((x + k // 16) % 2, (b + k) % 16)
        remote(errs.at[me_index], errs.at[me_index], esend.at[k], erecv.at[me_index], to).start()
        return carry

    def inputs(i, yy):
        zz = me.outward(i)
        from_core(dyall, 1, zz, yy)
        backward(zz * 2 + yy)

    def with_dy(j, p):
        if p == -1:

            pl.when(j == 5)(lambda: lead(1, 3))

            def late(n, carry):
                inputs(jnp.where(n == 0, 2, 3), jnp.where(n == 1, y, 1 - y))
                return carry

            @pl.when(j > 3)
            def _():
                lax.fori_loop((j - 4) * 2, j - 2, late, 0)

        elif p == 0:
            pl.when((j > 0) & (j < 4))(lambda: inputs(j - 1, y))
        elif p == CUTS - 1:

            @pl.when(j == 0)
            def _():
                lax.fori_loop(1, 32, tell, 0)
                close_sum(0)

            pl.when((j > 1) & (j < 4))(lambda: inputs(j - 2, 1 - y))

    gather(dyall, 1, with_dy)

    def in_grad(i):
        col = pl.ds(pl.multiple_of(i * 256, 256), 256)
        rows = nall[:, :, col].reshape(2048, 256)
        dwin[col, :] = lax.dot_general(
            rows, dpairs[...].reshape(2048, 768), TN, preferred_element_type=F32
        ).astype(BF)

    def out_grad(k, there):
        i = there // 24 * 3 + k
        col = pl.ds(pl.multiple_of(i * 256, 256), 256)
        right = dyall[:, :, col].reshape(2048, 256)
        value = lax.dot_general(zg[...].reshape(2048, 384), right, TN, preferred_element_type=F32)
        part_col = pl.ds(pl.multiple_of(k * 256, 256), 256)
        dwout[:, there : there + 24, part_col] = value.reshape(16, 24, 256)

    def over_in(k):
        src = dwin.at[pl.ds(pl.multiple_of((1 - x) * 768 + k * 256, 256), 256)]
        return remote(src, dwin_in.at[pl.ds(pl.multiple_of(k * 256, 256), 256)], xsend.at[5 + k], xrecv.at[5 + k], me.near("x"))

    def over_out():
        return remote(slab, dwout_in, xsend.at[8], xrecv.at[8], me.near("x"))

    def leads(j, carry):
        lead(1, j)
        return carry

    lax.fori_loop(0, 3, leads, 0)

    def hear(k, carry):
        left(errs.at[0], esend.at[k], me)
        s = ((x + k // 16) % 2) * 16 + (b + k) % 16
        arrived(errs.at[s], erecv.at[s], me)
        return carry

    def sums(j, carry):
        @pl.when(j == 3)
        def _():
            close_gather(dyall, 1)
            lax.fori_loop(1, 32, hear, 0)
            total = errs[0]
            for s in range(1, 32):
                total = total + errs[s]
            err[...] = total / (1536.0 * count[...])

        @pl.when(j == 0)
        def _():
            def one(k, carry):
                in_grad((1 - x) * 3 + k)
                over_in(k).start()
                return carry

            lax.fori_loop(0, 3, one, 0)

        @pl.when(j == 1)
        def _():
            def one(k, carry):
                out_grad(k, 0)
                out_grad(k, 24)
                return carry

            lax.fori_loop(0, 3, one, 0)
            slab[...] = dwout[...].astype(BF)
            pl.when(c != x)(lambda: over_out().start())

        @pl.when(j == 2)
        def _():
            def one(k, carry):
                in_grad(x * 3 + k)
                return carry

            lax.fori_loop(0, 3, one, 0)

        follow(1, j)
        return carry

    for k in range(4):
        over_weights(k).wait_send()
    pl.when(c == x)(lambda: over_down().wait_send())
    lax.fori_loop(0, 4, sums, 0)
    saved[2].start()
    saved[3].start()
    close_sum(1)

    for k in range(3):
        over_in(k).wait_send()
        here = pl.ds(pl.multiple_of(x * 768 + k * 256, 256), 256)
        there = pl.ds(k * 256, 256)
        arrived(dwin_in.at[there], xrecv.at[5 + k], me)
        dwin_in[there] = (dwin_in[there].astype(F32) + dwin[here, :].astype(F32)).astype(BF)
    out = pltpu.make_async_copy(dwin_in, dwin_out, own_sem.at[0])
    out.start()

    @pl.when(c == x)
    def _():
        arrived(dwout_in, xrecv.at[8], me)
        dwout_in[...] = (dwout_in[...].astype(F32) + dwout[...]).astype(BF)
        copy = pltpu.make_async_copy(dwout_in, dwout_out, own_sem.at[1])
        copy.start()
        copy.wait()

    pl.when(c != x)(lambda: over_out().wait_send())
    for copy in saved + [out]:
        copy.wait()


def run_experts(*operands):
    wide = (128, 1536)
    shard = (16,) + wide
    shape = jax.ShapeDtypeStruct
    return pl.pallas_call(
        experts_kernel,
        out_shape=(
            shape((8, 128), F32),
            shape(wide, BF),
            shape(wide, F32),
            shape(wide, F32),
            shape((768, 768), BF),
            shape((16, 48, 768), BF),
        ),
        in_specs=[ANY] * 9,
        out_specs=(ANY,) * 6,
        scratch_shapes=[
            pltpu.VMEM((TOP, 128), jnp.int32),
            pltpu.VMEM((TOP, 128), F32),
            pltpu.VMEM((1, 128), jnp.int32),
            pltpu.VMEM((8, 128), F32),
            pltpu.VMEM((8, 128), F32),
            pltpu.VMEM(wide, F32),
            pltpu.VMEM(wide, BF),
            pltpu.VMEM(wide, BF),
            pltpu.VMEM(wide, F32),
            pltpu.VMEM(shard, BF),
            pltpu.VMEM(shard, BF),
            pltpu.VMEM((8, 256, 768), F32),
            pltpu.VMEM((8, 256, 384), BF),
            pltpu.VMEM((8, 256, 768), BF),
            pltpu.VMEM(shard, BF),
            pltpu.VMEM((8,) + wide, BF),
            pltpu.VMEM((4,) + wide, BF),
            pltpu.VMEM((5,) + wide, BF),
            pltpu.VMEM((2, 5, PARTS[CUTS][1], 1536), BF),
            pltpu.VMEM((PARTS[CUTS][1], 1536), BF),
            pltpu.VMEM((PARTS[CUTS][1], 1536), F32),
            pltpu.VMEM(wide, F32),
            pltpu.VMEM((32, 8, 128), F32),
            pltpu.VMEM((16, 8, 128), F32),
            pltpu.VMEM((16, 128, 1), F32),
            pltpu.VMEM((2, 16, 48, 768), BF),
            pltpu.VMEM((16, 48, 768), BF),
            pltpu.VMEM((384, 1536), BF),
            pltpu.VMEM((1536, 768), BF),
            pltpu.VMEM((768, 768), BF),
            pltpu.VMEM((16, 48, 768), F32),
            pltpu.VMEM((16, 48, 768), BF),
            DMA((7,)),
            DMA((2,)),
            DMA((2, 4, CUTS + 1, 7)),
            DMA((2, 16, CUTS + 1)),
            DMA((2, 8)),
            DMA((2, 8)),
            DMA((2, 4, CUTS + 1)),
            DMA((2, 4, CUTS + 1)),
            DMA((2, 4, CUTS + 2, 2)),
            DMA((2, 5, CUTS + 2)),
            DMA((32,)),
            DMA((32,)),
            DMA((16,)),
            DMA((16,)),
            DMA((9,)),
            DMA((9,)),
        ],
        compiler_params=params(2, 62),
        name="experts",
    )(*operands)


def norm_back(values, gain, grad):
    scale = lax.rsqrt(jnp.mean(values * values, axis=-1, keepdims=True) + 1e-06)
    inner = grad * gain
    mean = jnp.mean(inner * values, axis=-1, keepdims=True)
    return scale * inner - values * (scale * scale * scale * mean), jnp.sum(
        grad * values * scale, axis=0, keepdims=True
    )


Q_PIECES = ((0, 1536),)
LAST = (1536, 640)


def back_kernel(
    doc_in, freq_in, gains_in, states_in, h_in, n1_in, qs_in, o_in, lse_in, dn2_in, dy_in, dwin, dwout, gq, go, kv_in,
    gx_out, gqw, gkw, gvw, gnorm_out, gout_out, gup, gdown,
    doc, freq, gains, gnorm, states, h, n1, qs, o, lse, dn2, dy, gx, gout, gkv,
    wq, wo, kv, pk, pw, dos, delta, dh, dq, dkv, dqkv, gqkv, *rest,
):
    sums = [(rest[i * 11 : i * 11 + 6], rest[i * 11 + 6 : i * 11 + 11]) for i in range(4)]
    load_sem, own_sem, asend, arecv, osend, orecv = rest[44:]
    me = Place()
    greet_all(me)
    x, y, z, b, c = me.x, me.y, me.z, me.b, me.c
    loads = [
        pltpu.make_async_copy(go, wo, own_sem.at[0]),
        pltpu.make_async_copy(kv_in, kv, own_sem.at[1]),
        pltpu.make_async_copy(gq, wq, own_sem.at[2]),
    ]
    small = [
        pltpu.make_async_copy(src, dst, load_sem.at[i])
        for i, (src, dst) in enumerate(
            (
                (h_in, h), (dn2_in, dn2), (dy_in, dy), (o_in, o), (qs_in, qs), (lse_in, lse),
                (n1_in, n1), (states_in, states), (doc_in, doc), (freq_in, freq), (gains_in, gains),
            )
        )
    ]
    for load in small[:3] + [small[10], loads[0]] + small[3:10] + [loads[1], loads[2]]:
        load.start()
    all_greeted()

    def own_piece(n):
        col = pl.multiple_of(n * 768 + c * 384, 128)
        return pltpu.make_async_copy(
            dwin.at[b, :, pl.ds(n * 384, 384)], gup.at[b // 2, :, pl.ds(col, 384)], own_sem.at[3 + n]
        )

    def own_down():
        return pltpu.make_async_copy(dwout.at[b], gdown.at[b // 2], own_sem.at[5])

    def deal(k, carry):
        t = (b + (k * 9) % 16) % 16
        for n in range(2):
            col = pl.multiple_of(n * 768 + c * 384, 128)
            remote(
                dwin.at[t, :, pl.ds(n * 384, 384)],
                gup.at[b // 2, :, pl.ds(col, 384)],
                asend.at[k, n],
                arecv.at[b, n],
                (x, t),
            ).start()
        pl.when(c == x)(
            lambda: remote(dwout.at[t], gdown.at[b // 2], osend.at[k], orecv.at[b // 2], (x, t)).start()
        )
        return carry

    for n in range(2):
        own_piece(n).start()
    pl.when(c == x)(lambda: own_down().start())
    lax.fori_loop(1, 16, deal, 0)
    for load in small[:3] + small[8:]:
        load.wait()
    res_grad, gain_two = norm_back(h[...], gains[1:2], dn2[...])
    dh[...] = dy[...] + res_grad
    da = dh[...].astype(BF)
    loads[0].wait()
    do = lax.dot_general(
        da, wo[...].reshape(1536, 1536), NT, preferred_element_type=F32
    ).astype(BF)
    small[3].wait()
    low = o[...].astype(BF)
    for i in range(4):
        part = lax.dot_general(low[:, i * 384 : i * 384 + 384], da, TN, preferred_element_type=F32)
        wo[i * 8 : i * 8 + 8] = part.astype(BF).reshape(8, 48, 1536)
    out_sum = Sum(me, wo, by_weight, gout, *sums[0])
    key_sum = Sum(me, pk, by_token, dkv, *sums[1], causal=True)

    def lead_all(which):
        def one(j, carry):
            which.lead(j)
            return carry

        lax.fori_loop(0, 4, one, 0)

    lead_all(out_sum)
    for i in range(QUERY_HEADS):
        col, r = i * 128, (i % GROUP) * 128
        dos[i // GROUP, r : r + 128] = do[:, col : col + 128]
        prod = do[:, col : col + 128].astype(F32) * o[:, col : col + 128]
        delta[i // GROUP, :, r : r + 128] = jnp.sum(prod.T, axis=0, keepdims=True)
    dq[...] = jnp.zeros_like(dq)
    bounds = query_bounds(me, doc)
    loads[1].wait()
    for load in small[4:6]:
        load.wait()

    def block(n):
        ok = allowed_keys(n * 256, bounds)
        for i in range(2):
            k = kv[pl.ds(n * 2, 2), :, i * 128 : i * 128 + 128].reshape(256, 128)
            v = kv[pl.ds(n * 2, 2), :, 256 + i * 128 : 384 + i * 128].reshape(256, 128)
            s = lax.dot_general(k, qs[i], NT, preferred_element_type=F32)
            p = jnp.where(ok, jnp.exp2(s * POWER - lse[i]), 0.0)
            dp = lax.dot_general(v, dos[i], NT, preferred_element_type=F32)
            ds = (p * (dp - delta[i])).astype(BF)
            dv = jnp.dot(p.astype(BF), dos[i], preferred_element_type=F32)
            dk = jnp.dot(ds, qs[i], preferred_element_type=F32) * SCALE
            pk[pl.ds(n * 2, 2), :, i * 128 : i * 128 + 128] = dk.astype(BF).reshape(2, 128, 128)
            pk[pl.ds(n * 2, 2), :, 256 + i * 128 : 384 + i * 128] = dv.astype(BF).reshape(2, 128, 128)
            dq[i] += lax.dot_general(k, ds, TN, preferred_element_type=F32)

    def turn(j, carry):
        out_sum.turn(j)

        @pl.when(key_sum.valid(j))
        def _():
            last = jnp.where(j == z, y * 2 + c, 3)

            def one(n, carry):
                block(j * 4 + n)
                return carry

            lax.fori_loop(0, last + 1, one, 0)

            def blank(n, carry):
                pk[pl.ds((j * 4 + n) * 2, 2)] = jnp.zeros((2, 128, 512), BF)
                return carry

            lax.fori_loop(last + 1, 4, blank, 0)
            key_sum.lead(j)

        key_sum.turn(j)
        return carry

    lax.fori_loop(0, 4, turn, 0)

    cos, sin = rotary_tables(me, doc, freq)
    for load in small[6:8] + [loads[2]]:
        load.wait()
    for i in range(QUERY_HEADS):
        r = (i % GROUP) * 128
        head = dq[i // GROUP, :, r : r + 128].T * SCALE
        dqkv[:, i * 128 : i * 128 + 128] = turned(head, cos, -sin).astype(BF)

    def weight_grad(start, width):
        for i in range(4):
            part = lax.dot_general(
                n1[:, i * 384 : i * 384 + 384], dqkv[:, start : start + width], TN, preferred_element_type=F32
            )
            pw[i * 8 : i * 8 + 8, :, start : start + width] = part.astype(BF).reshape(8, 48, width)

    weight_grad(0, 1536)
    proj = [Sum(me, pw, by_weight, gqkv, *sums[2 + i], Q_PIECES[i]) for i in range(1)]
    rest_sum = Sum(me, pw, by_weight, gqkv, *sums[3], LAST)
    for piece in proj:
        lead_all(piece)

    stores = [
        pltpu.make_async_copy(gx, gx_out, load_sem.at[0]),
        pltpu.make_async_copy(gout, gout_out, load_sem.at[1]),
        pltpu.make_async_copy(gqkv.at[:, pl.ds(0, 1536)], gqw, load_sem.at[2]),
        pltpu.make_async_copy(gkv.at[:, pl.ds(0, 256)], gkw, load_sem.at[3]),
        pltpu.make_async_copy(gkv.at[:, pl.ds(256, 256)], gvw, load_sem.at[4]),
        pltpu.make_async_copy(gnorm, gnorm_out, load_sem.at[5]),
    ]

    def close_deal(k, carry):
        f = (b + 16 - k) % 16
        for n in range(2):
            left(dwin.at[0, :, pl.ds(0, 384)], asend.at[k, n], me)
            col = pl.multiple_of(n * 768 + (f % 2) * 384, 128)
            arrived(gup.at[f // 2, :, pl.ds(col, 384)], arecv.at[f, n], me)
        pl.when(c == x)(lambda: left(dwout.at[0], osend.at[k], me))
        pl.when(f % 2 == x)(lambda: arrived(gdown.at[f // 2], orecv.at[f // 2], me))
        return carry

    def last_turn(j, carry):
        out_sum.turn(j + 4)
        pl.when(j < 2)(lambda: key_sum.turn(j + 4))
        for piece in proj:
            piece.turn(j)

        @pl.when(j == 1)
        def _():
            for i in range(2):
                part = dkv[:, i * 128 : i * 128 + 128]
                dqkv[:, 1536 + i * 128 : 1664 + i * 128] = turned(part, cos, -sin).astype(BF)
            dqkv[:, 1792:2048] = dkv[:, 256:512].astype(BF)
            weight_grad(1536, 512)
            dn1 = lax.dot_general(
                dqkv[...], wq[:, :, pl.ds(0, QKV)].reshape(1536, QKV), NT, preferred_element_type=F32
            )
            in_grad, gain_one = norm_back(states[...].astype(F32), gains[0:1], dn1)
            rows = lax.broadcasted_iota(jnp.int32, (128, 1536), 0)
            tail = jnp.where(rows == 0, gain_one, jnp.where(rows == 1, gain_two, 0.0)).T
            pw[:, :, pl.ds(QKV, 128)] = tail.astype(BF).reshape(32, 48, 128)
            lead_all(rest_sum)
            gx[...] = dh[...] + in_grad
            rest_sum.first_legs()

        rest_sum.rest(j - 2)

        @pl.when(j == 2)
        def _():
            stores[0].start()
            stores[1].start()
            out_sum.close()

        @pl.when(j == 3)
        def _():
            key_sum.close()
            lax.fori_loop(1, 16, close_deal, 0)

        @pl.when(j == 5)
        def _():
            stores[2].start()
            for piece in proj:
                piece.close()

        return carry

    lax.fori_loop(0, 7, last_turn, 0)
    gkv[...] = gqkv[:, 1536:2048]
    for store in stores[3:5]:
        store.start()
    gnorm[0:1, 0:48] = as_row(gqkv[:, 2048:2049])
    gnorm[1:2, 0:48] = as_row(gqkv[:, 2049:2050])
    stores[5].start()
    rest_sum.close()

    for n in range(2):
        own_piece(n).wait()
    pl.when(c == x)(lambda: own_down().wait())
    for store in stores:
        store.wait()


def run_back(*operands):
    shape = jax.ShapeDtypeStruct
    return pl.pallas_call(
        back_kernel,
        out_shape=(
            shape((128, 1536), F32),
            shape((48, 1536), F32),
            shape((48, 256), F32),
            shape((48, 256), F32),
            shape((8, 128), F32),
            shape((48, 1536), F32),
            shape((8, 48, 1536), BF),
            shape((8, 48, 768), BF),
        ),
        in_specs=[ANY] * 16,
        out_specs=(ANY,) * 8,
        scratch_shapes=[
            pltpu.VMEM(operands[0].shape, jnp.int32),
            pltpu.VMEM((1, 128), F32),
            pltpu.VMEM((8, 1536), F32),
            pltpu.VMEM((8, 128), F32),
            pltpu.VMEM((128, 1536), BF),
            pltpu.VMEM((128, 1536), F32),
            pltpu.VMEM((128, 1536), BF),
            pltpu.VMEM((2, LANES, 128), BF),
            pltpu.VMEM((128, 1536), F32),
            pltpu.VMEM((2, 1, LANES), F32),
            pltpu.VMEM((128, 1536), F32),
            pltpu.VMEM((128, 1536), F32),
            pltpu.VMEM((128, 1536), F32),
            pltpu.VMEM((48, 1536), F32),
            pltpu.VMEM((48, 512), F32),
            pltpu.VMEM((32, 48, WIDE), BF),
            pltpu.VMEM((32, 48, 1536), BF),
            pltpu.VMEM((32, 128, 512), BF),
            pltpu.VMEM((32, 128, 512), BF),
            pltpu.VMEM((32, 48, WIDE), BF),
            pltpu.VMEM((2, LANES, 128), BF),
            pltpu.VMEM((2, 1, LANES), F32),
            pltpu.VMEM((128, 1536), F32),
            pltpu.VMEM((2, 128, LANES), F32),
            pltpu.VMEM((128, 512), F32),
            pltpu.VMEM((128, QKV), BF),
            pltpu.VMEM((48, WIDE), F32),
        ]
        + Sum.room(48, 1536)
        + Sum.room(128, 512)
        + Sum.room(48, 1536)
        + Sum.room(48, LAST[1])
        + [DMA((11,)), DMA((6,)), DMA((16, 2)), DMA((16, 2)), DMA((16,)), DMA((8,))],
        compiler_params=params(3, 62),
        name="back",
    )(*operands)


def finish_kernel(
    err_in, gnorm_in, final, gx, gqw, gkw, gvw, gout, gup, gdown,
    loss_out, one_out, two_out, final_out, gx_out, gqw_out, gkw_out, gvw_out, gout_out, gup_out, gdown_out,
    low_up, low_down, wide_up, wide_down, *rest,
):
    rooms, (err, gnorm, loss, one, two, sem, out_sem) = rest[:6], rest[6:]
    whole = (
        (gup, low_up), (gdown, low_down), *zip((final, gx, gqw, gkw, gvw, gout), rooms), (err_in, err), (gnorm_in, gnorm)
    )
    copies = [pltpu.make_async_copy(src, dst, sem.at[i]) for i, (src, dst) in enumerate(whole)]
    for copy in copies:
        copy.start()
    outs = (final_out, gx_out, gqw_out, gkw_out, gvw_out, gout_out)
    last = []
    for i in range(6):
        copies[2 + i].wait()
        last.append(pltpu.make_async_copy(rooms[i], outs[i], out_sem.at[i]))
        last[i].start()
    copies[0].wait()
    wide_up[...] = low_up[...].astype(F32)
    last.append(pltpu.make_async_copy(wide_up, gup_out, out_sem.at[6]))
    last[6].start()
    copies[1].wait()
    for e in range(E):
        wide = low_down[e].astype(F32)
        wide_down[e, :, :768] = wide[:24]
        wide_down[e, :, 768:] = wide[24:]
    last.append(pltpu.make_async_copy(wide_down, gdown_out, out_sem.at[7]))
    last[7].start()
    copies[8].wait()
    copies[9].wait()
    loss[...] = err[0:1, 0:1]
    one[...] = gnorm[0:1, 0:48]
    two[...] = gnorm[1:2, 0:48]
    for i, (src, dst) in enumerate(((loss, loss_out), (one, one_out), (two, two_out))):
        last.append(pltpu.make_async_copy(src, dst, out_sem.at[8 + i]))
        last[8 + i].start()
    for copy in last:
        copy.wait()


def run_finish(*operands):
    shape = jax.ShapeDtypeStruct
    up, down = (8, 48, 1536), (8, 24, 1536)
    return pl.pallas_call(
        finish_kernel,
        out_shape=(
            shape((1, 1), F32),
            shape((1, 48), F32),
            shape((1, 48), F32),
            shape((128, 1536), BF),
            shape((128, 1536), F32),
            shape((48, 1536), F32),
            shape((48, 256), F32),
            shape((48, 256), F32),
            shape((48, 1536), F32),
            shape(up, F32),
            shape(down, F32),
        ),
        in_specs=[ANY] * 10,
        out_specs=(ANY,) * 11,
        scratch_shapes=[
            pltpu.VMEM(up, BF),
            pltpu.VMEM((8, 48, 768), BF),
            pltpu.VMEM(up, F32),
            pltpu.VMEM(down, F32),
            pltpu.VMEM((128, 1536), BF),
            pltpu.VMEM((128, 1536), F32),
            pltpu.VMEM((48, 1536), F32),
            pltpu.VMEM((48, 256), F32),
            pltpu.VMEM((48, 256), F32),
            pltpu.VMEM((48, 1536), F32),
            pltpu.VMEM((8, 128), F32),
            pltpu.VMEM((8, 128), F32),
            pltpu.VMEM((1, 1), F32),
            pltpu.VMEM((1, 48), F32),
            pltpu.VMEM((1, 48), F32),
            DMA((10,)),
            DMA((11,)),
        ],
        compiler_params=pltpu.CompilerParams(vmem_limit_bytes=60 << 20),
        name="finish",
    )(*operands)


def per_device(
    states, teacher, valid, routes, gates, doc_starts, norm_one,
    w_query, key_weight, value_weight, w_output, norm_two, expert_in, expert_out,
):
    tokens = states.shape[2]
    width = states.shape[3]
    half = HEAD_SIZE // 2
    freq = np.float32(ROTARY_BASE) ** (-np.arange(half).astype(np.float32) / np.float32(half))
    freq = jnp.asarray(np.concatenate([freq, freq])[None, :], F32)
    rows = states.reshape(tokens, width)
    kept = valid.reshape(1, tokens)
    doc = doc_starts.reshape(1, -1)
    gq, go, kv, win, wout, h, n2, n1, qs, o, lse, count, gains = run_front(
        doc, freq, norm_one.reshape(1, -1), norm_two.reshape(1, -1), kept, rows, expert_out,
        w_query, key_weight, value_weight, w_output, expert_in,
    )
    error, final, dn2, dy, dwin, dwout = run_experts(
        routes.reshape(tokens, TOP).T, gates.reshape(tokens, TOP).T, kept, count,
        n2, h, teacher.reshape(tokens, width), win, wout,
    )
    gx, gqw, gkw, gvw, gnorm, gout, gup, gdown = run_back(
        doc, freq, gains, rows, h, n1, qs, o, lse, dn2, dy, dwin.reshape(16, 48, 768), dwout, gq, go, kv
    )
    loss, one, two, final, gx, gqw, gkw, gvw, gout, gup, gdown = run_finish(
        error, gnorm, final, gx, gqw, gkw, gvw, gout, gup, gdown
    )
    shape = states.shape
    return (
        final.reshape(shape),
        loss.reshape(()),
        gx.reshape(shape),
        one.reshape(-1),
        gqw,
        gkw,
        gvw,
        gout,
        two.reshape(-1),
        gup,
        gdown,
    )


def solution(mesh):
    in_specs = (
        P("blk", "head", None, None),
        P("blk", "head", None, None),
        P("blk", "head", None),
        P("blk", "head", None, None),
        P("blk", "head", None, None),
        P(),
        P(("head", "blk")),
        P(("head", "blk"), None),
        P(("head", "blk"), None),
        P(("head", "blk"), None),
        P(("head", "blk"), None),
        P(("head", "blk")),
        P(None, ("head", "blk"), None),
        P(None, ("head", "blk"), None),
    )
    out_specs = (
        P("blk", "head", None, None),
        P(),
        P("blk", "head", None, None),
        P(("head", "blk")),
        P(("head", "blk"), None),
        P(("head", "blk"), None),
        P(("head", "blk"), None),
        P(("head", "blk"), None),
        P(("head", "blk")),
        P(None, ("head", "blk"), None),
        P(None, ("head", "blk"), None),
    )
    sizes = dict(mesh.shape)
    plan = per_device if sizes == {"head": 2, "blk": 4 * NZ} else per_device_plain
    return jax.shard_map(
        plan, mesh=mesh, in_specs=in_specs, out_specs=out_specs, check_vma=False
    )
```
